32 devices in a mesh: dp: 4 (over x, core), fsdp: 8 (over z, y).
Axes of the slice: x: 2, y: 2, z: 4, core: 2. Of those that a mesh axis runs over, the one named last changes fastest.
Arguments:
- tokens: bfloat16 [32768, 768], P(('dp', 'fsdp')), may hold values from -6 to 6
- lengths: int32 [64], P(('dp', 'fsdp')), may hold values from 65 to 512, as said below
- w_qkv: bfloat16 [768, 2304], P(('dp', 'fsdp')), may hold values from -0.21875 to 0.21875
- bias_q: bfloat16 [768], P(('dp', 'fsdp')), may hold values from -3 to 3
- bias_v: bfloat16 [768], P(('dp', 'fsdp')), may hold values from -3 to 3
- w_out: bfloat16 [768, 768], P(('dp', 'fsdp')), may hold values from -0.625 to 0.625
- bias_out: bfloat16 [768], P(('dp', 'fsdp')), may hold values from -3 to 3
- gain_one: bfloat16 [768], P(('dp', 'fsdp')), may hold values from 0.5 to 1.5
- shift_one: bfloat16 [768], P(('dp', 'fsdp')), may hold values from -2 to 2
- w_in: bfloat16 [768, 3072], P(('dp', 'fsdp')), may hold values from -0.21875 to 0.21875
- bias_in: bfloat16 [3072], P(('dp', 'fsdp')), may hold values from -3 to 3
- w_back: bfloat16 [3072, 768], P(('dp', 'fsdp')), may hold values from -0.109375 to 0.109375
- bias_back: bfloat16 [768], P(('dp', 'fsdp')), may hold values from -3 to 3
- gain_two: bfloat16 [768], P(('dp', 'fsdp')), may hold values from 0.5 to 1.5
- shift_two: bfloat16 [768], P(('dp', 'fsdp')), may hold values from -2 to 2
- cotangent: bfloat16 [32768, 768], P(('dp', 'fsdp')), may hold values from -6 to 6
Outputs:
- activations: bfloat16 [32768, 768], P(('dp', 'fsdp'))
- input_grad: bfloat16 [32768, 768], P(('dp', 'fsdp'))
- w_qkv_grad: float32 [768, 2304], P(('dp', 'fsdp'))
- bias_q_grad: float32 [768], P(('dp', 'fsdp'))
- bias_v_grad: float32 [768], P(('dp', 'fsdp'))
- w_out_grad: float32 [768, 768], P(('dp', 'fsdp'))
- bias_out_grad: float32 [768], P(('dp', 'fsdp'))
- gain_one_grad: float32 [768], P(('dp', 'fsdp'))
- shift_one_grad: float32 [768], P(('dp', 'fsdp'))
- w_in_grad: float32 [768, 3072], P(('dp', 'fsdp'))
- bias_in_grad: float32 [3072], P(('dp', 'fsdp'))
- w_back_grad: float32 [3072, 768], P(('dp', 'fsdp'))
- bias_back_grad: float32 [768], P(('dp', 'fsdp'))
- gain_two_grad: float32 [768], P(('dp', 'fsdp'))
- shift_two_grad: float32 [768], P(('dp', 'fsdp'))
The draws below stay inside these ranges and needn't reach their ends.
Inputs may be any that keep to these rules, and one draw needn't show every extreme that they name: Tokens at positions 512 * s + t with t < lengths[s] are real, the rest padding; some sequence has exactly 512.
All inputs are finite; a program needn't handle non-finite values.
Results may differ from the reference program's by a relative error of at most 0.019.
Values may be sent and summed in bfloat16 or wider, within the bound.
No kernel may reach another device: no remote copies, remote signals or barrier semaphores. Data moves between devices by JAX's collectives and lax.ppermute only.
A program may use at most 192 MiB of HBM per device.

```python
import jax
import jax.numpy as jnp
from jax import lax

D = 768
HEADS = 12
HEAD_DIM = 64
FF = 3072
SEQ_LEN = 512
SEQ_DEV = 2
APPS = 2
NSEQ = 64
TOKENS = 32768


def draw_lengths(key, part):
    key = jax.random.fold_in(key, 11)
    kind_key, short_key, long_key, pick_key = jax.random.split(key, 4)
    quarter = max(SEQ_LEN // 4, 1)
    longer = jax.random.randint(kind_key, (NSEQ,), 0, 5) < 3
    short_len = jax.random.randint(short_key, (NSEQ,), SEQ_LEN // 8 + 1, quarter + 1)
    long_len = jax.random.randint(long_key, (NSEQ,), SEQ_LEN // 2 + 1, SEQ_LEN + 1)
    chosen = jnp.where(longer, long_len, short_len)
    picked = jax.random.randint(pick_key, (), 0, NSEQ)
    return jnp.where(jnp.arange(NSEQ) == picked, SEQ_LEN, chosen).astype(jnp.int32)


def block_levels(stream_key, extent, cuts, least, top_value):
    factor_of = 1.0
    for dim, shards_of in cuts:
        steps = jax.random.uniform(jax.random.fold_in(jax.random.fold_in(stream_key, 6), dim), (shards_of,), jnp.float32, least / len(cuts), top_value / len(cuts))
        factor_of = factor_of * jnp.repeat(jnp.exp(steps), extent[dim] // shards_of).reshape((-1,) + (1,) * (len(extent) - 1 - dim))
    return factor_of


def scatter_about(own_key, extent, deviation, most, shards=(), held_as=jnp.bfloat16):
    factor_of = block_levels(own_key, extent, shards, -0.22, 0.18) if shards else 1.0
    values = jax.random.normal(own_key, extent, jnp.float32) * deviation * factor_of
    return jnp.minimum(jnp.maximum(values, -most), most).astype(held_as)


def setup_inputs(seed: int = 0) -> dict:
    key_of = jax.random.split(jax.random.key(seed), 17)
    tokens = scatter_about(key_of[0], (TOKENS, D), 1.0, 6.0, ((0, 32),))
    lengths = draw_lengths(jax.random.fold_in(key_of[16], 71), 0)
    w_qkv = scatter_about(key_of[2], (D, 3 * D), D ** -0.5, 0.21875, ((0, 32),))
    bias_q = scatter_about(key_of[3], (D,), 0.5, 3.0, ((0, 32),))
    bias_v = scatter_about(key_of[4], (D,), 0.5, 3.0, ((0, 32),))
    w_out = scatter_about(key_of[5], (D, D), (D // 8) ** -0.5, 0.625, ((0, 32),))
    bias_out = scatter_about(key_of[6], (D,), 0.5, 3.0, ((0, 32),))
    gain_one = jnp.clip(1.0 + 0.1 * jax.random.normal(key_of[7], (D,), jnp.float32), 0.5, 1.5).astype(jnp.bfloat16)
    shift_one = scatter_about(key_of[8], (D,), 0.3, 2.0, ((0, 32),))
    w_in = scatter_about(key_of[9], (D, FF), D ** -0.5, 0.21875, ((0, 32),))
    bias_in = scatter_about(key_of[10], (FF,), 0.5, 3.0, ((0, 32),))
    w_back = scatter_about(key_of[11], (FF, D), FF ** -0.5, 0.109375, ((0, 32),))
    bias_back = scatter_about(key_of[12], (D,), 0.5, 3.0, ((0, 32),))
    gain_two = jnp.clip(1.0 + 0.1 * jax.random.normal(key_of[13], (D,), jnp.float32), 0.5, 1.5).astype(jnp.bfloat16)
    shift_two = scatter_about(key_of[14], (D,), 0.3, 2.0, ((0, 32),))
    cotangent = scatter_about(key_of[15], (TOKENS, D), 1.0, 6.0, ((0, 32),))
    return dict(tokens=tokens, lengths=lengths, w_qkv=w_qkv, bias_q=bias_q, bias_v=bias_v, w_out=w_out, bias_out=bias_out, gain_one=gain_one, shift_one=shift_one, w_in=w_in, bias_in=bias_in, w_back=w_back, bias_back=bias_back, gain_two=gain_two, shift_two=shift_two, cotangent=cotangent)


highest = lax.Precision.HIGHEST

@jax.custom_vjp
def low(v):
    return lax.optimization_barrier(v.astype(jnp.bfloat16)).astype(jnp.float32)

@jax.custom_vjp
def low_back(v):
    return v

def low_keep(v):
    return (low(v), None)

def low_pass(kept, grad):
    return (grad,)

def back_keep(v):
    return (v, None)

def back_low(kept, grad):
    return (low(grad),)
low.defvjp(low_keep, low_pass)
low_back.defvjp(back_keep, back_low)

def normalize(value, gain, shift):
    centered = value - lax.optimization_barrier(jnp.mean(value, axis=-1, keepdims=True))
    variance = lax.optimization_barrier(jnp.mean(centered * centered, axis=-1, keepdims=True))
    return centered * lax.rsqrt(variance + 1e-12) * gain + shift

def shared_layer(inputs, params, valid_keys):
    w_qkv, bias_q, bias_v, w_out, bias_out, gain_one, shift_one, w_in, bias_in, w_back, bias_back, gain_two, shift_two = params
    count = valid_keys.shape[0]
    projected = jnp.dot(low(inputs), w_qkv, precision=highest)
    queries = low(low_back(projected[:, :D] + bias_q))
    key_rows = low(low_back(projected[:, D:2 * D]))
    value_rows = low(low_back(projected[:, 2 * D:] + bias_v))
    shape_four = (count, SEQ_LEN, HEADS, HEAD_DIM)
    scores = jnp.einsum('sqhd,skhd->shqk', queries.reshape(shape_four), key_rows.reshape(shape_four), precision=highest) * 0.125
    scores = low_back(scores)
    scores = jnp.where(valid_keys[:, None, None, :], scores, -1e+30)
    probs = low(jax.nn.softmax(scores, axis=-1))
    context = jnp.einsum('shqk,skhd->sqhd', probs, value_rows.reshape(shape_four), precision=highest)
    context = low(low_back(context.reshape(count * SEQ_LEN, D)))
    attended = low_back(jnp.dot(context, w_out, precision=highest) + bias_out)
    middle = normalize(inputs + attended, gain_one, shift_one)
    before = low_back(jnp.dot(low(middle), w_in, precision=highest) + bias_in)
    hidden = low(jax.nn.gelu(before, approximate=True))
    branch = low_back(jnp.dot(hidden, w_back, precision=highest) + bias_back)
    return normalize(middle + branch, gain_two, shift_two)

def reference(tokens, lengths, w_qkv, bias_q, bias_v, w_out, bias_out, gain_one, shift_one, w_in, bias_in, w_back, bias_back, gain_two, shift_two, cotangent):
    params = tuple((item.astype(jnp.float32) for item in (w_qkv, bias_q, bias_v, w_out, bias_out, gain_one, shift_one, w_in, bias_in, w_back, bias_back, gain_two, shift_two)))
    groups = NSEQ // SEQ_DEV
    inputs = tokens.astype(jnp.float32).reshape(groups, SEQ_DEV * SEQ_LEN, D)
    out_grads = cotangent.astype(jnp.float32).reshape(groups, SEQ_DEV * SEQ_LEN, D)
    seq_lengths = lengths.reshape(groups, SEQ_DEV)
    positions = jnp.arange(SEQ_LEN, dtype=jnp.int32)

    def one_group(running, pieces):
        block, block_grad, block_lengths = pieces
        valid_keys = positions[None, :] < block_lengths[:, None]

        def stacked(start, *weights):
            current = start
            for step in range(APPS):
                current = shared_layer(current, weights, valid_keys)
            return current
        result, pullback = jax.vjp(stacked, block, *params)
        grads = pullback(block_grad)
        running = tuple((held + added for held, added in zip(running, grads[1:])))
        return (running, (result, grads[0]))
    zeros = tuple((jnp.zeros_like(item) for item in params))
    totals, (results, input_grads) = lax.scan(one_group, zeros, (inputs, out_grads, seq_lengths))
    return (results.reshape(TOKENS, D).astype(jnp.bfloat16), input_grads.reshape(TOKENS, D).astype(jnp.bfloat16), totals[0], totals[1], totals[2], totals[3], totals[4], totals[5], totals[6], totals[7], totals[8], totals[9], totals[10], totals[11], totals[12])
```

```python
import jax
import jax.numpy as jnp
from jax import lax
from jax.experimental import pallas as pl
from jax.experimental.pallas import tpu as pltpu
from jax.sharding import PartitionSpec as P

D = 768
HEADS = 12
HEAD_DIM = 64
APPS = 2
PAIR = 2 * HEAD_DIM
AXES = ("dp", "fsdp")
BF = jnp.bfloat16
F32 = jnp.float32
NN = (((1,), (0,)), ((), ()))
NT = (((1,), (1,)), ((), ()))
TN = (((0,), (0,)), ((), ()))
VMEM = 56 * 2**20
BQ, BV, BO, G1, S1, BB, G2, S2 = range(8)


def mm(left, right, dims):
    return lax.dot_general(left, right, dims, preferred_element_type=F32)


def params(limit=VMEM):
    return pltpu.CompilerParams(vmem_limit_bytes=limit)


def cost(flops, nbytes, trans=0):
    return pl.CostEstimate(flops=int(flops), bytes_accessed=int(nbytes), transcendentals=int(trans))


def once(shape, index):
    return pl.BlockSpec(shape, index, pipeline_mode=pl.Buffered(1))


def normed(z):
    centered = z - jnp.mean(z, axis=-1, keepdims=True)
    root = lax.rsqrt(jnp.mean(centered * centered, axis=-1, keepdims=True) + 1e-12)
    return centered * root, root


def normed_back(n, root, e):
    return root * (e - jnp.mean(e, axis=-1, keepdims=True) - n * jnp.mean(e * n, axis=-1, keepdims=True))


def colsum(v):
    return jnp.sum(v, axis=0, keepdims=True)


def qkv_body(x_ref, w_ref, vec_ref, o_ref, xt_ref):
    part = pl.program_id(0)

    @pl.when(part == 0)
    def _():
        xt_ref[...] = x_ref[...].T

    acc = mm(x_ref[...], w_ref[...], NN)
    bias = jnp.where(part == 0, vec_ref[BQ : BQ + 1, :], jnp.where(part == 2, vec_ref[BV : BV + 1, :], 0.0))
    o_ref[...] = (acc + bias).astype(BF)


def qkv_call(x, w, vec):
    rows = x.shape[0]
    return pl.pallas_call(
        qkv_body,
        grid=(3,),
        in_specs=[
            once((rows, D), lambda i: (0, 0)),
            pl.BlockSpec((D, D), lambda i: (0, i)),
            once((8, D), lambda i: (0, 0)),
        ],
        out_specs=[pl.BlockSpec((rows, D), lambda i: (0, i)), pl.BlockSpec((D, rows), lambda i: (0, 0))],
        out_shape=[jax.ShapeDtypeStruct((rows, 3 * D), BF), jax.ShapeDtypeStruct((D, rows), BF)],
        compiler_params=params(),
        cost_estimate=cost(6 * rows * D * D, 2 * (rows * D * 5 + 3 * D * D)),
        name="qkv",
    )(x, w, vec)


def attend_body(seq, pairs, len_ref, q_ref, k_ref, v_ref, o_ref, l_ref):
    count = len_ref[pl.program_id(0)]
    lane = lax.broadcasted_iota(jnp.int32, (seq, PAIR), 1)
    ok = lax.broadcasted_iota(jnp.int32, (1, seq), 1) < count
    units = [(pr, h) for pr in range(pairs) for h in range(2)]

    def score(unit):
        pr, h = unit
        cols = slice(pr * PAIR, (pr + 1) * PAIR)
        mine = (lane >= HEAD_DIM) == (h == 1)
        q = jnp.where(mine, q_ref[:, cols] * BF(0.125), BF(0))
        return jnp.where(ok, mm(q, k_ref[:, cols], NT), -1e30)

    ahead = score(units[0])
    held = {}
    for i, (pr, h) in enumerate(units):
        s = ahead
        if i + 1 < len(units):
            ahead = score(units[i + 1])
        cols = slice(pr * PAIR, (pr + 1) * PAIR)
        top = jnp.max(s, axis=1, keepdims=True)
        p = jnp.exp(s - top)
        total = jnp.sum(p, axis=1, keepdims=True)
        held[h] = mm(p.astype(BF), v_ref[:, cols], NN) / total
        l_ref[0, pr, h : h + 1, :] = (top + jnp.log(total)).reshape(1, seq)
        if h == 1:
            o_ref[:, cols] = jnp.where(lane < HEAD_DIM, held[0], held[1]).astype(BF)


def attend_call(qkv, lengths, pairs=3):
    rows = qkv.shape[0]
    count = lengths.shape[0]
    seq = rows // count
    groups = D // PAIR // pairs
    wide = PAIR * pairs

    def part(o):
        return pl.BlockSpec((seq, wide), lambda s, p, n: (s, o * groups + p))

    def body(*refs):
        attend_body(seq, pairs, *refs)

    flops = 4 * count * HEADS * seq * seq * HEAD_DIM
    return pl.pallas_call(
        body,
        grid_spec=pltpu.PrefetchScalarGridSpec(
            num_scalar_prefetch=1,
            grid=(count, groups),
            in_specs=[part(0), part(1), part(2)],
            out_specs=[part(0), pl.BlockSpec((1, pairs, 2, seq), lambda s, p, n: (s, p, 0, 0))],
        ),
        out_shape=[
            jax.ShapeDtypeStruct((rows, D), BF),
            jax.ShapeDtypeStruct((count, D // PAIR, 2, seq), F32),
        ],
        compiler_params=params(),
        cost_estimate=cost(4 * flops, 8 * rows * D, count * HEADS * seq * seq),
        name="attend",
    )(lengths, qkv, qkv, qkv)


def gelu_both(u):
    a = 0.7978845608028654
    sq = u * u
    t = jnp.tanh(u * (a + (a * 0.044715) * sq))
    half = 0.5 + 0.5 * t
    slope = half + (u * (0.5 - 0.5 * t * t)) * (a + (3 * a * 0.044715) * sq)
    return u * half, slope


def ffn_body(
    steps, x_ref, ctx_ref, wo_ref, vec_ref, wi_ref, bi_ref, wb_ref,
    z1_ref, h1t_ref, ctxt_ref, g_ref, gp_ref, z2_ref, y_ref, yb_ref,
    h1_s, h1b_s, acc_s,
):
    step = pl.program_id(0)

    @pl.when(step == 0)
    def _():
        ctx = ctx_ref[...]
        z1 = x_ref[...].astype(F32) + mm(ctx, wo_ref[...], NN) + vec_ref[BO : BO + 1, :]
        z1_ref[...] = z1
        n, _ = normed(z1)
        h1 = n * vec_ref[G1 : G1 + 1, :] + vec_ref[S1 : S1 + 1, :]
        h1_s[...] = h1
        low = h1.astype(BF)
        h1b_s[...] = low
        h1t_ref[...] = low.T
        ctxt_ref[...] = ctx.T

    f = mm(h1b_s[...], wi_ref[...], NN) + bi_ref[...]
    g, slope = gelu_both(f)
    g = g.astype(BF)
    g_ref[...] = g
    gp_ref[...] = slope.astype(BF)
    more = mm(g, wb_ref[...], NN)

    @pl.when(step == 0)
    def _():
        acc_s[...] = more

    @pl.when(step > 0)
    def _():
        acc_s[...] += more

    @pl.when(step == steps - 1)
    def _():
        z2 = h1_s[...] + acc_s[...] + vec_ref[BB : BB + 1, :]
        z2_ref[...] = z2
        n, _ = normed(z2)
        y = n * vec_ref[G2 : G2 + 1, :] + vec_ref[S2 : S2 + 1, :]
        y_ref[...] = y
        yb_ref[...] = y.astype(BF)


def ffn_call(x, ctx, wo, vec, wi, bi, wb, chunk=512):
    rows = x.shape[0]
    ff = wi.shape[1]
    steps = ff // chunk
    full = once((rows, D), lambda i: (0, 0))
    keep = once((rows, D), lambda i: (0, 0))
    cols = pl.BlockSpec((rows, chunk), lambda i: (0, i))
    flip = once((D, rows), lambda i: (0, 0))

    def body(*refs):
        ffn_body(steps, *refs)

    return pl.pallas_call(
        body,
        grid=(steps,),
        in_specs=[
            full,
            full,
            once((D, D), lambda i: (0, 0)),
            once((8, D), lambda i: (0, 0)),
            pl.BlockSpec((D, chunk), lambda i: (0, i)),
            pl.BlockSpec((1, chunk), lambda i: (0, i)),
            pl.BlockSpec((chunk, D), lambda i: (i, 0)),
        ],
        out_specs=[keep, flip, flip, cols, cols, keep, keep, keep],
        out_shape=[
            jax.ShapeDtypeStruct((rows, D), F32),
            jax.ShapeDtypeStruct((D, rows), BF),
            jax.ShapeDtypeStruct((D, rows), BF),
            jax.ShapeDtypeStruct((rows, ff), BF),
            jax.ShapeDtypeStruct((rows, ff), BF),
            jax.ShapeDtypeStruct((rows, D), F32),
            jax.ShapeDtypeStruct((rows, D), F32),
            jax.ShapeDtypeStruct((rows, D), BF),
        ],
        scratch_shapes=[pltpu.VMEM((rows, D), F32), pltpu.VMEM((rows, D), BF), pltpu.VMEM((rows, D), F32)],
        compiler_params=params(),
        cost_estimate=cost(2 * rows * D * (D + 2 * ff), 20 * rows * D + 4 * rows * ff + 4 * D * ff, rows * ff),
        name="ffn",
    )(x, ctx, wo, vec, wi, bi, wb)


def ffn_back_body(
    steps, dy_ref, z2_ref, z1_ref, gp_ref, wb_ref, wi_ref, wo_ref, vec_ref,
    e2_ref, e1_ref, dz1_ref, ea_ref, dctx_ref, sums_ref, bi_ref,
    dz2_s, acc_s,
):
    step = pl.program_id(0)

    @pl.when(step == 0)
    def _():
        dy = dy_ref[...].astype(F32)
        n, root = normed(z2_ref[...])
        sums_ref[G2 : G2 + 1, :] = colsum(dy * n)
        sums_ref[S2 : S2 + 1, :] = colsum(dy)
        dz2 = normed_back(n, root, dy * vec_ref[G2 : G2 + 1, :])
        dz2_s[...] = dz2
        low = dz2.astype(BF)
        e2_ref[...] = low
        sums_ref[BB : BB + 1, :] = colsum(low.astype(F32))

    df = mm(e2_ref[...], wb_ref[...], NT) * gp_ref[...].astype(F32)
    e1 = df.astype(BF)
    e1_ref[...] = e1
    bi_ref[...] = colsum(e1.astype(F32))
    more = mm(e1, wi_ref[...], NT)

    @pl.when(step == 0)
    def _():
        acc_s[...] = more

    @pl.when(step > 0)
    def _():
        acc_s[...] += more

    @pl.when(step == steps - 1)
    def _():
        dh1 = dz2_s[...] + acc_s[...]
        n, root = normed(z1_ref[...])
        sums_ref[G1 : G1 + 1, :] = colsum(dh1 * n)
        sums_ref[S1 : S1 + 1, :] = colsum(dh1)
        dz1 = normed_back(n, root, dh1 * vec_ref[G1 : G1 + 1, :])
        dz1_ref[...] = dz1
        low = dz1.astype(BF)
        ea_ref[...] = low
        sums_ref[BO : BO + 1, :] = colsum(low.astype(F32))
        sums_ref[BQ : BQ + 1, :] = jnp.zeros((1, D), F32)
        sums_ref[BV : BV + 1, :] = jnp.zeros((1, D), F32)
        dctx_ref[...] = mm(low, wo_ref[...], NT).astype(BF)


def ffn_back_call(dy, z2, z1, gp, wb, wi, wo, vec, chunk=512):
    rows = dy.shape[0]
    ff = wi.shape[1]
    steps = ff // chunk
    keep = once((rows, D), lambda i: (0, 0))
    cols = pl.BlockSpec((rows, chunk), lambda i: (0, i))

    def body(*refs):
        ffn_back_body(steps, *refs)

    return pl.pallas_call(
        body,
        grid=(steps,),
        in_specs=[
            keep,
            keep,
            keep,
            cols,
            pl.BlockSpec((chunk, D), lambda i: (i, 0)),
            pl.BlockSpec((D, chunk), lambda i: (0, i)),
            once((D, D), lambda i: (0, 0)),
            once((8, D), lambda i: (0, 0)),
        ],
        out_specs=[
            keep,
            cols,
            keep,
            keep,
            keep,
            once((8, D), lambda i: (0, 0)),
            pl.BlockSpec((1, chunk), lambda i: (0, i)),
        ],
        out_shape=[
            jax.ShapeDtypeStruct((rows, D), BF),
            jax.ShapeDtypeStruct((rows, ff), BF),
            jax.ShapeDtypeStruct((rows, D), F32),
            jax.ShapeDtypeStruct((rows, D), BF),
            jax.ShapeDtypeStruct((rows, D), BF),
            jax.ShapeDtypeStruct((8, D), F32),
            jax.ShapeDtypeStruct((1, ff), F32),
        ],
        scratch_shapes=[pltpu.VMEM((rows, D), F32), pltpu.VMEM((rows, D), F32)],
        compiler_params=params(),
        cost_estimate=cost(2 * rows * D * (D + 2 * ff), 20 * rows * D + 4 * rows * ff + 4 * D * ff),
        name="ffn_back",
    )(dy, z2, z1, gp, wb, wi, wo, vec)


def attend_back_body(seq, pairs, len_ref, q_ref, k_ref, v_ref, d_ref, l_ref, eq_ref, ek_ref, ev_ref, bq_ref, bv_ref):
    count = len_ref[pl.program_id(0)]
    lane = lax.broadcasted_iota(jnp.int32, (seq, PAIR), 1)
    ok = lax.broadcasted_iota(jnp.int32, (seq, seq), 0) < count
    units = [(pr, h) for pr in range(pairs) for h in range(2)]

    def score(unit):
        pr, h = unit
        cols = slice(pr * PAIR, (pr + 1) * PAIR)
        mine = (lane >= HEAD_DIM) == (h == 1)
        q = jnp.where(mine, q_ref[:, cols] * BF(0.125), BF(0))
        s = jnp.where(ok, mm(k_ref[:, cols], q, NT), -1e30)
        return s, mm(v_ref[:, cols], jnp.where(mine, d_ref[:, cols], BF(0)), NT)

    ahead = score(units[0])
    eq, ek, ev = {}, {}, {}
    for i, (pr, h) in enumerate(units):
        s, dp = ahead
        if i + 1 < len(units):
            ahead = score(units[i + 1])
        cols = slice(pr * PAIR, (pr + 1) * PAIR)
        if h == 0:
            kt = (k_ref[:, cols] * BF(0.125)).T
        p = jnp.exp(s - l_ref[0, pr, h : h + 1, :])
        pd = p * dp
        ds = (pd - p * colsum(pd)).astype(BF)
        ev[h] = mm(p.astype(BF), d_ref[:, cols], NN)
        ek[h] = mm(ds, q_ref[:, cols] * BF(0.125), NN)
        eq[h] = mm(kt[h * HEAD_DIM : (h + 1) * HEAD_DIM], ds, NN)
        if h == 1:
            low = jnp.concatenate([eq[0], eq[1]], axis=0).T.astype(BF)
            eq_ref[:, cols] = low
            bq_ref[0, :, cols] = colsum(low.astype(F32))
            ek_ref[:, cols] = jnp.where(lane < HEAD_DIM, ek[0], ek[1]).astype(BF)
            low = jnp.where(lane < HEAD_DIM, ev[0], ev[1]).astype(BF)
            ev_ref[:, cols] = low
            bv_ref[0, :, cols] = colsum(low.astype(F32))


def attend_back_call(qkv, dctx, lse, lengths, pairs=3):
    rows = qkv.shape[0]
    count = lengths.shape[0]
    seq = rows // count
    groups = D // PAIR // pairs
    wide = PAIR * pairs

    def part(o):
        return pl.BlockSpec((seq, wide), lambda s, p, n: (s, o * groups + p))

    def body(*refs):
        attend_back_body(seq, pairs, *refs)

    flops = 10 * count * HEADS * seq * seq * HEAD_DIM
    line = pl.BlockSpec((1, 1, wide), lambda s, p, n: (s, 0, p))
    return pl.pallas_call(
        body,
        grid_spec=pltpu.PrefetchScalarGridSpec(
            num_scalar_prefetch=1,
            grid=(count, groups),
            in_specs=[
                part(0),
                part(1),
                part(2),
                part(0),
                pl.BlockSpec((1, pairs, 2, seq), lambda s, p, n: (s, p, 0, 0)),
            ],
            out_specs=[part(0), part(0), part(0), line, line],
        ),
        out_shape=[jax.ShapeDtypeStruct((rows, D), BF)] * 3 + [jax.ShapeDtypeStruct((count, 1, D), F32)] * 2,
        compiler_params=params(),
        cost_estimate=cost(4 * flops, 14 * rows * D, count * HEADS * seq * seq),
        name="attend_back",
    )(lengths, qkv, qkv, qkv, dctx, lse)


def dx_body(dz1_ref, eq_ref, ek_ref, ev_ref, w_ref, o_ref):
    acc = mm(eq_ref[...], w_ref[:, :D], NT)
    acc += mm(ek_ref[...], w_ref[:, D : 2 * D], NT)
    acc += mm(ev_ref[...], w_ref[:, 2 * D :], NT)
    o_ref[...] = (dz1_ref[...] + acc).astype(o_ref.dtype)


def dx_call(dz1, eq, ek, ev, w, dtype, block=256):
    rows = dz1.shape[0]
    line = pl.BlockSpec((block, D), lambda i: (i, 0))
    return pl.pallas_call(
        dx_body,
        grid=(rows // block,),
        in_specs=[line, line, line, line, once((D, 3 * D), lambda i: (0, 0))],
        out_specs=line,
        out_shape=jax.ShapeDtypeStruct((rows, D), dtype),
        compiler_params=params(),
        cost_estimate=cost(6 * rows * D * D, 14 * rows * D + 6 * D * D),
        name="dx",
    )(dz1, eq, ek, ev, w)


def wgrad_t_body(a_ref, b_ref, c_ref, d_ref, o_ref):
    o_ref[...] = (mm(a_ref[...], b_ref[...], TN) + mm(c_ref[...], d_ref[...], TN)).astype(BF)


def wgrad_t_call(a, b, c, d, block=768):
    rows, m = a.shape
    n = b.shape[1]
    part = pl.BlockSpec((rows, block), lambda i: (0, i))
    held = once((rows, n), lambda i: (0, 0))
    return pl.pallas_call(
        wgrad_t_body,
        grid=(m // block,),
        in_specs=[part, held, part, held],
        out_specs=pl.BlockSpec((block, n), lambda i: (i, 0)),
        out_shape=jax.ShapeDtypeStruct((m, n), BF),
        compiler_params=params(),
        cost_estimate=cost(4 * rows * m * n, 4 * rows * (m + n) + 2 * m * n),
        name="wgrad_t",
    )(a, b, c, d)


def wgrad_body(a_ref, b_ref, c_ref, d_ref, o_ref):
    o_ref[...] = (mm(a_ref[...], b_ref[...], NN) + mm(c_ref[...], d_ref[...], NN)).astype(BF)


def wgrad_call(a, b, c, d, block=768):
    m, rows = a.shape
    n = b.shape[1]
    block = min(block, n)
    held = once((m, rows), lambda i: (0, 0))
    part = pl.BlockSpec((rows, block), lambda i: (0, i))
    return pl.pallas_call(
        wgrad_body,
        grid=(n // block,),
        in_specs=[held, part, held, part],
        out_specs=pl.BlockSpec((m, block), lambda i: (0, i)),
        out_shape=jax.ShapeDtypeStruct((m, n), BF),
        compiler_params=params(),
        cost_estimate=cost(4 * rows * m * n, 4 * rows * (m + n) + 2 * m * n),
        name="wgrad",
    )(a, b, c, d)


def layer_forward(x, low, weights, lengths):
    w_qkv, w_out, w_in, w_back, vec, bias_in = weights
    qkv, lowt = qkv_call(low, w_qkv, vec)
    ctx, lse = attend_call(qkv, lengths)
    z1, h1t, ctxt, g, slope, z2, y, y_low = ffn_call(x, ctx, w_out, vec, w_in, bias_in, w_back)
    return y, y_low, (lowt, qkv, lse, z1, h1t, ctxt, g, slope, z2)


class Grid:
    def __init__(self, sizes):
        self.dp, self.fsdp = sizes["dp"], sizes["fsdp"]
        self.count = self.dp * self.fsdp
        self.x, self.core = self.dp // 2, 2
        self.y = self.fsdp // 4
        self.z = self.fsdp // self.y if self.y else 0
        self.staged = self.x == 2 and self.y == 2

    def place(self):
        dp, fsdp = lax.axis_index("dp"), lax.axis_index("fsdp")
        return dp // 2, dp % 2, fsdp // self.y, fsdp % self.y

    def shift(self, dim, step):
        sizes = (self.x, self.core, self.z, self.y)
        pairs = []
        for i in range(self.count):
            at = [i // (self.core * self.fsdp), i // self.fsdp % self.core, i % self.fsdp // self.y, i % self.y]
            at[dim] = (at[dim] + step) % sizes[dim]
            pairs.append((i, ((at[0] * self.core + at[1]) * self.z + at[2]) * self.y + at[3]))
        return pairs

    def send(self, value, dim, step=1):
        return lax.ppermute(value, AXES, self.shift(dim, step))


X, CORE, Z, Y = range(4)


def assemble_body(half, at_ref, *refs):
    parts, out_ref, sems = refs[:16], refs[16], refs[17]
    x, core, y = at_ref[0], at_ref[1], at_ref[2]
    copies = []
    for i, part in enumerate(parts):
        side, dx, dc, dy = i >> 3, (i >> 2) & 1, (i >> 1) & 1, i & 1
        target = out_ref.at[
            (x + dx) % 2, (core + dc) % 2, :, (y + dy) % 2, :, pl.ds(side * half, half)
        ]
        copies.append(pltpu.make_async_copy(part, target, sems.at[i]))
    for copy in copies:
        copy.start()
    for copy in copies:
        copy.wait()


def gather_rows(grid, shard):
    rows, cols = shard.shape
    half = cols // 2
    x, core, z, y = grid.place()
    ring = [shard] + [grid.send(shard, Z, k) for k in range(1, grid.z)]
    ring = ring[::-1]
    line = lax.dynamic_slice_in_dim(jnp.stack(ring + ring), grid.z - 1 - z, grid.z, 0)
    left, right = line[:, :, :half], line[:, :, half:]
    left_y = grid.send(left, Y)
    right_x = grid.send(right, X)
    left_x, left_xy = grid.send(left, X), grid.send(left_y, X)
    right_y, right_xy = grid.send(right, Y), grid.send(right_x, Y)
    parts = []
    for near, by_y, by_x, both in ((left, left_y, left_x, left_xy), (right, right_y, right_x, right_xy)):
        for pair in ((near, by_y), (by_x, both)):
            parts += list(pair)
            parts += [grid.send(v, CORE) for v in pair]
    whole = pl.pallas_call(
        lambda *refs: assemble_body(half, *refs),
        grid_spec=pltpu.PrefetchScalarGridSpec(
            num_scalar_prefetch=1,
            grid=(1,),
            in_specs=[pl.BlockSpec(memory_space=pl.ANY)] * 16,
            out_specs=pl.BlockSpec(memory_space=pl.ANY),
            scratch_shapes=[pltpu.SemaphoreType.DMA((16,))],
        ),
        out_shape=jax.ShapeDtypeStruct((2, 2, grid.z, 2, rows, cols), shard.dtype),
        compiler_params=pltpu.CompilerParams(vmem_limit_bytes=2 * 2**20),
        cost_estimate=cost(0, 4 * rows * cols * grid.count),
        name="assemble",
    )(jnp.stack([x, core, y]).astype(jnp.int32), *parts)
    return whole.reshape(grid.count * rows, cols)


def pick(value, index, dim):
    return lax.dynamic_index_in_dim(value, index, dim, keepdims=False)


def scatter_rows(grid, total):
    rows = total.shape[0] // grid.count
    cols = total.shape[1]
    half = cols // 2
    kind = total.dtype
    x, core, z, y = grid.place()
    view = total.reshape(2, 2, grid.z, 2, rows, cols)
    came = grid.send(pick(view, 1 - core, 1), CORE)
    mine = pick(view, core, 1)

    def both(pieces):
        a, b = pieces
        return (a.astype(F32) + b.astype(F32)).astype(kind)

    left, right = (mine[..., :half], came[..., :half]), (mine[..., half:], came[..., half:])
    left_out = both([pick(v, 1 - x, 0) for v in left])
    left_keep = both([pick(v, x, 0) for v in left])
    right_out = both([pick(v, 1 - y, 2) for v in right])
    right_keep = both([pick(v, y, 2) for v in right])
    left_in, right_in = grid.send(left_out, X), grid.send(right_out, Y)
    left, right = (left_keep, left_in), (right_keep, right_in)
    left_out = both([pick(v, 1 - y, 1) for v in left])
    left_keep = both([pick(v, y, 1) for v in left])
    right_out = both([pick(v, 1 - x, 0) for v in right])
    right_keep = both([pick(v, x, 0) for v in right])
    left_in, right_in = grid.send(left_out, Y), grid.send(right_out, X)
    line = jnp.concatenate([both((left_keep, left_in)), both((right_keep, right_in))], axis=-1)
    result = pick(line, z, 0).astype(F32)
    for k in range(1, grid.z):
        result += grid.send(pick(line, (z + k) % grid.z, 0), Z, k).astype(F32)
    return result


def gather(grid, shard):
    if grid.staged:
        return gather_rows(grid, shard)
    return lax.all_gather(shard, AXES, axis=0, tiled=True)


def scatter(grid, total):
    if grid.staged:
        return scatter_rows(grid, total)
    return lax.psum_scatter(total.astype(F32), AXES, scatter_dimension=0, tiled=True)


def pad_to(value, rows, cols):
    return jnp.pad(value, ((0, rows - value.shape[0]), (0, cols - value.shape[1])))


def make_local(grid):
    def local(
        tokens, lengths, w_qkv, bias_q, bias_v, w_out, bias_out, gain_one, shift_one, w_in, bias_in,
        w_back, bias_back, gain_two, shift_two, cotangent,
    ):
        rows = bias_q.shape[0]
        span = bias_in.shape[0]
        small = jnp.concatenate(
            [bias_q, bias_v, bias_out, gain_one, shift_one, bias_back, gain_two, shift_two, bias_in]
        )
        tail = 8
        packed = jnp.concatenate([w_out, pad_to(small[None], tail, D)], axis=0)
        packed = gather(grid, packed).reshape(grid.count, rows + tail, D)
        w_qkv = gather(grid, w_qkv)
        w_in = gather(grid, w_in)
        w_back = gather(grid, w_back)
        w_out = packed[:, :rows].reshape(D, D)
        small = packed[:, rows, : 8 * rows + span].astype(F32)
        vec = small[:, : 8 * rows].reshape(grid.count, 8, rows).swapaxes(0, 1).reshape(8, D)
        bias_in = small[:, 8 * rows :].reshape(1, -1)
        weights = (w_qkv, w_out, w_in, w_back, vec, bias_in)

        x, low = tokens, tokens
        saved = []
        for _ in range(APPS):
            x, low, stored = layer_forward(x, low, weights, lengths)
            saved.append(stored)
        activations = low

        grad = cotangent
        back = [None] * APPS
        for step in reversed(range(APPS)):
            lowt, qkv, lse, z1, h1t, ctxt, g, slope, z2 = saved[step]
            e2, e1, dz1, ea, dctx, sums, sum_in = ffn_back_call(grad, z2, z1, slope, w_back, w_in, w_out, vec)
            eq, ek, ev, sum_q, sum_v = attend_back_call(qkv, dctx, lse, lengths)
            grad = dx_call(dz1, eq, ek, ev, w_qkv, F32 if step else BF)
            back[step] = (e2, e1, ea, eq, ek, ev, sums, sum_in, sum_q, sum_v)
        one, two = back
        w_back_grad = scatter(grid, wgrad_t_call(saved[1][6], two[0], saved[0][6], one[0]))
        w_in_grad = scatter(grid, wgrad_call(saved[1][4], two[1], saved[0][4], one[1]))
        w_out_grad = scatter(grid, wgrad_call(saved[1][5], two[2], saved[0][5], one[2]))
        parts = [scatter(grid, wgrad_call(saved[1][0], two[i], saved[0][0], one[i])) for i in (3, 4, 5)]
        w_qkv_grad = jnp.concatenate(parts, axis=1)

        sums = one[6] + two[6]
        sum_q = jnp.sum(one[8] + two[8], axis=(0, 1))
        sum_v = jnp.sum(one[9] + two[9], axis=(0, 1))
        sums = jnp.concatenate([sum_q[None], sum_v[None], sums[2:]], axis=0)
        sums = sums.reshape(8, grid.count, rows).swapaxes(0, 1).reshape(grid.count, 8 * rows)
        sums = jnp.concatenate([sums, (one[7] + two[7]).reshape(grid.count, span)], axis=1)
        wide = -(-(8 * rows + span) // 256) * 256
        owned = scatter(grid, jnp.pad(sums[:, None, :], ((0, 0), (0, 7), (0, wide - sums.shape[1]))).reshape(-1, wide))[0]
        owned = [owned[i * rows : (i + 1) * rows] for i in range(8)] + [owned[8 * rows : 8 * rows + span]]
        return (
            activations, grad, w_qkv_grad, owned[BQ], owned[BV], w_out_grad, owned[BO], owned[G1], owned[S1],
            w_in_grad, owned[8], w_back_grad, owned[BB], owned[G2], owned[S2],
        )

    return local


def solution(mesh):
    wide, line = P(AXES, None), P(AXES)
    return jax.shard_map(
        make_local(Grid(mesh.shape)),
        mesh=mesh,
        in_specs=(wide, line, wide, line, line, wide, line, line, line, wide, line, wide, line, line, line, wide),
        out_specs=(wide, wide, wide, line, line, wide, line, line, line, wide, line, wide, line, line, line),
        check_vma=False,
    )
```

```python
import jax
import jax.numpy as jnp
from jax import lax
from jax.experimental import pallas as pl
from jax.experimental.pallas import tpu as pltpu
from jax.sharding import PartitionSpec as P

D = 768
HEADS = 12
HEAD_DIM = 64
APPS = 2
PAIR = 2 * HEAD_DIM
AXES = ("dp", "fsdp")
BF = jnp.bfloat16
F32 = jnp.float32
NN = (((1,), (0,)), ((), ()))
NT = (((1,), (1,)), ((), ()))
TN = (((0,), (0,)), ((), ()))
VMEM = 56 * 2**20
BQ, BV, BO, G1, S1, BB, G2, S2 = range(8)


def mm(left, right, dims):
    return lax.dot_general(left, right, dims, preferred_element_type=F32)


def params(limit=VMEM):
    return pltpu.CompilerParams(vmem_limit_bytes=limit)


def cost(flops, nbytes, trans=0):
    return pl.CostEstimate(flops=int(flops), bytes_accessed=int(nbytes), transcendentals=int(trans))


def once(shape, index):
    return pl.BlockSpec(shape, index, pipeline_mode=pl.Buffered(1))


def normed(z):
    centered = z - jnp.mean(z, axis=-1, keepdims=True)
    root = lax.rsqrt(jnp.mean(centered * centered, axis=-1, keepdims=True) + 1e-12)
    return centered * root, root


def normed_back(n, root, e):
    return root * (e - jnp.mean(e, axis=-1, keepdims=True) - n * jnp.mean(e * n, axis=-1, keepdims=True))


def colsum(v):
    return jnp.sum(v, axis=0, keepdims=True)


def qkv_body(x_ref, w_ref, vec_ref, o_ref, xt_ref):
    part = pl.program_id(0)

    @pl.when(part == 0)
    def _():
        xt_ref[...] = x_ref[...].T

    acc = mm(x_ref[...], w_ref[0], NN)
    bias = jnp.where(part == 0, vec_ref[BQ : BQ + 1, :], jnp.where(part == 2, vec_ref[BV : BV + 1, :], 0.0))
    o_ref[...] = (acc + bias).astype(BF)


def qkv_call(x, w, vec):
    rows = x.shape[0]
    return pl.pallas_call(
        qkv_body,
        grid=(3,),
        in_specs=[
            once((rows, D), lambda i: (0, 0)),
            pl.BlockSpec((1, D, D), lambda i: (i, 0, 0)),
            once(vec.shape, lambda i: (0, 0)),
        ],
        out_specs=[pl.BlockSpec((rows, D), lambda i: (0, i)), pl.BlockSpec((D, rows), lambda i: (0, 0))],
        out_shape=[jax.ShapeDtypeStruct((rows, 3 * D), BF), jax.ShapeDtypeStruct((D, rows), BF)],
        compiler_params=params(),
        cost_estimate=cost(6 * rows * D * D, 2 * (rows * D * 5 + 3 * D * D)),
        name="qkv",
    )(x, w, vec)


def attend_body(seq, pairs, len_ref, q_ref, k_ref, v_ref, o_ref, l_ref):
    count = len_ref[pl.program_id(0)]
    lane = lax.broadcasted_iota(jnp.int32, (seq, PAIR), 1)
    ok = lax.broadcasted_iota(jnp.int32, (1, seq), 1) < count
    units = [(pr, h) for pr in range(pairs) for h in range(2)]

    def score(unit):
        pr, h = unit
        cols = slice(pr * PAIR, (pr + 1) * PAIR)
        mine = (lane >= HEAD_DIM) == (h == 1)
        q = jnp.where(mine, q_ref[:, cols] * BF(0.125), BF(0))
        return jnp.where(ok, mm(q, k_ref[:, cols], NT), -1e30)

    ahead = score(units[0])
    held = {}
    for i, (pr, h) in enumerate(units):
        s = ahead
        if i + 1 < len(units):
            ahead = score(units[i + 1])
        cols = slice(pr * PAIR, (pr + 1) * PAIR)
        top = jnp.max(s, axis=1, keepdims=True)
        p = jnp.exp(s - top)
        total = jnp.sum(p, axis=1, keepdims=True)
        held[h] = mm(p.astype(BF), v_ref[:, cols], NN) / total
        l_ref[0, pr, h : h + 1, :] = (top + jnp.log(total)).reshape(1, seq)
        if h == 1:
            o_ref[:, cols] = jnp.where(lane < HEAD_DIM, held[0], held[1]).astype(BF)


def attend_call(qkv, lengths, pairs=3):
    rows = qkv.shape[0]
    count = lengths.shape[0]
    seq = rows // count
    groups = D // PAIR // pairs
    wide = PAIR * pairs

    def part(o):
        return pl.BlockSpec((seq, wide), lambda s, p, n: (s, o * groups + p))

    def body(*refs):
        attend_body(seq, pairs, *refs)

    flops = 4 * count * HEADS * seq * seq * HEAD_DIM
    return pl.pallas_call(
        body,
        grid_spec=pltpu.PrefetchScalarGridSpec(
            num_scalar_prefetch=1,
            grid=(count, groups),
            in_specs=[part(0), part(1), part(2)],
            out_specs=[part(0), pl.BlockSpec((1, pairs, 2, seq), lambda s, p, n: (s, p, 0, 0))],
        ),
        out_shape=[
            jax.ShapeDtypeStruct((rows, D), BF),
            jax.ShapeDtypeStruct((count, D // PAIR, 2, seq), F32),
        ],
        compiler_params=params(),
        cost_estimate=cost(4 * flops, 8 * rows * D, count * HEADS * seq * seq),
        name="attend",
    )(lengths, qkv, qkv, qkv)


def gelu_both(u):
    a = 0.7978845608028654
    sq = u * u
    t = jnp.tanh(u * (a + (a * 0.044715) * sq))
    half = 0.5 + 0.5 * t
    slope = half + (u * (0.5 - 0.5 * t * t)) * (a + (3 * a * 0.044715) * sq)
    return u * half, slope


def ffn_body(
    steps, x_ref, ctx_ref, wo_ref, vec_ref, wi_ref, wb_ref,
    z1_ref, h1t_ref, ctxt_ref, g_ref, gp_ref, z2_ref, y_ref, yb_ref,
    h1_s, h1b_s, acc_s,
):
    step = pl.program_id(0)

    @pl.when(step == 0)
    def _():
        ctx = ctx_ref[...]
        z1 = x_ref[...].astype(F32) + mm(ctx, wo_ref[0], NN) + vec_ref[BO : BO + 1, :]
        z1_ref[...] = z1
        n, _ = normed(z1)
        h1 = n * vec_ref[G1 : G1 + 1, :] + vec_ref[S1 : S1 + 1, :]
        h1_s[...] = h1
        low = h1.astype(BF)
        h1b_s[...] = low
        h1t_ref[...] = low.T
        ctxt_ref[...] = ctx.T

    f = mm(h1b_s[...], wi_ref[0], NN) + vec_ref[pl.ds(8 + step, 1), :]
    g, slope = gelu_both(f)
    g = g.astype(BF)
    g_ref[...] = g
    gp_ref[...] = slope.astype(BF)
    more = mm(g, wb_ref[...], NN)

    @pl.when(step == 0)
    def _():
        acc_s[...] = more

    @pl.when(step > 0)
    def _():
        acc_s[...] += more

    @pl.when(step == steps - 1)
    def _():
        z2 = h1_s[...] + acc_s[...] + vec_ref[BB : BB + 1, :]
        z2_ref[...] = z2
        n, _ = normed(z2)
        y = n * vec_ref[G2 : G2 + 1, :] + vec_ref[S2 : S2 + 1, :]
        y_ref[...] = y
        yb_ref[...] = y.astype(BF)


def ffn_call(x, ctx, wo, vec, wi, wb):
    rows = x.shape[0]
    ff = wb.shape[0]
    chunk = D
    steps = ff // chunk
    full = once((rows, D), lambda i: (0, 0))
    keep = once((rows, D), lambda i: (0, 0))
    cols = pl.BlockSpec((rows, chunk), lambda i: (0, i))
    flip = once((D, rows), lambda i: (0, 0))

    def body(*refs):
        ffn_body(steps, *refs)

    return pl.pallas_call(
        body,
        grid=(steps,),
        in_specs=[
            full,
            full,
            once((1, D, D), lambda i: (3, 0, 0)),
            once(vec.shape, lambda i: (0, 0)),
            pl.BlockSpec((1, D, chunk), lambda i: (i, 0, 0)),
            pl.BlockSpec((chunk, D), lambda i: (i, 0)),
        ],
        out_specs=[keep, flip, flip, cols, cols, keep, keep, keep],
        out_shape=[
            jax.ShapeDtypeStruct((rows, D), F32),
            jax.ShapeDtypeStruct((D, rows), BF),
            jax.ShapeDtypeStruct((D, rows), BF),
            jax.ShapeDtypeStruct((rows, ff), BF),
            jax.ShapeDtypeStruct((rows, ff), BF),
            jax.ShapeDtypeStruct((rows, D), F32),
            jax.ShapeDtypeStruct((rows, D), F32),
            jax.ShapeDtypeStruct((rows, D), BF),
        ],
        scratch_shapes=[pltpu.VMEM((rows, D), F32), pltpu.VMEM((rows, D), BF), pltpu.VMEM((rows, D), F32)],
        compiler_params=params(),
        cost_estimate=cost(2 * rows * D * (D + 2 * ff), 20 * rows * D + 4 * rows * ff + 4 * D * ff, rows * ff),
        name="ffn",
    )(x, ctx, wo, vec, wi, wb)


def ffn_back_body(
    steps, dy_ref, z2_ref, z1_ref, gp_ref, wb_ref, wi_ref, wo_ref, vec_ref,
    e2_ref, e1_ref, dz1_ref, ea_ref, dctx_ref, sums_ref,
    dz2_s, acc_s,
):
    step = pl.program_id(0)

    @pl.when(step == 0)
    def _():
        sums_ref[...] = jnp.zeros_like(sums_ref)
        dy = dy_ref[...].astype(F32)
        n, root = normed(z2_ref[...])
        sums_ref[G2 : G2 + 1, :] = colsum(dy * n)
        sums_ref[S2 : S2 + 1, :] = colsum(dy)
        dz2 = normed_back(n, root, dy * vec_ref[G2 : G2 + 1, :])
        dz2_s[...] = dz2
        low = dz2.astype(BF)
        e2_ref[...] = low
        sums_ref[BB : BB + 1, :] = colsum(low.astype(F32))

    df = mm(e2_ref[...], wb_ref[...], NT) * gp_ref[...].astype(F32)
    e1 = df.astype(BF)
    e1_ref[...] = e1
    sums_ref[pl.ds(8 + step, 1), :] = colsum(e1.astype(F32))
    more = mm(e1, wi_ref[0], NT)

    @pl.when(step == 0)
    def _():
        acc_s[...] = more

    @pl.when(step > 0)
    def _():
        acc_s[...] += more

    @pl.when(step == steps - 1)
    def _():
        dh1 = dz2_s[...] + acc_s[...]
        n, root = normed(z1_ref[...])
        sums_ref[G1 : G1 + 1, :] = colsum(dh1 * n)
        sums_ref[S1 : S1 + 1, :] = colsum(dh1)
        dz1 = normed_back(n, root, dh1 * vec_ref[G1 : G1 + 1, :])
        dz1_ref[...] = dz1
        low = dz1.astype(BF)
        ea_ref[...] = low
        sums_ref[BO : BO + 1, :] = colsum(low.astype(F32))
        dctx_ref[...] = mm(low, wo_ref[0], NT).astype(BF)


def ffn_back_call(dy, z2, z1, gp, wb, wi, wo, vec):
    rows = dy.shape[0]
    ff = wb.shape[0]
    chunk = D
    steps = ff // chunk
    keep = once((rows, D), lambda i: (0, 0))
    cols = pl.BlockSpec((rows, chunk), lambda i: (0, i))

    def body(*refs):
        ffn_back_body(steps, *refs)

    return pl.pallas_call(
        body,
        grid=(steps,),
        in_specs=[
            keep,
            keep,
            keep,
            cols,
            pl.BlockSpec((chunk, D), lambda i: (i, 0)),
            pl.BlockSpec((1, D, chunk), lambda i: (i, 0, 0)),
            once((1, D, D), lambda i: (3, 0, 0)),
            once(vec.shape, lambda i: (0, 0)),
        ],
        out_specs=[
            keep,
            cols,
            keep,
            keep,
            keep,
            once(vec.shape, lambda i: (0, 0)),
        ],
        out_shape=[
            jax.ShapeDtypeStruct((rows, D), BF),
            jax.ShapeDtypeStruct((rows, ff), BF),
            jax.ShapeDtypeStruct((rows, D), F32),
            jax.ShapeDtypeStruct((rows, D), BF),
            jax.ShapeDtypeStruct((rows, D), BF),
            jax.ShapeDtypeStruct(vec.shape, F32),
        ],
        scratch_shapes=[pltpu.VMEM((rows, D), F32), pltpu.VMEM((rows, D), F32)],
        compiler_params=params(),
        cost_estimate=cost(2 * rows * D * (D + 2 * ff), 20 * rows * D + 4 * rows * ff + 4 * D * ff),
        name="ffn_back",
    )(dy, z2, z1, gp, wb, wi, wo, vec)


def attend_back_body(seq, pairs, len_ref, q_ref, k_ref, v_ref, d_ref, l_ref, *rest):
    e_ref, bq_ref, bv_ref = rest[-3:]
    count = len_ref[pl.program_id(0)]
    lane = lax.broadcasted_iota(jnp.int32, (seq, PAIR), 1)
    ok = lax.broadcasted_iota(jnp.int32, (seq, seq), 0) < count
    units = [(pr, h) for pr in range(pairs) for h in range(2)]

    def score(unit):
        pr, h = unit
        cols = slice(pr * PAIR, (pr + 1) * PAIR)
        mine = (lane >= HEAD_DIM) == (h == 1)
        q = jnp.where(mine, q_ref[:, cols] * BF(0.125), BF(0))
        s = jnp.where(ok, mm(k_ref[:, cols], q, NT), -1e30)
        return s, mm(v_ref[:, cols], jnp.where(mine, d_ref[:, cols], BF(0)), NT)

    ahead = score(units[0])
    eq, ek, ev = {}, {}, {}
    for i, (pr, h) in enumerate(units):
        s, dp = ahead
        if i + 1 < len(units):
            ahead = score(units[i + 1])
        cols = slice(pr * PAIR, (pr + 1) * PAIR)
        if h == 0:
            kt = (k_ref[:, cols] * BF(0.125)).T
        p = jnp.exp(s - l_ref[0, pr, h : h + 1, :])
        pd = p * dp
        ds = (pd - p * colsum(pd)).astype(BF)
        ev[h] = mm(p.astype(BF), d_ref[:, cols], NN)
        ek[h] = mm(ds, q_ref[:, cols] * BF(0.125), NN)
        eq[h] = mm(kt[h * HEAD_DIM : (h + 1) * HEAD_DIM], ds, NN)
        if h == 1:
            low = jnp.concatenate([eq[0], eq[1]], axis=0).T.astype(BF)
            e_ref[0, :, cols] = low
            bq_ref[0, :, cols] = colsum(low.astype(F32))
            e_ref[1, :, cols] = jnp.where(lane < HEAD_DIM, ek[0], ek[1]).astype(BF)
            low = jnp.where(lane < HEAD_DIM, ev[0], ev[1]).astype(BF)
            e_ref[2, :, cols] = low
            bv_ref[0, :, cols] = colsum(low.astype(F32))


GROUPS = 2
WIDE = D // GROUPS


def attend_back_call(qkv, dctx, lse, lengths, group, after=()):
    rows = qkv.shape[0]
    count = lengths.shape[0]
    seq = rows // count
    pairs = WIDE // PAIR

    def part(o):
        return pl.BlockSpec((seq, WIDE), lambda s, n: (s, o * GROUPS + group))

    def body(*refs):
        attend_back_body(seq, pairs, *refs)

    flops = 10 * count * 2 * pairs * seq * seq * HEAD_DIM
    line = pl.BlockSpec((1, 1, WIDE), lambda s, n: (s, 0, 0))
    return pl.pallas_call(
        body,
        grid_spec=pltpu.PrefetchScalarGridSpec(
            num_scalar_prefetch=1,
            grid=(count,),
            in_specs=[
                part(0),
                part(1),
                part(2),
                part(0),
                pl.BlockSpec((1, pairs, 2, seq), lambda s, n: (s, group, 0, 0)),
            ]
            + [pl.BlockSpec(memory_space=pl.ANY)] * len(after),
            out_specs=[pl.BlockSpec((3, seq, WIDE), lambda s, n: (0, s, 0)), line, line],
        ),
        out_shape=[jax.ShapeDtypeStruct((3, rows, WIDE), BF)] + [jax.ShapeDtypeStruct((count, 1, WIDE), F32)] * 2,
        compiler_params=params(),
        cost_estimate=cost(4 * flops, 14 * rows * WIDE, count * 2 * pairs * seq * seq),
        name="attend_back",
    )(lengths, qkv, qkv, qkv, dctx, lse, *after)


def dx_body(dz1_ref, e0_ref, e1_ref, w_ref, *rest):
    o_ref = rest[-1]
    acc = dz1_ref[...]
    for i in range(3):
        acc += mm(e0_ref[i], w_ref[i, :, :WIDE], NT)
        acc += mm(e1_ref[i], w_ref[i, :, WIDE:], NT)
    o_ref[...] = acc.astype(o_ref.dtype)


def dx_call(dz1, e0, e1, w, dtype, after=(), block=256):
    rows = dz1.shape[0]
    line = pl.BlockSpec((block, D), lambda i: (i, 0))
    part = pl.BlockSpec((3, block, WIDE), lambda i: (0, i, 0))
    return pl.pallas_call(
        dx_body,
        grid=(rows // block,),
        in_specs=[line, part, part, once((3, D, D), lambda i: (0, 0, 0))]
        + [pl.BlockSpec(memory_space=pl.ANY)] * len(after),
        out_specs=line,
        out_shape=jax.ShapeDtypeStruct((rows, D), dtype),
        compiler_params=params(),
        cost_estimate=cost(6 * rows * D * D, 14 * rows * D + 6 * D * D),
        name="dx",
    )(dz1, e0, e1, w, *after)


def wgrad_body(rows, core_ref, a_ref, c_ref, b_ref, d_ref, *rest):
    keep_ref, send_ref, acc_s = rest[-3:]
    b = b_ref[...].reshape(b_ref.shape[-2:])
    d = d_ref[...].reshape(d_ref.shape[-2:])
    acc_s[...] = mm(a_ref[...], b, NN) + mm(c_ref[...], d, NN)
    part = 8 * rows
    for out, core in ((keep_ref, core_ref[0]), (send_ref, 1 - core_ref[0])):
        for xi in range(2):
            for s in range(8):
                start = pl.multiple_of(core * part + (2 * xi * part + s * rows), 8)
                out[xi, s // 2, s % 2, 0] = acc_s[pl.ds(start, rows), :].astype(BF)


def wgrad_call(core, a, c, b, d, rows, spec, units, width, after=()):
    m, k = a.shape
    held = once((m, k), lambda i, n: (0, 0))
    out = pl.BlockSpec((2, 4, 2, 1, rows, width), lambda i, n: (0, 0, 0, i, 0, 0))
    return pl.pallas_call(
        lambda *refs: wgrad_body(rows, *refs),
        grid_spec=pltpu.PrefetchScalarGridSpec(
            num_scalar_prefetch=1,
            grid=(units,),
            in_specs=[held, held, spec, spec] + [pl.BlockSpec(memory_space=pl.ANY)] * len(after),
            out_specs=[out, out],
            scratch_shapes=[pltpu.VMEM((m, width), F32)],
        ),
        out_shape=[jax.ShapeDtypeStruct((2, 4, 2, units, rows, width), BF)] * 2,
        compiler_params=params(),
        cost_estimate=cost(4 * k * m * width * units, 4 * k * (m + units * width) + 2 * m * width * units),
        name="wgrad",
    )(core, a, c, b, d, *after)


def wgrad_back_call(core, two, one, e_two, e_one, rows):
    k, ff = two.shape
    block = ff // 8

    def cols(other):
        def index(x, s, n):
            c = 1 - n[0] if other else n[0]
            return (0, (x * 2 + c) * 2 + s)

        return pl.BlockSpec((k, block), index)

    held = once((k, D), lambda x, s, n: (0, 0))
    out = pl.BlockSpec((1, 2, 2, 4, rows, D), lambda x, s, n: (x, s, 0, 0, 0, 0))

    def body(core_ref, g2k, g1k, g2s, g1s, e2_ref, e1_ref, keep_ref, send_ref):
        for a, c, o in ((g2k, g1k, keep_ref), (g2s, g1s, send_ref)):
            acc = mm(a[...], e2_ref[...], TN) + mm(c[...], e1_ref[...], TN)
            for s in range(16):
                o[0, s // 8, s // 4 % 2, s % 4] = acc[s * rows : (s + 1) * rows].astype(BF)

    return pl.pallas_call(
        body,
        grid_spec=pltpu.PrefetchScalarGridSpec(
            num_scalar_prefetch=1,
            grid=(2, 2),
            in_specs=[cols(False), cols(False), cols(True), cols(True), held, held],
            out_specs=[out, out],
        ),
        out_shape=[jax.ShapeDtypeStruct((2, 4, 2, 4, rows, D), BF)] * 2,
        compiler_params=params(),
        cost_estimate=cost(4 * k * ff * D, 4 * k * (ff + D) + 2 * ff * D),
        name="wgrad_back",
    )(core, two, one, two, one, e_two, e_one)


def layer_forward(x, low, weights, lengths):
    first, w_in, w_back, vec = weights
    qkv, lowt = qkv_call(low, first, vec)
    ctx, lse = attend_call(qkv, lengths)
    z1, h1t, ctxt, g, slope, z2, y, y_low = ffn_call(x, ctx, first, vec, w_in, w_back)
    return y, y_low, (lowt, qkv, lse, z1, h1t, ctxt, g, slope, z2)


class Grid:
    def __init__(self, sizes):
        self.dp, self.fsdp = sizes["dp"], sizes["fsdp"]
        self.count = self.dp * self.fsdp
        self.x, self.core = self.dp // 2, 2
        self.y = self.fsdp // 4
        self.z = self.fsdp // self.y if self.y else 0
        self.staged = self.x == 2 and self.y == 2

    def place(self):
        dp, fsdp = lax.axis_index("dp"), lax.axis_index("fsdp")
        return dp // 2, dp % 2, fsdp // self.y, fsdp % self.y

    def shift(self, dim, step):
        sizes = (self.x, self.core, self.z, self.y)
        pairs = []
        for i in range(self.count):
            at = [i // (self.core * self.fsdp), i // self.fsdp % self.core, i % self.fsdp // self.y, i % self.y]
            at[dim] = (at[dim] + step) % sizes[dim]
            pairs.append((i, ((at[0] * self.core + at[1]) * self.z + at[2]) * self.y + at[3]))
        return pairs

    def send(self, value, dim, step=1):
        return lax.ppermute(value, AXES, self.shift(dim, step))


X, CORE, Z, Y = range(4)


def pack_body(at_ref, wq_ref, wo_ref, wi_ref, wb_ref, *rest):
    vectors, span_ref, one_ref, two_ref, line_s = rest[:8], rest[8], rest[9], rest[10], rest[11]
    rows = wq_ref.shape[0]
    for i in range(3):
        one_ref[i] = wq_ref[:, i * D : (i + 1) * D]
    one_ref[3] = wo_ref[...]
    for i in range(4):
        two_ref[i] = wi_ref[:, i * D : (i + 1) * D]
        two_ref[4 + i] = wb_ref[i * rows : (i + 1) * rows]
    line_s[...] = jnp.zeros_like(line_s)
    for i, ref in enumerate(vectors):
        line_s[i : i + 1, :rows] = ref[...].astype(F32)
    span = span_ref.shape[1]
    line_s[8:9, :span] = span_ref[...].astype(F32)
    device = at_ref[0]
    per = D // span
    top = pltpu.roll(line_s[:8], device * rows, 1)
    low = pltpu.roll(line_s[8:16], lax.rem(device, per) * span, 1)
    here = lax.broadcasted_iota(jnp.int32, (8, D), 0) == lax.div(device, per)
    low = jnp.where(here, jnp.broadcast_to(low[:1], (8, D)), 0.0)
    one_ref[4] = jnp.concatenate([top, low, jnp.zeros((rows - 16, D), F32)], axis=0).astype(BF)


def pack(device, w_qkv, w_out, w_in, w_back, vectors, span):
    rows = w_qkv.shape[0]
    return pl.pallas_call(
        pack_body,
        grid_spec=pltpu.PrefetchScalarGridSpec(
            num_scalar_prefetch=1,
            grid=(1,),
            in_specs=[pl.BlockSpec(memory_space=pltpu.VMEM)] * 13,
            out_specs=[pl.BlockSpec(memory_space=pltpu.VMEM)] * 2,
            scratch_shapes=[pltpu.VMEM((16, D), F32)],
        ),
        out_shape=[jax.ShapeDtypeStruct((5, rows, D), BF), jax.ShapeDtypeStruct((8, rows, D), BF)],
        compiler_params=params(8 * 2**20),
        name="pack",
    )(device, w_qkv, w_out, w_in, w_back, *[v[None] for v in vectors], span[None])


def place_body(split, at_ref, *refs):
    parts, outs, sems = refs[:8], refs[8:-1], refs[-1]
    x, core, z, y = at_ref[0], at_ref[1], at_ref[2], at_ref[3]
    copies = []
    for i, part in enumerate(parts):
        side, far, other = i >> 2, (i >> 1) & 1, i & 1
        count = part.shape[2]
        for near in range(2):
            px = (x + (far if side == 0 else near)) % 2
            py = (y + (near if side == 0 else far)) % 2
            pc = (core + other) % 2
            for dz in range(4):
                pz = (z + 4 - dz) % 4
                if split:
                    target = outs[side].at[:, px, pc, pz, py] if side == 0 else outs[side].at[px, pc, pz, py]
                else:
                    target = outs[0].at[pl.ds(0 if side == 0 else 5 - count, count), px, pc, pz, py]
                copies.append(pltpu.make_async_copy(part.at[near, dz], target, sems.at[len(copies)]))
    for copy in copies:
        copy.start()
    for copy in copies:
        copy.wait()


def place(at, parts, split):
    rows = parts[0].shape[3]
    if split:
        shapes = [(4, 2, 2, 4, 2, rows, D), (2, 2, 4, 2, 4, rows, D)]
    else:
        shapes = [(5, 2, 2, 4, 2, rows, D)]
    return pl.pallas_call(
        lambda *refs: place_body(split, *refs),
        grid_spec=pltpu.PrefetchScalarGridSpec(
            num_scalar_prefetch=1,
            grid=(1,),
            in_specs=[pl.BlockSpec(memory_space=pl.ANY)] * 8,
            out_specs=[pl.BlockSpec(memory_space=pl.ANY)] * len(shapes),
            scratch_shapes=[pltpu.SemaphoreType.DMA((64,))],
        ),
        out_shape=[jax.ShapeDtypeStruct(shape, BF) for shape in shapes],
        compiler_params=params(2 * 2**20),
        name="place",
    )(at, *parts)


def gather_packet(grid, at, packet, first, split):
    ring = [packet] + [grid.send(packet, Z, k) for k in range(1, 4)]
    parts = []
    for units, order in ((slice(0, first), (Y, X)), (slice(first, None), (X, Y))):
        line = jnp.stack([r[units] for r in ring])
        near = jnp.stack([line, grid.send(line, order[0])])
        far = grid.send(near, order[1])
        parts += [near, grid.send(near, CORE), far, grid.send(far, CORE)]
    return place(at, parts, split)


def pick(value, index, dim):
    return lax.dynamic_index_in_dim(value, index, dim, keepdims=False)


def added(a, b, *picks):
    for index, dim in picks:
        a, b = pick(a, index, dim), pick(b, index, dim)
    return (a.astype(F32) + b.astype(F32)).astype(BF)


class Sum:
    def __init__(self, grid, place, left, right):
        self.grid, self.place = grid, place
        self.left = (left[0], grid.send(left[1], CORE))
        self.right = (right[0], grid.send(right[1], CORE))

    def one(self):
        x, _, _, y = self.place
        out_l, out_r = added(*self.left, (1 - x, 0)), added(*self.right, (1 - y, 2))
        keep_l, keep_r = added(*self.left, (x, 0)), added(*self.right, (y, 2))
        self.left = (keep_l, self.grid.send(out_l, X))
        self.right = (keep_r, self.grid.send(out_r, Y))
        return [out_l, out_r]

    def two(self):
        x, _, _, y = self.place
        out_l, out_r = added(*self.left, (1 - y, 1)), added(*self.right, (1 - x, 0))
        keep_l, keep_r = added(*self.left, (y, 1)), added(*self.right, (x, 0))
        self.left = (keep_l, self.grid.send(out_l, Y))
        self.right = (keep_r, self.grid.send(out_r, X))
        return [out_l, out_r]

    def three(self):
        z = self.place[2]
        line = jnp.concatenate([added(*self.left), added(*self.right)], axis=1)
        self.own = pick(line, z, 0)
        self.came = [self.grid.send(pick(line, (z + k) % 4, 0), Z, k) for k in range(1, 4)]
        return [line]

    def result(self):
        total = self.own.astype(F32)
        for piece in self.came:
            total += piece.astype(F32)
        return total


def staged(grid, lengths, tokens, cotangent, shards):
    w_qkv, bias_q, bias_v, w_out, bias_out, gain_one, shift_one, w_in, bias_in, w_back, bias_back, gain_two, shift_two = shards
    rows, span = bias_q.shape[0], bias_in.shape[0]
    where = grid.place()
    x, core, z, y = where
    device = lax.axis_index(AXES)
    at = jnp.stack([x, core, z, y]).astype(jnp.int32)
    core = core.astype(jnp.int32)[None]
    vectors = [bias_q, bias_v, bias_out, gain_one, shift_one, bias_back, gain_two, shift_two]
    one, two = pack(device.astype(jnp.int32)[None], w_qkv, w_out, w_in, w_back, vectors, bias_in)
    (first,) = gather_packet(grid, at, one, 2, False)
    w_in, w_back = gather_packet(grid, at, two, 4, True)
    first = first.reshape(5, grid.count * rows, D)
    w_in = w_in.reshape(4, grid.count * rows, D)
    w_back = w_back.reshape(grid.count * span, D)
    vec = jnp.sum(first[4].reshape(grid.count, rows, D).astype(F32), axis=0)
    weights = (first, w_in, w_back, vec)

    value, low = tokens, tokens
    saved = []
    for _ in range(APPS):
        value, low, stored = layer_forward(value, low, weights, lengths)
        saved.append(stored)
    activations = low

    lowt2, qkv, lse, z1, h1t2, ctxt2, g2, slope, z2 = saved[1]
    e2_2, e1_2, dz1, ea_2, dctx, sums_2 = ffn_back_call(cotangent, z2, z1, slope, w_back, w_in, first, vec)
    heads_2 = [attend_back_call(qkv, dctx, lse, lengths, i) for i in range(GROUPS)]
    grad = dx_call(dz1, heads_2[0][0], heads_2[1][0], first, F32)

    lowt1, qkv, lse, z1, h1t1, ctxt1, g1, slope, z2 = saved[0]
    e2_1, e1_1, dz1, ea_1, dctx, sums_1 = ffn_back_call(grad, z2, z1, slope, w_back, w_in, first, vec)
    right = wgrad_back_call(core, g2, g1, e2_2, e2_1, rows)
    left = wgrad_call(
        core, h1t2, h1t1, e1_2, e1_1, rows, pl.BlockSpec((tokens.shape[0], D), lambda i, n: (0, i)), 4, D
    )
    wide = Sum(grid, where, left, right)

    def by_heads(i, after):
        spec = pl.BlockSpec((1, tokens.shape[0], WIDE), lambda i, n: (i, 0, 0))
        return wgrad_call(core, lowt2, lowt1, heads_2[i][0], heads_1[i][0], rows, spec, 3, WIDE, after)

    heads_1 = [attend_back_call(qkv, dctx, lse, lengths, 0)]
    left = by_heads(0, ())
    right = wgrad_call(
        core, ctxt2, ctxt1, ea_2, ea_1, rows, pl.BlockSpec((tokens.shape[0], WIDE), lambda i, n: (0, i)), 2, WIDE
    )
    group_0 = Sum(grid, where, left, right)
    heads_1.append(attend_back_call(qkv, dctx, lse, lengths, 1, wide.one()))
    after = group_0.one() + wide.two()
    left = by_heads(1, after)
    sums = sums_1 + sums_2
    by_group = [[a + b for a, b in zip(heads_1[i][1:], heads_2[i][1:])] for i in range(GROUPS)]
    line_q, line_v = [jnp.concatenate([jnp.sum(by_group[i][j], axis=0) for i in range(GROUPS)], axis=1) for j in range(2)]
    small = jnp.concatenate([line_q, line_v, sums[2:12]], axis=0).astype(BF)
    small = jnp.concatenate([small[:, :WIDE], small[:, WIDE:]], axis=0)
    small = jnp.broadcast_to(small, (2, 4, 2, 1) + small.shape)
    group_1 = Sum(grid, where, left, (small, small))
    after = group_1.one() + group_0.two()
    grad = dx_call(dz1, heads_1[0][0], heads_1[1][0], first, BF, after)
    wide.three()
    group_0.three()
    group_1.two()
    group_1.three()
    total, half_0, half_1 = wide.result(), group_0.result(), group_1.result()

    w_in_grad = total[:4].swapaxes(0, 1).reshape(rows, 4 * D)
    w_back_grad = total[4:].reshape(4 * rows, D)
    w_qkv_grad = jnp.stack([half_0[:3], half_1[:3]], axis=1).transpose(2, 0, 1, 3).reshape(rows, 3 * D)
    w_out_grad = half_0[3:].swapaxes(0, 1).reshape(rows, D)
    small = half_1[3]
    small = jnp.concatenate([small[:12], small[12:]], axis=1)
    mine = lax.dynamic_slice(small, (0, device * rows), (8, rows))
    per = D // span
    last = lax.dynamic_slice(small, (8 + device // per, device % per * span), (1, span))[0]
    return activations, grad, w_qkv_grad, w_out_grad, w_in_grad, w_back_grad, [mine[i] for i in range(8)] + [last]


def plain(grid, lengths, tokens, cotangent, shards):
    w_qkv, bias_q, bias_v, w_out, bias_out, gain_one, shift_one, w_in, bias_in, w_back, bias_back, gain_two, shift_two = shards
    vectors = [bias_q, bias_v, bias_out, gain_one, shift_one, bias_back, gain_two, shift_two]

    def whole(v):
        return lax.all_gather(v, AXES, axis=0, tiled=True)

    lines = jnp.stack([whole(v) for v in vectors])
    vec = jnp.concatenate([lines, whole(bias_in).reshape(4, D), jnp.zeros((4, D), BF)], axis=0).astype(F32)

    def blocks(w):
        return w.reshape(D, -1, D).swapaxes(0, 1)

    first = jnp.concatenate([blocks(whole(w_qkv)), whole(w_out)[None], jnp.zeros((1, D, D), BF)], axis=0)
    w_in, w_back = blocks(whole(w_in)), whole(w_back)
    weights = (first, w_in, w_back, vec)
    value, low = tokens, tokens
    saved = []
    for _ in range(APPS):
        value, low, stored = layer_forward(value, low, weights, lengths)
        saved.append(stored)
    activations, grad, totals = low, cotangent, None
    for step in reversed(range(APPS)):
        lowt, qkv, lse, z1, h1t, ctxt, g, slope, z2 = saved[step]
        e2, e1, dz1, ea, dctx, sums = ffn_back_call(grad, z2, z1, slope, w_back, w_in, first, vec)
        heads = [attend_back_call(qkv, dctx, lse, lengths, i) for i in range(GROUPS)]
        grad = dx_call(dz1, heads[0][0], heads[1][0], first, F32 if step else BF)
        e = jnp.concatenate([heads[i][0] for i in range(GROUPS)], axis=2).swapaxes(0, 1).reshape(-1, 3 * D)
        lines = [jnp.concatenate([jnp.sum(heads[i][j], axis=0) for i in range(GROUPS)], axis=1) for j in (1, 2)]
        grads = [mm(lowt, e, NN), mm(ctxt, ea, NN), mm(h1t, e1, NN), mm(g, e2, TN)]
        grads += [jnp.concatenate(lines + [sums[2:]], axis=0)]
        totals = grads if totals is None else [a + b for a, b in zip(totals, grads)]
    lines = list(totals.pop())
    totals += lines[:8] + [jnp.concatenate(lines[8:12])]
    owned = [lax.psum_scatter(v, AXES, scatter_dimension=0, tiled=True) for v in totals]
    return activations, grad, *owned[:4], owned[4:]


def make_local(grid):
    def local(tokens, lengths, *rest):
        run = staged if grid.staged else plain
        activations, grad, w_qkv, w_out, w_in, w_back, lines = run(grid, lengths, tokens, rest[-1], rest[:-1])
        return (
            activations, grad, w_qkv, lines[BQ], lines[BV], w_out, lines[BO], lines[G1], lines[S1],
            w_in, lines[8], w_back, lines[BB], lines[G2], lines[S2],
        )

    return local


def solution(mesh):
    wide, line = P(AXES, None), P(AXES)
    return jax.shard_map(
        make_local(Grid(mesh.shape)),
        mesh=mesh,
        in_specs=(wide, line, wide, line, line, wide, line, line, line, wide, line, wide, line, line, line, wide),
        out_specs=(wide, wide, wide, line, line, wide, line, line, line, wide, line, wide, line, line, line),
        check_vma=False,
    )
```

```python
import jax
import jax.numpy as jnp
from jax import lax
from jax.experimental import pallas as pl
from jax.experimental.pallas import tpu as pltpu
from jax.sharding import PartitionSpec as P

D = 768
HEADS = 12
HEAD_DIM = 64
APPS = 2
PAIR = 2 * HEAD_DIM
AXES = ("dp", "fsdp")
BF = jnp.bfloat16
F32 = jnp.float32
NN = (((1,), (0,)), ((), ()))
NT = (((1,), (1,)), ((), ()))
TN = (((0,), (0,)), ((), ()))
VMEM = 56 * 2**20
BQ, BV, BO, G1, S1, BB, G2, S2 = range(8)


def mm(left, right, dims):
    return lax.dot_general(left, right, dims, preferred_element_type=F32)


def params(limit=VMEM):
    return pltpu.CompilerParams(vmem_limit_bytes=limit)


def cost(flops, nbytes, trans=0):
    return pl.CostEstimate(flops=int(flops), bytes_accessed=int(nbytes), transcendentals=int(trans))


def once(shape, index):
    return pl.BlockSpec(shape, index, pipeline_mode=pl.Buffered(1))


def normed(z):
    centered = z - jnp.mean(z, axis=-1, keepdims=True)
    root = lax.rsqrt(jnp.mean(centered * centered, axis=-1, keepdims=True) + 1e-12)
    return centered * root, root


def normed_back(n, root, e):
    return root * (e - jnp.mean(e, axis=-1, keepdims=True) - n * jnp.mean(e * n, axis=-1, keepdims=True))


def colsum(v):
    return jnp.sum(v, axis=0, keepdims=True)


def qkv_body(x_ref, w_ref, vec_ref, o_ref):
    part = pl.program_id(0)
    acc = mm(x_ref[...], w_ref[0], NN)
    bias = jnp.where(part == 0, vec_ref[BQ : BQ + 1, :], jnp.where(part == 2, vec_ref[BV : BV + 1, :], 0.0))
    o_ref[...] = (acc + bias).astype(BF)


def qkv_call(x, w, vec):
    rows = x.shape[0]
    return pl.pallas_call(
        qkv_body,
        grid=(3,),
        in_specs=[
            once((rows, D), lambda i: (0, 0)),
            pl.BlockSpec((1, D, D), lambda i: (i, 0, 0)),
            once(vec.shape, lambda i: (0, 0)),
        ],
        out_specs=pl.BlockSpec((rows, D), lambda i: (0, i)),
        out_shape=jax.ShapeDtypeStruct((rows, 3 * D), BF),
        compiler_params=params(),
        cost_estimate=cost(6 * rows * D * D, 2 * (rows * D * 4 + 3 * D * D)),
        name="qkv",
    )(x, w, vec)


def attend_body(seq, pairs, len_ref, q_ref, k_ref, v_ref, o_ref, l_ref):
    count = len_ref[pl.program_id(0)]
    lane = lax.broadcasted_iota(jnp.int32, (seq, PAIR), 1)
    ok = lax.broadcasted_iota(jnp.int32, (1, seq), 1) < count
    units = [(pr, h) for pr in range(pairs) for h in range(2)]

    def score(unit):
        pr, h = unit
        cols = slice(pr * PAIR, (pr + 1) * PAIR)
        mine = (lane >= HEAD_DIM) == (h == 1)
        q = jnp.where(mine, q_ref[:, cols] * BF(0.125), BF(0))
        return jnp.where(ok, mm(q, k_ref[:, cols], NT), -1e30)

    ahead = score(units[0])
    held = {}
    for i, (pr, h) in enumerate(units):
        s = ahead
        if i + 1 < len(units):
            ahead = score(units[i + 1])
        cols = slice(pr * PAIR, (pr + 1) * PAIR)
        top = jnp.max(s, axis=1, keepdims=True)
        p = jnp.exp(s - top)
        total = jnp.sum(p, axis=1, keepdims=True)
        held[h] = mm(p.astype(BF), v_ref[:, cols], NN) / total
        l_ref[0, pr, h : h + 1, :] = (top + jnp.log(total)).reshape(1, seq)
        if h == 1:
            o_ref[:, cols] = jnp.where(lane < HEAD_DIM, held[0], held[1]).astype(BF)


def attend_call(qkv, lengths, pairs=3):
    rows = qkv.shape[0]
    count = lengths.shape[0]
    seq = rows // count
    groups = D // PAIR // pairs
    wide = PAIR * pairs

    def part(o):
        return pl.BlockSpec((seq, wide), lambda s, p, n: (s, o * groups + p))

    def body(*refs):
        attend_body(seq, pairs, *refs)

    flops = 4 * count * HEADS * seq * seq * HEAD_DIM
    return pl.pallas_call(
        body,
        grid_spec=pltpu.PrefetchScalarGridSpec(
            num_scalar_prefetch=1,
            grid=(count, groups),
            in_specs=[part(0), part(1), part(2)],
            out_specs=[part(0), pl.BlockSpec((1, pairs, 2, seq), lambda s, p, n: (s, p, 0, 0))],
        ),
        out_shape=[
            jax.ShapeDtypeStruct((rows, D), BF),
            jax.ShapeDtypeStruct((count, D // PAIR, 2, seq), F32),
        ],
        compiler_params=params(),
        cost_estimate=cost(4 * flops, 8 * rows * D, count * HEADS * seq * seq),
        name="attend",
    )(lengths, qkv, qkv, qkv)


def gelu_both(u):
    a = 0.7978845608028654
    c = a + (a * 0.044715) * (u * u)
    s = 0.5 + 0.5 * jnp.tanh(u * c)
    g = u * s
    return g, s + (g * (1.0 - s)) * (6.0 * c - 4.0 * a)


ANY = pl.BlockSpec(memory_space=pl.ANY)


def by_rows(block, width):
    return pl.BlockSpec((block, width), lambda i: (i, 0))


def ffn_body(
    renorm, x_ref, ctx_ref, vec_ref, wo_h, wi_h, wb_h,
    z1_ref, h1_ref, g_ref, slope_ref, z2_ref, y_ref, wo_s, wi_s, wb_s, sems,
):
    step = pl.program_id(0)
    copies = [
        pltpu.make_async_copy(wo_h.at[3], wo_s, sems.at[0]),
        pltpu.make_async_copy(wi_h, wi_s, sems.at[1]),
        pltpu.make_async_copy(wb_h, wb_s, sems.at[2]),
    ]

    @pl.when(step == 0)
    def _():
        for copy in copies:
            copy.start()
        copies[0].wait()

    x = x_ref[...].astype(F32)
    if renorm:
        n, _ = normed(x)
        x = n * vec_ref[G2 : G2 + 1, :] + vec_ref[S2 : S2 + 1, :]
    z1 = x + mm(ctx_ref[...], wo_s[...], NN) + vec_ref[BO : BO + 1, :]
    z1_ref[...] = z1
    n, _ = normed(z1)
    h1 = n * vec_ref[G1 : G1 + 1, :] + vec_ref[S1 : S1 + 1, :]
    low = h1.astype(BF)
    h1_ref[...] = low

    @pl.when(step == 0)
    def _():
        copies[1].wait()
        copies[2].wait()

    units = wi_s.shape[0]

    def up(j):
        return mm(low, wi_s[j], NN) + vec_ref[8 + j : 9 + j, :]

    acc = h1 + vec_ref[BB : BB + 1, :]
    f = up(0)
    for j in range(units):
        ahead = up(j + 1) if j + 1 < units else None
        cols = slice(j * D, (j + 1) * D)
        g, slope = gelu_both(f)
        g = g.astype(BF)
        g_ref[:, cols] = g
        slope_ref[:, cols] = slope.astype(BF)
        acc += mm(g, wb_s[cols, :], NN)
        f = ahead
    z2_ref[...] = acc
    n, _ = normed(acc)
    y_ref[...] = (n * vec_ref[G2 : G2 + 1, :] + vec_ref[S2 : S2 + 1, :]).astype(BF)


def weight_scratch(ff):
    return [
        pltpu.VMEM((D, D), BF),
        pltpu.VMEM((ff // D, D, D), BF),
        pltpu.VMEM((ff, D), BF),
        pltpu.SemaphoreType.DMA((3,)),
    ]


def ffn_call(x, ctx, first, vec, wi, wb, renorm, block=512):
    rows = x.shape[0]
    ff = wb.shape[0]
    line, wide = by_rows(block, D), by_rows(block, ff)
    return pl.pallas_call(
        lambda *refs: ffn_body(renorm, *refs),
        grid=(rows // block,),
        in_specs=[line, line, once(vec.shape, lambda i: (0, 0)), ANY, ANY, ANY],
        out_specs=[line, line, wide, wide, line, line],
        out_shape=[
            jax.ShapeDtypeStruct((rows, D), F32),
            jax.ShapeDtypeStruct((rows, D), BF),
            jax.ShapeDtypeStruct((rows, ff), BF),
            jax.ShapeDtypeStruct((rows, ff), BF),
            jax.ShapeDtypeStruct((rows, D), F32),
            jax.ShapeDtypeStruct((rows, D), BF),
        ],
        scratch_shapes=weight_scratch(ff),
        compiler_params=params(),
        cost_estimate=cost(2 * rows * D * (D + 2 * ff), 20 * rows * D + 4 * rows * ff + 4 * D * ff, rows * ff),
        name="ffn",
    )(x, ctx, vec, first, wi, wb)


def ffn_back_body(
    dy_ref, z2_ref, z1_ref, slope_ref, vec_ref, wb_h, wi_h, wo_h,
    e2_ref, e1_ref, dz1_ref, ea_ref, dctx_ref, sums_ref, wo_s, wi_s, wb_s, sems,
):
    step = pl.program_id(0)
    copies = [
        pltpu.make_async_copy(wb_h, wb_s, sems.at[0]),
        pltpu.make_async_copy(wi_h, wi_s, sems.at[1]),
        pltpu.make_async_copy(wo_h.at[3], wo_s, sems.at[2]),
    ]

    @pl.when(step == 0)
    def _():
        for copy in copies:
            copy.start()
        sums_ref[...] = jnp.zeros_like(sums_ref)

    dy = dy_ref[...].astype(F32)
    n, root = normed(z2_ref[...])
    sums_ref[G2 : G2 + 1, :] += colsum(dy * n)
    sums_ref[S2 : S2 + 1, :] += colsum(dy)
    dz2 = normed_back(n, root, dy * vec_ref[G2 : G2 + 1, :])
    e2 = dz2.astype(BF)
    e2_ref[...] = e2
    sums_ref[BB : BB + 1, :] += colsum(e2.astype(F32))

    @pl.when(step == 0)
    def _():
        for copy in copies:
            copy.wait()

    units = wi_s.shape[0]

    def up(j):
        return mm(e2, wb_s[j * D : (j + 1) * D, :], NT)

    acc = dz2
    f = up(0)
    for j in range(units):
        ahead = up(j + 1) if j + 1 < units else None
        cols = slice(j * D, (j + 1) * D)
        e1 = (f * slope_ref[:, cols].astype(F32)).astype(BF)
        e1_ref[:, cols] = e1
        sums_ref[8 + j : 9 + j, :] += colsum(e1.astype(F32))
        acc += mm(e1, wi_s[j], NT)
        f = ahead
    n, root = normed(z1_ref[...])
    sums_ref[G1 : G1 + 1, :] += colsum(acc * n)
    sums_ref[S1 : S1 + 1, :] += colsum(acc)
    dz1 = normed_back(n, root, acc * vec_ref[G1 : G1 + 1, :])
    dz1_ref[...] = dz1
    ea = dz1.astype(BF)
    ea_ref[...] = ea
    sums_ref[BO : BO + 1, :] += colsum(ea.astype(F32))
    dctx_ref[...] = mm(ea, wo_s[...], NT).astype(BF)


def ffn_back_call(dy, z2, z1, slope, wb, wi, first, vec, block=256):
    rows = dy.shape[0]
    ff = wb.shape[0]
    line, wide = by_rows(block, D), by_rows(block, ff)
    held = once(vec.shape, lambda i: (0, 0))
    return pl.pallas_call(
        ffn_back_body,
        grid=(rows // block,),
        in_specs=[line, line, line, wide, held, ANY, ANY, ANY],
        out_specs=[line, wide, line, line, line, held],
        out_shape=[
            jax.ShapeDtypeStruct((rows, D), BF),
            jax.ShapeDtypeStruct((rows, ff), BF),
            jax.ShapeDtypeStruct((rows, D), F32),
            jax.ShapeDtypeStruct((rows, D), BF),
            jax.ShapeDtypeStruct((rows, D), BF),
            jax.ShapeDtypeStruct(vec.shape, F32),
        ],
        scratch_shapes=weight_scratch(ff),
        compiler_params=params(),
        cost_estimate=cost(2 * rows * D * (D + 2 * ff), 20 * rows * D + 4 * rows * ff + 4 * D * ff),
        name="ffn_back",
    )(dy, z2, z1, slope, vec, wb, wi, first)


def attend_back_body(seq, pairs, len_ref, q_ref, k_ref, v_ref, d_ref, l_ref, e_ref, bq_ref, bv_ref):
    count = len_ref[pl.program_id(0)]
    lane = lax.broadcasted_iota(jnp.int32, (seq, PAIR), 1)
    ok = lax.broadcasted_iota(jnp.int32, (seq, seq), 0) < count
    units = [(pr, h) for pr in range(pairs) for h in range(2)]

    def score(unit):
        pr, h = unit
        cols = slice(pr * PAIR, (pr + 1) * PAIR)
        mine = (lane >= HEAD_DIM) == (h == 1)
        q = jnp.where(mine, q_ref[:, cols] * BF(0.125), BF(0))
        s = jnp.where(ok, mm(k_ref[:, cols], q, NT), -1e30)
        return s, mm(v_ref[:, cols], jnp.where(mine, d_ref[:, cols], BF(0)), NT)

    ahead = score(units[0])
    eq, ek, ev = {}, {}, {}
    for i, (pr, h) in enumerate(units):
        s, dp = ahead
        if i + 1 < len(units):
            ahead = score(units[i + 1])
        cols = slice(pr * PAIR, (pr + 1) * PAIR)
        if h == 0:
            kt = (k_ref[:, cols] * BF(0.125)).T
        p = jnp.exp(s - l_ref[0, pr, h : h + 1, :])
        pd = p * dp
        ds = (pd - p * colsum(pd)).astype(BF)
        ev[h] = mm(p.astype(BF), d_ref[:, cols], NN)
        ek[h] = mm(ds, q_ref[:, cols] * BF(0.125), NN)
        eq[h] = mm(kt[h * HEAD_DIM : (h + 1) * HEAD_DIM], ds, NN)
        if h == 1:
            low = jnp.concatenate([eq[0], eq[1]], axis=0).T.astype(BF)
            e_ref[0, :, cols] = low
            bq_ref[0, :, cols] = colsum(low.astype(F32))
            e_ref[1, :, cols] = jnp.where(lane < HEAD_DIM, ek[0], ek[1]).astype(BF)
            low = jnp.where(lane < HEAD_DIM, ev[0], ev[1]).astype(BF)
            e_ref[2, :, cols] = low
            bv_ref[0, :, cols] = colsum(low.astype(F32))


GROUPS = 2
WIDE = D // GROUPS


def attend_back_call(qkv, dctx, lse, lengths, group):
    rows = qkv.shape[0]
    count = lengths.shape[0]
    seq = rows // count
    pairs = WIDE // PAIR

    def part(o):
        return pl.BlockSpec((seq, WIDE), lambda s, n: (s, o * GROUPS + group))

    def body(*refs):
        attend_back_body(seq, pairs, *refs)

    flops = 10 * count * 2 * pairs * seq * seq * HEAD_DIM
    line = pl.BlockSpec((1, 1, WIDE), lambda s, n: (s, 0, 0))
    return pl.pallas_call(
        body,
        grid_spec=pltpu.PrefetchScalarGridSpec(
            num_scalar_prefetch=1,
            grid=(count,),
            in_specs=[
                part(0),
                part(1),
                part(2),
                part(0),
                pl.BlockSpec((1, pairs, 2, seq), lambda s, n: (s, group, 0, 0)),
            ],
            out_specs=[pl.BlockSpec((3, seq, WIDE), lambda s, n: (0, s, 0)), line, line],
        ),
        out_shape=[jax.ShapeDtypeStruct((3, rows, WIDE), BF)] + [jax.ShapeDtypeStruct((count, 1, WIDE), F32)] * 2,
        compiler_params=params(),
        cost_estimate=cost(4 * flops, 14 * rows * WIDE, count * 2 * pairs * seq * seq),
        name="attend_back",
    )(lengths, qkv, qkv, qkv, dctx, lse)


def dx_body(dz1_ref, e0_ref, e1_ref, w_ref, o_ref):
    acc = dz1_ref[...]
    for i in range(3):
        acc += mm(e0_ref[i], w_ref[i, :, :WIDE], NT)
        acc += mm(e1_ref[i], w_ref[i, :, WIDE:], NT)
    o_ref[...] = acc.astype(o_ref.dtype)


def dx_call(dz1, e0, e1, w, dtype, block=256):
    rows = dz1.shape[0]
    line = pl.BlockSpec((block, D), lambda i: (i, 0))
    part = pl.BlockSpec((3, block, WIDE), lambda i: (0, i, 0))
    return pl.pallas_call(
        dx_body,
        grid=(rows // block,),
        in_specs=[line, part, part, once((3, D, D), lambda i: (0, 0, 0))],
        out_specs=line,
        out_shape=jax.ShapeDtypeStruct((rows, D), dtype),
        compiler_params=params(),
        cost_estimate=cost(6 * rows * D * D, 14 * rows * D + 6 * D * D),
        name="dx",
    )(dz1, e0, e1, w)


def wgrad_body(rows, x_first, core_ref, a_ref, c_ref, b_ref, d_ref, keep_ref, send_ref, acc_s):
    b = b_ref[...].reshape(b_ref.shape[-2:])
    d = d_ref[...].reshape(d_ref.shape[-2:])
    acc_s[...] = mm(a_ref[...], b, TN) + mm(c_ref[...], d, TN)
    part = 8 * rows
    for out, core in ((keep_ref, core_ref[0]), (send_ref, 1 - core_ref[0])):
        for xi in range(2):
            for s in range(8):
                zi, yi = s // 2, s % 2
                start = pl.multiple_of(core * part + (2 * xi * part + s * rows), 8)
                value = acc_s[pl.ds(start, rows), :].astype(BF)
                if x_first:
                    out[xi, yi, zi, 0] = value
                else:
                    out[yi, xi, zi, 0] = value


def wgrad_call(core, a, c, b, d, rows, spec, units, width, x_first):
    k, m = a.shape
    held = once((k, m), lambda i, n: (0, 0))
    out = pl.BlockSpec((2, 2, 4, 1, rows, width), lambda i, n: (0, 0, 0, i, 0, 0))
    return pl.pallas_call(
        lambda *refs: wgrad_body(rows, x_first, *refs),
        grid_spec=pltpu.PrefetchScalarGridSpec(
            num_scalar_prefetch=1,
            grid=(units,),
            in_specs=[held, held, spec, spec],
            out_specs=[out, out],
            scratch_shapes=[pltpu.VMEM((m, width), F32)],
        ),
        out_shape=[jax.ShapeDtypeStruct((2, 2, 4, units, rows, width), BF)] * 2,
        compiler_params=params(),
        cost_estimate=cost(4 * k * m * width * units, 4 * k * (m + units * width) + 2 * m * width * units),
        name="wgrad",
    )(core, a, c, b, d)


def wgrad_back_call(core, two, one, e_two, e_one, rows):
    k, ff = two.shape
    block = ff // 8

    def cols(other):
        def index(x, s, n):
            c = 1 - n[0] if other else n[0]
            return (0, (x * 2 + c) * 2 + s)

        return pl.BlockSpec((k, block), index)

    held = once((k, D), lambda x, s, n: (0, 0))
    out = pl.BlockSpec((2, 1, 2, 4, rows, D), lambda x, s, n: (0, x, s, 0, 0, 0))

    def body(core_ref, g2k, g1k, g2s, g1s, e2_ref, e1_ref, keep_ref, send_ref):
        for a, c, o in ((g2k, g1k, keep_ref), (g2s, g1s, send_ref)):
            acc = mm(a[...], e2_ref[...], TN) + mm(c[...], e1_ref[...], TN)
            for s in range(16):
                o[s // 4 % 2, 0, s // 8, s % 4] = acc[s * rows : (s + 1) * rows].astype(BF)

    return pl.pallas_call(
        body,
        grid_spec=pltpu.PrefetchScalarGridSpec(
            num_scalar_prefetch=1,
            grid=(2, 2),
            in_specs=[cols(False), cols(False), cols(True), cols(True), held, held],
            out_specs=[out, out],
        ),
        out_shape=[jax.ShapeDtypeStruct((2, 2, 4, 4, rows, D), BF)] * 2,
        compiler_params=params(),
        cost_estimate=cost(4 * k * ff * D, 4 * k * (ff + D) + 2 * ff * D),
        name="wgrad_back",
    )(core, two, one, two, one, e_two, e_one)


def layer_forward(x, low, weights, lengths, renorm):
    first, w_in, w_back, vec = weights
    qkv = qkv_call(low, first, vec)
    ctx, lse = attend_call(qkv, lengths)
    z1, h1, g, slope, z2, y = ffn_call(x, ctx, first, vec, w_in, w_back, renorm)
    return z2, y, (low, qkv, lse, ctx, z1, h1, g, slope, z2)


class Grid:
    def __init__(self, sizes):
        self.dp, self.fsdp = sizes["dp"], sizes["fsdp"]
        self.count = self.dp * self.fsdp
        self.x, self.core = self.dp // 2, 2
        self.y = self.fsdp // 4
        self.z = self.fsdp // self.y if self.y else 0
        self.staged = self.x == 2 and self.y == 2

    def place(self):
        dp, fsdp = lax.axis_index("dp"), lax.axis_index("fsdp")
        return dp // 2, dp % 2, fsdp // self.y, fsdp % self.y

    def shift(self, dim, step):
        sizes = (self.x, self.core, self.z, self.y)
        pairs = []
        for i in range(self.count):
            at = [i // (self.core * self.fsdp), i // self.fsdp % self.core, i % self.fsdp // self.y, i % self.y]
            at[dim] = (at[dim] + step) % sizes[dim]
            pairs.append((i, ((at[0] * self.core + at[1]) * self.z + at[2]) * self.y + at[3]))
        return pairs

    def send(self, value, dim, step=1):
        return lax.ppermute(value, AXES, self.shift(dim, step))


X, CORE, Z, Y = range(4)


def pack_one_body(at_ref, wq_ref, wo_ref, *rest):
    vectors, span_ref, one_ref, line_s = rest[:8], rest[8], rest[9], rest[10]
    rows = wq_ref.shape[0]
    for i in range(3):
        one_ref[i] = wq_ref[:, i * D : (i + 1) * D]
    one_ref[3] = wo_ref[...]
    line_s[...] = jnp.zeros_like(line_s)
    for i, ref in enumerate(vectors):
        line_s[i : i + 1, :rows] = ref[...].astype(F32)
    span = span_ref.shape[1]
    line_s[8:9, :span] = span_ref[...].astype(F32)
    device = at_ref[0]
    per = D // span
    top = pltpu.roll(line_s[:8], device * rows, 1)
    low = pltpu.roll(line_s[8:16], lax.rem(device, per) * span, 1)
    here = lax.broadcasted_iota(jnp.int32, (8, D), 0) == lax.div(device, per)
    low = jnp.where(here, jnp.broadcast_to(low[:1], (8, D)), 0.0)
    one_ref[4] = jnp.concatenate([top, low, jnp.zeros((rows - 16, D), F32)], axis=0).astype(BF)


def whole_block(v):
    return pl.BlockSpec(v.shape, lambda *_: (0,) * v.ndim)


def pack_one(device, w_qkv, w_out, vectors, span):
    rows = w_qkv.shape[0]
    operands = [w_qkv, w_out, *[v[None] for v in vectors], span[None]]
    return pl.pallas_call(
        pack_one_body,
        grid_spec=pltpu.PrefetchScalarGridSpec(
            num_scalar_prefetch=1,
            grid=(1,),
            in_specs=[whole_block(v) for v in operands],
            out_specs=pl.BlockSpec((5, rows, D), lambda *_: (0, 0, 0)),
            scratch_shapes=[pltpu.VMEM((16, D), F32)],
        ),
        out_shape=jax.ShapeDtypeStruct((5, rows, D), BF),
        compiler_params=params(),
        name="pack_one",
    )(device, *operands)


def pack_two_body(wi_ref, wb_ref, two_ref):
    rows = wi_ref.shape[0]
    for i in range(4):
        two_ref[i] = wi_ref[:, i * D : (i + 1) * D]
        two_ref[4 + i] = wb_ref[i * rows : (i + 1) * rows]


def pack_two(w_in, w_back):
    rows = w_in.shape[0]
    return pl.pallas_call(
        pack_two_body,
        grid=(1,),
        in_specs=[whole_block(w_in), whole_block(w_back)],
        out_specs=pl.BlockSpec((8, rows, D), lambda *_: (0, 0, 0)),
        out_shape=jax.ShapeDtypeStruct((8, rows, D), BF),
        compiler_params=params(),
        name="pack_two",
    )(w_in, w_back)


def place_body(split, at_ref, *refs):
    parts, outs, sems = refs[:8], refs[8:-1], refs[-1]
    x, core, z, y = at_ref[0], at_ref[1], at_ref[2], at_ref[3]
    copies = []
    for i, part in enumerate(parts):
        side, far, other = i >> 2, (i >> 1) & 1, i & 1
        count = part.shape[2]
        for near in range(2):
            px = (x + (far if side == 0 else near)) % 2
            py = (y + (near if side == 0 else far)) % 2
            pc = (core + other) % 2
            for dz in range(4):
                pz = (z + 4 - dz) % 4
                if split:
                    target = outs[side].at[:, px, pc, pz, py] if side == 0 else outs[side].at[px, pc, pz, py]
                else:
                    target = outs[0].at[pl.ds(0 if side == 0 else 5 - count, count), px, pc, pz, py]
                copies.append(pltpu.make_async_copy(part.at[near, dz], target, sems.at[len(copies)]))
    for copy in copies:
        copy.start()
    for copy in copies:
        copy.wait()


def place(at, parts, split):
    rows = parts[0].shape[3]
    if split:
        shapes = [(4, 2, 2, 4, 2, rows, D), (2, 2, 4, 2, 4, rows, D)]
    else:
        shapes = [(5, 2, 2, 4, 2, rows, D)]
    return pl.pallas_call(
        lambda *refs: place_body(split, *refs),
        grid_spec=pltpu.PrefetchScalarGridSpec(
            num_scalar_prefetch=1,
            grid=(1,),
            in_specs=[ANY] * 8,
            out_specs=[ANY] * len(shapes),
            scratch_shapes=[pltpu.SemaphoreType.DMA((64,))],
        ),
        out_shape=[jax.ShapeDtypeStruct(shape, BF) for shape in shapes],
        compiler_params=params(),
        name="place",
    )(at, *parts)


def after(value, *others):
    return lax.optimization_barrier((value, *others))[0]


class Gather:
    def __init__(self, grid, packet, first):
        self.grid, self.first = grid, first
        self.ring = [packet] + [grid.send(packet, Z, k) for k in range(1, 4)]

    def one(self, *others):
        ring = lax.optimization_barrier((*self.ring, *others))[:4]
        self.line = [jnp.stack([r[: self.first] for r in ring]), jnp.stack([r[self.first :] for r in ring])]
        self.came = [self.grid.send(v, d) for v, d in zip(self.line, (Y, X))]

    def two(self):
        self.near = [jnp.stack(pair) for pair in zip(self.line, self.came)]
        self.far = [self.grid.send(v, d) for v, d in zip(self.near, (X, Y))]

    def parts(self):
        out = []
        for near, far in zip(self.near, self.far):
            out += [near, self.grid.send(near, CORE), far, self.grid.send(far, CORE)]
        return out


def pick(value, index, dim):
    return lax.dynamic_index_in_dim(value, index, dim, keepdims=False)


def added(a, b, *picks):
    for index, dim in picks:
        a, b = pick(a, index, dim), pick(b, index, dim)
    return (a.astype(F32) + b.astype(F32)).astype(BF)


class Sum:
    def __init__(self, grid, place, left, right):
        self.grid, self.place = grid, place
        self.left = (left[0], grid.send(left[1], CORE))
        self.right = (right[0], grid.send(right[1], CORE))

    def one(self, *others):
        x, _, _, y = self.place
        self.left = (after(self.left[0], *others), self.left[1])
        self.right = (after(self.right[0], *others), self.right[1])
        out_l, out_r = added(*self.left, (1 - x, 0)), added(*self.right, (1 - y, 0))
        keep_l, keep_r = added(*self.left, (x, 0)), added(*self.right, (y, 0))
        self.left = (keep_l, self.grid.send(out_l, X))
        self.right = (keep_r, self.grid.send(out_r, Y))
        return [out_l, out_r]

    def two(self):
        x, _, _, y = self.place
        out_l, out_r = added(*self.left, (1 - y, 0)), added(*self.right, (1 - x, 0))
        keep_l, keep_r = added(*self.left, (y, 0)), added(*self.right, (x, 0))
        self.left = (keep_l, self.grid.send(out_l, Y))
        self.right = (keep_r, self.grid.send(out_r, X))
        return [out_l, out_r]

    def three(self, *others):
        z = self.place[2]
        self.left = (after(self.left[0], *others), self.left[1])
        line = jnp.concatenate([added(*self.left), added(*self.right)], axis=1)
        self.own = pick(line, z, 0)
        self.came = [self.grid.send(pick(line, (z + k) % 4, 0), Z, k) for k in range(1, 4)]
        return [line]

    def result(self):
        total = self.own.astype(F32)
        for piece in self.came:
            total += piece.astype(F32)
        return total


def staged(grid, lengths, tokens, cotangent, shards):
    w_qkv, bias_q, bias_v, w_out, bias_out, gain_one, shift_one, w_in, bias_in, w_back, bias_back, gain_two, shift_two = shards
    rows, span = bias_q.shape[0], bias_in.shape[0]
    where = grid.place()
    x, core, z, y = where
    device = lax.axis_index(AXES)
    at = jnp.stack([x, core, z, y]).astype(jnp.int32)
    core = core.astype(jnp.int32)[None]
    vectors = [bias_q, bias_v, bias_out, gain_one, shift_one, bias_back, gain_two, shift_two]
    one = Gather(grid, pack_one(device.astype(jnp.int32)[None], w_qkv, w_out, vectors, bias_in), 2)
    two = Gather(grid, after(pack_two(w_in, w_back), *one.ring), 4)
    one.one()
    one.two()
    two.one(*one.far)
    (first,) = place(at, one.parts(), False)
    first = first.reshape(5, grid.count * rows, D)
    vec = jnp.sum(first[4].reshape(grid.count, rows, D).astype(F32), axis=0)
    qkv = qkv_call(tokens, first, vec)
    two.two()
    ctx, lse = attend_call(after(qkv, *two.near), lengths)
    w_in, w_back = place(at, two.parts(), True)
    w_in = w_in.reshape(4, grid.count * rows, D)
    w_back = w_back.reshape(grid.count * span, D)
    z1, h1, g, slope, z2, low = ffn_call(tokens, ctx, first, vec, w_in, w_back, False)
    saved = [(tokens, qkv, lse, ctx, z1, h1, g, slope, z2)]
    weights = (first, w_in, w_back, vec)
    _, low, stored = layer_forward(z2, low, weights, lengths, True)
    saved.append(stored)
    activations = low

    low2, qkv, lse, ctx2, z1, h2, g2, slope, z2 = saved[1]
    e2_2, e1_2, dz1, ea_2, dctx, sums_2 = ffn_back_call(cotangent, z2, z1, slope, w_back, w_in, first, vec)
    heads_2 = [attend_back_call(qkv, dctx, lse, lengths, i) for i in range(GROUPS)]
    grad = dx_call(dz1, heads_2[0][0], heads_2[1][0], first, F32)

    low1, qkv, lse, ctx1, z1, h1, g1, slope, z2 = saved[0]
    e2_1, e1_1, dz1, ea_1, dctx, sums_1 = ffn_back_call(grad, z2, z1, slope, w_back, w_in, first, vec)
    count = tokens.shape[0]

    def by_heads(i, low2):
        spec = pl.BlockSpec((1, count, WIDE), lambda i, n: (i, 0, 0))
        return wgrad_call(core, low2, low1, heads_2[i][0], heads_1[i][0], rows, spec, 3, WIDE, True)

    right = wgrad_back_call(core, g2, g1, e2_2, e2_1, rows)
    spec = pl.BlockSpec((count, D), lambda i, n: (0, i))
    left = wgrad_call(core, after(h2, right[0]), h1, e1_2, e1_1, rows, spec, 4, D, True)
    wide = Sum(grid, where, left, right)
    heads_1 = [attend_back_call(qkv, after(dctx, left[0]), lse, lengths, 0)]
    steps = wide.one()
    heads_1.append(attend_back_call(qkv, after(dctx, heads_1[0][0], *steps), lse, lengths, 1))
    spec = pl.BlockSpec((count, WIDE), lambda i, n: (0, i))
    right = wgrad_call(core, after(ctx2, heads_1[1][0]), ctx1, ea_2, ea_1, rows, spec, 2, WIDE, False)
    left = by_heads(0, after(low2, right[0]))
    group_0 = Sum(grid, where, left, right)
    steps = wide.two()
    left = by_heads(1, after(low2, left[0], *steps))
    sums = sums_1 + sums_2
    by_group = [[a + b for a, b in zip(heads_1[i][1:], heads_2[i][1:])] for i in range(GROUPS)]
    line_q, line_v = [jnp.concatenate([jnp.sum(by_group[i][j], axis=0) for i in range(GROUPS)], axis=1) for j in range(2)]
    small = jnp.concatenate([line_q, line_v, sums[2:12]], axis=0).astype(BF)
    small = jnp.concatenate([small[:, :WIDE], small[:, WIDE:]], axis=0)
    small = jnp.broadcast_to(small, (2, 2, 4, 1) + small.shape)
    small = after(small, left[0])
    group_1 = Sum(grid, where, left, (small, small))
    steps = group_0.one(left[0]) + wide.three(left[0])
    grad = dx_call(after(dz1, left[0], *steps), heads_1[0][0], heads_1[1][0], first, BF)
    group_1.one()
    group_0.two()
    group_1.two()
    group_0.three()
    group_1.three()
    total, half_0, half_1 = wide.result(), group_0.result(), group_1.result()

    w_in_grad = total[:4].swapaxes(0, 1).reshape(rows, 4 * D)
    w_back_grad = total[4:].reshape(4 * rows, D)
    w_qkv_grad = jnp.stack([half_0[:3], half_1[:3]], axis=1).transpose(2, 0, 1, 3).reshape(rows, 3 * D)
    w_out_grad = half_0[3:].swapaxes(0, 1).reshape(rows, D)
    small = half_1[3]
    small = jnp.concatenate([small[:12], small[12:]], axis=1)
    mine = lax.dynamic_slice(small, (0, device * rows), (8, rows))
    per = D // span
    last = lax.dynamic_slice(small, (8 + device // per, device % per * span), (1, span))[0]
    return activations, grad, w_qkv_grad, w_out_grad, w_in_grad, w_back_grad, [mine[i] for i in range(8)] + [last]


def plain(grid, lengths, tokens, cotangent, shards):
    w_qkv, bias_q, bias_v, w_out, bias_out, gain_one, shift_one, w_in, bias_in, w_back, bias_back, gain_two, shift_two = shards
    vectors = [bias_q, bias_v, bias_out, gain_one, shift_one, bias_back, gain_two, shift_two]

    def whole(v):
        return lax.all_gather(v, AXES, axis=0, tiled=True)

    lines = jnp.stack([whole(v) for v in vectors])
    vec = jnp.concatenate([lines, whole(bias_in).reshape(4, D), jnp.zeros((4, D), BF)], axis=0).astype(F32)

    def blocks(w):
        return w.reshape(D, -1, D).swapaxes(0, 1)

    first = jnp.concatenate([blocks(whole(w_qkv)), whole(w_out)[None], jnp.zeros((1, D, D), BF)], axis=0)
    w_in, w_back = blocks(whole(w_in)), whole(w_back)
    weights = (first, w_in, w_back, vec)
    value, low = tokens, tokens
    saved = []
    for step in range(APPS):
        value, low, stored = layer_forward(value, low, weights, lengths, step > 0)
        saved.append(stored)
    activations, grad, totals = low, cotangent, None
    for step in reversed(range(APPS)):
        low, qkv, lse, ctx, z1, h1, g, slope, z2 = saved[step]
        e2, e1, dz1, ea, dctx, sums = ffn_back_call(grad, z2, z1, slope, w_back, w_in, first, vec)
        heads = [attend_back_call(qkv, dctx, lse, lengths, i) for i in range(GROUPS)]
        grad = dx_call(dz1, heads[0][0], heads[1][0], first, F32 if step else BF)
        e = jnp.concatenate([heads[i][0] for i in range(GROUPS)], axis=2).swapaxes(0, 1).reshape(-1, 3 * D)
        lines = [jnp.concatenate([jnp.sum(heads[i][j], axis=0) for i in range(GROUPS)], axis=1) for j in (1, 2)]
        grads = [mm(low, e, TN), mm(ctx, ea, TN), mm(h1, e1, TN), mm(g, e2, TN)]
        grads += [jnp.concatenate(lines + [sums[2:]], axis=0)]
        totals = grads if totals is None else [a + b for a, b in zip(totals, grads)]
    lines = list(totals.pop())
    totals += lines[:8] + [jnp.concatenate(lines[8:12])]
    owned = [lax.psum_scatter(v, AXES, scatter_dimension=0, tiled=True) for v in totals]
    return activations, grad, *owned[:4], owned[4:]


def make_local(grid):
    def local(tokens, lengths, *rest):
        run = staged if grid.staged else plain
        activations, grad, w_qkv, w_out, w_in, w_back, lines = run(grid, lengths, tokens, rest[-1], rest[:-1])
        return (
            activations, grad, w_qkv, lines[BQ], lines[BV], w_out, lines[BO], lines[G1], lines[S1],
            w_in, lines[8], w_back, lines[BB], lines[G2], lines[S2],
        )

    return local


def solution(mesh):
    wide, line = P(AXES, None), P(AXES)
    return jax.shard_map(
        make_local(Grid(mesh.shape)),
        mesh=mesh,
        in_specs=(wide, line, wide, line, line, wide, line, line, line, wide, line, wide, line, line, line, wide),
        out_specs=(wide, wide, wide, line, line, wide, line, line, line, wide, line, wide, line, line, line),
        check_vma=False,
    )
```

```python
import jax
import jax.numpy as jnp
from jax import lax
from jax.experimental import pallas as pl
from jax.experimental.pallas import tpu as pltpu
from jax.sharding import PartitionSpec as P

D = 768
HEADS = 12
HEAD_DIM = 64
APPS = 2
PAIR = 2 * HEAD_DIM
AXES = ("dp", "fsdp")
BF = jnp.bfloat16
F32 = jnp.float32
NN = (((1,), (0,)), ((), ()))
NT = (((1,), (1,)), ((), ()))
TN = (((0,), (0,)), ((), ()))
VMEM = 56 * 2**20
BQ, BV, BO, G1, S1, BB, G2, S2 = range(8)


def mm(left, right, dims):
    return lax.dot_general(left, right, dims, preferred_element_type=F32)


def params(limit=VMEM):
    return pltpu.CompilerParams(vmem_limit_bytes=limit)


def cost():
    return pl.CostEstimate(flops=1, bytes_accessed=1, transcendentals=0)


def once(shape, index):
    return pl.BlockSpec(shape, index, pipeline_mode=pl.Buffered(1))


def whole_block(v):
    return pl.BlockSpec(v.shape, lambda *_: (0,) * v.ndim)


def normed(z):
    centered = z - jnp.mean(z, axis=-1, keepdims=True)
    root = lax.rsqrt(jnp.mean(centered * centered, axis=-1, keepdims=True) + 1e-12)
    return centered * root, root


def normed_back(n, root, e):
    return root * (e - jnp.mean(e, axis=-1, keepdims=True) - n * jnp.mean(e * n, axis=-1, keepdims=True))


def colsum(v):
    return jnp.sum(v, axis=0, keepdims=True)


def qkv_body(x_ref, w_ref, vec_ref, o_ref):
    part = pl.program_id(0)
    acc = mm(x_ref[...], w_ref[0], NN)
    bias = jnp.where(part == 0, vec_ref[BQ : BQ + 1, :], jnp.where(part == 2, vec_ref[BV : BV + 1, :], 0.0))
    o_ref[...] = (acc + bias).astype(BF)


def qkv_call(x, w, vec):
    rows = x.shape[0]
    return pl.pallas_call(
        qkv_body,
        grid=(3,),
        in_specs=[
            once((rows, D), lambda i: (0, 0)),
            pl.BlockSpec((1, D, D), lambda i: (i, 0, 0)),
            once(vec.shape, lambda i: (0, 0)),
        ],
        out_specs=pl.BlockSpec((rows, D), lambda i: (0, i)),
        out_shape=jax.ShapeDtypeStruct((rows, 3 * D), BF),
        compiler_params=params(),
        cost_estimate=cost(),
        name="qkv",
    )(x, w, vec)


def attend_body(seq, pairs, len_ref, q_ref, k_ref, v_ref, o_ref, l_ref):
    count = len_ref[pl.program_id(0)]
    lane = lax.broadcasted_iota(jnp.int32, (seq, PAIR), 1)
    ok = lax.broadcasted_iota(jnp.int32, (1, seq), 1) < count
    units = [(pr, h) for pr in range(pairs) for h in range(2)]

    def score(unit):
        pr, h = unit
        cols = slice(pr * PAIR, (pr + 1) * PAIR)
        mine = (lane >= HEAD_DIM) == (h == 1)
        q = jnp.where(mine, q_ref[:, cols] * BF(0.125), BF(0))
        return jnp.where(ok, mm(q, k_ref[:, cols], NT), -1e30)

    ahead = score(units[0])
    held = {}
    for i, (pr, h) in enumerate(units):
        s = ahead
        if i + 1 < len(units):
            ahead = score(units[i + 1])
        cols = slice(pr * PAIR, (pr + 1) * PAIR)
        top = jnp.max(s, axis=1, keepdims=True)
        p = jnp.exp(s - top)
        total = jnp.sum(p, axis=1, keepdims=True)
        held[h] = mm(p.astype(BF), v_ref[:, cols], NN) / total
        l_ref[0, pr, h : h + 1, :] = (top + jnp.log(total)).reshape(1, seq)
        if h == 1:
            o_ref[:, cols] = jnp.where(lane < HEAD_DIM, held[0], held[1]).astype(BF)


def attend_call(qkv, lengths, pairs=3):
    rows = qkv.shape[0]
    count = lengths.shape[0]
    seq = rows // count
    groups = D // PAIR // pairs
    wide = PAIR * pairs

    def part(o):
        return pl.BlockSpec((seq, wide), lambda s, p, n: (s, o * groups + p))

    def body(*refs):
        attend_body(seq, pairs, *refs)

    return pl.pallas_call(
        body,
        grid_spec=pltpu.PrefetchScalarGridSpec(
            num_scalar_prefetch=1,
            grid=(count, groups),
            in_specs=[part(0), part(1), part(2)],
            out_specs=[part(0), pl.BlockSpec((1, pairs, 2, seq), lambda s, p, n: (s, p, 0, 0))],
        ),
        out_shape=[
            jax.ShapeDtypeStruct((rows, D), BF),
            jax.ShapeDtypeStruct((count, D // PAIR, 2, seq), F32),
        ],
        compiler_params=params(),
        cost_estimate=cost(),
        name="attend",
    )(lengths, qkv, qkv, qkv)


def gelu_both(u):
    a = 0.7978845608028654
    c = a + (a * 0.044715) * (u * u)
    s = 0.5 + 0.5 * jnp.tanh(u * c)
    g = u * s
    return g, s + (g * (1.0 - s)) * (6.0 * c - 4.0 * a)


ANY = pl.BlockSpec(memory_space=pl.ANY)


def by_rows(block, width):
    return pl.BlockSpec((block, width), lambda i: (i, 0))


def ffn_body(
    renorm, x_ref, ctx_ref, vec_ref, wo_h, wi_h, wb_h,
    z1_ref, h1_ref, g_ref, slope_ref, z2_ref, y_ref, wo_s, wi_s, wb_s, sems,
):
    step = pl.program_id(0)
    copies = [
        pltpu.make_async_copy(wo_h.at[3], wo_s, sems.at[0]),
        pltpu.make_async_copy(wi_h, wi_s, sems.at[1]),
        pltpu.make_async_copy(wb_h, wb_s, sems.at[2]),
    ]

    @pl.when(step == 0)
    def _():
        for copy in copies:
            copy.start()
        copies[0].wait()

    x = x_ref[...].astype(F32)
    if renorm:
        n, _ = normed(x)
        x = n * vec_ref[G2 : G2 + 1, :] + vec_ref[S2 : S2 + 1, :]
    z1 = x + mm(ctx_ref[...], wo_s[...], NN) + vec_ref[BO : BO + 1, :]
    z1_ref[...] = z1
    n, _ = normed(z1)
    h1 = n * vec_ref[G1 : G1 + 1, :] + vec_ref[S1 : S1 + 1, :]
    low = h1.astype(BF)
    h1_ref[...] = low

    @pl.when(step == 0)
    def _():
        copies[1].wait()
        copies[2].wait()

    units = wi_s.shape[0]

    def up(j):
        return mm(low, wi_s[j], NN) + vec_ref[8 + j : 9 + j, :]

    acc = h1 + vec_ref[BB : BB + 1, :]
    f = up(0)
    for j in range(units):
        ahead = up(j + 1) if j + 1 < units else None
        cols = slice(j * D, (j + 1) * D)
        g, slope = gelu_both(f)
        g = g.astype(BF)
        g_ref[:, cols] = g
        slope_ref[:, cols] = slope.astype(BF)
        acc += mm(g, wb_s[cols, :], NN)
        f = ahead
    z2_ref[...] = acc
    n, _ = normed(acc)
    y_ref[...] = (n * vec_ref[G2 : G2 + 1, :] + vec_ref[S2 : S2 + 1, :]).astype(BF)


def weight_scratch(ff):
    return [
        pltpu.VMEM((D, D), BF),
        pltpu.VMEM((ff // D, D, D), BF),
        pltpu.VMEM((ff, D), BF),
        pltpu.SemaphoreType.DMA((3,)),
    ]


def ffn_call(x, ctx, first, vec, wi, wb, renorm, block=512):
    rows = x.shape[0]
    ff = wb.shape[0]
    line, wide = by_rows(block, D), by_rows(block, ff)
    return pl.pallas_call(
        lambda *refs: ffn_body(renorm, *refs),
        grid=(rows // block,),
        in_specs=[line, line, once(vec.shape, lambda i: (0, 0)), ANY, ANY, ANY],
        out_specs=[line, line, wide, wide, line, line],
        out_shape=[
            jax.ShapeDtypeStruct((rows, D), F32),
            jax.ShapeDtypeStruct((rows, D), BF),
            jax.ShapeDtypeStruct((rows, ff), BF),
            jax.ShapeDtypeStruct((rows, ff), BF),
            jax.ShapeDtypeStruct((rows, D), F32),
            jax.ShapeDtypeStruct((rows, D), BF),
        ],
        scratch_shapes=weight_scratch(ff),
        compiler_params=params(),
        cost_estimate=cost(),
        name="ffn",
    )(x, ctx, vec, first, wi, wb)


def ffn_back_body(
    dy_ref, z2_ref, z1_ref, slope_ref, vec_ref, wb_h, wi_h, wo_h,
    e2_ref, e1_ref, dz1_ref, ea_ref, dctx_ref, sums_ref, wo_s, wi_s, wb_s, sems,
):
    step = pl.program_id(0)
    copies = [
        pltpu.make_async_copy(wb_h, wb_s, sems.at[0]),
        pltpu.make_async_copy(wi_h, wi_s, sems.at[1]),
        pltpu.make_async_copy(wo_h.at[3], wo_s, sems.at[2]),
    ]

    @pl.when(step == 0)
    def _():
        for copy in copies:
            copy.start()
        sums_ref[...] = jnp.zeros_like(sums_ref)

    dy = dy_ref[...].astype(F32)
    n, root = normed(z2_ref[...])
    sums_ref[G2 : G2 + 1, :] += colsum(dy * n)
    sums_ref[S2 : S2 + 1, :] += colsum(dy)
    dz2 = normed_back(n, root, dy * vec_ref[G2 : G2 + 1, :])
    e2 = dz2.astype(BF)
    e2_ref[...] = e2
    sums_ref[BB : BB + 1, :] += colsum(e2.astype(F32))

    @pl.when(step == 0)
    def _():
        for copy in copies:
            copy.wait()

    units = wi_s.shape[0]

    def up(j):
        return mm(e2, wb_s[j * D : (j + 1) * D, :], NT)

    acc = dz2
    f = up(0)
    for j in range(units):
        ahead = up(j + 1) if j + 1 < units else None
        cols = slice(j * D, (j + 1) * D)
        e1 = (f * slope_ref[:, cols].astype(F32)).astype(BF)
        e1_ref[:, cols] = e1
        sums_ref[8 + j : 9 + j, :] += colsum(e1.astype(F32))
        acc += mm(e1, wi_s[j], NT)
        f = ahead
    n, root = normed(z1_ref[...])
    sums_ref[G1 : G1 + 1, :] += colsum(acc * n)
    sums_ref[S1 : S1 + 1, :] += colsum(acc)
    dz1 = normed_back(n, root, acc * vec_ref[G1 : G1 + 1, :])
    dz1_ref[...] = dz1
    ea = dz1.astype(BF)
    ea_ref[...] = ea
    sums_ref[BO : BO + 1, :] += colsum(ea.astype(F32))
    dctx_ref[...] = mm(ea, wo_s[...], NT).astype(BF)


def ffn_back_call(dy, z2, z1, slope, wb, wi, first, vec, block=256):
    rows = dy.shape[0]
    ff = wb.shape[0]
    line, wide = by_rows(block, D), by_rows(block, ff)
    held = once(vec.shape, lambda i: (0, 0))
    return pl.pallas_call(
        ffn_back_body,
        grid=(rows // block,),
        in_specs=[line, line, line, wide, held, ANY, ANY, ANY],
        out_specs=[line, wide, line, line, line, held],
        out_shape=[
            jax.ShapeDtypeStruct((rows, D), BF),
            jax.ShapeDtypeStruct((rows, ff), BF),
            jax.ShapeDtypeStruct((rows, D), F32),
            jax.ShapeDtypeStruct((rows, D), BF),
            jax.ShapeDtypeStruct((rows, D), BF),
            jax.ShapeDtypeStruct(vec.shape, F32),
        ],
        scratch_shapes=weight_scratch(ff),
        compiler_params=params(),
        cost_estimate=cost(),
        name="ffn_back",
    )(dy, z2, z1, slope, vec, wb, wi, first)


def attend_back_body(seq, pairs, len_ref, q_ref, k_ref, v_ref, d_ref, l_ref, e_ref, bq_ref, bv_ref):
    count = len_ref[pl.program_id(0)]
    lane = lax.broadcasted_iota(jnp.int32, (seq, PAIR), 1)
    ok = lax.broadcasted_iota(jnp.int32, (seq, seq), 0) < count
    units = [(pr, h) for pr in range(pairs) for h in range(2)]

    def score(unit):
        pr, h = unit
        cols = slice(pr * PAIR, (pr + 1) * PAIR)
        mine = (lane >= HEAD_DIM) == (h == 1)
        q = jnp.where(mine, q_ref[:, cols] * BF(0.125), BF(0))
        s = jnp.where(ok, mm(k_ref[:, cols], q, NT), -1e30)
        return s, mm(v_ref[:, cols], jnp.where(mine, d_ref[:, cols], BF(0)), NT)

    ahead = score(units[0])
    eq, ek, ev = {}, {}, {}
    for i, (pr, h) in enumerate(units):
        s, dp = ahead
        if i + 1 < len(units):
            ahead = score(units[i + 1])
        cols = slice(pr * PAIR, (pr + 1) * PAIR)
        if h == 0:
            kt = (k_ref[:, cols] * BF(0.125)).T
        p = jnp.exp(s - l_ref[0, pr, h : h + 1, :])
        pd = p * dp
        ds = (pd - p * colsum(pd)).astype(BF)
        ev[h] = mm(p.astype(BF), d_ref[:, cols], NN)
        ek[h] = mm(ds, q_ref[:, cols] * BF(0.125), NN)
        eq[h] = mm(kt[h * HEAD_DIM : (h + 1) * HEAD_DIM], ds, NN)
        if h == 1:
            low = jnp.concatenate([eq[0], eq[1]], axis=0).T.astype(BF)
            e_ref[0, :, cols] = low
            bq_ref[0, :, cols] = colsum(low.astype(F32))
            e_ref[1, :, cols] = jnp.where(lane < HEAD_DIM, ek[0], ek[1]).astype(BF)
            low = jnp.where(lane < HEAD_DIM, ev[0], ev[1]).astype(BF)
            e_ref[2, :, cols] = low
            bv_ref[0, :, cols] = colsum(low.astype(F32))


GROUPS = 2
WIDE = D // GROUPS


def attend_back_call(qkv, dctx, lse, lengths, group):
    rows = qkv.shape[0]
    count = lengths.shape[0]
    seq = rows // count
    pairs = WIDE // PAIR

    def part(o):
        return pl.BlockSpec((seq, WIDE), lambda s, n: (s, o * GROUPS + group))

    def body(*refs):
        attend_back_body(seq, pairs, *refs)

    line = pl.BlockSpec((1, 1, WIDE), lambda s, n: (s, 0, 0))
    return pl.pallas_call(
        body,
        grid_spec=pltpu.PrefetchScalarGridSpec(
            num_scalar_prefetch=1,
            grid=(count,),
            in_specs=[
                part(0),
                part(1),
                part(2),
                part(0),
                pl.BlockSpec((1, pairs, 2, seq), lambda s, n: (s, group, 0, 0)),
            ],
            out_specs=[pl.BlockSpec((3, seq, WIDE), lambda s, n: (0, s, 0)), line, line],
        ),
        out_shape=[jax.ShapeDtypeStruct((3, rows, WIDE), BF)] + [jax.ShapeDtypeStruct((count, 1, WIDE), F32)] * 2,
        compiler_params=params(),
        cost_estimate=cost(),
        name="attend_back",
    )(lengths, qkv, qkv, qkv, dctx, lse)


def dx_body(dz1_ref, e0_ref, e1_ref, w_ref, o_ref):
    acc = dz1_ref[...]
    for i in range(3):
        acc += mm(e0_ref[i], w_ref[i, :, :WIDE], NT)
        acc += mm(e1_ref[i], w_ref[i, :, WIDE:], NT)
    o_ref[...] = acc.astype(o_ref.dtype)


def dx_call(dz1, e0, e1, w, dtype, block=256):
    rows = dz1.shape[0]
    line = pl.BlockSpec((block, D), lambda i: (i, 0))
    part = pl.BlockSpec((3, block, WIDE), lambda i: (0, i, 0))
    return pl.pallas_call(
        dx_body,
        grid=(rows // block,),
        in_specs=[line, part, part, once((3, D, D), lambda i: (0, 0, 0))],
        out_specs=line,
        out_shape=jax.ShapeDtypeStruct((rows, D), dtype),
        compiler_params=params(),
        cost_estimate=cost(),
        name="dx",
    )(dz1, e0, e1, w)


def deal(acc_s, rows, x_first, core_ref, keep_ref, send_ref):
    part = 8 * rows
    for out, core in ((keep_ref, core_ref[0]), (send_ref, 1 - core_ref[0])):
        for xi in range(2):
            for s in range(8):
                zi, yi = s // 2, s % 2
                start = pl.multiple_of(core * part + (2 * xi * part + s * rows), 8)
                value = acc_s[pl.ds(start, rows), :].astype(BF)
                if x_first:
                    out[xi, yi, zi, 0] = value
                else:
                    out[yi, xi, zi, 0] = value


def packet(rows, units, width):
    spec = pl.BlockSpec((2, 2, 4, 1, rows, width), lambda i, n: (0, 0, 0, i, 0, 0))
    return [spec] * 2, [jax.ShapeDtypeStruct((2, 2, 4, units, rows, width), BF)] * 2


def wgrad_in_call(core, a, c, b, d, rows):
    k, n = b.shape
    held = once((k, D), lambda i, n: (0, 0))
    spec = pl.BlockSpec((k, D), lambda i, n: (0, i))
    out_specs, out_shape = packet(rows, n // D, D)

    def body(core_ref, a_ref, c_ref, b_ref, d_ref, keep_ref, send_ref, acc_s):
        acc_s[...] = mm(a_ref[...], b_ref[...], TN) + mm(c_ref[...], d_ref[...], TN)
        deal(acc_s, rows, True, core_ref, keep_ref, send_ref)

    return pl.pallas_call(
        body,
        grid_spec=pltpu.PrefetchScalarGridSpec(
            num_scalar_prefetch=1,
            grid=(n // D,),
            in_specs=[held, held, spec, spec],
            out_specs=out_specs,
            scratch_shapes=[pltpu.VMEM((D, D), F32)],
        ),
        out_shape=out_shape,
        compiler_params=params(),
        cost_estimate=cost(),
        name="wgrad_in",
    )(core, a, c, b, d)


def wgrad_heads_call(core, low2, low1, e2, e1, rows, others, x_first):
    k = low2.shape[0]
    last = len(others) == 4
    held = once((k, D), lambda i, n: (0, 0))
    spec = pl.BlockSpec((1, k, WIDE), lambda i, n: (jnp.minimum(i, 2), 0, 0))
    units = 5 if last else 4
    out_specs, out_shape = packet(rows, units, WIDE)
    if last:
        half = pl.BlockSpec((k, WIDE), lambda i, n: (0, jnp.maximum(i - 3, 0)))
        more = [held, held, half, half]
    else:
        more = [whole_block(v) for v in others]

    def body(core_ref, a_ref, c_ref, b_ref, d_ref, *rest):
        rest, (keep_ref, send_ref, acc_s) = rest[:-3], rest[-3:]
        step = pl.program_id(0)

        @pl.when(step < 3)
        def _():
            acc_s[...] = mm(a_ref[...], b_ref[0], TN) + mm(c_ref[...], d_ref[0], TN)

        if last:

            @pl.when(step >= 3)
            def _():
                acc_s[...] = mm(rest[0][...], rest[2][...], TN) + mm(rest[1][...], rest[3][...], TN)

            deal(acc_s, rows, x_first, core_ref, keep_ref, send_ref)
        else:

            @pl.when(step < 3)
            def _():
                deal(acc_s, rows, x_first, core_ref, keep_ref, send_ref)

            @pl.when(step == 3)
            def _():
                sums = rest[0][...] + rest[1][...]
                small = []
                for g in range(GROUPS):
                    lines = rest[2 + 4 * g : 6 + 4 * g]
                    small.append(colsum(lines[0][:, 0, :] + lines[1][:, 0, :]))
                    small.append(colsum(lines[2][:, 0, :] + lines[3][:, 0, :]))
                    small.append(sums[2 : rows // 2, g * WIDE : (g + 1) * WIDE])
                small = jnp.concatenate(small, axis=0).astype(BF)
                for i in range(16):
                    keep_ref[i // 8, i // 4 % 2, i % 4, 0] = small
                    send_ref[i // 8, i // 4 % 2, i % 4, 0] = small

    return pl.pallas_call(
        body,
        grid_spec=pltpu.PrefetchScalarGridSpec(
            num_scalar_prefetch=1,
            grid=(units,),
            in_specs=[held, held, spec, spec] + more,
            out_specs=out_specs,
            scratch_shapes=[pltpu.VMEM((D, WIDE), F32)],
        ),
        out_shape=out_shape,
        compiler_params=params(),
        cost_estimate=cost(),
        name="wgrad_heads",
    )(core, low2, low1, e2, e1, *others)


def wgrad_back_call(core, two, one, e_two, e_one, rows):
    k, ff = two.shape
    block = ff // 8

    def cols(other):
        def index(x, s, n):
            c = 1 - n[0] if other else n[0]
            return (0, (x * 2 + c) * 2 + s)

        return pl.BlockSpec((k, block), index)

    held = once((k, D), lambda x, s, n: (0, 0))
    out = pl.BlockSpec((2, 1, 2, 4, rows, D), lambda x, s, n: (0, x, s, 0, 0, 0))

    def body(core_ref, g2k, g1k, g2s, g1s, e2_ref, e1_ref, keep_ref, send_ref):
        for a, c, o in ((g2k, g1k, keep_ref), (g2s, g1s, send_ref)):
            acc = mm(a[...], e2_ref[...], TN) + mm(c[...], e1_ref[...], TN)
            for s in range(16):
                o[s // 4 % 2, 0, s // 8, s % 4] = acc[s * rows : (s + 1) * rows].astype(BF)

    return pl.pallas_call(
        body,
        grid_spec=pltpu.PrefetchScalarGridSpec(
            num_scalar_prefetch=1,
            grid=(2, 2),
            in_specs=[cols(False), cols(False), cols(True), cols(True), held, held],
            out_specs=[out, out],
        ),
        out_shape=[jax.ShapeDtypeStruct((2, 2, 4, 4, rows, D), BF)] * 2,
        compiler_params=params(),
        cost_estimate=cost(),
        name="wgrad_back",
    )(core, two, one, two, one, e_two, e_one)


def layer_forward(x, low, weights, lengths, renorm):
    first, w_in, w_back, vec = weights
    qkv = qkv_call(low, first, vec)
    ctx, lse = attend_call(qkv, lengths)
    z1, h1, g, slope, z2, y = ffn_call(x, ctx, first, vec, w_in, w_back, renorm)
    return z2, y, (low, qkv, lse, ctx, z1, h1, g, slope, z2)


class Grid:
    def __init__(self, sizes):
        self.dp, self.fsdp = sizes["dp"], sizes["fsdp"]
        self.count = self.dp * self.fsdp
        self.x, self.core = self.dp // 2, 2
        self.y = self.fsdp // 4
        self.z = self.fsdp // self.y if self.y else 0
        self.staged = self.x == 2 and self.y == 2

    def place(self):
        dp, fsdp = lax.axis_index("dp"), lax.axis_index("fsdp")
        return dp // 2, dp % 2, fsdp // self.y, fsdp % self.y

    def shift(self, dim, step):
        sizes = (self.x, self.core, self.z, self.y)
        pairs = []
        for i in range(self.count):
            at = [i // (self.core * self.fsdp), i // self.fsdp % self.core, i % self.fsdp // self.y, i % self.y]
            at[dim] = (at[dim] + step) % sizes[dim]
            pairs.append((i, ((at[0] * self.core + at[1]) * self.z + at[2]) * self.y + at[3]))
        return pairs

    def send(self, value, dim, step=1):
        return lax.ppermute(value, AXES, self.shift(dim, step))


X, CORE, Z, Y = range(4)


def pack_one_body(at_ref, wq_ref, wo_ref, *rest):
    vectors, span_ref, one_ref, line_s = rest[:8], rest[8], rest[9], rest[10]
    rows = wq_ref.shape[0]
    for i in range(3):
        one_ref[i] = wq_ref[:, i * D : (i + 1) * D]
    one_ref[3] = wo_ref[...]
    line_s[...] = jnp.zeros_like(line_s)
    for i, ref in enumerate(vectors):
        line_s[i : i + 1, :rows] = ref[...].astype(F32)
    span = span_ref.shape[1]
    line_s[8:9, :span] = span_ref[...].astype(F32)
    device = at_ref[0]
    per = D // span
    top = pltpu.roll(line_s[:8], device * rows, 1)
    low = pltpu.roll(line_s[8:16], lax.rem(device, per) * span, 1)
    here = lax.broadcasted_iota(jnp.int32, (8, D), 0) == lax.div(device, per)
    low = jnp.where(here, jnp.broadcast_to(low[:1], (8, D)), 0.0)
    one_ref[4] = jnp.concatenate([top, low, jnp.zeros((rows - 16, D), F32)], axis=0).astype(BF)


def pack_one(device, w_qkv, w_out, vectors, span):
    rows = w_qkv.shape[0]
    operands = [w_qkv, w_out, *[v[None] for v in vectors], span[None]]
    return pl.pallas_call(
        pack_one_body,
        grid_spec=pltpu.PrefetchScalarGridSpec(
            num_scalar_prefetch=1,
            grid=(1,),
            in_specs=[whole_block(v) for v in operands],
            out_specs=pl.BlockSpec((5, rows, D), lambda *_: (0, 0, 0)),
            scratch_shapes=[pltpu.VMEM((16, D), F32)],
        ),
        out_shape=jax.ShapeDtypeStruct((5, rows, D), BF),
        compiler_params=params(),
        name="pack_one",
    )(device, *operands)


def pack_two_body(wi_ref, wb_ref, two_ref):
    rows = wi_ref.shape[0]
    for i in range(4):
        two_ref[i] = wi_ref[:, i * D : (i + 1) * D]
        two_ref[4 + i] = wb_ref[i * rows : (i + 1) * rows]


def pack_two(w_in, w_back):
    rows = w_in.shape[0]
    return pl.pallas_call(
        pack_two_body,
        grid=(1,),
        in_specs=[whole_block(w_in), whole_block(w_back)],
        out_specs=pl.BlockSpec((8, rows, D), lambda *_: (0, 0, 0)),
        out_shape=jax.ShapeDtypeStruct((8, rows, D), BF),
        compiler_params=params(),
        name="pack_two",
    )(w_in, w_back)


def place_body(split, at_ref, *refs):
    outs = 2 if split else 1
    parts, outs, held, sems, out_sems = refs[:8], refs[8 : 8 + outs], refs[8 + outs : -2], refs[-2], refs[-1]
    x, core, z, y = at_ref[0], at_ref[1], at_ref[2], at_ref[3]
    sides = ([], [])
    for i, part in enumerate(parts):
        side, far, other = i >> 2, (i >> 1) & 1, i & 1
        count = part.shape[2]
        for near in range(2):
            px = (x + (far if side == 0 else near)) % 2
            py = (y + (near if side == 0 else far)) % 2
            pc = (core + other) % 2
            for dz in range(4):
                pz = (z + 4 - dz) % 4
                if split:
                    target = held[side].at[:, px, pc, pz, py] if side == 0 else held[side].at[px, pc, pz, py]
                else:
                    target = held[0].at[pl.ds(0 if side == 0 else 5 - count, count), px, pc, pz, py]
                sem = sems.at[i * 8 + near * 4 + dz]
                sides[side].append(pltpu.make_async_copy(part.at[near, dz], target, sem))
    for side in sides:
        for copy in side:
            copy.start()
    back = []
    for side in range(2):
        for copy in sides[side]:
            copy.wait()
        if split:
            pair = held[side], outs[side]
        else:
            count = parts[4 * side].shape[2]
            span = pl.ds(0 if side == 0 else 5 - count, count)
            pair = held[0].at[span], outs[0].at[span]
        back.append(pltpu.make_async_copy(*pair, out_sems.at[side]))
        back[-1].start()
    for copy in back:
        copy.wait()


def place(at, parts, split):
    rows = parts[0].shape[3]
    if split:
        shapes = [(4, 2, 2, 4, 2, rows, D), (2, 2, 4, 2, 4, rows, D)]
    else:
        shapes = [(5, 2, 2, 4, 2, rows, D)]
    return pl.pallas_call(
        lambda *refs: place_body(split, *refs),
        grid_spec=pltpu.PrefetchScalarGridSpec(
            num_scalar_prefetch=1,
            grid=(1,),
            in_specs=[ANY] * 8,
            out_specs=[ANY] * len(shapes),
            scratch_shapes=[pltpu.VMEM(shape, BF) for shape in shapes]
            + [pltpu.SemaphoreType.DMA((64,)), pltpu.SemaphoreType.DMA((2,))],
        ),
        out_shape=[jax.ShapeDtypeStruct(shape, BF) for shape in shapes],
        compiler_params=params(),
        cost_estimate=cost(),
        name="place",
    )(at, *parts)


def after(value, *others):
    return lax.optimization_barrier((value, *others))[0]


class Gather:
    def __init__(self, grid, packet, first):
        self.grid, self.first = grid, first
        self.ring = [packet] + [grid.send(packet, Z, k) for k in range(1, 4)]

    def one(self, *others):
        ring = lax.optimization_barrier((*self.ring, *others))[:4]
        self.line = [jnp.stack([r[: self.first] for r in ring]), jnp.stack([r[self.first :] for r in ring])]
        self.came = [self.grid.send(v, d) for v, d in zip(self.line, (Y, X))]

    def two(self, *others):
        held = lax.optimization_barrier((*self.line, *others))
        self.near = [jnp.stack(pair) for pair in zip(held, self.came)]
        self.far = [self.grid.send(v, d) for v, d in zip(self.near, (X, Y))]

    def parts(self, *others):
        out = []
        held = lax.optimization_barrier((*self.near, *self.far, *others))
        for near, far in zip(held[:2], held[2:4]):
            out += [near, self.grid.send(near, CORE), far, self.grid.send(far, CORE)]
        return out


def pick(value, index, dim):
    return lax.dynamic_index_in_dim(value, index, dim, keepdims=False)


def added(a, b, *picks):
    for index, dim in picks:
        a, b = pick(a, index, dim), pick(b, index, dim)
    return (a.astype(F32) + b.astype(F32)).astype(BF)


class Sum:
    def __init__(self, grid, place, order, pair):
        self.grid, self.place, self.order = grid, place, order
        self.mine, self.came = pair[0], grid.send(pair[1], CORE)

    def cut(self, dim, others):
        here = self.place[dim]
        mine = after(self.mine, *others)
        out = added(mine, self.came, (1 - here, 0))
        self.mine = added(mine, self.came, (here, 0))
        self.came = self.grid.send(out, dim)
        return [out, self.mine]

    def one(self, *others):
        return self.cut(self.order[0], others)

    def two(self, *others):
        return self.cut(self.order[1], others)

    def three(self, *others):
        z = self.place[2]
        line = added(after(self.mine, *others), self.came)
        self.mine = pick(line, z, 0)
        self.came = [self.grid.send(pick(line, (z + k) % 4, 0), Z, k) for k in range(1, 4)]
        return [line]

    def result(self):
        total = self.mine.astype(F32)
        for piece in self.came:
            total += piece.astype(F32)
        return total


def staged(grid, lengths, tokens, cotangent, shards):
    w_qkv, bias_q, bias_v, w_out, bias_out, gain_one, shift_one, w_in, bias_in, w_back, bias_back, gain_two, shift_two = shards
    rows, span = bias_q.shape[0], bias_in.shape[0]
    where = grid.place()
    x, core, z, y = where
    device = lax.axis_index(AXES)
    at = jnp.stack([x, core, z, y]).astype(jnp.int32)
    core = core.astype(jnp.int32)[None]
    vectors = [bias_q, bias_v, bias_out, gain_one, shift_one, bias_back, gain_two, shift_two]
    one = Gather(grid, pack_one(device.astype(jnp.int32)[None], w_qkv, w_out, vectors, bias_in), 2)
    two = Gather(grid, pack_two(w_in, w_back), 4)
    one.one()
    one.two()
    two.one(*one.far)
    (first,) = place(at, one.parts(), False)
    first = first.reshape(5, grid.count * rows, D)
    vec = jnp.sum(first[4].reshape(grid.count, rows, D).astype(F32), axis=0)
    qkv = qkv_call(tokens, first, vec)
    two.two(qkv)
    ctx, lse = attend_call(after(qkv, *two.near), lengths)
    w_in, w_back = place(at, two.parts(ctx), True)
    w_in = w_in.reshape(4, grid.count * rows, D)
    w_back = w_back.reshape(grid.count * span, D)
    z1, h1, g, slope, z2, low = ffn_call(tokens, ctx, first, vec, w_in, w_back, False)
    saved = [(tokens, qkv, lse, ctx, z1, h1, g, slope, z2)]
    weights = (first, w_in, w_back, vec)
    _, low, stored = layer_forward(z2, low, weights, lengths, True)
    saved.append(stored)
    activations = low

    low2, qkv, lse, ctx2, z1, h2, g2, slope, z2 = saved[1]
    e2_2, e1_2, dz1, ea_2, dctx, sums_2 = ffn_back_call(cotangent, z2, z1, slope, w_back, w_in, first, vec)
    heads_2 = [attend_back_call(qkv, dctx, lse, lengths, i) for i in range(GROUPS)]
    grad = dx_call(dz1, heads_2[0][0], heads_2[1][0], first, F32)

    low1, qkv, lse, ctx1, z1, h1, g1, slope, z2 = saved[0]
    e2_1, e1_1, dz1, ea_1, dctx, sums_1 = ffn_back_call(grad, z2, z1, slope, w_back, w_in, first, vec)
    count = tokens.shape[0]

    heads_1 = []
    back = wgrad_back_call(core, g2, g1, e2_2, e2_1, rows)
    sum_back = Sum(grid, where, (Y, X), back)
    into = wgrad_in_call(core, after(h2, back[0]), h1, e1_2, e1_1, rows)
    sum_in = Sum(grid, where, (X, Y), into)
    steps = sum_back.one(into[0])
    heads_1.append(attend_back_call(qkv, after(dctx, *steps), lse, lengths, 0))
    steps = sum_in.one(heads_1[0][0])
    heads_1.append(attend_back_call(qkv, after(dctx, *steps), lse, lengths, 1))
    steps = sum_back.two(heads_1[1][0])
    group = wgrad_heads_call(
        core, after(low2, *steps), low1, heads_2[0][0], heads_1[0][0], rows, [ctx2, ctx1, ea_2, ea_1], False
    )
    sum_0 = Sum(grid, where, (Y, X), group)
    steps = sum_in.two(group[0]) + sum_back.three(group[0])
    lines = [heads[i][j] for i in range(GROUPS) for j in (1, 2) for heads in (heads_1, heads_2)]
    group = wgrad_heads_call(
        core, after(low2, *steps), low1, heads_2[1][0], heads_1[1][0], rows, [sums_1, sums_2, *lines], True
    )
    sum_1 = Sum(grid, where, (X, Y), group)
    steps = sum_0.one(group[0]) + sum_1.one()
    grad = dx_call(after(dz1, *steps), heads_1[0][0], heads_1[1][0], first, BF)
    sum_in.three(grad)
    sum_0.two(grad)
    sum_1.two(grad)
    sum_0.three()
    sum_1.three()
    total_in, total_back, half_0, half_1 = sum_in.result(), sum_back.result(), sum_0.result(), sum_1.result()

    w_in_grad = total_in.swapaxes(0, 1).reshape(rows, 4 * D)
    w_back_grad = total_back.reshape(4 * rows, D)
    w_qkv_grad = jnp.stack([half_0[:3], half_1[:3]], axis=1).transpose(2, 0, 1, 3).reshape(rows, 3 * D)
    w_out_grad = half_0[3:].swapaxes(0, 1).reshape(rows, D)
    small = jnp.concatenate([half_1[3][: rows // 2], half_1[3][rows // 2 :]], axis=1)
    mine = lax.dynamic_slice(small, (0, device * rows), (8, rows))
    per = D // span
    last = lax.dynamic_slice(small, (8 + device // per, device % per * span), (1, span))[0]
    return activations, grad, w_qkv_grad, w_out_grad, w_in_grad, w_back_grad, [mine[i] for i in range(8)] + [last]


def plain(grid, lengths, tokens, cotangent, shards):
    w_qkv, bias_q, bias_v, w_out, bias_out, gain_one, shift_one, w_in, bias_in, w_back, bias_back, gain_two, shift_two = shards
    vectors = [bias_q, bias_v, bias_out, gain_one, shift_one, bias_back, gain_two, shift_two]

    def whole(v):
        return lax.all_gather(v, AXES, axis=0, tiled=True)

    lines = jnp.stack([whole(v) for v in vectors])
    vec = jnp.concatenate([lines, whole(bias_in).reshape(4, D), jnp.zeros((4, D), BF)], axis=0).astype(F32)

    def blocks(w):
        return w.reshape(D, -1, D).swapaxes(0, 1)

    first = jnp.concatenate([blocks(whole(w_qkv)), whole(w_out)[None], jnp.zeros((1, D, D), BF)], axis=0)
    w_in, w_back = blocks(whole(w_in)), whole(w_back)
    weights = (first, w_in, w_back, vec)
    value, low = tokens, tokens
    saved = []
    for step in range(APPS):
        value, low, stored = layer_forward(value, low, weights, lengths, step > 0)
        saved.append(stored)
    activations, grad, totals = low, cotangent, None
    for step in reversed(range(APPS)):
        low, qkv, lse, ctx, z1, h1, g, slope, z2 = saved[step]
        e2, e1, dz1, ea, dctx, sums = ffn_back_call(grad, z2, z1, slope, w_back, w_in, first, vec)
        heads = [attend_back_call(qkv, dctx, lse, lengths, i) for i in range(GROUPS)]
        grad = dx_call(dz1, heads[0][0], heads[1][0], first, F32 if step else BF)
        e = jnp.concatenate([heads[i][0] for i in range(GROUPS)], axis=2).swapaxes(0, 1).reshape(-1, 3 * D)
        lines = [jnp.concatenate([jnp.sum(heads[i][j], axis=0) for i in range(GROUPS)], axis=1) for j in (1, 2)]
        grads = [mm(low, e, TN), mm(ctx, ea, TN), mm(h1, e1, TN), mm(g, e2, TN)]
        grads += [jnp.concatenate(lines + [sums[2:]], axis=0)]
        totals = grads if totals is None else [a + b for a, b in zip(totals, grads)]
    lines = list(totals.pop())
    totals += lines[:8] + [jnp.concatenate(lines[8:12])]
    owned = [lax.psum_scatter(v, AXES, scatter_dimension=0, tiled=True) for v in totals]
    return activations, grad, *owned[:4], owned[4:]


def make_local(grid):
    def local(tokens, lengths, *rest):
        run = staged if grid.staged else plain
        activations, grad, w_qkv, w_out, w_in, w_back, lines = run(grid, lengths, tokens, rest[-1], rest[:-1])
        return (
            activations, grad, w_qkv, lines[BQ], lines[BV], w_out, lines[BO], lines[G1], lines[S1],
            w_in, lines[8], w_back, lines[BB], lines[G2], lines[S2],
        )

    return local


def solution(mesh):
    wide, line = P(AXES, None), P(AXES)
    return jax.shard_map(
        make_local(Grid(mesh.shape)),
        mesh=mesh,
        in_specs=(wide, line, wide, line, line, wide, line, line, line, wide, line, wide, line, line, line, wide),
        out_specs=(wide, wide, wide, line, line, wide, line, line, line, wide, line, wide, line, line, line),
        check_vma=False,
    )
```

```python
import jax
import jax.numpy as jnp
from jax import lax
from jax.experimental import pallas as pl
from jax.experimental.pallas import tpu as pltpu
from jax.sharding import PartitionSpec as P

D = 768
HEADS = 12
HEAD_DIM = 64
APPS = 2
PAIR = 2 * HEAD_DIM
AXES = ("dp", "fsdp")
BF = jnp.bfloat16
F32 = jnp.float32
NN = (((1,), (0,)), ((), ()))
NT = (((1,), (1,)), ((), ()))
TN = (((0,), (0,)), ((), ()))
VMEM = 56 * 2**20
BQ, BV, BO, G1, S1, BB, G2, S2 = range(8)


def mm(left, right, dims):
    return lax.dot_general(left, right, dims, preferred_element_type=F32)


def params(limit=VMEM):
    return pltpu.CompilerParams(vmem_limit_bytes=limit)


def cost(micros):
    return pl.CostEstimate(flops=int(micros * 2e8), bytes_accessed=int(micros * 1e5), transcendentals=0)


def once(shape, index):
    return pl.BlockSpec(shape, index, pipeline_mode=pl.Buffered(1))


def whole_block(v):
    return pl.BlockSpec(v.shape, lambda *_: (0,) * v.ndim)


def normed(z):
    centered = z - jnp.mean(z, axis=-1, keepdims=True)
    root = lax.rsqrt(jnp.mean(centered * centered, axis=-1, keepdims=True) + 1e-12)
    return centered * root, root


def normed_back(n, root, e):
    return root * (e - jnp.mean(e, axis=-1, keepdims=True) - n * jnp.mean(e * n, axis=-1, keepdims=True))


def colsum(v):
    return jnp.sum(v, axis=0, keepdims=True)


def qkv_body(x_ref, w_ref, vec_ref, o_ref):
    part = pl.program_id(0)
    acc = mm(x_ref[...], w_ref[0], NN)
    bias = jnp.where(part == 0, vec_ref[BQ : BQ + 1, :], jnp.where(part == 2, vec_ref[BV : BV + 1, :], 0.0))
    o_ref[...] = (acc + bias).astype(BF)


def qkv_call(x, w, vec):
    rows = x.shape[0]
    return pl.pallas_call(
        qkv_body,
        grid=(3,),
        in_specs=[
            once((rows, D), lambda i: (0, 0)),
            pl.BlockSpec((1, D, D), lambda i: (i, 0, 0)),
            once(vec.shape, lambda i: (0, 0)),
        ],
        out_specs=pl.BlockSpec((rows, D), lambda i: (0, i)),
        out_shape=jax.ShapeDtypeStruct((rows, 3 * D), BF),
        compiler_params=params(),
        cost_estimate=cost(8),
        name="qkv",
    )(x, w, vec)


def attend_body(seq, pairs, len_ref, q_ref, k_ref, v_ref, o_ref, l_ref):
    count = len_ref[pl.program_id(0)]
    lane = lax.broadcasted_iota(jnp.int32, (seq, PAIR), 1)
    ok = lax.broadcasted_iota(jnp.int32, (1, seq), 1) < count
    units = [(pr, h) for pr in range(pairs) for h in range(2)]

    def score(unit):
        pr, h = unit
        cols = slice(pr * PAIR, (pr + 1) * PAIR)
        mine = (lane >= HEAD_DIM) == (h == 1)
        q = jnp.where(mine, q_ref[:, cols] * BF(0.125), BF(0))
        return jnp.where(ok, mm(q, k_ref[:, cols], NT), -1e30)

    ahead = score(units[0])
    held = {}
    for i, (pr, h) in enumerate(units):
        s = ahead
        if i + 1 < len(units):
            ahead = score(units[i + 1])
        cols = slice(pr * PAIR, (pr + 1) * PAIR)
        top = jnp.max(s, axis=1, keepdims=True)
        p = jnp.exp(s - top)
        total = jnp.sum(p, axis=1, keepdims=True)
        held[h] = mm(p.astype(BF), v_ref[:, cols], NN) / total
        l_ref[0, pr, h : h + 1, :] = (top + jnp.log(total)).reshape(1, seq)
        if h == 1:
            o_ref[:, cols] = jnp.where(lane < HEAD_DIM, held[0], held[1]).astype(BF)


def attend_call(qkv, lengths, pairs=3):
    rows = qkv.shape[0]
    count = lengths.shape[0]
    seq = rows // count
    groups = D // PAIR // pairs
    wide = PAIR * pairs

    def part(o):
        return pl.BlockSpec((seq, wide), lambda s, p, n: (s, o * groups + p))

    def body(*refs):
        attend_body(seq, pairs, *refs)

    return pl.pallas_call(
        body,
        grid_spec=pltpu.PrefetchScalarGridSpec(
            num_scalar_prefetch=1,
            grid=(count, groups),
            in_specs=[part(0), part(1), part(2)],
            out_specs=[part(0), pl.BlockSpec((1, pairs, 2, seq), lambda s, p, n: (s, p, 0, 0))],
        ),
        out_shape=[
            jax.ShapeDtypeStruct((rows, D), BF),
            jax.ShapeDtypeStruct((count, D // PAIR, 2, seq), F32),
        ],
        compiler_params=params(),
        cost_estimate=cost(13),
        name="attend",
    )(lengths, qkv, qkv, qkv)


def gelu_both(u):
    a = 0.7978845608028654
    c = a + (a * 0.044715) * (u * u)
    s = 0.5 + 0.5 * jnp.tanh(u * c)
    g = u * s
    return g, s + (g * (1.0 - s)) * (6.0 * c - 4.0 * a)


ANY = pl.BlockSpec(memory_space=pl.ANY)


def by_rows(block, width):
    return pl.BlockSpec((block, width), lambda i: (i, 0))


def ffn_body(
    renorm, x_ref, ctx_ref, vec_ref, wo_h, wi_h, wb_h,
    z1_ref, h1_ref, g_ref, slope_ref, z2_ref, y_ref, wo_s, wi_s, wb_s, sems,
):
    step = pl.program_id(0)
    copies = [
        pltpu.make_async_copy(wo_h.at[3], wo_s, sems.at[0]),
        pltpu.make_async_copy(wi_h, wi_s, sems.at[1]),
        pltpu.make_async_copy(wb_h, wb_s, sems.at[2]),
    ]

    @pl.when(step == 0)
    def _():
        for copy in copies:
            copy.start()
        copies[0].wait()

    x = x_ref[...].astype(F32)
    if renorm:
        n, _ = normed(x)
        x = n * vec_ref[G2 : G2 + 1, :] + vec_ref[S2 : S2 + 1, :]
    z1 = x + mm(ctx_ref[...], wo_s[...], NN) + vec_ref[BO : BO + 1, :]
    z1_ref[...] = z1
    n, _ = normed(z1)
    h1 = n * vec_ref[G1 : G1 + 1, :] + vec_ref[S1 : S1 + 1, :]
    low = h1.astype(BF)
    h1_ref[...] = low

    @pl.when(step == 0)
    def _():
        copies[1].wait()
        copies[2].wait()

    units = wi_s.shape[0]

    def up(j):
        return mm(low, wi_s[j], NN) + vec_ref[8 + j : 9 + j, :]

    acc = h1 + vec_ref[BB : BB + 1, :]
    f = up(0)
    for j in range(units):
        ahead = up(j + 1) if j + 1 < units else None
        cols = slice(j * D, (j + 1) * D)
        g, slope = gelu_both(f)
        g = g.astype(BF)
        g_ref[:, cols] = g
        slope_ref[:, cols] = slope.astype(BF)
        acc += mm(g, wb_s[cols, :], NN)
        f = ahead
    z2_ref[...] = acc
    n, _ = normed(acc)
    y_ref[...] = (n * vec_ref[G2 : G2 + 1, :] + vec_ref[S2 : S2 + 1, :]).astype(BF)


def weight_scratch(ff):
    return [
        pltpu.VMEM((D, D), BF),
        pltpu.VMEM((ff // D, D, D), BF),
        pltpu.VMEM((ff, D), BF),
        pltpu.SemaphoreType.DMA((3,)),
    ]


def ffn_call(x, ctx, first, vec, wi, wb, renorm, block=512):
    rows = x.shape[0]
    ff = wb.shape[0]
    line, wide = by_rows(block, D), by_rows(block, ff)
    return pl.pallas_call(
        lambda *refs: ffn_body(renorm, *refs),
        grid=(rows // block,),
        in_specs=[line, line, once(vec.shape, lambda i: (0, 0)), ANY, ANY, ANY],
        out_specs=[line, line, wide, wide, line, line],
        out_shape=[
            jax.ShapeDtypeStruct((rows, D), F32),
            jax.ShapeDtypeStruct((rows, D), BF),
            jax.ShapeDtypeStruct((rows, ff), BF),
            jax.ShapeDtypeStruct((rows, ff), BF),
            jax.ShapeDtypeStruct((rows, D), F32),
            jax.ShapeDtypeStruct((rows, D), BF),
        ],
        scratch_shapes=weight_scratch(ff),
        compiler_params=params(),
        cost_estimate=cost(22),
        name="ffn",
    )(x, ctx, vec, first, wi, wb)


def ffn_back_body(
    dy_ref, z2_ref, z1_ref, slope_ref, vec_ref, wb_h, wi_h, wo_h,
    e2_ref, e1_ref, dz1_ref, ea_ref, dctx_ref, sums_ref, wo_s, wi_s, wb_s, sems,
):
    step = pl.program_id(0)
    copies = [
        pltpu.make_async_copy(wb_h, wb_s, sems.at[0]),
        pltpu.make_async_copy(wi_h, wi_s, sems.at[1]),
        pltpu.make_async_copy(wo_h.at[3], wo_s, sems.at[2]),
    ]

    @pl.when(step == 0)
    def _():
        for copy in copies:
            copy.start()
        sums_ref[...] = jnp.zeros_like(sums_ref)

    dy = dy_ref[...].astype(F32)
    n, root = normed(z2_ref[...])
    sums_ref[G2 : G2 + 1, :] += colsum(dy * n)
    sums_ref[S2 : S2 + 1, :] += colsum(dy)
    dz2 = normed_back(n, root, dy * vec_ref[G2 : G2 + 1, :])
    e2 = dz2.astype(BF)
    e2_ref[...] = e2
    sums_ref[BB : BB + 1, :] += colsum(e2.astype(F32))

    @pl.when(step == 0)
    def _():
        for copy in copies:
            copy.wait()

    units = wi_s.shape[0]

    def up(j):
        return mm(e2, wb_s[j * D : (j + 1) * D, :], NT)

    acc = dz2
    f = up(0)
    for j in range(units):
        ahead = up(j + 1) if j + 1 < units else None
        cols = slice(j * D, (j + 1) * D)
        e1 = (f * slope_ref[:, cols].astype(F32)).astype(BF)
        e1_ref[:, cols] = e1
        sums_ref[8 + j : 9 + j, :] += colsum(e1.astype(F32))
        acc += mm(e1, wi_s[j], NT)
        f = ahead
    n, root = normed(z1_ref[...])
    sums_ref[G1 : G1 + 1, :] += colsum(acc * n)
    sums_ref[S1 : S1 + 1, :] += colsum(acc)
    dz1 = normed_back(n, root, acc * vec_ref[G1 : G1 + 1, :])
    dz1_ref[...] = dz1
    ea = dz1.astype(BF)
    ea_ref[...] = ea
    sums_ref[BO : BO + 1, :] += colsum(ea.astype(F32))
    dctx_ref[...] = mm(ea, wo_s[...], NT).astype(BF)


def ffn_back_call(dy, z2, z1, slope, wb, wi, first, vec, block=256):
    rows = dy.shape[0]
    ff = wb.shape[0]
    line, wide = by_rows(block, D), by_rows(block, ff)
    held = once(vec.shape, lambda i: (0, 0))
    return pl.pallas_call(
        ffn_back_body,
        grid=(rows // block,),
        in_specs=[line, line, line, wide, held, ANY, ANY, ANY],
        out_specs=[line, wide, line, line, line, held],
        out_shape=[
            jax.ShapeDtypeStruct((rows, D), BF),
            jax.ShapeDtypeStruct((rows, ff), BF),
            jax.ShapeDtypeStruct((rows, D), F32),
            jax.ShapeDtypeStruct((rows, D), BF),
            jax.ShapeDtypeStruct((rows, D), BF),
            jax.ShapeDtypeStruct(vec.shape, F32),
        ],
        scratch_shapes=weight_scratch(ff),
        compiler_params=params(),
        cost_estimate=cost(24),
        name="ffn_back",
    )(dy, z2, z1, slope, vec, wb, wi, first)


def attend_back_body(seq, pairs, len_ref, q_ref, k_ref, v_ref, d_ref, l_ref, e_ref, bq_ref, bv_ref):
    count = len_ref[pl.program_id(0)]
    lane = lax.broadcasted_iota(jnp.int32, (seq, PAIR), 1)
    ok = lax.broadcasted_iota(jnp.int32, (seq, seq), 0) < count
    units = [(pr, h) for pr in range(pairs) for h in range(2)]

    def score(unit):
        pr, h = unit
        cols = slice(pr * PAIR, (pr + 1) * PAIR)
        mine = (lane >= HEAD_DIM) == (h == 1)
        q = jnp.where(mine, q_ref[:, cols] * BF(0.125), BF(0))
        s = jnp.where(ok, mm(k_ref[:, cols], q, NT), -1e30)
        return s, mm(v_ref[:, cols], jnp.where(mine, d_ref[:, cols], BF(0)), NT)

    ahead = score(units[0])
    eq, ek, ev = {}, {}, {}
    for i, (pr, h) in enumerate(units):
        s, dp = ahead
        if i + 1 < len(units):
            ahead = score(units[i + 1])
        cols = slice(pr * PAIR, (pr + 1) * PAIR)
        if h == 0:
            kt = (k_ref[:, cols] * BF(0.125)).T
        p = jnp.exp(s - l_ref[0, pr, h : h + 1, :])
        pd = p * dp
        ds = (pd - p * colsum(pd)).astype(BF)
        ev[h] = mm(p.astype(BF), d_ref[:, cols], NN)
        ek[h] = mm(ds, q_ref[:, cols] * BF(0.125), NN)
        eq[h] = mm(kt[h * HEAD_DIM : (h + 1) * HEAD_DIM], ds, NN)
        if h == 1:
            low = jnp.concatenate([eq[0], eq[1]], axis=0).T.astype(BF)
            e_ref[0, :, cols] = low
            bq_ref[0, :, cols] = colsum(low.astype(F32))
            e_ref[1, :, cols] = jnp.where(lane < HEAD_DIM, ek[0], ek[1]).astype(BF)
            low = jnp.where(lane < HEAD_DIM, ev[0], ev[1]).astype(BF)
            e_ref[2, :, cols] = low
            bv_ref[0, :, cols] = colsum(low.astype(F32))


GROUPS = 2
WIDE = D // GROUPS


def attend_back_call(qkv, dctx, lse, lengths, group):
    rows = qkv.shape[0]
    count = lengths.shape[0]
    seq = rows // count
    pairs = WIDE // PAIR

    def part(o):
        return pl.BlockSpec((seq, WIDE), lambda s, n: (s, o * GROUPS + group))

    def body(*refs):
        attend_back_body(seq, pairs, *refs)

    line = pl.BlockSpec((1, 1, WIDE), lambda s, n: (s, 0, 0))
    return pl.pallas_call(
        body,
        grid_spec=pltpu.PrefetchScalarGridSpec(
            num_scalar_prefetch=1,
            grid=(count,),
            in_specs=[
                part(0),
                part(1),
                part(2),
                part(0),
                pl.BlockSpec((1, pairs, 2, seq), lambda s, n: (s, group, 0, 0)),
            ],
            out_specs=[pl.BlockSpec((3, seq, WIDE), lambda s, n: (0, s, 0)), line, line],
        ),
        out_shape=[jax.ShapeDtypeStruct((3, rows, WIDE), BF)] + [jax.ShapeDtypeStruct((count, 1, WIDE), F32)] * 2,
        compiler_params=params(),
        cost_estimate=cost(12),
        name="attend_back",
    )(lengths, qkv, qkv, qkv, dctx, lse)


def dx_body(dz1_ref, e0_ref, e1_ref, w_ref, o_ref):
    acc = dz1_ref[...]
    for i in range(3):
        acc += mm(e0_ref[i], w_ref[i, :, :WIDE], NT)
        acc += mm(e1_ref[i], w_ref[i, :, WIDE:], NT)
    o_ref[...] = acc.astype(o_ref.dtype)


def dx_call(dz1, e0, e1, w, dtype, block=256):
    rows = dz1.shape[0]
    line = pl.BlockSpec((block, D), lambda i: (i, 0))
    part = pl.BlockSpec((3, block, WIDE), lambda i: (0, i, 0))
    return pl.pallas_call(
        dx_body,
        grid=(rows // block,),
        in_specs=[line, part, part, once((3, D, D), lambda i: (0, 0, 0))],
        out_specs=line,
        out_shape=jax.ShapeDtypeStruct((rows, D), dtype),
        compiler_params=params(),
        cost_estimate=cost(9),
        name="dx",
    )(dz1, e0, e1, w)


def deal(acc_s, rows, x_first, core_ref, keep_ref, send_ref):
    part = 8 * rows
    for out, core in ((keep_ref, core_ref[0]), (send_ref, 1 - core_ref[0])):
        for xi in range(2):
            for s in range(8):
                zi, yi = s // 2, s % 2
                start = pl.multiple_of(core * part + (2 * xi * part + s * rows), 8)
                value = acc_s[pl.ds(start, rows), :].astype(BF)
                if x_first:
                    out[xi, yi, zi, 0] = value
                else:
                    out[yi, xi, zi, 0] = value


def packet(rows, units, width):
    spec = pl.BlockSpec((2, 2, 4, 1, rows, width), lambda i, n: (0, 0, 0, i, 0, 0))
    return [spec] * 2, [jax.ShapeDtypeStruct((2, 2, 4, units, rows, width), BF)] * 2


def wgrad_in_call(core, a, c, b, d, rows):
    k, n = b.shape
    held = once((k, D), lambda i, n: (0, 0))
    spec = pl.BlockSpec((k, D), lambda i, n: (0, i))
    out_specs, out_shape = packet(rows, n // D, D)

    def body(core_ref, a_ref, c_ref, b_ref, d_ref, keep_ref, send_ref, acc_s):
        acc_s[...] = mm(a_ref[...], b_ref[...], TN) + mm(c_ref[...], d_ref[...], TN)
        deal(acc_s, rows, True, core_ref, keep_ref, send_ref)

    return pl.pallas_call(
        body,
        grid_spec=pltpu.PrefetchScalarGridSpec(
            num_scalar_prefetch=1,
            grid=(n // D,),
            in_specs=[held, held, spec, spec],
            out_specs=out_specs,
            scratch_shapes=[pltpu.VMEM((D, D), F32)],
        ),
        out_shape=out_shape,
        compiler_params=params(),
        cost_estimate=cost(15),
        name="wgrad_in",
    )(core, a, c, b, d)


def wgrad_heads_call(core, low2, low1, e2, e1, rows, others, x_first):
    k = low2.shape[0]
    last = len(others) == 4
    held = once((k, D), lambda i, n: (0, 0))
    spec = pl.BlockSpec((1, k, WIDE), lambda i, n: (jnp.minimum(i, 2), 0, 0))
    units = 5 if last else 4
    out_specs, out_shape = packet(rows, units, WIDE)
    if last:
        half = pl.BlockSpec((k, WIDE), lambda i, n: (0, jnp.maximum(i - 3, 0)))
        more = [held, held, half, half]
    else:
        more = [whole_block(v) for v in others]

    def body(core_ref, a_ref, c_ref, b_ref, d_ref, *rest):
        rest, (keep_ref, send_ref, acc_s) = rest[:-3], rest[-3:]
        step = pl.program_id(0)

        @pl.when(step < 3)
        def _():
            acc_s[...] = mm(a_ref[...], b_ref[0], TN) + mm(c_ref[...], d_ref[0], TN)

        if last:

            @pl.when(step >= 3)
            def _():
                acc_s[...] = mm(rest[0][...], rest[2][...], TN) + mm(rest[1][...], rest[3][...], TN)

            deal(acc_s, rows, x_first, core_ref, keep_ref, send_ref)
        else:

            @pl.when(step < 3)
            def _():
                deal(acc_s, rows, x_first, core_ref, keep_ref, send_ref)

            @pl.when(step == 3)
            def _():
                sums = rest[0][...] + rest[1][...]
                small = []
                for g in range(GROUPS):
                    lines = rest[2 + 4 * g : 6 + 4 * g]
                    small.append(colsum(lines[0][:, 0, :] + lines[1][:, 0, :]))
                    small.append(colsum(lines[2][:, 0, :] + lines[3][:, 0, :]))
                    small.append(sums[2 : rows // 2, g * WIDE : (g + 1) * WIDE])
                small = jnp.concatenate(small, axis=0).astype(BF)
                for i in range(16):
                    keep_ref[i // 8, i // 4 % 2, i % 4, 0] = small
                    send_ref[i // 8, i // 4 % 2, i % 4, 0] = small

    return pl.pallas_call(
        body,
        grid_spec=pltpu.PrefetchScalarGridSpec(
            num_scalar_prefetch=1,
            grid=(units,),
            in_specs=[held, held, spec, spec] + more,
            out_specs=out_specs,
            scratch_shapes=[pltpu.VMEM((D, WIDE), F32)],
        ),
        out_shape=out_shape,
        compiler_params=params(),
        cost_estimate=cost(12),
        name="wgrad_heads",
    )(core, low2, low1, e2, e1, *others)


def wgrad_back_call(core, two, one, e_two, e_one, rows):
    k, ff = two.shape
    block = ff // 8

    def cols(other):
        def index(x, s, n):
            c = 1 - n[0] if other else n[0]
            return (0, (x * 2 + c) * 2 + s)

        return pl.BlockSpec((k, block), index)

    held = once((k, D), lambda x, s, n: (0, 0))
    out = pl.BlockSpec((2, 1, 2, 4, rows, D), lambda x, s, n: (0, x, s, 0, 0, 0))

    def body(core_ref, g2k, g1k, g2s, g1s, e2_ref, e1_ref, keep_ref, send_ref):
        for a, c, o in ((g2k, g1k, keep_ref), (g2s, g1s, send_ref)):
            acc = mm(a[...], e2_ref[...], TN) + mm(c[...], e1_ref[...], TN)
            for s in range(16):
                o[s // 4 % 2, 0, s // 8, s % 4] = acc[s * rows : (s + 1) * rows].astype(BF)

    return pl.pallas_call(
        body,
        grid_spec=pltpu.PrefetchScalarGridSpec(
            num_scalar_prefetch=1,
            grid=(2, 2),
            in_specs=[cols(False), cols(False), cols(True), cols(True), held, held],
            out_specs=[out, out],
        ),
        out_shape=[jax.ShapeDtypeStruct((2, 2, 4, 4, rows, D), BF)] * 2,
        compiler_params=params(),
        cost_estimate=cost(15),
        name="wgrad_back",
    )(core, two, one, two, one, e_two, e_one)


def layer_forward(x, low, weights, lengths, renorm):
    first, w_in, w_back, vec = weights
    qkv = qkv_call(low, first, vec)
    ctx, lse = attend_call(qkv, lengths)
    z1, h1, g, slope, z2, y = ffn_call(x, ctx, first, vec, w_in, w_back, renorm)
    return z2, y, (low, qkv, lse, ctx, z1, h1, g, slope, z2)


class Grid:
    def __init__(self, sizes):
        self.dp, self.fsdp = sizes["dp"], sizes["fsdp"]
        self.count = self.dp * self.fsdp
        self.x, self.core = self.dp // 2, 2
        self.y = self.fsdp // 4
        self.z = self.fsdp // self.y if self.y else 0
        self.staged = self.x == 2 and self.y == 2

    def place(self):
        dp, fsdp = lax.axis_index("dp"), lax.axis_index("fsdp")
        return dp // 2, dp % 2, fsdp // self.y, fsdp % self.y

    def shift(self, dim, step):
        sizes = (self.x, self.core, self.z, self.y)
        pairs = []
        for i in range(self.count):
            at = [i // (self.core * self.fsdp), i // self.fsdp % self.core, i % self.fsdp // self.y, i % self.y]
            at[dim] = (at[dim] + step) % sizes[dim]
            pairs.append((i, ((at[0] * self.core + at[1]) * self.z + at[2]) * self.y + at[3]))
        return pairs

    def send(self, value, dim, step=1):
        return lax.ppermute(value, AXES, self.shift(dim, step))

    def swap(self, value, bit):
        pairs = [(i, i ^ (bit * self.y)) for i in range(self.count)]
        return lax.ppermute(value, AXES, pairs)


X, CORE, Z, Y = range(4)


def pack_one_body(at_ref, wq_ref, wo_ref, *rest):
    vectors, span_ref, one_ref, line_s = rest[:8], rest[8], rest[9], rest[10]
    rows = wq_ref.shape[0]
    for i in range(3):
        one_ref[i] = wq_ref[:, i * D : (i + 1) * D]
    one_ref[3] = wo_ref[...]
    line_s[...] = jnp.zeros_like(line_s)
    for i, ref in enumerate(vectors):
        line_s[i : i + 1, :rows] = ref[...].astype(F32)
    span = span_ref.shape[1]
    line_s[8:9, :span] = span_ref[...].astype(F32)
    device = at_ref[0]
    per = D // span
    top = pltpu.roll(line_s[:8], device * rows, 1)
    low = pltpu.roll(line_s[8:16], lax.rem(device, per) * span, 1)
    here = lax.broadcasted_iota(jnp.int32, (8, D), 0) == lax.div(device, per)
    low = jnp.where(here, jnp.broadcast_to(low[:1], (8, D)), 0.0)
    one_ref[4] = jnp.concatenate([top, low, jnp.zeros((rows - 16, D), F32)], axis=0).astype(BF)


def pack_one(device, w_qkv, w_out, vectors, span):
    rows = w_qkv.shape[0]
    operands = [w_qkv, w_out, *[v[None] for v in vectors], span[None]]
    return pl.pallas_call(
        pack_one_body,
        grid_spec=pltpu.PrefetchScalarGridSpec(
            num_scalar_prefetch=1,
            grid=(1,),
            in_specs=[whole_block(v) for v in operands],
            out_specs=pl.BlockSpec((5, rows, D), lambda *_: (0, 0, 0)),
            scratch_shapes=[pltpu.VMEM((16, D), F32)],
        ),
        out_shape=jax.ShapeDtypeStruct((5, rows, D), BF),
        compiler_params=params(),
        name="pack_one",
    )(device, *operands)


def pack_two_body(wi_ref, wb_ref, two_ref):
    rows = wi_ref.shape[0]
    for i in range(4):
        two_ref[i] = wi_ref[:, i * D : (i + 1) * D]
        two_ref[4 + i] = wb_ref[i * rows : (i + 1) * rows]


def pack_two(w_in, w_back):
    rows = w_in.shape[0]
    return pl.pallas_call(
        pack_two_body,
        grid=(1,),
        in_specs=[whole_block(w_in), whole_block(w_back)],
        out_specs=pl.BlockSpec((8, rows, D), lambda *_: (0, 0, 0)),
        out_shape=jax.ShapeDtypeStruct((8, rows, D), BF),
        compiler_params=params(),
        name="pack_two",
    )(w_in, w_back)


def place_body(split, at_ref, *refs):
    outs = 2 if split else 1
    parts, outs, held, sems, out_sems = refs[:8], refs[8 : 8 + outs], refs[8 + outs : -2], refs[-2], refs[-1]
    x, core, z, y = at_ref[0], at_ref[1], at_ref[2], at_ref[3]
    sides = ([], [])
    for i, part in enumerate(parts):
        side, far, other = i >> 2, (i >> 1) & 1, i & 1
        count = part.shape[2]
        for near in range(2):
            px = (x + (far if side == 0 else near)) % 2
            py = (y + (near if side == 0 else far)) % 2
            pc = (core + other) % 2
            for dz in range(4):
                pz = lax.bitwise_xor(z, dz) if split else (z + 4 - dz) % 4
                if split:
                    target = held[side].at[:, px, pc, pz, py] if side == 0 else held[side].at[px, pc, pz, py]
                else:
                    target = held[0].at[pl.ds(0 if side == 0 else 5 - count, count), px, pc, pz, py]
                sem = sems.at[i * 8 + near * 4 + dz]
                sides[side].append(pltpu.make_async_copy(part.at[near, dz], target, sem))
    for side in sides:
        for copy in side:
            copy.start()
    back = []
    for side in range(2):
        for copy in sides[side]:
            copy.wait()
        if split:
            pair = held[side], outs[side]
        else:
            count = parts[4 * side].shape[2]
            span = pl.ds(0 if side == 0 else 5 - count, count)
            pair = held[0].at[span], outs[0].at[span]
        back.append(pltpu.make_async_copy(*pair, out_sems.at[side]))
        back[-1].start()
    for copy in back:
        copy.wait()


def place(at, parts, split):
    rows = parts[0].shape[3]
    if split:
        shapes = [(4, 2, 2, 4, 2, rows, D), (2, 2, 4, 2, 4, rows, D)]
    else:
        shapes = [(5, 2, 2, 4, 2, rows, D)]
    return pl.pallas_call(
        lambda *refs: place_body(split, *refs),
        grid_spec=pltpu.PrefetchScalarGridSpec(
            num_scalar_prefetch=1,
            grid=(1,),
            in_specs=[ANY] * 8,
            out_specs=[ANY] * len(shapes),
            scratch_shapes=[pltpu.VMEM(shape, BF) for shape in shapes]
            + [pltpu.SemaphoreType.DMA((64,)), pltpu.SemaphoreType.DMA((2,))],
        ),
        out_shape=[jax.ShapeDtypeStruct(shape, BF) for shape in shapes],
        compiler_params=params(),
        cost_estimate=cost(6),
        name="place",
    )(at, *parts)


def after(value, *others):
    return lax.optimization_barrier((value, *others))[0]


class Gather:
    def __init__(self, grid, packet, first, by_bits):
        self.grid, self.first = grid, first
        if by_bits:
            pair = jnp.stack([packet, grid.swap(packet, 1)])
            far = grid.swap(pair, 2)
            self.ring = [pair[0], pair[1], far[0], far[1]]
        else:
            self.ring = [packet] + [grid.send(packet, Z, k) for k in range(1, 4)]

    def one(self, *others):
        ring = lax.optimization_barrier((*self.ring, *others))[:4]
        self.line = [jnp.stack([r[: self.first] for r in ring]), jnp.stack([r[self.first :] for r in ring])]
        self.came = [self.grid.send(v, d) for v, d in zip(self.line, (Y, X))]

    def two(self, *others):
        held = lax.optimization_barrier((*self.line, *others))
        self.near = [jnp.stack(pair) for pair in zip(held, self.came)]
        self.far = [self.grid.send(v, d) for v, d in zip(self.near, (X, Y))]
        self.near_core = [self.grid.send(v, CORE) for v in self.near]

    def parts(self, *others):
        far = lax.optimization_barrier((*self.far, *others))[:2]
        out = []
        for i in range(2):
            out += [self.near[i], self.near_core[i], far[i], self.grid.send(far[i], CORE)]
        return out


def pick(value, index, dim):
    return lax.dynamic_index_in_dim(value, index, dim, keepdims=False)


def added(a, b, *picks):
    for index, dim in picks:
        a, b = pick(a, index, dim), pick(b, index, dim)
    return (a.astype(F32) + b.astype(F32)).astype(BF)


class Sum:
    def __init__(self, grid, place, order, pair):
        self.grid, self.place, self.order = grid, place, order
        self.mine, self.came = pair[0], grid.send(pair[1], CORE)

    def cut(self, dim, others):
        here = self.place[dim]
        mine = after(self.mine, *others)
        out = added(mine, self.came, (1 - here, 0))
        self.mine = added(mine, self.came, (here, 0))
        self.came = self.grid.send(out, dim)
        return [out, self.mine]

    def one(self, *others):
        return self.cut(self.order[0], others)

    def two(self, *others):
        return self.cut(self.order[1], others)

    def three(self, *others):
        z = self.place[2]
        line = added(after(self.mine, *others), self.came)
        self.mine = pick(line, z, 0)
        self.came = [self.grid.send(pick(line, (z + k) % 4, 0), Z, k) for k in range(1, 4)]
        return [line]

    def result(self):
        total = self.mine.astype(F32)
        for piece in self.came:
            total += piece.astype(F32)
        return total


def staged(grid, lengths, tokens, cotangent, shards):
    w_qkv, bias_q, bias_v, w_out, bias_out, gain_one, shift_one, w_in, bias_in, w_back, bias_back, gain_two, shift_two = shards
    rows, span = bias_q.shape[0], bias_in.shape[0]
    where = grid.place()
    x, core, z, y = where
    device = lax.axis_index(AXES)
    at = jnp.stack([x, core, z, y]).astype(jnp.int32)
    core = core.astype(jnp.int32)[None]
    vectors = [bias_q, bias_v, bias_out, gain_one, shift_one, bias_back, gain_two, shift_two]
    one = Gather(grid, pack_one(device.astype(jnp.int32)[None], w_qkv, w_out, vectors, bias_in), 2, False)
    two = Gather(grid, pack_two(w_in, w_back), 4, True)
    one.one()
    one.two()
    two.one(*one.far)
    (first,) = place(at, one.parts(), False)
    first = first.reshape(5, grid.count * rows, D)
    vec = jnp.sum(first[4].reshape(grid.count, rows, D).astype(F32), axis=0)
    qkv = qkv_call(tokens, first, vec)
    two.two(qkv)
    ctx, lse = attend_call(after(qkv, *two.near), lengths)
    w_in, w_back = place(at, two.parts(ctx), True)
    w_in = w_in.reshape(4, grid.count * rows, D)
    w_back = w_back.reshape(grid.count * span, D)
    z1, h1, g, slope, z2, low = ffn_call(tokens, ctx, first, vec, w_in, w_back, False)
    saved = [(tokens, qkv, lse, ctx, z1, h1, g, slope, z2)]
    weights = (first, w_in, w_back, vec)
    _, low, stored = layer_forward(z2, low, weights, lengths, True)
    saved.append(stored)
    activations = low

    low2, qkv, lse, ctx2, z1, h2, g2, slope, z2 = saved[1]
    e2_2, e1_2, dz1, ea_2, dctx, sums_2 = ffn_back_call(cotangent, z2, z1, slope, w_back, w_in, first, vec)
    heads_2 = [attend_back_call(qkv, dctx, lse, lengths, i) for i in range(GROUPS)]
    grad = dx_call(dz1, heads_2[0][0], heads_2[1][0], first, F32)

    low1, qkv, lse, ctx1, z1, h1, g1, slope, z2 = saved[0]
    e2_1, e1_1, dz1, ea_1, dctx, sums_1 = ffn_back_call(grad, z2, z1, slope, w_back, w_in, first, vec)
    count = tokens.shape[0]

    heads_1 = []
    back = wgrad_back_call(core, g2, g1, e2_2, e2_1, rows)
    sum_back = Sum(grid, where, (Y, X), back)
    into = wgrad_in_call(core, after(h2, back[0]), h1, e1_2, e1_1, rows)
    sum_in = Sum(grid, where, (X, Y), into)
    steps = sum_back.one(into[0]) + sum_in.one(into[0])
    heads_1.append(attend_back_call(qkv, after(dctx, *steps), lse, lengths, 0))
    heads_1.append(attend_back_call(qkv, after(dctx, heads_1[0][0]), lse, lengths, 1))
    steps = sum_back.two(heads_1[1][0]) + sum_in.two(heads_1[1][0])
    group = wgrad_heads_call(
        core, after(low2, *steps), low1, heads_2[0][0], heads_1[0][0], rows, [ctx2, ctx1, ea_2, ea_1], False
    )
    sum_0 = Sum(grid, where, (Y, X), group)
    steps = sum_back.three(group[0]) + sum_in.three(group[0])
    lines = [heads[i][j] for i in range(GROUPS) for j in (1, 2) for heads in (heads_1, heads_2)]
    group = wgrad_heads_call(
        core, after(low2, *steps), low1, heads_2[1][0], heads_1[1][0], rows, [sums_1, sums_2, *lines], True
    )
    sum_1 = Sum(grid, where, (X, Y), group)
    steps = sum_0.one(group[0]) + sum_1.one()
    total_back = sum_back.result()
    grad = dx_call(after(dz1, total_back, *steps), heads_1[0][0], heads_1[1][0], first, BF)
    sum_0.two(grad)
    sum_1.two(grad)
    sum_0.three()
    sum_1.three()
    total_in, half_0, half_1 = sum_in.result(), sum_0.result(), sum_1.result()

    w_in_grad = total_in.swapaxes(0, 1).reshape(rows, 4 * D)
    w_back_grad = total_back.reshape(4 * rows, D)
    w_qkv_grad = jnp.stack([half_0[:3], half_1[:3]], axis=1).transpose(2, 0, 1, 3).reshape(rows, 3 * D)
    w_out_grad = half_0[3:].swapaxes(0, 1).reshape(rows, D)
    small = jnp.concatenate([half_1[3][: rows // 2], half_1[3][rows // 2 :]], axis=1)
    mine = lax.dynamic_slice(small, (0, device * rows), (8, rows))
    per = D // span
    last = lax.dynamic_slice(small, (8 + device // per, device % per * span), (1, span))[0]
    return activations, grad, w_qkv_grad, w_out_grad, w_in_grad, w_back_grad, [mine[i] for i in range(8)] + [last]


def plain(grid, lengths, tokens, cotangent, shards):
    w_qkv, bias_q, bias_v, w_out, bias_out, gain_one, shift_one, w_in, bias_in, w_back, bias_back, gain_two, shift_two = shards
    vectors = [bias_q, bias_v, bias_out, gain_one, shift_one, bias_back, gain_two, shift_two]

    def whole(v):
        return lax.all_gather(v, AXES, axis=0, tiled=True)

    lines = jnp.stack([whole(v) for v in vectors])
    vec = jnp.concatenate([lines, whole(bias_in).reshape(4, D), jnp.zeros((4, D), BF)], axis=0).astype(F32)

    def blocks(w):
        return w.reshape(D, -1, D).swapaxes(0, 1)

    first = jnp.concatenate([blocks(whole(w_qkv)), whole(w_out)[None], jnp.zeros((1, D, D), BF)], axis=0)
    w_in, w_back = blocks(whole(w_in)), whole(w_back)
    weights = (first, w_in, w_back, vec)
    value, low = tokens, tokens
    saved = []
    for step in range(APPS):
        value, low, stored = layer_forward(value, low, weights, lengths, step > 0)
        saved.append(stored)
    activations, grad, totals = low, cotangent, None
    for step in reversed(range(APPS)):
        low, qkv, lse, ctx, z1, h1, g, slope, z2 = saved[step]
        e2, e1, dz1, ea, dctx, sums = ffn_back_call(grad, z2, z1, slope, w_back, w_in, first, vec)
        heads = [attend_back_call(qkv, dctx, lse, lengths, i) for i in range(GROUPS)]
        grad = dx_call(dz1, heads[0][0], heads[1][0], first, F32 if step else BF)
        e = jnp.concatenate([heads[i][0] for i in range(GROUPS)], axis=2).swapaxes(0, 1).reshape(-1, 3 * D)
        lines = [jnp.concatenate([jnp.sum(heads[i][j], axis=0) for i in range(GROUPS)], axis=1) for j in (1, 2)]
        grads = [mm(low, e, TN), mm(ctx, ea, TN), mm(h1, e1, TN), mm(g, e2, TN)]
        grads += [jnp.concatenate(lines + [sums[2:]], axis=0)]
        totals = grads if totals is None else [a + b for a, b in zip(totals, grads)]
    lines = list(totals.pop())
    totals += lines[:8] + [jnp.concatenate(lines[8:12])]
    owned = [lax.psum_scatter(v, AXES, scatter_dimension=0, tiled=True) for v in totals]
    return activations, grad, *owned[:4], owned[4:]


def make_local(grid):
    def local(tokens, lengths, *rest):
        run = staged if grid.staged else plain
        activations, grad, w_qkv, w_out, w_in, w_back, lines = run(grid, lengths, tokens, rest[-1], rest[:-1])
        return (
            activations, grad, w_qkv, lines[BQ], lines[BV], w_out, lines[BO], lines[G1], lines[S1],
            w_in, lines[8], w_back, lines[BB], lines[G2], lines[S2],
        )

    return local


def solution(mesh):
    wide, line = P(AXES, None), P(AXES)
    return jax.shard_map(
        make_local(Grid(mesh.shape)),
        mesh=mesh,
        in_specs=(wide, line, wide, line, line, wide, line, line, line, wide, line, wide, line, line, line, wide),
        out_specs=(wide, wide, wide, line, line, wide, line, line, line, wide, line, wide, line, line, line),
        check_vma=False,
    )
```

```python
import jax
import jax.numpy as jnp
from jax import lax
from jax.experimental import pallas as pl
from jax.experimental.pallas import tpu as pltpu
from jax.sharding import PartitionSpec as P

D = 768
HEADS = 12
HEAD_DIM = 64
APPS = 2
PAIR = 2 * HEAD_DIM
AXES = ("dp", "fsdp")
BF = jnp.bfloat16
F32 = jnp.float32
NN = (((1,), (0,)), ((), ()))
NT = (((1,), (1,)), ((), ()))
TN = (((0,), (0,)), ((), ()))
VMEM = 56 * 2**20
BQ, BV, BO, G1, S1, BB, G2, S2 = range(8)


def mm(left, right, dims):
    return lax.dot_general(left, right, dims, preferred_element_type=F32)


def params(limit=VMEM):
    return pltpu.CompilerParams(vmem_limit_bytes=limit)


def cost(micros):
    return pl.CostEstimate(flops=int(micros * 2e8), bytes_accessed=int(micros * 1e5), transcendentals=0)


def once(shape, index):
    return pl.BlockSpec(shape, index, pipeline_mode=pl.Buffered(1))


def whole_block(v):
    return pl.BlockSpec(v.shape, lambda *_: (0,) * v.ndim)


def normed(z):
    centered = z - jnp.mean(z, axis=-1, keepdims=True)
    root = lax.rsqrt(jnp.mean(centered * centered, axis=-1, keepdims=True) + 1e-12)
    return centered * root, root


def normed_back(n, root, e):
    return root * (e - jnp.mean(e, axis=-1, keepdims=True) - n * jnp.mean(e * n, axis=-1, keepdims=True))


def colsum(v):
    return jnp.sum(v, axis=0, keepdims=True)


def qkv_body(x_ref, w_ref, vec_ref, o_ref):
    part = pl.program_id(0)
    acc = mm(x_ref[...], w_ref[0], NN)
    bias = jnp.where(part == 0, vec_ref[BQ : BQ + 1, :], jnp.where(part == 2, vec_ref[BV : BV + 1, :], 0.0))
    o_ref[...] = (acc + bias).astype(BF)


def qkv_call(x, w, vec):
    rows = x.shape[0]
    return pl.pallas_call(
        qkv_body,
        grid=(3,),
        in_specs=[
            once((rows, D), lambda i: (0, 0)),
            pl.BlockSpec((1, D, D), lambda i: (i, 0, 0)),
            once(vec.shape, lambda i: (0, 0)),
        ],
        out_specs=pl.BlockSpec((rows, D), lambda i: (0, i)),
        out_shape=jax.ShapeDtypeStruct((rows, 3 * D), BF),
        compiler_params=params(),
        cost_estimate=cost(8),
        name="qkv",
    )(x, w, vec)


def attend_body(seq, pairs, len_ref, q_ref, k_ref, v_ref, o_ref, l_ref):
    count = len_ref[pl.program_id(0)]
    lane = lax.broadcasted_iota(jnp.int32, (seq, PAIR), 1)
    ok = lax.broadcasted_iota(jnp.int32, (1, seq), 1) < count
    units = [(pr, h) for pr in range(pairs) for h in range(2)]

    def score(unit):
        pr, h = unit
        cols = slice(pr * PAIR, (pr + 1) * PAIR)
        mine = (lane >= HEAD_DIM) == (h == 1)
        q = jnp.where(mine, q_ref[:, cols] * BF(0.125), BF(0))
        return jnp.where(ok, mm(q, k_ref[:, cols], NT), -1e30)

    ahead = score(units[0])
    held = {}
    for i, (pr, h) in enumerate(units):
        s = ahead
        if i + 1 < len(units):
            ahead = score(units[i + 1])
        cols = slice(pr * PAIR, (pr + 1) * PAIR)
        top = jnp.max(s, axis=1, keepdims=True)
        p = jnp.exp(s - top)
        total = jnp.sum(p, axis=1, keepdims=True)
        held[h] = mm(p.astype(BF), v_ref[:, cols], NN) / total
        l_ref[0, pr, h : h + 1, :] = (top + jnp.log(total)).reshape(1, seq)
        if h == 1:
            o_ref[:, cols] = jnp.where(lane < HEAD_DIM, held[0], held[1]).astype(BF)


def attend_call(qkv, lengths, pairs=3):
    rows = qkv.shape[0]
    count = lengths.shape[0]
    seq = rows // count
    groups = D // PAIR // pairs
    wide = PAIR * pairs

    def part(o):
        return pl.BlockSpec((seq, wide), lambda s, p, n: (s, o * groups + p))

    def body(*refs):
        attend_body(seq, pairs, *refs)

    return pl.pallas_call(
        body,
        grid_spec=pltpu.PrefetchScalarGridSpec(
            num_scalar_prefetch=1,
            grid=(count, groups),
            in_specs=[part(0), part(1), part(2)],
            out_specs=[part(0), pl.BlockSpec((1, pairs, 2, seq), lambda s, p, n: (s, p, 0, 0))],
        ),
        out_shape=[
            jax.ShapeDtypeStruct((rows, D), BF),
            jax.ShapeDtypeStruct((count, D // PAIR, 2, seq), F32),
        ],
        compiler_params=params(),
        cost_estimate=cost(13),
        name="attend",
    )(lengths, qkv, qkv, qkv)


def gelu_both(u):
    a = 0.7978845608028654
    c = a + (a * 0.044715) * (u * u)
    s = 0.5 + 0.5 * jnp.tanh(u * c)
    g = u * s
    return g, s + (g * (1.0 - s)) * (6.0 * c - 4.0 * a)


ANY = pl.BlockSpec(memory_space=pl.ANY)


def by_rows(block, width):
    return pl.BlockSpec((block, width), lambda i: (i, 0))


def ffn_body(
    renorm, x_ref, ctx_ref, vec_ref, wo_h, wi_h, wb_h,
    z1_ref, h1_ref, g_ref, slope_ref, z2_ref, y_ref, wo_s, wi_s, wb_s, sems,
):
    step = pl.program_id(0)
    copies = [
        pltpu.make_async_copy(wo_h.at[3], wo_s, sems.at[0]),
        pltpu.make_async_copy(wi_h, wi_s, sems.at[1]),
        pltpu.make_async_copy(wb_h, wb_s, sems.at[2]),
    ]

    @pl.when(step == 0)
    def _():
        for copy in copies:
            copy.start()
        copies[0].wait()

    x = x_ref[...].astype(F32)
    if renorm:
        n, _ = normed(x)
        x = n * vec_ref[G2 : G2 + 1, :] + vec_ref[S2 : S2 + 1, :]
    z1 = x + mm(ctx_ref[...], wo_s[...], NN) + vec_ref[BO : BO + 1, :]
    z1_ref[...] = z1
    n, _ = normed(z1)
    h1 = n * vec_ref[G1 : G1 + 1, :] + vec_ref[S1 : S1 + 1, :]
    low = h1.astype(BF)
    h1_ref[...] = low

    @pl.when(step == 0)
    def _():
        copies[1].wait()
        copies[2].wait()

    units = wi_s.shape[0]

    def up(j):
        return mm(low, wi_s[j], NN) + vec_ref[8 + j : 9 + j, :]

    acc = h1 + vec_ref[BB : BB + 1, :]
    f = up(0)
    for j in range(units):
        ahead = up(j + 1) if j + 1 < units else None
        cols = slice(j * D, (j + 1) * D)
        g, slope = gelu_both(f)
        g = g.astype(BF)
        g_ref[:, cols] = g
        slope_ref[:, cols] = slope.astype(BF)
        acc += mm(g, wb_s[cols, :], NN)
        f = ahead
    z2_ref[...] = acc
    n, _ = normed(acc)
    y_ref[...] = (n * vec_ref[G2 : G2 + 1, :] + vec_ref[S2 : S2 + 1, :]).astype(BF)


def weight_scratch(ff):
    return [
        pltpu.VMEM((D, D), BF),
        pltpu.VMEM((ff // D, D, D), BF),
        pltpu.VMEM((ff, D), BF),
        pltpu.SemaphoreType.DMA((3,)),
    ]


def ffn_call(x, ctx, first, vec, wi, wb, renorm, block=512):
    rows = x.shape[0]
    ff = wb.shape[0]
    line, wide = by_rows(block, D), by_rows(block, ff)
    return pl.pallas_call(
        lambda *refs: ffn_body(renorm, *refs),
        grid=(rows // block,),
        in_specs=[line, line, once(vec.shape, lambda i: (0, 0)), ANY, ANY, ANY],
        out_specs=[line, line, wide, wide, line, line],
        out_shape=[
            jax.ShapeDtypeStruct((rows, D), F32),
            jax.ShapeDtypeStruct((rows, D), BF),
            jax.ShapeDtypeStruct((rows, ff), BF),
            jax.ShapeDtypeStruct((rows, ff), BF),
            jax.ShapeDtypeStruct((rows, D), F32),
            jax.ShapeDtypeStruct((rows, D), BF),
        ],
        scratch_shapes=weight_scratch(ff),
        compiler_params=params(),
        cost_estimate=cost(22),
        name="ffn",
    )(x, ctx, vec, first, wi, wb)


def ffn_back_body(
    dy_ref, z2_ref, z1_ref, slope_ref, vec_ref, wb_h, wi_h, wo_h,
    e2_ref, e1_ref, dz1_ref, ea_ref, dctx_ref, sums_ref, wo_s, wi_s, wb_s, sems,
):
    step = pl.program_id(0)
    copies = [
        pltpu.make_async_copy(wb_h, wb_s, sems.at[0]),
        pltpu.make_async_copy(wi_h, wi_s, sems.at[1]),
        pltpu.make_async_copy(wo_h.at[3], wo_s, sems.at[2]),
    ]

    @pl.when(step == 0)
    def _():
        for copy in copies:
            copy.start()
        sums_ref[...] = jnp.zeros_like(sums_ref)

    dy = dy_ref[...].astype(F32)
    n, root = normed(z2_ref[...])
    sums_ref[G2 : G2 + 1, :] += colsum(dy * n)
    sums_ref[S2 : S2 + 1, :] += colsum(dy)
    dz2 = normed_back(n, root, dy * vec_ref[G2 : G2 + 1, :])
    e2 = dz2.astype(BF)
    e2_ref[...] = e2
    sums_ref[BB : BB + 1, :] += colsum(e2.astype(F32))

    @pl.when(step == 0)
    def _():
        for copy in copies:
            copy.wait()

    units = wi_s.shape[0]

    def up(j):
        return mm(e2, wb_s[j * D : (j + 1) * D, :], NT)

    acc = dz2
    f = up(0)
    for j in range(units):
        ahead = up(j + 1) if j + 1 < units else None
        cols = slice(j * D, (j + 1) * D)
        e1 = (f * slope_ref[:, cols].astype(F32)).astype(BF)
        e1_ref[:, cols] = e1
        sums_ref[8 + j : 9 + j, :] += colsum(e1.astype(F32))
        acc += mm(e1, wi_s[j], NT)
        f = ahead
    n, root = normed(z1_ref[...])
    sums_ref[G1 : G1 + 1, :] += colsum(acc * n)
    sums_ref[S1 : S1 + 1, :] += colsum(acc)
    dz1 = normed_back(n, root, acc * vec_ref[G1 : G1 + 1, :])
    dz1_ref[...] = dz1
    ea = dz1.astype(BF)
    ea_ref[...] = ea
    sums_ref[BO : BO + 1, :] += colsum(ea.astype(F32))
    dctx_ref[...] = mm(ea, wo_s[...], NT).astype(BF)


def ffn_back_call(dy, z2, z1, slope, wb, wi, first, vec, block=256):
    rows = dy.shape[0]
    ff = wb.shape[0]
    line, wide = by_rows(block, D), by_rows(block, ff)
    held = once(vec.shape, lambda i: (0, 0))
    return pl.pallas_call(
        ffn_back_body,
        grid=(rows // block,),
        in_specs=[line, line, line, wide, held, ANY, ANY, ANY],
        out_specs=[line, wide, line, line, line, held],
        out_shape=[
            jax.ShapeDtypeStruct((rows, D), BF),
            jax.ShapeDtypeStruct((rows, ff), BF),
            jax.ShapeDtypeStruct((rows, D), F32),
            jax.ShapeDtypeStruct((rows, D), BF),
            jax.ShapeDtypeStruct((rows, D), BF),
            jax.ShapeDtypeStruct(vec.shape, F32),
        ],
        scratch_shapes=weight_scratch(ff),
        compiler_params=params(),
        cost_estimate=cost(24),
        name="ffn_back",
    )(dy, z2, z1, slope, vec, wb, wi, first)


def attend_back_body(seq, pairs, len_ref, q_ref, k_ref, v_ref, d_ref, l_ref, e_ref, bq_ref, bv_ref):
    count = len_ref[pl.program_id(0)]
    lane = lax.broadcasted_iota(jnp.int32, (seq, PAIR), 1)
    ok = lax.broadcasted_iota(jnp.int32, (seq, seq), 0) < count
    units = [(pr, h) for pr in range(pairs) for h in range(2)]

    def score(unit):
        pr, h = unit
        cols = slice(pr * PAIR, (pr + 1) * PAIR)
        mine = (lane >= HEAD_DIM) == (h == 1)
        q = jnp.where(mine, q_ref[:, cols] * BF(0.125), BF(0))
        s = jnp.where(ok, mm(k_ref[:, cols], q, NT), -1e30)
        return s, mm(v_ref[:, cols], jnp.where(mine, d_ref[:, cols], BF(0)), NT)

    ahead = score(units[0])
    eq, ek, ev = {}, {}, {}
    for i, (pr, h) in enumerate(units):
        s, dp = ahead
        if i + 1 < len(units):
            ahead = score(units[i + 1])
        cols = slice(pr * PAIR, (pr + 1) * PAIR)
        if h == 0:
            kt = (k_ref[:, cols] * BF(0.125)).T
        p = jnp.exp(s - l_ref[0, pr, h : h + 1, :])
        pd = p * dp
        ds = (pd - p * colsum(pd)).astype(BF)
        ev[h] = mm(p.astype(BF), d_ref[:, cols], NN)
        ek[h] = mm(ds, q_ref[:, cols] * BF(0.125), NN)
        eq[h] = mm(kt[h * HEAD_DIM : (h + 1) * HEAD_DIM], ds, NN)
        if h == 1:
            low = jnp.concatenate([eq[0], eq[1]], axis=0).T.astype(BF)
            e_ref[0, :, cols] = low
            bq_ref[0, :, cols] = colsum(low.astype(F32))
            e_ref[1, :, cols] = jnp.where(lane < HEAD_DIM, ek[0], ek[1]).astype(BF)
            low = jnp.where(lane < HEAD_DIM, ev[0], ev[1]).astype(BF)
            e_ref[2, :, cols] = low
            bv_ref[0, :, cols] = colsum(low.astype(F32))


GROUPS = 2
WIDE = D // GROUPS


def attend_back_call(qkv, dctx, lse, lengths, group):
    rows = qkv.shape[0]
    count = lengths.shape[0]
    seq = rows // count
    pairs = WIDE // PAIR

    def part(o):
        return pl.BlockSpec((seq, WIDE), lambda s, n: (s, o * GROUPS + group))

    def body(*refs):
        attend_back_body(seq, pairs, *refs)

    line = pl.BlockSpec((1, 1, WIDE), lambda s, n: (s, 0, 0))
    return pl.pallas_call(
        body,
        grid_spec=pltpu.PrefetchScalarGridSpec(
            num_scalar_prefetch=1,
            grid=(count,),
            in_specs=[
                part(0),
                part(1),
                part(2),
                part(0),
                pl.BlockSpec((1, pairs, 2, seq), lambda s, n: (s, group, 0, 0)),
            ],
            out_specs=[pl.BlockSpec((3, seq, WIDE), lambda s, n: (0, s, 0)), line, line],
        ),
        out_shape=[jax.ShapeDtypeStruct((3, rows, WIDE), BF)] + [jax.ShapeDtypeStruct((count, 1, WIDE), F32)] * 2,
        compiler_params=params(),
        cost_estimate=cost(12),
        name="attend_back",
    )(lengths, qkv, qkv, qkv, dctx, lse)


def dx_body(dz1_ref, e0_ref, e1_ref, w_ref, o_ref):
    acc = dz1_ref[...]
    for i in range(3):
        acc += mm(e0_ref[i], w_ref[i, :, :WIDE], NT)
        acc += mm(e1_ref[i], w_ref[i, :, WIDE:], NT)
    o_ref[...] = acc.astype(o_ref.dtype)


def dx_call(dz1, e0, e1, w, dtype, block=256):
    rows = dz1.shape[0]
    line = pl.BlockSpec((block, D), lambda i: (i, 0))
    part = pl.BlockSpec((3, block, WIDE), lambda i: (0, i, 0))
    return pl.pallas_call(
        dx_body,
        grid=(rows // block,),
        in_specs=[line, part, part, once((3, D, D), lambda i: (0, 0, 0))],
        out_specs=line,
        out_shape=jax.ShapeDtypeStruct((rows, D), dtype),
        compiler_params=params(),
        cost_estimate=cost(9),
        name="dx",
    )(dz1, e0, e1, w)


def deal(acc_s, rows, x_first, core_ref, keep_ref, send_ref):
    part = 8 * rows
    for out, core in ((keep_ref, core_ref[0]), (send_ref, 1 - core_ref[0])):
        for xi in range(2):
            for s in range(8):
                zi, yi = s // 2, s % 2
                start = pl.multiple_of(core * part + (2 * xi * part + s * rows), 8)
                value = acc_s[pl.ds(start, rows), :].astype(BF)
                if x_first:
                    out[xi, yi, zi, 0] = value
                else:
                    out[yi, xi, zi, 0] = value


def packet(rows, units, width):
    spec = pl.BlockSpec((2, 2, 4, 1, rows, width), lambda i, n: (0, 0, 0, i, 0, 0))
    return [spec] * 2, [jax.ShapeDtypeStruct((2, 2, 4, units, rows, width), BF)] * 2


def wgrad_in_call(core, a, c, b, d, rows):
    k, n = b.shape
    held = once((k, D), lambda i, n: (0, 0))
    spec = pl.BlockSpec((k, D), lambda i, n: (0, i))
    out_specs, out_shape = packet(rows, n // D, D)

    def body(core_ref, a_ref, c_ref, b_ref, d_ref, keep_ref, send_ref, acc_s):
        acc_s[...] = mm(a_ref[...], b_ref[...], TN) + mm(c_ref[...], d_ref[...], TN)
        deal(acc_s, rows, True, core_ref, keep_ref, send_ref)

    return pl.pallas_call(
        body,
        grid_spec=pltpu.PrefetchScalarGridSpec(
            num_scalar_prefetch=1,
            grid=(n // D,),
            in_specs=[held, held, spec, spec],
            out_specs=out_specs,
            scratch_shapes=[pltpu.VMEM((D, D), F32)],
        ),
        out_shape=out_shape,
        compiler_params=params(),
        cost_estimate=cost(15),
        name="wgrad_in",
    )(core, a, c, b, d)


def wgrad_heads_call(core, low2, low1, e2, e1, rows, others, x_first):
    k = low2.shape[0]
    last = len(others) == 4
    held = once((k, D), lambda i, n: (0, 0))
    spec = pl.BlockSpec((1, k, WIDE), lambda i, n: (jnp.minimum(i, 2), 0, 0))
    units = 5 if last else 4
    out_specs, out_shape = packet(rows, units, WIDE)
    if last:
        half = pl.BlockSpec((k, WIDE), lambda i, n: (0, jnp.maximum(i - 3, 0)))
        more = [held, held, half, half]
    else:
        more = [whole_block(v) for v in others]

    def body(core_ref, a_ref, c_ref, b_ref, d_ref, *rest):
        rest, (keep_ref, send_ref, acc_s) = rest[:-3], rest[-3:]
        step = pl.program_id(0)

        @pl.when(step < 3)
        def _():
            acc_s[...] = mm(a_ref[...], b_ref[0], TN) + mm(c_ref[...], d_ref[0], TN)

        if last:

            @pl.when(step >= 3)
            def _():
                acc_s[...] = mm(rest[0][...], rest[2][...], TN) + mm(rest[1][...], rest[3][...], TN)

            deal(acc_s, rows, x_first, core_ref, keep_ref, send_ref)
        else:

            @pl.when(step < 3)
            def _():
                deal(acc_s, rows, x_first, core_ref, keep_ref, send_ref)

            @pl.when(step == 3)
            def _():
                sums = rest[0][...] + rest[1][...]
                small = []
                for g in range(GROUPS):
                    lines = rest[2 + 4 * g : 6 + 4 * g]
                    small.append(colsum(lines[0][:, 0, :] + lines[1][:, 0, :]))
                    small.append(colsum(lines[2][:, 0, :] + lines[3][:, 0, :]))
                    small.append(sums[2 : rows // 2, g * WIDE : (g + 1) * WIDE])
                small = jnp.concatenate(small, axis=0).astype(BF)
                for i in range(16):
                    keep_ref[i // 8, i // 4 % 2, i % 4, 0] = small
                    send_ref[i // 8, i // 4 % 2, i % 4, 0] = small

    return pl.pallas_call(
        body,
        grid_spec=pltpu.PrefetchScalarGridSpec(
            num_scalar_prefetch=1,
            grid=(units,),
            in_specs=[held, held, spec, spec] + more,
            out_specs=out_specs,
            scratch_shapes=[pltpu.VMEM((D, WIDE), F32)],
        ),
        out_shape=out_shape,
        compiler_params=params(),
        cost_estimate=cost(12),
        name="wgrad_heads",
    )(core, low2, low1, e2, e1, *others)


def wgrad_back_call(core, two, one, e_two, e_one, rows):
    k, ff = two.shape
    block = ff // 8

    def cols(other):
        def index(x, s, n):
            c = 1 - n[0] if other else n[0]
            return (0, (x * 2 + c) * 2 + s)

        return pl.BlockSpec((k, block), index)

    held = once((k, D), lambda x, s, n: (0, 0))
    out = pl.BlockSpec((2, 1, 2, 4, rows, D), lambda x, s, n: (0, x, s, 0, 0, 0))

    def body(core_ref, g2k, g1k, g2s, g1s, e2_ref, e1_ref, keep_ref, send_ref):
        for a, c, o in ((g2k, g1k, keep_ref), (g2s, g1s, send_ref)):
            acc = mm(a[...], e2_ref[...], TN) + mm(c[...], e1_ref[...], TN)
            for s in range(16):
                o[s // 4 % 2, 0, s // 8, s % 4] = acc[s * rows : (s + 1) * rows].astype(BF)

    return pl.pallas_call(
        body,
        grid_spec=pltpu.PrefetchScalarGridSpec(
            num_scalar_prefetch=1,
            grid=(2, 2),
            in_specs=[cols(False), cols(False), cols(True), cols(True), held, held],
            out_specs=[out, out],
        ),
        out_shape=[jax.ShapeDtypeStruct((2, 2, 4, 4, rows, D), BF)] * 2,
        compiler_params=params(),
        cost_estimate=cost(15),
        name="wgrad_back",
    )(core, two, one, two, one, e_two, e_one)


def layer_forward(x, low, weights, lengths, renorm):
    first, w_in, w_back, vec = weights
    qkv = qkv_call(low, first, vec)
    ctx, lse = attend_call(qkv, lengths)
    z1, h1, g, slope, z2, y = ffn_call(x, ctx, first, vec, w_in, w_back, renorm)
    return z2, y, (low, qkv, lse, ctx, z1, h1, g, slope, z2)


class Grid:
    def __init__(self, sizes):
        self.dp, self.fsdp = sizes["dp"], sizes["fsdp"]
        self.count = self.dp * self.fsdp
        self.x, self.core = self.dp // 2, 2
        self.y = self.fsdp // 4
        self.z = self.fsdp // self.y if self.y else 0
        self.staged = self.x == 2 and self.y == 2

    def place(self):
        dp, fsdp = lax.axis_index("dp"), lax.axis_index("fsdp")
        return dp // 2, dp % 2, fsdp // self.y, fsdp % self.y

    def shift(self, dim, step):
        sizes = (self.x, self.core, self.z, self.y)
        pairs = []
        for i in range(self.count):
            at = [i // (self.core * self.fsdp), i // self.fsdp % self.core, i % self.fsdp // self.y, i % self.y]
            at[dim] = (at[dim] + step) % sizes[dim]
            pairs.append((i, ((at[0] * self.core + at[1]) * self.z + at[2]) * self.y + at[3]))
        return pairs

    def send(self, value, dim, step=1):
        return lax.ppermute(value, AXES, self.shift(dim, step))

    def trade(self, value):
        groups = [[z * self.y + y for z in range(self.z)] for y in range(self.y)]
        return lax.all_to_all(value, "fsdp", 0, 0, tiled=True, axis_index_groups=groups)


X, CORE, Z, Y = range(4)


def pack_one_body(at_ref, wq_ref, wo_ref, *rest):
    vectors, span_ref, one_ref, line_s = rest[:8], rest[8], rest[9], rest[10]
    rows = wq_ref.shape[0]
    for i in range(3):
        one_ref[i] = wq_ref[:, i * D : (i + 1) * D]
    one_ref[3] = wo_ref[...]
    line_s[...] = jnp.zeros_like(line_s)
    for i, ref in enumerate(vectors):
        line_s[i : i + 1, :rows] = ref[...].astype(F32)
    span = span_ref.shape[1]
    line_s[8:9, :span] = span_ref[...].astype(F32)
    device = at_ref[0]
    per = D // span
    top = pltpu.roll(line_s[:8], device * rows, 1)
    low = pltpu.roll(line_s[8:16], lax.rem(device, per) * span, 1)
    here = lax.broadcasted_iota(jnp.int32, (8, D), 0) == lax.div(device, per)
    low = jnp.where(here, jnp.broadcast_to(low[:1], (8, D)), 0.0)
    one_ref[4] = jnp.concatenate([top, low, jnp.zeros((rows - 16, D), F32)], axis=0).astype(BF)


def pack_one(device, w_qkv, w_out, vectors, span):
    rows = w_qkv.shape[0]
    operands = [w_qkv, w_out, *[v[None] for v in vectors], span[None]]
    return pl.pallas_call(
        pack_one_body,
        grid_spec=pltpu.PrefetchScalarGridSpec(
            num_scalar_prefetch=1,
            grid=(1,),
            in_specs=[whole_block(v) for v in operands],
            out_specs=pl.BlockSpec((5, rows, D), lambda *_: (0, 0, 0)),
            scratch_shapes=[pltpu.VMEM((16, D), F32)],
        ),
        out_shape=jax.ShapeDtypeStruct((5, rows, D), BF),
        compiler_params=params(),
        name="pack_one",
    )(device, *operands)


def pack_two_body(wi_ref, wb_ref, two_ref):
    rows = wi_ref.shape[0]
    for i in range(4):
        two_ref[i] = wi_ref[:, i * D : (i + 1) * D]
        two_ref[4 + i] = wb_ref[i * rows : (i + 1) * rows]


def pack_two(w_in, w_back):
    rows = w_in.shape[0]
    return pl.pallas_call(
        pack_two_body,
        grid=(1,),
        in_specs=[whole_block(w_in), whole_block(w_back)],
        out_specs=pl.BlockSpec((8, rows, D), lambda *_: (0, 0, 0)),
        out_shape=jax.ShapeDtypeStruct((8, rows, D), BF),
        compiler_params=params(),
        name="pack_two",
    )(w_in, w_back)


def place_body(split, at_ref, *refs):
    outs = 2 if split else 1
    parts, outs, held, sems, out_sems = refs[:8], refs[8 : 8 + outs], refs[8 + outs : -2], refs[-2], refs[-1]
    x, core, z, y = at_ref[0], at_ref[1], at_ref[2], at_ref[3]
    sides = ([], [])
    for i, part in enumerate(parts):
        side, far, other = i >> 2, (i >> 1) & 1, i & 1
        count = part.shape[2]
        for near in range(2):
            px = (x + (far if side == 0 else near)) % 2
            py = (y + (near if side == 0 else far)) % 2
            pc = (core + other) % 2
            for dz in range(4):
                pz = dz if split else (z + 4 - dz) % 4
                if split:
                    target = held[side].at[:, px, pc, pz, py] if side == 0 else held[side].at[px, pc, pz, py]
                else:
                    target = held[0].at[pl.ds(0 if side == 0 else 5 - count, count), px, pc, pz, py]
                sem = sems.at[i * 8 + near * 4 + dz]
                sides[side].append(pltpu.make_async_copy(part.at[near, dz], target, sem))
    for side in sides:
        for copy in side:
            copy.start()
    back = []
    for side in range(2):
        for copy in sides[side]:
            copy.wait()
        if split:
            pair = held[side], outs[side]
        else:
            count = parts[4 * side].shape[2]
            span = pl.ds(0 if side == 0 else 5 - count, count)
            pair = held[0].at[span], outs[0].at[span]
        back.append(pltpu.make_async_copy(*pair, out_sems.at[side]))
        back[-1].start()
    for copy in back:
        copy.wait()


def place(at, parts, split):
    rows = parts[0].shape[3]
    if split:
        shapes = [(4, 2, 2, 4, 2, rows, D), (2, 2, 4, 2, 4, rows, D)]
    else:
        shapes = [(5, 2, 2, 4, 2, rows, D)]
    return pl.pallas_call(
        lambda *refs: place_body(split, *refs),
        grid_spec=pltpu.PrefetchScalarGridSpec(
            num_scalar_prefetch=1,
            grid=(1,),
            in_specs=[ANY] * 8,
            out_specs=[ANY] * len(shapes),
            scratch_shapes=[pltpu.VMEM(shape, BF) for shape in shapes]
            + [pltpu.SemaphoreType.DMA((64,)), pltpu.SemaphoreType.DMA((2,))],
        ),
        out_shape=[jax.ShapeDtypeStruct(shape, BF) for shape in shapes],
        compiler_params=params(),
        cost_estimate=cost(6),
        name="place",
    )(at, *parts)


def after(value, *others):
    return lax.optimization_barrier((value, *others))[0]


class Gather:
    def __init__(self, grid, packet, first, at_once):
        self.grid, self.first = grid, first
        if at_once:
            self.ring = grid.trade(jnp.broadcast_to(packet, (4,) + packet.shape))
        else:
            self.ring = jnp.stack([packet] + [grid.send(packet, Z, k) for k in range(1, 4)])

    def one(self, *others):
        ring = after(self.ring, *others)
        self.line = [ring[:, : self.first], ring[:, self.first :]]
        self.came = [self.grid.send(v, d) for v, d in zip(self.line, (Y, X))]

    def two(self, *others):
        held = lax.optimization_barrier((*self.line, *others))
        self.near = [jnp.stack(pair) for pair in zip(held, self.came)]
        self.far = [self.grid.send(v, d) for v, d in zip(self.near, (X, Y))]
        self.near_core = [self.grid.send(v, CORE) for v in self.near]

    def parts(self, *others):
        far = lax.optimization_barrier((*self.far, *others))[:2]
        out = []
        for i in range(2):
            out += [self.near[i], self.near_core[i], far[i], self.grid.send(far[i], CORE)]
        return out


def pick(value, index, dim):
    return lax.dynamic_index_in_dim(value, index, dim, keepdims=False)


def added(a, b, *picks):
    for index, dim in picks:
        a, b = pick(a, index, dim), pick(b, index, dim)
    return (a.astype(F32) + b.astype(F32)).astype(BF)


class Sum:
    def __init__(self, grid, place, order, pair):
        self.grid, self.place, self.order = grid, place, order
        self.mine, self.came = pair[0], grid.send(pair[1], CORE)

    def cut(self, dim, others):
        here = self.place[dim]
        mine = after(self.mine, *others)
        out = added(mine, self.came, (1 - here, 0))
        self.mine = added(mine, self.came, (here, 0))
        self.came = self.grid.send(out, dim)
        return [out, self.mine]

    def one(self, *others):
        return self.cut(self.order[0], others)

    def two(self, *others):
        return self.cut(self.order[1], others)

    def three(self, *others):
        z = self.place[2]
        line = added(after(self.mine, *others), self.came)
        self.mine = pick(line, z, 0)
        self.came = [self.grid.send(pick(line, (z + k) % 4, 0), Z, k) for k in range(1, 4)]
        return [line]

    def result(self):
        total = self.mine.astype(F32)
        for piece in self.came:
            total += piece.astype(F32)
        return total


def staged(grid, lengths, tokens, cotangent, shards):
    w_qkv, bias_q, bias_v, w_out, bias_out, gain_one, shift_one, w_in, bias_in, w_back, bias_back, gain_two, shift_two = shards
    rows, span = bias_q.shape[0], bias_in.shape[0]
    where = grid.place()
    x, core, z, y = where
    device = lax.axis_index(AXES)
    at = jnp.stack([x, core, z, y]).astype(jnp.int32)
    core = core.astype(jnp.int32)[None]
    vectors = [bias_q, bias_v, bias_out, gain_one, shift_one, bias_back, gain_two, shift_two]
    one = Gather(grid, pack_one(device.astype(jnp.int32)[None], w_qkv, w_out, vectors, bias_in), 2, False)
    two = Gather(grid, pack_two(w_in, w_back), 4, True)
    one.one()
    one.two()
    two.one(*one.far)
    (first,) = place(at, one.parts(), False)
    first = first.reshape(5, grid.count * rows, D)
    vec = jnp.sum(first[4].reshape(grid.count, rows, D).astype(F32), axis=0)
    qkv = qkv_call(tokens, first, vec)
    two.two()
    ctx, lse = attend_call(after(qkv, *two.near), lengths)
    w_in, w_back = place(at, two.parts(ctx), True)
    w_in = w_in.reshape(4, grid.count * rows, D)
    w_back = w_back.reshape(grid.count * span, D)
    z1, h1, g, slope, z2, low = ffn_call(tokens, ctx, first, vec, w_in, w_back, False)
    saved = [(tokens, qkv, lse, ctx, z1, h1, g, slope, z2)]
    weights = (first, w_in, w_back, vec)
    _, low, stored = layer_forward(z2, low, weights, lengths, True)
    saved.append(stored)
    activations = low

    low2, qkv, lse, ctx2, z1, h2, g2, slope, z2 = saved[1]
    e2_2, e1_2, dz1, ea_2, dctx, sums_2 = ffn_back_call(cotangent, z2, z1, slope, w_back, w_in, first, vec)
    heads_2 = [attend_back_call(qkv, dctx, lse, lengths, i) for i in range(GROUPS)]
    grad = dx_call(dz1, heads_2[0][0], heads_2[1][0], first, F32)

    low1, qkv, lse, ctx1, z1, h1, g1, slope, z2 = saved[0]
    e2_1, e1_1, dz1, ea_1, dctx, sums_1 = ffn_back_call(grad, z2, z1, slope, w_back, w_in, first, vec)
    count = tokens.shape[0]

    heads_1 = []
    back = wgrad_back_call(core, g2, g1, e2_2, e2_1, rows)
    sum_back = Sum(grid, where, (Y, X), back)
    into = wgrad_in_call(core, after(h2, back[0]), h1, e1_2, e1_1, rows)
    sum_in = Sum(grid, where, (X, Y), into)
    steps = sum_back.one(into[0]) + sum_in.one(into[0])
    heads_1.append(attend_back_call(qkv, after(dctx, *steps), lse, lengths, 0))
    heads_1.append(attend_back_call(qkv, after(dctx, heads_1[0][0]), lse, lengths, 1))
    steps = sum_back.two(heads_1[1][0]) + sum_in.two(heads_1[1][0])
    group = wgrad_heads_call(
        core, after(low2, *steps), low1, heads_2[0][0], heads_1[0][0], rows, [ctx2, ctx1, ea_2, ea_1], False
    )
    sum_0 = Sum(grid, where, (Y, X), group)
    steps = sum_back.three(group[0]) + sum_in.three(group[0])
    lines = [heads[i][j] for i in range(GROUPS) for j in (1, 2) for heads in (heads_1, heads_2)]
    group = wgrad_heads_call(
        core, after(low2, *steps), low1, heads_2[1][0], heads_1[1][0], rows, [sums_1, sums_2, *lines], True
    )
    sum_1 = Sum(grid, where, (X, Y), group)
    steps = sum_0.one(group[0]) + sum_1.one()
    total_back = sum_back.result()
    grad = dx_call(after(dz1, total_back, *steps), heads_1[0][0], heads_1[1][0], first, BF)
    sum_0.two(grad)
    sum_1.two(grad)
    sum_0.three()
    sum_1.three()
    total_in, half_0, half_1 = sum_in.result(), sum_0.result(), sum_1.result()

    w_in_grad = total_in.swapaxes(0, 1).reshape(rows, 4 * D)
    w_back_grad = total_back.reshape(4 * rows, D)
    w_qkv_grad = jnp.stack([half_0[:3], half_1[:3]], axis=1).transpose(2, 0, 1, 3).reshape(rows, 3 * D)
    w_out_grad = half_0[3:].swapaxes(0, 1).reshape(rows, D)
    small = jnp.concatenate([half_1[3][: rows // 2], half_1[3][rows // 2 :]], axis=1)
    mine = lax.dynamic_slice(small, (0, device * rows), (8, rows))
    per = D // span
    last = lax.dynamic_slice(small, (8 + device // per, device % per * span), (1, span))[0]
    return activations, grad, w_qkv_grad, w_out_grad, w_in_grad, w_back_grad, [mine[i] for i in range(8)] + [last]


def plain(grid, lengths, tokens, cotangent, shards):
    w_qkv, bias_q, bias_v, w_out, bias_out, gain_one, shift_one, w_in, bias_in, w_back, bias_back, gain_two, shift_two = shards
    vectors = [bias_q, bias_v, bias_out, gain_one, shift_one, bias_back, gain_two, shift_two]

    def whole(v):
        return lax.all_gather(v, AXES, axis=0, tiled=True)

    lines = jnp.stack([whole(v) for v in vectors])
    vec = jnp.concatenate([lines, whole(bias_in).reshape(4, D), jnp.zeros((4, D), BF)], axis=0).astype(F32)

    def blocks(w):
        return w.reshape(D, -1, D).swapaxes(0, 1)

    first = jnp.concatenate([blocks(whole(w_qkv)), whole(w_out)[None], jnp.zeros((1, D, D), BF)], axis=0)
    w_in, w_back = blocks(whole(w_in)), whole(w_back)
    weights = (first, w_in, w_back, vec)
    value, low = tokens, tokens
    saved = []
    for step in range(APPS):
        value, low, stored = layer_forward(value, low, weights, lengths, step > 0)
        saved.append(stored)
    activations, grad, totals = low, cotangent, None
    for step in reversed(range(APPS)):
        low, qkv, lse, ctx, z1, h1, g, slope, z2 = saved[step]
        e2, e1, dz1, ea, dctx, sums = ffn_back_call(grad, z2, z1, slope, w_back, w_in, first, vec)
        heads = [attend_back_call(qkv, dctx, lse, lengths, i) for i in range(GROUPS)]
        grad = dx_call(dz1, heads[0][0], heads[1][0], first, F32 if step else BF)
        e = jnp.concatenate([heads[i][0] for i in range(GROUPS)], axis=2).swapaxes(0, 1).reshape(-1, 3 * D)
        lines = [jnp.concatenate([jnp.sum(heads[i][j], axis=0) for i in range(GROUPS)], axis=1) for j in (1, 2)]
        grads = [mm(low, e, TN), mm(ctx, ea, TN), mm(h1, e1, TN), mm(g, e2, TN)]
        grads += [jnp.concatenate(lines + [sums[2:]], axis=0)]
        totals = grads if totals is None else [a + b for a, b in zip(totals, grads)]
    lines = list(totals.pop())
    totals += lines[:8] + [jnp.concatenate(lines[8:12])]
    owned = [lax.psum_scatter(v, AXES, scatter_dimension=0, tiled=True) for v in totals]
    return activations, grad, *owned[:4], owned[4:]


def make_local(grid):
    def local(tokens, lengths, *rest):
        run = staged if grid.staged else plain
        activations, grad, w_qkv, w_out, w_in, w_back, lines = run(grid, lengths, tokens, rest[-1], rest[:-1])
        return (
            activations, grad, w_qkv, lines[BQ], lines[BV], w_out, lines[BO], lines[G1], lines[S1],
            w_in, lines[8], w_back, lines[BB], lines[G2], lines[S2],
        )

    return local


def solution(mesh):
    wide, line = P(AXES, None), P(AXES)
    return jax.shard_map(
        make_local(Grid(mesh.shape)),
        mesh=mesh,
        in_specs=(wide, line, wide, line, line, wide, line, line, line, wide, line, wide, line, line, line, wide),
        out_specs=(wide, wide, wide, line, line, wide, line, line, line, wide, line, wide, line, line, line),
        check_vma=False,
    )
```

```python
import jax
import jax.numpy as jnp
from jax import lax
from jax.experimental import pallas as pl
from jax.experimental.pallas import tpu as pltpu
from jax.sharding import PartitionSpec as P

D = 768
HEADS = 12
HEAD_DIM = 64
APPS = 2
PAIR = 2 * HEAD_DIM
AXES = ("dp", "fsdp")
BF = jnp.bfloat16
F32 = jnp.float32
NN = (((1,), (0,)), ((), ()))
NT = (((1,), (1,)), ((), ()))
TN = (((0,), (0,)), ((), ()))
VMEM = 56 * 2**20
BQ, BV, BO, G1, S1, BB, G2, S2 = range(8)


def mm(left, right, dims):
    return lax.dot_general(left, right, dims, preferred_element_type=F32)


def params(limit=VMEM):
    return pltpu.CompilerParams(vmem_limit_bytes=limit)


def cost(micros):
    return pl.CostEstimate(flops=int(micros * 2e8), bytes_accessed=int(micros * 1e5), transcendentals=0)


def once(shape, index):
    return pl.BlockSpec(shape, index, pipeline_mode=pl.Buffered(1))


def whole_block(v):
    return pl.BlockSpec(v.shape, lambda *_: (0,) * v.ndim)


def normed(z):
    centered = z - jnp.mean(z, axis=-1, keepdims=True)
    root = lax.rsqrt(jnp.mean(centered * centered, axis=-1, keepdims=True) + 1e-12)
    return centered * root, root


def normed_back(n, root, e):
    return root * (e - jnp.mean(e, axis=-1, keepdims=True) - n * jnp.mean(e * n, axis=-1, keepdims=True))


def colsum(v):
    return jnp.sum(v, axis=0, keepdims=True)


def qkv_body(x_ref, w_ref, vec_ref, o_ref):
    part = pl.program_id(0)
    acc = mm(x_ref[...], w_ref[0], NN)
    bias = jnp.where(part == 0, vec_ref[BQ : BQ + 1, :], jnp.where(part == 2, vec_ref[BV : BV + 1, :], 0.0))
    o_ref[...] = (acc + bias).astype(BF)


def qkv_call(x, w, vec):
    rows = x.shape[0]
    return pl.pallas_call(
        qkv_body,
        grid=(3,),
        in_specs=[
            once((rows, D), lambda i: (0, 0)),
            pl.BlockSpec((1, D, D), lambda i: (i, 0, 0)),
            once(vec.shape, lambda i: (0, 0)),
        ],
        out_specs=pl.BlockSpec((rows, D), lambda i: (0, i)),
        out_shape=jax.ShapeDtypeStruct((rows, 3 * D), BF),
        compiler_params=params(),
        cost_estimate=cost(8),
        name="qkv",
    )(x, w, vec)


def attend_body(seq, pairs, len_ref, q_ref, k_ref, v_ref, o_ref, l_ref):
    count = len_ref[pl.program_id(0)]
    lane = lax.broadcasted_iota(jnp.int32, (seq, PAIR), 1)
    row = lax.broadcasted_iota(jnp.int32, (seq, PAIR), 0)
    mask = jnp.where(row < count, 0.0, -1e30).astype(BF)
    units = [(pr, h) for pr in range(pairs) for h in range(2)]

    def score(unit):
        pr, h = unit
        cols = slice(pr * PAIR, (pr + 1) * PAIR)
        mine = (lane >= HEAD_DIM) == (h == 1)
        spare = lane == HEAD_DIM * (1 - h)
        q = jnp.where(mine, q_ref[:, cols] * BF(0.125), jnp.where(spare, BF(1), BF(0)))
        k = jnp.where(mine, k_ref[:, cols], jnp.where(spare, mask, BF(0)))
        return mm(q, k, NT)

    ahead = score(units[0])
    held = {}
    for i, (pr, h) in enumerate(units):
        s = ahead
        if i + 1 < len(units):
            ahead = score(units[i + 1])
        cols = slice(pr * PAIR, (pr + 1) * PAIR)
        top = jnp.max(s, axis=1, keepdims=True)
        p = jnp.exp(s - top)
        total = jnp.sum(p, axis=1, keepdims=True)
        held[h] = mm(p.astype(BF), v_ref[:, cols], NN) / total
        l_ref[0, pr, h : h + 1, :] = (top + jnp.log(total)).reshape(1, seq)
        if h == 1:
            o_ref[:, cols] = jnp.where(lane < HEAD_DIM, held[0], held[1]).astype(BF)


def attend_call(qkv, lengths, pairs=3):
    rows = qkv.shape[0]
    count = lengths.shape[0]
    seq = rows // count
    groups = D // PAIR // pairs
    wide = PAIR * pairs

    def part(o):
        return pl.BlockSpec((seq, wide), lambda s, p, n: (s, o * groups + p))

    def body(*refs):
        attend_body(seq, pairs, *refs)

    return pl.pallas_call(
        body,
        grid_spec=pltpu.PrefetchScalarGridSpec(
            num_scalar_prefetch=1,
            grid=(count, groups),
            in_specs=[part(0), part(1), part(2)],
            out_specs=[part(0), pl.BlockSpec((1, pairs, 2, seq), lambda s, p, n: (s, p, 0, 0))],
        ),
        out_shape=[
            jax.ShapeDtypeStruct((rows, D), BF),
            jax.ShapeDtypeStruct((count, D // PAIR, 2, seq), F32),
        ],
        compiler_params=params(),
        cost_estimate=cost(13),
        name="attend",
    )(lengths, qkv, qkv, qkv)


def gelu_both(u):
    a = 0.7978845608028654
    c = a + (a * 0.044715) * (u * u)
    s = 0.5 + 0.5 * jnp.tanh(u * c)
    g = u * s
    return g, s + (g * (1.0 - s)) * (6.0 * c - 4.0 * a)


ANY = pl.BlockSpec(memory_space=pl.ANY)


def by_rows(block, width):
    return pl.BlockSpec((block, width), lambda i: (i, 0))


def ffn_body(
    renorm, x_ref, ctx_ref, vec_ref, wo_h, wi_h, wb_h,
    z1_ref, h1_ref, g_ref, slope_ref, z2_ref, y_ref, wo_s, wi_s, wb_s, sems,
):
    step = pl.program_id(0)
    copies = [
        pltpu.make_async_copy(wo_h.at[3], wo_s, sems.at[0]),
        pltpu.make_async_copy(wi_h, wi_s, sems.at[1]),
        pltpu.make_async_copy(wb_h, wb_s, sems.at[2]),
    ]

    @pl.when(step == 0)
    def _():
        for copy in copies:
            copy.start()
        copies[0].wait()

    x = x_ref[...].astype(F32)
    if renorm:
        n, _ = normed(x)
        x = n * vec_ref[G2 : G2 + 1, :] + vec_ref[S2 : S2 + 1, :]
    z1 = x + mm(ctx_ref[...], wo_s[...], NN) + vec_ref[BO : BO + 1, :]
    z1_ref[...] = z1
    n, _ = normed(z1)
    h1 = n * vec_ref[G1 : G1 + 1, :] + vec_ref[S1 : S1 + 1, :]
    low = h1.astype(BF)
    h1_ref[...] = low

    @pl.when(step == 0)
    def _():
        copies[1].wait()
        copies[2].wait()

    units = wi_s.shape[0]

    def up(j):
        return mm(low, wi_s[j], NN) + vec_ref[8 + j : 9 + j, :]

    acc = h1 + vec_ref[BB : BB + 1, :]
    f = up(0)
    for j in range(units):
        ahead = up(j + 1) if j + 1 < units else None
        cols = slice(j * D, (j + 1) * D)
        g, slope = gelu_both(f)
        g = g.astype(BF)
        g_ref[:, cols] = g
        slope_ref[:, cols] = slope.astype(BF)
        acc += mm(g, wb_s[cols, :], NN)
        f = ahead
    z2_ref[...] = acc
    n, _ = normed(acc)
    y_ref[...] = (n * vec_ref[G2 : G2 + 1, :] + vec_ref[S2 : S2 + 1, :]).astype(BF)


def weight_scratch(ff):
    return [
        pltpu.VMEM((D, D), BF),
        pltpu.VMEM((ff // D, D, D), BF),
        pltpu.VMEM((ff, D), BF),
        pltpu.SemaphoreType.DMA((3,)),
    ]


def ffn_call(x, ctx, first, vec, wi, wb, renorm, block=512):
    rows = x.shape[0]
    ff = wb.shape[0]
    line, wide = by_rows(block, D), by_rows(block, ff)
    return pl.pallas_call(
        lambda *refs: ffn_body(renorm, *refs),
        grid=(rows // block,),
        in_specs=[line, line, once(vec.shape, lambda i: (0, 0)), ANY, ANY, ANY],
        out_specs=[line, line, wide, wide, line, line],
        out_shape=[
            jax.ShapeDtypeStruct((rows, D), F32),
            jax.ShapeDtypeStruct((rows, D), BF),
            jax.ShapeDtypeStruct((rows, ff), BF),
            jax.ShapeDtypeStruct((rows, ff), BF),
            jax.ShapeDtypeStruct((rows, D), F32),
            jax.ShapeDtypeStruct((rows, D), BF),
        ],
        scratch_shapes=weight_scratch(ff),
        compiler_params=params(),
        cost_estimate=cost(22),
        name="ffn",
    )(x, ctx, vec, first, wi, wb)


def ffn_back_body(
    dy_ref, z2_ref, z1_ref, slope_ref, vec_ref, wb_h, wi_h, wo_h,
    e2_ref, e1_ref, dz1_ref, ea_ref, dctx_ref, sums_ref, wo_s, wi_s, wb_s, sems,
):
    step = pl.program_id(0)
    copies = [
        pltpu.make_async_copy(wb_h, wb_s, sems.at[0]),
        pltpu.make_async_copy(wi_h, wi_s, sems.at[1]),
        pltpu.make_async_copy(wo_h.at[3], wo_s, sems.at[2]),
    ]

    @pl.when(step == 0)
    def _():
        for copy in copies:
            copy.start()
        sums_ref[...] = jnp.zeros_like(sums_ref)

    dy = dy_ref[...].astype(F32)
    n, root = normed(z2_ref[...])
    sums_ref[G2 : G2 + 1, :] += colsum(dy * n)
    sums_ref[S2 : S2 + 1, :] += colsum(dy)
    dz2 = normed_back(n, root, dy * vec_ref[G2 : G2 + 1, :])
    e2 = dz2.astype(BF)
    e2_ref[...] = e2
    sums_ref[BB : BB + 1, :] += colsum(e2.astype(F32))

    @pl.when(step == 0)
    def _():
        for copy in copies:
            copy.wait()

    units = wi_s.shape[0]

    def up(j):
        return mm(e2, wb_s[j * D : (j + 1) * D, :], NT)

    acc = dz2
    f = up(0)
    for j in range(units):
        ahead = up(j + 1) if j + 1 < units else None
        cols = slice(j * D, (j + 1) * D)
        e1 = (f * slope_ref[:, cols].astype(F32)).astype(BF)
        e1_ref[:, cols] = e1
        sums_ref[8 + j : 9 + j, :] += colsum(e1.astype(F32))
        acc += mm(e1, wi_s[j], NT)
        f = ahead
    n, root = normed(z1_ref[...])
    sums_ref[G1 : G1 + 1, :] += colsum(acc * n)
    sums_ref[S1 : S1 + 1, :] += colsum(acc)
    dz1 = normed_back(n, root, acc * vec_ref[G1 : G1 + 1, :])
    dz1_ref[...] = dz1
    ea = dz1.astype(BF)
    ea_ref[...] = ea
    sums_ref[BO : BO + 1, :] += colsum(ea.astype(F32))
    dctx_ref[...] = mm(ea, wo_s[...], NT).astype(BF)


def ffn_back_call(dy, z2, z1, slope, wb, wi, first, vec, block=256):
    rows = dy.shape[0]
    ff = wb.shape[0]
    line, wide = by_rows(block, D), by_rows(block, ff)
    held = once(vec.shape, lambda i: (0, 0))
    return pl.pallas_call(
        ffn_back_body,
        grid=(rows // block,),
        in_specs=[line, line, line, wide, held, ANY, ANY, ANY],
        out_specs=[line, wide, line, line, line, held],
        out_shape=[
            jax.ShapeDtypeStruct((rows, D), BF),
            jax.ShapeDtypeStruct((rows, ff), BF),
            jax.ShapeDtypeStruct((rows, D), F32),
            jax.ShapeDtypeStruct((rows, D), BF),
            jax.ShapeDtypeStruct((rows, D), BF),
            jax.ShapeDtypeStruct(vec.shape, F32),
        ],
        scratch_shapes=weight_scratch(ff),
        compiler_params=params(),
        cost_estimate=cost(24),
        name="ffn_back",
    )(dy, z2, z1, slope, vec, wb, wi, first)


def attend_back_body(seq, pairs, len_ref, q_ref, k_ref, v_ref, d_ref, l_ref, e_ref, bq_ref, bv_ref):
    count = len_ref[pl.program_id(0)]
    lane = lax.broadcasted_iota(jnp.int32, (seq, PAIR), 1)
    ok = lax.broadcasted_iota(jnp.int32, (seq, seq), 0) < count
    units = [(pr, h) for pr in range(pairs) for h in range(2)]

    def score(unit):
        pr, h = unit
        cols = slice(pr * PAIR, (pr + 1) * PAIR)
        mine = (lane >= HEAD_DIM) == (h == 1)
        q = jnp.where(mine, q_ref[:, cols] * BF(0.125), BF(0))
        s = jnp.where(ok, mm(k_ref[:, cols], q, NT), -1e30)
        return s, mm(v_ref[:, cols], jnp.where(mine, d_ref[:, cols], BF(0)), NT)

    ahead = score(units[0])
    eq, ek, ev = {}, {}, {}
    for i, (pr, h) in enumerate(units):
        s, dp = ahead
        if i + 1 < len(units):
            ahead = score(units[i + 1])
        cols = slice(pr * PAIR, (pr + 1) * PAIR)
        if h == 0:
            kt = (k_ref[:, cols] * BF(0.125)).T
        p = jnp.exp(s - l_ref[0, pr, h : h + 1, :])
        pd = p * dp
        ds = (pd - p * colsum(pd)).astype(BF)
        ev[h] = mm(p.astype(BF), d_ref[:, cols], NN)
        ek[h] = mm(ds, q_ref[:, cols] * BF(0.125), NN)
        eq[h] = mm(kt[h * HEAD_DIM : (h + 1) * HEAD_DIM], ds, NN)
        if h == 1:
            low = jnp.concatenate([eq[0], eq[1]], axis=0).T.astype(BF)
            e_ref[0, :, cols] = low
            bq_ref[0, :, cols] = colsum(low.astype(F32))
            e_ref[1, :, cols] = jnp.where(lane < HEAD_DIM, ek[0], ek[1]).astype(BF)
            low = jnp.where(lane < HEAD_DIM, ev[0], ev[1]).astype(BF)
            e_ref[2, :, cols] = low
            bv_ref[0, :, cols] = colsum(low.astype(F32))


WIDE = 3 * PAIR
PARTS = D // WIDE


def attend_back_call(qkv, dctx, lse, lengths, start, number):
    rows = qkv.shape[0]
    count = lengths.shape[0]
    seq = rows // count
    pairs = WIDE // PAIR

    def part(o):
        return pl.BlockSpec((seq, WIDE), lambda s, p, n: (s, o * PARTS + start + p))

    def body(*refs):
        attend_back_body(seq, pairs, *refs)

    line = pl.BlockSpec((1, 1, WIDE), lambda s, p, n: (s, 0, p))
    return pl.pallas_call(
        body,
        grid_spec=pltpu.PrefetchScalarGridSpec(
            num_scalar_prefetch=1,
            grid=(count, number),
            in_specs=[
                part(0),
                part(1),
                part(2),
                part(0),
                pl.BlockSpec((1, pairs, 2, seq), lambda s, p, n: (s, start + p, 0, 0)),
            ],
            out_specs=[pl.BlockSpec((3, seq, WIDE), lambda s, p, n: (0, s, p)), line, line],
        ),
        out_shape=[jax.ShapeDtypeStruct((3, rows, number * WIDE), BF)]
        + [jax.ShapeDtypeStruct((count, 1, number * WIDE), F32)] * 2,
        compiler_params=params(),
        cost_estimate=cost(12 * number),
        name="attend_back",
    )(lengths, qkv, qkv, qkv, dctx, lse)


def dx_body(dz1_ref, *rest):
    e_refs, w_ref, o_ref = rest[:-2], rest[-2], rest[-1]
    acc = dz1_ref[...]
    for i in range(3):
        at = 0
        for e_ref in e_refs:
            width = e_ref.shape[2]
            acc += mm(e_ref[i], w_ref[i, :, at : at + width], NT)
            at += width
    o_ref[...] = acc.astype(o_ref.dtype)


def dx_call(dz1, parts, w, dtype, block=256):
    rows = dz1.shape[0]
    line = pl.BlockSpec((block, D), lambda i: (i, 0))
    specs = [pl.BlockSpec((3, block, e.shape[2]), lambda i: (0, i, 0)) for e in parts]
    return pl.pallas_call(
        dx_body,
        grid=(rows // block,),
        in_specs=[line, *specs, once((3, D, D), lambda i: (0, 0, 0))],
        out_specs=line,
        out_shape=jax.ShapeDtypeStruct((rows, D), dtype),
        compiler_params=params(),
        cost_estimate=cost(9),
        name="dx",
    )(dz1, *parts, w)


def deal(acc_s, rows, x_first, core_ref, keep_ref, send_ref):
    part = 8 * rows
    for out, core in ((keep_ref, core_ref[0]), (send_ref, 1 - core_ref[0])):
        for xi in range(2):
            for s in range(8):
                zi, yi = s // 2, s % 2
                start = pl.multiple_of(core * part + (2 * xi * part + s * rows), 8)
                value = acc_s[pl.ds(start, rows), :].astype(BF)
                if x_first:
                    out[xi, yi, zi, 0] = value
                else:
                    out[yi, xi, zi, 0] = value


def packet(rows, units, width):
    spec = pl.BlockSpec((2, 2, 4, 1, rows, width), lambda i, n: (0, 0, 0, i, 0, 0))
    return [spec] * 2, [jax.ShapeDtypeStruct((2, 2, 4, units, rows, width), BF)] * 2


def wgrad_in_call(core, a, c, b, d, rows):
    k, n = b.shape
    held = once((k, D), lambda i, n: (0, 0))
    spec = pl.BlockSpec((k, D), lambda i, n: (0, i))
    out_specs, out_shape = packet(rows, n // D, D)

    def body(core_ref, a_ref, c_ref, b_ref, d_ref, keep_ref, send_ref, acc_s):
        acc_s[...] = mm(a_ref[...], b_ref[...], TN) + mm(c_ref[...], d_ref[...], TN)
        deal(acc_s, rows, True, core_ref, keep_ref, send_ref)

    return pl.pallas_call(
        body,
        grid_spec=pltpu.PrefetchScalarGridSpec(
            num_scalar_prefetch=1,
            grid=(n // D,),
            in_specs=[held, held, spec, spec],
            out_specs=out_specs,
            scratch_shapes=[pltpu.VMEM((D, D), F32)],
        ),
        out_shape=out_shape,
        compiler_params=params(),
        cost_estimate=cost(15),
        name="wgrad_in",
    )(core, a, c, b, d)


def wgrad_heads_call(core, low2, low1, e2, e1, rows, group, others, x_first):
    k = low2.shape[0]
    last = len(others) == 4
    held = once((k, D), lambda i, n: (0, 0))
    spec_2 = pl.BlockSpec((1, k, WIDE), lambda i, n: (jnp.minimum(i, 2), 0, group))
    spec_1 = pl.BlockSpec((1, k, WIDE), lambda i, n: (jnp.minimum(i, 2), 0, 0))
    units = 5 if last else 4
    out_specs, out_shape = packet(rows, units, WIDE)
    if last:
        half = pl.BlockSpec((k, WIDE), lambda i, n: (0, jnp.maximum(i - 3, 0)))
        more = [held, held, half, half]
    else:
        more = [whole_block(v) for v in others]

    def body(core_ref, a_ref, c_ref, b_ref, d_ref, *rest):
        rest, (keep_ref, send_ref, acc_s) = rest[:-3], rest[-3:]
        step = pl.program_id(0)

        @pl.when(step < 3)
        def _():
            acc_s[...] = mm(a_ref[...], b_ref[0], TN) + mm(c_ref[...], d_ref[0], TN)

        if last:

            @pl.when(step >= 3)
            def _():
                acc_s[...] = mm(rest[0][...], rest[2][...], TN) + mm(rest[1][...], rest[3][...], TN)

            deal(acc_s, rows, x_first, core_ref, keep_ref, send_ref)
        else:

            @pl.when(step < 3)
            def _():
                deal(acc_s, rows, x_first, core_ref, keep_ref, send_ref)

            @pl.when(step == 3)
            def _():
                sums = rest[0][...] + rest[1][...]
                small = []
                for g in range(PARTS):
                    cols = slice(g * WIDE, (g + 1) * WIDE)
                    for j in range(2):
                        small.append(colsum(rest[2 + j][:, 0, cols] + rest[4 + 2 * g + j][:, 0, :]))
                    small.append(sums[2 : rows // 2, g * WIDE : (g + 1) * WIDE])
                small = jnp.concatenate(small, axis=0).astype(BF)
                for i in range(16):
                    keep_ref[i // 8, i // 4 % 2, i % 4, 0] = small
                    send_ref[i // 8, i // 4 % 2, i % 4, 0] = small

    return pl.pallas_call(
        body,
        grid_spec=pltpu.PrefetchScalarGridSpec(
            num_scalar_prefetch=1,
            grid=(units,),
            in_specs=[held, held, spec_2, spec_1] + more,
            out_specs=out_specs,
            scratch_shapes=[pltpu.VMEM((D, WIDE), F32)],
        ),
        out_shape=out_shape,
        compiler_params=params(),
        cost_estimate=cost(12),
        name="wgrad_heads",
    )(core, low2, low1, e2, e1, *others)


def wgrad_back_call(core, two, one, e_two, e_one, rows):
    k, ff = two.shape
    block = ff // 8

    def cols(other):
        def index(x, s, n):
            c = 1 - n[0] if other else n[0]
            return (0, (x * 2 + c) * 2 + s)

        return pl.BlockSpec((k, block), index)

    held = once((k, D), lambda x, s, n: (0, 0))
    out = pl.BlockSpec((2, 1, 2, 4, rows, D), lambda x, s, n: (0, x, s, 0, 0, 0))

    def body(core_ref, g2k, g1k, g2s, g1s, e2_ref, e1_ref, keep_ref, send_ref):
        for a, c, o in ((g2k, g1k, keep_ref), (g2s, g1s, send_ref)):
            acc = mm(a[...], e2_ref[...], TN) + mm(c[...], e1_ref[...], TN)
            for s in range(16):
                o[s // 4 % 2, 0, s // 8, s % 4] = acc[s * rows : (s + 1) * rows].astype(BF)

    return pl.pallas_call(
        body,
        grid_spec=pltpu.PrefetchScalarGridSpec(
            num_scalar_prefetch=1,
            grid=(2, 2),
            in_specs=[cols(False), cols(False), cols(True), cols(True), held, held],
            out_specs=[out, out],
        ),
        out_shape=[jax.ShapeDtypeStruct((2, 2, 4, 4, rows, D), BF)] * 2,
        compiler_params=params(),
        cost_estimate=cost(15),
        name="wgrad_back",
    )(core, two, one, two, one, e_two, e_one)


def layer_forward(x, low, weights, lengths, renorm):
    first, w_in, w_back, vec = weights
    qkv = qkv_call(low, first, vec)
    ctx, lse = attend_call(qkv, lengths)
    z1, h1, g, slope, z2, y = ffn_call(x, ctx, first, vec, w_in, w_back, renorm)
    return z2, y, (low, qkv, lse, ctx, z1, h1, g, slope, z2)


class Grid:
    def __init__(self, sizes):
        self.dp, self.fsdp = sizes["dp"], sizes["fsdp"]
        self.count = self.dp * self.fsdp
        self.x, self.core = self.dp // 2, 2
        self.y = self.fsdp // 4
        self.z = self.fsdp // self.y if self.y else 0
        self.staged = self.x == 2 and self.y == 2

    def place(self):
        dp, fsdp = lax.axis_index("dp"), lax.axis_index("fsdp")
        return dp // 2, dp % 2, fsdp // self.y, fsdp % self.y

    def shift(self, dim, step):
        sizes = (self.x, self.core, self.z, self.y)
        pairs = []
        for i in range(self.count):
            at = [i // (self.core * self.fsdp), i // self.fsdp % self.core, i % self.fsdp // self.y, i % self.y]
            at[dim] = (at[dim] + step) % sizes[dim]
            pairs.append((i, ((at[0] * self.core + at[1]) * self.z + at[2]) * self.y + at[3]))
        return pairs

    def send(self, value, dim, step=1):
        return lax.ppermute(value, AXES, self.shift(dim, step))

    def trade(self, value):
        groups = [[z * self.y + y for z in range(self.z)] for y in range(self.y)]
        return lax.all_to_all(value, "fsdp", 0, 0, tiled=True, axis_index_groups=groups)


X, CORE, Z, Y = range(4)


def pack_one_body(at_ref, wq_ref, wo_ref, *rest):
    vectors, span_ref, one_ref, line_s = rest[:8], rest[8], rest[9], rest[10]
    rows = wq_ref.shape[0]
    for i in range(3):
        one_ref[i] = wq_ref[:, i * D : (i + 1) * D]
    one_ref[3] = wo_ref[...]
    line_s[...] = jnp.zeros_like(line_s)
    for i, ref in enumerate(vectors):
        line_s[i : i + 1, :rows] = ref[...].astype(F32)
    span = span_ref.shape[1]
    line_s[8:9, :span] = span_ref[...].astype(F32)
    device = at_ref[0]
    per = D // span
    top = pltpu.roll(line_s[:8], device * rows, 1)
    low = pltpu.roll(line_s[8:16], lax.rem(device, per) * span, 1)
    here = lax.broadcasted_iota(jnp.int32, (8, D), 0) == lax.div(device, per)
    low = jnp.where(here, jnp.broadcast_to(low[:1], (8, D)), 0.0)
    one_ref[4] = jnp.concatenate([top, low, jnp.zeros((rows - 16, D), F32)], axis=0).astype(BF)


def pack_one(device, w_qkv, w_out, vectors, span):
    rows = w_qkv.shape[0]
    operands = [w_qkv, w_out, *[v[None] for v in vectors], span[None]]
    return pl.pallas_call(
        pack_one_body,
        grid_spec=pltpu.PrefetchScalarGridSpec(
            num_scalar_prefetch=1,
            grid=(1,),
            in_specs=[whole_block(v) for v in operands],
            out_specs=pl.BlockSpec((5, rows, D), lambda *_: (0, 0, 0)),
            scratch_shapes=[pltpu.VMEM((16, D), F32)],
        ),
        out_shape=jax.ShapeDtypeStruct((5, rows, D), BF),
        compiler_params=params(),
        name="pack_one",
    )(device, *operands)


def pack_two_body(wi_ref, wb_ref, two_ref):
    rows = wi_ref.shape[0]
    for i in range(4):
        two_ref[i] = wi_ref[:, i * D : (i + 1) * D]
        two_ref[4 + i] = wb_ref[i * rows : (i + 1) * rows]


def pack_two(w_in, w_back):
    rows = w_in.shape[0]
    return pl.pallas_call(
        pack_two_body,
        grid=(1,),
        in_specs=[whole_block(w_in), whole_block(w_back)],
        out_specs=pl.BlockSpec((8, rows, D), lambda *_: (0, 0, 0)),
        out_shape=jax.ShapeDtypeStruct((8, rows, D), BF),
        compiler_params=params(),
        name="pack_two",
    )(w_in, w_back)


def place_body(split, at_ref, *refs):
    outs = 2 if split else 1
    parts, outs, held, sems, out_sems = refs[:8], refs[8 : 8 + outs], refs[8 + outs : -2], refs[-2], refs[-1]
    x, core, z, y = at_ref[0], at_ref[1], at_ref[2], at_ref[3]
    sides = ([], [])
    for i, part in enumerate(parts):
        side, far, other = i >> 2, (i >> 1) & 1, i & 1
        count = part.shape[2]
        for near in range(2):
            px = (x + (far if side == 0 else near)) % 2
            py = (y + (near if side == 0 else far)) % 2
            pc = (core + other) % 2
            for dz in range(4):
                pz = dz if split else (z + 4 - dz) % 4
                if split:
                    target = held[side].at[:, px, pc, pz, py] if side == 0 else held[side].at[px, pc, pz, py]
                else:
                    target = held[0].at[pl.ds(0 if side == 0 else 5 - count, count), px, pc, pz, py]
                sem = sems.at[i * 8 + near * 4 + dz]
                sides[side].append(pltpu.make_async_copy(part.at[near, dz], target, sem))
    for side in sides:
        for copy in side:
            copy.start()
    back = []
    for side in range(2):
        for copy in sides[side]:
            copy.wait()
        if split:
            pair = held[side], outs[side]
        else:
            count = parts[4 * side].shape[2]
            span = pl.ds(0 if side == 0 else 5 - count, count)
            pair = held[0].at[span], outs[0].at[span]
        back.append(pltpu.make_async_copy(*pair, out_sems.at[side]))
        back[-1].start()
    for copy in back:
        copy.wait()


def place(at, parts, split):
    rows = parts[0].shape[3]
    if split:
        shapes = [(4, 2, 2, 4, 2, rows, D), (2, 2, 4, 2, 4, rows, D)]
    else:
        shapes = [(5, 2, 2, 4, 2, rows, D)]
    return pl.pallas_call(
        lambda *refs: place_body(split, *refs),
        grid_spec=pltpu.PrefetchScalarGridSpec(
            num_scalar_prefetch=1,
            grid=(1,),
            in_specs=[ANY] * 8,
            out_specs=[ANY] * len(shapes),
            scratch_shapes=[pltpu.VMEM(shape, BF) for shape in shapes]
            + [pltpu.SemaphoreType.DMA((64,)), pltpu.SemaphoreType.DMA((2,))],
        ),
        out_shape=[jax.ShapeDtypeStruct(shape, BF) for shape in shapes],
        compiler_params=params(),
        cost_estimate=cost(6),
        name="place",
    )(at, *parts)


def after(value, *others):
    return lax.optimization_barrier((value, *others))[0]


class Gather:
    def __init__(self, grid, packet, first, at_once):
        self.grid, self.first = grid, first
        if at_once:
            self.ring = grid.trade(jnp.broadcast_to(packet, (4,) + packet.shape))
        else:
            self.ring = jnp.stack([packet] + [grid.send(packet, Z, k) for k in range(1, 4)])

    def one(self, *others):
        ring = after(self.ring, *others)
        self.line = [ring[:, : self.first], ring[:, self.first :]]
        self.came = [self.grid.send(v, d) for v, d in zip(self.line, (Y, X))]

    def two(self, *others):
        held = lax.optimization_barrier((*self.line, *others))
        self.near = [jnp.stack(pair) for pair in zip(held, self.came)]
        self.far = [self.grid.send(v, d) for v, d in zip(self.near, (X, Y))]
        self.near_core = [self.grid.send(v, CORE) for v in self.near]

    def parts(self, *others):
        far = lax.optimization_barrier((*self.far, *others))[:2]
        out = []
        for i in range(2):
            out += [self.near[i], self.near_core[i], far[i], self.grid.send(far[i], CORE)]
        return out


def pick(value, index, dim):
    return lax.dynamic_index_in_dim(value, index, dim, keepdims=False)


def added(a, b, *picks):
    for index, dim in picks:
        a, b = pick(a, index, dim), pick(b, index, dim)
    return (a.astype(F32) + b.astype(F32)).astype(BF)


class Sum:
    def __init__(self, grid, place, order, pair, later=()):
        self.grid, self.place, self.order = grid, place, order
        self.mine, self.came = pair[0], grid.send(after(pair[1], *later), CORE)

    def cut(self, dim, others):
        here = self.place[dim]
        mine = after(self.mine, *others)
        out = added(mine, self.came, (1 - here, 0))
        self.mine = added(mine, self.came, (here, 0))
        self.came = self.grid.send(out, dim)
        return [out, self.mine]

    def one(self, *others):
        return self.cut(self.order[0], others)

    def two(self, *others):
        return self.cut(self.order[1], others)

    def three(self, *others):
        return added(after(self.mine, *others), self.came)


def along_z(grid, lines):
    line = jnp.concatenate(lines, axis=1)
    return line, jnp.sum(grid.trade(line).astype(F32), axis=0)


def staged(grid, lengths, tokens, cotangent, shards):
    w_qkv, bias_q, bias_v, w_out, bias_out, gain_one, shift_one, w_in, bias_in, w_back, bias_back, gain_two, shift_two = shards
    rows, span = bias_q.shape[0], bias_in.shape[0]
    where = grid.place()
    x, core, z, y = where
    device = lax.axis_index(AXES)
    at = jnp.stack([x, core, z, y]).astype(jnp.int32)
    core = core.astype(jnp.int32)[None]
    vectors = [bias_q, bias_v, bias_out, gain_one, shift_one, bias_back, gain_two, shift_two]
    one = Gather(grid, pack_one(device.astype(jnp.int32)[None], w_qkv, w_out, vectors, bias_in), 2, False)
    packet = after(pack_two(w_in, w_back), one.ring)
    two = Gather(grid, packet, 4, True)
    one.one()
    one.two()
    two.one(*one.far)
    (first,) = place(at, one.parts(), False)
    first = first.reshape(5, grid.count * rows, D)
    vec = jnp.sum(first[4].reshape(grid.count, rows, D).astype(F32), axis=0)
    qkv = qkv_call(tokens, first, vec)
    two.two(first)
    ctx, lse = attend_call(after(qkv, *two.near), lengths)
    w_in, w_back = place(at, two.parts(ctx), True)
    w_in = w_in.reshape(4, grid.count * rows, D)
    w_back = w_back.reshape(grid.count * span, D)
    z1, h1, g, slope, z2, low = ffn_call(tokens, ctx, first, vec, w_in, w_back, False)
    saved = [(tokens, qkv, lse, ctx, z1, h1, g, slope, z2)]
    weights = (first, w_in, w_back, vec)
    _, low, stored = layer_forward(z2, low, weights, lengths, True)
    saved.append(stored)
    activations = low

    low2, qkv, lse, ctx2, z1, h2, g2, slope, z2 = saved[1]
    e2_2, e1_2, dz1, ea_2, dctx, sums_2 = ffn_back_call(cotangent, z2, z1, slope, w_back, w_in, first, vec)
    e_qkv_2, *lines_2 = attend_back_call(qkv, dctx, lse, lengths, 0, PARTS)
    grad = dx_call(dz1, [e_qkv_2], first, F32)

    low1, qkv, lse, ctx1, z1, h1, g1, slope, z2 = saved[0]
    e2_1, e1_1, dz1, ea_1, dctx, sums_1 = ffn_back_call(grad, z2, z1, slope, w_back, w_in, first, vec)
    count = tokens.shape[0]

    back = wgrad_back_call(core, g2, g1, e2_2, e2_1, rows)
    sum_back = Sum(grid, where, (Y, X), back)
    into = wgrad_in_call(core, after(h2, back[0]), h1, e1_2, e1_1, rows)
    sum_in = Sum(grid, where, (X, Y), into)
    steps = sum_back.one(into[0]) + sum_in.one(into[0])
    e_0, *lines_0 = attend_back_call(qkv, after(dctx, *steps), lse, lengths, 0, 1)
    e_1, *lines_1 = attend_back_call(qkv, after(dctx, e_0), lse, lengths, 1, 1)
    steps = sum_back.two(e_1) + sum_in.two(e_1)
    others = [ctx2, ctx1, ea_2, ea_1]
    group = wgrad_heads_call(core, after(low2, *steps), low1, e_qkv_2, e_0, rows, 0, others, False)
    line, total = along_z(grid, [sum_in.three(group[0]), sum_back.three(group[0])])
    sum_0 = Sum(grid, where, (Y, X), group, [line])
    steps = [line]
    sums = [sums_1, sums_2, *lines_2, *lines_0, *lines_1]
    group = wgrad_heads_call(core, after(low2, *steps), low1, e_qkv_2, e_1, rows, 1, sums, True)
    sum_1 = Sum(grid, where, (X, Y), group)
    steps = sum_0.one(group[0]) + sum_1.one()
    grad = dx_call(after(dz1, *steps), [e_0, e_1], first, BF)
    sum_0.two(grad)
    sum_1.two(grad)
    _, halves = along_z(grid, [sum_0.three(), sum_1.three()])
    total_in, total_back, half_0, half_1 = total[:4], total[4:], halves[:5], halves[5:]

    w_in_grad = total_in.swapaxes(0, 1).reshape(rows, 4 * D)
    w_back_grad = total_back.reshape(4 * rows, D)
    w_qkv_grad = jnp.stack([half_0[:3], half_1[:3]], axis=1).transpose(2, 0, 1, 3).reshape(rows, 3 * D)
    w_out_grad = half_0[3:].swapaxes(0, 1).reshape(rows, D)
    small = jnp.concatenate([half_1[3][: rows // 2], half_1[3][rows // 2 :]], axis=1)
    mine = lax.dynamic_slice(small, (0, device * rows), (8, rows))
    per = D // span
    last = lax.dynamic_slice(small, (8 + device // per, device % per * span), (1, span))[0]
    return activations, grad, w_qkv_grad, w_out_grad, w_in_grad, w_back_grad, [mine[i] for i in range(8)] + [last]


def plain(grid, lengths, tokens, cotangent, shards):
    w_qkv, bias_q, bias_v, w_out, bias_out, gain_one, shift_one, w_in, bias_in, w_back, bias_back, gain_two, shift_two = shards
    vectors = [bias_q, bias_v, bias_out, gain_one, shift_one, bias_back, gain_two, shift_two]

    def whole(v):
        return lax.all_gather(v, AXES, axis=0, tiled=True)

    lines = jnp.stack([whole(v) for v in vectors])
    vec = jnp.concatenate([lines, whole(bias_in).reshape(4, D), jnp.zeros((4, D), BF)], axis=0).astype(F32)

    def blocks(w):
        return w.reshape(D, -1, D).swapaxes(0, 1)

    first = jnp.concatenate([blocks(whole(w_qkv)), whole(w_out)[None], jnp.zeros((1, D, D), BF)], axis=0)
    w_in, w_back = blocks(whole(w_in)), whole(w_back)
    weights = (first, w_in, w_back, vec)
    value, low = tokens, tokens
    saved = []
    for step in range(APPS):
        value, low, stored = layer_forward(value, low, weights, lengths, step > 0)
        saved.append(stored)
    activations, grad, totals = low, cotangent, None
    for step in reversed(range(APPS)):
        low, qkv, lse, ctx, z1, h1, g, slope, z2 = saved[step]
        e2, e1, dz1, ea, dctx, sums = ffn_back_call(grad, z2, z1, slope, w_back, w_in, first, vec)
        e, *lines = attend_back_call(qkv, dctx, lse, lengths, 0, PARTS)
        grad = dx_call(dz1, [e], first, F32 if step else BF)
        e = e.swapaxes(0, 1).reshape(-1, 3 * D)
        lines = [jnp.sum(v, axis=0) for v in lines]
        grads = [mm(low, e, TN), mm(ctx, ea, TN), mm(h1, e1, TN), mm(g, e2, TN)]
        grads += [jnp.concatenate(lines + [sums[2:]], axis=0)]
        totals = grads if totals is None else [a + b for a, b in zip(totals, grads)]
    lines = list(totals.pop())
    totals += lines[:8] + [jnp.concatenate(lines[8:12])]
    owned = [lax.psum_scatter(v, AXES, scatter_dimension=0, tiled=True) for v in totals]
    return activations, grad, *owned[:4], owned[4:]


def make_local(grid):
    def local(tokens, lengths, *rest):
        run = staged if grid.staged else plain
        activations, grad, w_qkv, w_out, w_in, w_back, lines = run(grid, lengths, tokens, rest[-1], rest[:-1])
        return (
            activations, grad, w_qkv, lines[BQ], lines[BV], w_out, lines[BO], lines[G1], lines[S1],
            w_in, lines[8], w_back, lines[BB], lines[G2], lines[S2],
        )

    return local


def solution(mesh):
    wide, line = P(AXES, None), P(AXES)
    return jax.shard_map(
        make_local(Grid(mesh.shape)),
        mesh=mesh,
        in_specs=(wide, line, wide, line, line, wide, line, line, line, wide, line, wide, line, line, line, wide),
        out_specs=(wide, wide, wide, line, line, wide, line, line, line, wide, line, wide, line, line, line),
        check_vma=False,
    )
```

```python
import jax
import jax.numpy as jnp
from jax import lax
from jax.experimental import pallas as pl
from jax.experimental.pallas import tpu as pltpu
from jax.sharding import PartitionSpec as P

D = 768
HEADS = 12
HEAD_DIM = 64
APPS = 2
PAIR = 2 * HEAD_DIM
AXES = ("dp", "fsdp")
BF = jnp.bfloat16
F32 = jnp.float32
NN = (((1,), (0,)), ((), ()))
NT = (((1,), (1,)), ((), ()))
TN = (((0,), (0,)), ((), ()))
VMEM = 56 * 2**20
BQ, BV, BO, G1, S1, BB, G2, S2 = range(8)


def mm(left, right, dims):
    return lax.dot_general(left, right, dims, preferred_element_type=F32)


def params(limit=VMEM):
    return pltpu.CompilerParams(vmem_limit_bytes=limit)


def cost(micros):
    return pl.CostEstimate(flops=int(micros * 2e8), bytes_accessed=int(micros * 1e5), transcendentals=0)


def once(shape, index):
    return pl.BlockSpec(shape, index, pipeline_mode=pl.Buffered(1))


def whole_block(v):
    return pl.BlockSpec(v.shape, lambda *_: (0,) * v.ndim)


def normed(z):
    centered = z - jnp.mean(z, axis=-1, keepdims=True)
    root = lax.rsqrt(jnp.mean(centered * centered, axis=-1, keepdims=True) + 1e-12)
    return centered * root, root


def normed_back(n, root, e):
    return root * (e - jnp.mean(e, axis=-1, keepdims=True) - n * jnp.mean(e * n, axis=-1, keepdims=True))


def colsum(v):
    return jnp.sum(v, axis=0, keepdims=True)


def qkv_body(x_ref, a_ref, b_ref, vec_ref, o_ref):
    part = pl.program_id(0)

    @pl.when(part == 0)
    def _():
        o_ref[...] = (mm(x_ref[...], a_ref[0], NN) + vec_ref[BQ : BQ + 1, :]).astype(BF)

    @pl.when(part == 1)
    def _():
        o_ref[...] = mm(x_ref[...], a_ref[0], NN).astype(BF)

    @pl.when(part == 2)
    def _():
        o_ref[...] = (mm(x_ref[...], b_ref[0], NN) + vec_ref[BV : BV + 1, :]).astype(BF)


def qkv_call(x, first, vec):
    rows = x.shape[0]
    return pl.pallas_call(
        qkv_body,
        grid=(3,),
        in_specs=[
            once((rows, D), lambda i: (0, 0)),
            pl.BlockSpec((1, D, D), lambda i: (jnp.minimum(i, 1), 0, 0)),
            once((1, D, D), lambda i: (0, 0, 0)),
            once(vec.shape, lambda i: (0, 0)),
        ],
        out_specs=pl.BlockSpec((rows, D), lambda i: (0, i)),
        out_shape=jax.ShapeDtypeStruct((rows, 3 * D), BF),
        compiler_params=params(),
        cost_estimate=cost(8),
        name="qkv",
    )(x, *first, vec)


def attend_body(seq, pairs, len_ref, q_ref, k_ref, v_ref, o_ref, l_ref):
    count = len_ref[pl.program_id(0)]
    lane = lax.broadcasted_iota(jnp.int32, (seq, PAIR), 1)
    row = lax.broadcasted_iota(jnp.int32, (seq, PAIR), 0)
    mask = jnp.where(row < count, 0.0, -1e30).astype(BF)
    units = [(pr, h) for pr in range(pairs) for h in range(2)]

    def score(unit):
        pr, h = unit
        cols = slice(pr * PAIR, (pr + 1) * PAIR)
        mine = (lane >= HEAD_DIM) == (h == 1)
        spare = lane == HEAD_DIM * (1 - h)
        q = jnp.where(mine, q_ref[:, cols] * BF(0.125), jnp.where(spare, BF(1), BF(0)))
        k = jnp.where(mine, k_ref[:, cols], jnp.where(spare, mask, BF(0)))
        return mm(q, k, NT)

    ahead = score(units[0])
    held = {}
    for i, (pr, h) in enumerate(units):
        s = ahead
        if i + 1 < len(units):
            ahead = score(units[i + 1])
        cols = slice(pr * PAIR, (pr + 1) * PAIR)
        top = jnp.max(s, axis=1, keepdims=True)
        p = jnp.exp(s - top)
        total = jnp.sum(p, axis=1, keepdims=True)
        held[h] = mm(p.astype(BF), v_ref[:, cols], NN) / total
        l_ref[0, pr, h : h + 1, :] = (top + jnp.log(total)).reshape(1, seq)
        if h == 1:
            o_ref[:, cols] = jnp.where(lane < HEAD_DIM, held[0], held[1]).astype(BF)


def attend_call(qkv, lengths, pairs=3):
    rows = qkv.shape[0]
    count = lengths.shape[0]
    seq = rows // count
    groups = D // PAIR // pairs
    wide = PAIR * pairs

    def part(o):
        return pl.BlockSpec((seq, wide), lambda s, p, n: (s, o * groups + p))

    def body(*refs):
        attend_body(seq, pairs, *refs)

    return pl.pallas_call(
        body,
        grid_spec=pltpu.PrefetchScalarGridSpec(
            num_scalar_prefetch=1,
            grid=(count, groups),
            in_specs=[part(0), part(1), part(2)],
            out_specs=[part(0), pl.BlockSpec((1, pairs, 2, seq), lambda s, p, n: (s, p, 0, 0))],
        ),
        out_shape=[
            jax.ShapeDtypeStruct((rows, D), BF),
            jax.ShapeDtypeStruct((count, D // PAIR, 2, seq), F32),
        ],
        compiler_params=params(),
        cost_estimate=cost(13),
        name="attend",
    )(lengths, qkv, qkv, qkv)


def gelu_both(u):
    a = 0.7978845608028654
    c = a + (a * 0.044715) * (u * u)
    s = 0.5 + 0.5 * jnp.tanh(u * c)
    g = u * s
    return g, s + (g * (1.0 - s)) * (6.0 * c - 4.0 * a)


ANY = pl.BlockSpec(memory_space=pl.ANY)


def by_rows(block, width):
    return pl.BlockSpec((block, width), lambda i: (i, 0))


def ffn_body(
    renorm, x_ref, ctx_ref, vec_ref, wo_h, wi_h, wb_h,
    z1_ref, h1_ref, g_ref, slope_ref, z2_ref, y_ref, wo_s, wi_s, wb_s, sems,
):
    step = pl.program_id(0)
    copies = [
        pltpu.make_async_copy(wo_h.at[1], wo_s, sems.at[0]),
        pltpu.make_async_copy(wi_h, wi_s, sems.at[1]),
        pltpu.make_async_copy(wb_h, wb_s, sems.at[2]),
    ]

    @pl.when(step == 0)
    def _():
        for copy in copies:
            copy.start()
        copies[0].wait()

    x = x_ref[...].astype(F32)
    if renorm:
        n, _ = normed(x)
        x = n * vec_ref[G2 : G2 + 1, :] + vec_ref[S2 : S2 + 1, :]
    z1 = x + mm(ctx_ref[...], wo_s[...], NN) + vec_ref[BO : BO + 1, :]
    z1_ref[...] = z1
    n, _ = normed(z1)
    h1 = n * vec_ref[G1 : G1 + 1, :] + vec_ref[S1 : S1 + 1, :]
    low = h1.astype(BF)
    h1_ref[...] = low

    @pl.when(step == 0)
    def _():
        copies[1].wait()
        copies[2].wait()

    units = wi_s.shape[0]

    def up(j):
        return mm(low, wi_s[j], NN) + vec_ref[8 + j : 9 + j, :]

    acc = h1 + vec_ref[BB : BB + 1, :]
    f = up(0)
    for j in range(units):
        ahead = up(j + 1) if j + 1 < units else None
        cols = slice(j * D, (j + 1) * D)
        g, slope = gelu_both(f)
        g = g.astype(BF)
        g_ref[:, cols] = g
        slope_ref[:, cols] = slope.astype(BF)
        acc += mm(g, wb_s[cols, :], NN)
        f = ahead
    z2_ref[...] = acc
    n, _ = normed(acc)
    y_ref[...] = (n * vec_ref[G2 : G2 + 1, :] + vec_ref[S2 : S2 + 1, :]).astype(BF)


def weight_scratch(ff):
    return [
        pltpu.VMEM((D, D), BF),
        pltpu.VMEM((ff // D, D, D), BF),
        pltpu.VMEM((ff, D), BF),
        pltpu.SemaphoreType.DMA((3,)),
    ]


def ffn_call(x, ctx, first, vec, wi, wb, renorm, block=512):
    rows = x.shape[0]
    ff = wb.shape[0]
    line, wide = by_rows(block, D), by_rows(block, ff)
    return pl.pallas_call(
        lambda *refs: ffn_body(renorm, *refs),
        grid=(rows // block,),
        in_specs=[line, line, once(vec.shape, lambda i: (0, 0)), ANY, ANY, ANY],
        out_specs=[line, line, wide, wide, line, line],
        out_shape=[
            jax.ShapeDtypeStruct((rows, D), F32),
            jax.ShapeDtypeStruct((rows, D), BF),
            jax.ShapeDtypeStruct((rows, ff), BF),
            jax.ShapeDtypeStruct((rows, ff), BF),
            jax.ShapeDtypeStruct((rows, D), F32),
            jax.ShapeDtypeStruct((rows, D), BF),
        ],
        scratch_shapes=weight_scratch(ff),
        compiler_params=params(),
        cost_estimate=cost(22),
        name="ffn",
    )(x, ctx, vec, first[1], wi, wb)


def ffn_back_body(
    dy_ref, z2_ref, z1_ref, slope_ref, vec_ref, wb_h, wi_h, wo_h,
    e2_ref, e1_ref, dz1_ref, ea_ref, dctx_ref, sums_ref, wo_s, wi_s, wb_s, sems,
):
    step = pl.program_id(0)
    copies = [
        pltpu.make_async_copy(wb_h, wb_s, sems.at[0]),
        pltpu.make_async_copy(wi_h, wi_s, sems.at[1]),
        pltpu.make_async_copy(wo_h.at[1], wo_s, sems.at[2]),
    ]

    @pl.when(step == 0)
    def _():
        for copy in copies:
            copy.start()
        sums_ref[...] = jnp.zeros_like(sums_ref)

    dy = dy_ref[...].astype(F32)
    n, root = normed(z2_ref[...])
    sums_ref[G2 : G2 + 1, :] += colsum(dy * n)
    sums_ref[S2 : S2 + 1, :] += colsum(dy)
    dz2 = normed_back(n, root, dy * vec_ref[G2 : G2 + 1, :])
    e2 = dz2.astype(BF)
    e2_ref[...] = e2
    sums_ref[BB : BB + 1, :] += colsum(e2.astype(F32))

    @pl.when(step == 0)
    def _():
        for copy in copies:
            copy.wait()

    units = wi_s.shape[0]

    def up(j):
        return mm(e2, wb_s[j * D : (j + 1) * D, :], NT)

    acc = dz2
    f = up(0)
    for j in range(units):
        ahead = up(j + 1) if j + 1 < units else None
        cols = slice(j * D, (j + 1) * D)
        e1 = (f * slope_ref[:, cols].astype(F32)).astype(BF)
        e1_ref[:, cols] = e1
        sums_ref[8 + j : 9 + j, :] += colsum(e1.astype(F32))
        acc += mm(e1, wi_s[j], NT)
        f = ahead
    n, root = normed(z1_ref[...])
    sums_ref[G1 : G1 + 1, :] += colsum(acc * n)
    sums_ref[S1 : S1 + 1, :] += colsum(acc)
    dz1 = normed_back(n, root, acc * vec_ref[G1 : G1 + 1, :])
    dz1_ref[...] = dz1
    ea = dz1.astype(BF)
    ea_ref[...] = ea
    sums_ref[BO : BO + 1, :] += colsum(ea.astype(F32))
    dctx_ref[...] = mm(ea, wo_s[...], NT).astype(BF)


def ffn_back_call(dy, z2, z1, slope, wb, wi, first, vec, block=256):
    rows = dy.shape[0]
    ff = wb.shape[0]
    line, wide = by_rows(block, D), by_rows(block, ff)
    held = once(vec.shape, lambda i: (0, 0))
    return pl.pallas_call(
        ffn_back_body,
        grid=(rows // block,),
        in_specs=[line, line, line, wide, held, ANY, ANY, ANY],
        out_specs=[line, wide, line, line, line, held],
        out_shape=[
            jax.ShapeDtypeStruct((rows, D), BF),
            jax.ShapeDtypeStruct((rows, ff), BF),
            jax.ShapeDtypeStruct((rows, D), F32),
            jax.ShapeDtypeStruct((rows, D), BF),
            jax.ShapeDtypeStruct((rows, D), BF),
            jax.ShapeDtypeStruct(vec.shape, F32),
        ],
        scratch_shapes=weight_scratch(ff),
        compiler_params=params(),
        cost_estimate=cost(24),
        name="ffn_back",
    )(dy, z2, z1, slope, vec, wb, wi, first[1])


def attend_back_body(seq, pairs, len_ref, q_ref, k_ref, v_ref, d_ref, l_ref, e_ref, bq_ref, bv_ref):
    count = len_ref[pl.program_id(0)]
    lane = lax.broadcasted_iota(jnp.int32, (seq, PAIR), 1)
    ok = lax.broadcasted_iota(jnp.int32, (seq, seq), 0) < count
    units = [(pr, h) for pr in range(pairs) for h in range(2)]

    def score(unit):
        pr, h = unit
        cols = slice(pr * PAIR, (pr + 1) * PAIR)
        mine = (lane >= HEAD_DIM) == (h == 1)
        q = jnp.where(mine, q_ref[:, cols] * BF(0.125), BF(0))
        s = jnp.where(ok, mm(k_ref[:, cols], q, NT), -1e30)
        return s, mm(v_ref[:, cols], jnp.where(mine, d_ref[:, cols], BF(0)), NT)

    ahead = score(units[0])
    eq, ek, ev = {}, {}, {}
    for i, (pr, h) in enumerate(units):
        s, dp = ahead
        if i + 1 < len(units):
            ahead = score(units[i + 1])
        cols = slice(pr * PAIR, (pr + 1) * PAIR)
        if h == 0:
            kt = (k_ref[:, cols] * BF(0.125)).T
        p = jnp.exp(s - l_ref[0, pr, h : h + 1, :])
        pd = p * dp
        ds = (pd - p * colsum(pd)).astype(BF)
        ev[h] = mm(p.astype(BF), d_ref[:, cols], NN)
        ek[h] = mm(ds, q_ref[:, cols] * BF(0.125), NN)
        eq[h] = mm(kt[h * HEAD_DIM : (h + 1) * HEAD_DIM], ds, NN)
        if h == 1:
            low = jnp.concatenate([eq[0], eq[1]], axis=0).T.astype(BF)
            e_ref[0, :, cols] = low
            bq_ref[0, :, cols] = colsum(low.astype(F32))
            e_ref[1, :, cols] = jnp.where(lane < HEAD_DIM, ek[0], ek[1]).astype(BF)
            low = jnp.where(lane < HEAD_DIM, ev[0], ev[1]).astype(BF)
            e_ref[2, :, cols] = low
            bv_ref[0, :, cols] = colsum(low.astype(F32))


WIDE = 3 * PAIR
PARTS = D // WIDE


def attend_back_call(qkv, dctx, lse, lengths, start, number):
    rows = qkv.shape[0]
    count = lengths.shape[0]
    seq = rows // count
    pairs = WIDE // PAIR

    def part(o):
        return pl.BlockSpec((seq, WIDE), lambda s, p, n: (s, o * PARTS + start + p))

    def body(*refs):
        attend_back_body(seq, pairs, *refs)

    line = pl.BlockSpec((1, 1, WIDE), lambda s, p, n: (s, 0, p))
    return pl.pallas_call(
        body,
        grid_spec=pltpu.PrefetchScalarGridSpec(
            num_scalar_prefetch=1,
            grid=(count, number),
            in_specs=[
                part(0),
                part(1),
                part(2),
                part(0),
                pl.BlockSpec((1, pairs, 2, seq), lambda s, p, n: (s, start + p, 0, 0)),
            ],
            out_specs=[pl.BlockSpec((3, seq, WIDE), lambda s, p, n: (0, s, p)), line, line],
        ),
        out_shape=[jax.ShapeDtypeStruct((3, rows, number * WIDE), BF)]
        + [jax.ShapeDtypeStruct((count, 1, number * WIDE), F32)] * 2,
        compiler_params=params(),
        cost_estimate=cost(12 * number),
        name="attend_back",
    )(lengths, qkv, qkv, qkv, dctx, lse)


def dx_body(dz1_ref, *rest):
    e_refs, (a_ref, b_ref, o_ref) = rest[:-3], rest[-3:]
    acc = dz1_ref[...]
    for i in range(3):
        at = 0
        for e_ref in e_refs:
            width = e_ref.shape[2]
            w = a_ref[i, :, at : at + width] if i < 2 else b_ref[0, :, at : at + width]
            acc += mm(e_ref[i], w, NT)
            at += width
    o_ref[...] = acc.astype(o_ref.dtype)


def dx_call(dz1, parts, w, dtype, block=256):
    rows = dz1.shape[0]
    line = pl.BlockSpec((block, D), lambda i: (i, 0))
    specs = [pl.BlockSpec((3, block, e.shape[2]), lambda i: (0, i, 0)) for e in parts]
    return pl.pallas_call(
        dx_body,
        grid=(rows // block,),
        in_specs=[line, *specs, once((2, D, D), lambda i: (0, 0, 0)), once((1, D, D), lambda i: (0, 0, 0))],
        out_specs=line,
        out_shape=jax.ShapeDtypeStruct((rows, D), dtype),
        compiler_params=params(),
        cost_estimate=cost(9),
        name="dx",
    )(dz1, *parts, *w)


def deal(acc_s, rows, x_first, core_ref, keep_ref, send_ref):
    part = 8 * rows
    for out, core in ((keep_ref, core_ref[0]), (send_ref, 1 - core_ref[0])):
        for xi in range(2):
            for s in range(8):
                zi, yi = s // 2, s % 2
                start = pl.multiple_of(core * part + (2 * xi * part + s * rows), 8)
                value = acc_s[pl.ds(start, rows), :].astype(BF)
                if x_first:
                    out[xi, yi, zi, 0] = value
                else:
                    out[yi, xi, zi, 0] = value


def packet(rows, units, width):
    spec = pl.BlockSpec((2, 2, 4, 1, rows, width), lambda i, n: (0, 0, 0, i, 0, 0))
    return [spec] * 2, [jax.ShapeDtypeStruct((2, 2, 4, units, rows, width), BF)] * 2


def wgrad_in_call(core, a, c, b, d, rows):
    k, n = b.shape
    held = once((k, D), lambda i, n: (0, 0))
    spec = pl.BlockSpec((k, D), lambda i, n: (0, i))
    out_specs, out_shape = packet(rows, n // D, D)

    def body(core_ref, a_ref, c_ref, b_ref, d_ref, keep_ref, send_ref, acc_s):
        acc_s[...] = mm(a_ref[...], b_ref[...], TN) + mm(c_ref[...], d_ref[...], TN)
        deal(acc_s, rows, True, core_ref, keep_ref, send_ref)

    return pl.pallas_call(
        body,
        grid_spec=pltpu.PrefetchScalarGridSpec(
            num_scalar_prefetch=1,
            grid=(n // D,),
            in_specs=[held, held, spec, spec],
            out_specs=out_specs,
            scratch_shapes=[pltpu.VMEM((D, D), F32)],
        ),
        out_shape=out_shape,
        compiler_params=params(),
        cost_estimate=cost(15),
        name="wgrad_in",
    )(core, a, c, b, d)


def wgrad_heads_call(core, low2, low1, e2, e1, rows, group, others, x_first):
    k = low2.shape[0]
    last = len(others) == 4
    held = once((k, D), lambda i, n: (0, 0))
    spec_2 = pl.BlockSpec((1, k, WIDE), lambda i, n: (jnp.minimum(i, 2), 0, group))
    spec_1 = pl.BlockSpec((1, k, WIDE), lambda i, n: (jnp.minimum(i, 2), 0, 0))
    units = 5 if last else 4
    out_specs, out_shape = packet(rows, units, WIDE)
    if last:
        half = pl.BlockSpec((k, WIDE), lambda i, n: (0, jnp.maximum(i - 3, 0)))
        more = [held, held, half, half]
    else:
        more = [whole_block(v) for v in others]

    def body(core_ref, a_ref, c_ref, b_ref, d_ref, *rest):
        rest, (keep_ref, send_ref, acc_s) = rest[:-3], rest[-3:]
        step = pl.program_id(0)

        @pl.when(step < 3)
        def _():
            acc_s[...] = mm(a_ref[...], b_ref[0], TN) + mm(c_ref[...], d_ref[0], TN)

        if last:

            @pl.when(step >= 3)
            def _():
                acc_s[...] = mm(rest[0][...], rest[2][...], TN) + mm(rest[1][...], rest[3][...], TN)

            deal(acc_s, rows, x_first, core_ref, keep_ref, send_ref)
        else:

            @pl.when(step < 3)
            def _():
                deal(acc_s, rows, x_first, core_ref, keep_ref, send_ref)

            @pl.when(step == 3)
            def _():
                sums = rest[0][...] + rest[1][...]
                small = []
                for g in range(PARTS):
                    cols = slice(g * WIDE, (g + 1) * WIDE)
                    for j in range(2):
                        small.append(colsum(rest[2 + j][:, 0, cols] + rest[4 + 2 * g + j][:, 0, :]))
                    small.append(sums[2 : rows // 2, g * WIDE : (g + 1) * WIDE])
                small = jnp.concatenate(small, axis=0).astype(BF)
                for i in range(16):
                    keep_ref[i // 8, i // 4 % 2, i % 4, 0] = small
                    send_ref[i // 8, i // 4 % 2, i % 4, 0] = small

    return pl.pallas_call(
        body,
        grid_spec=pltpu.PrefetchScalarGridSpec(
            num_scalar_prefetch=1,
            grid=(units,),
            in_specs=[held, held, spec_2, spec_1] + more,
            out_specs=out_specs,
            scratch_shapes=[pltpu.VMEM((D, WIDE), F32)],
        ),
        out_shape=out_shape,
        compiler_params=params(),
        cost_estimate=cost(12),
        name="wgrad_heads",
    )(core, low2, low1, e2, e1, *others)


def wgrad_back_call(core, two, one, e_two, e_one, rows):
    k, ff = two.shape
    block = ff // 8

    def cols(other):
        def index(x, s, n):
            c = 1 - n[0] if other else n[0]
            return (0, (x * 2 + c) * 2 + s)

        return pl.BlockSpec((k, block), index)

    held = once((k, D), lambda x, s, n: (0, 0))
    out = pl.BlockSpec((2, 1, 2, 4, rows, D), lambda x, s, n: (0, x, s, 0, 0, 0))

    def body(core_ref, g2k, g1k, g2s, g1s, e2_ref, e1_ref, keep_ref, send_ref):
        for a, c, o in ((g2k, g1k, keep_ref), (g2s, g1s, send_ref)):
            acc = mm(a[...], e2_ref[...], TN) + mm(c[...], e1_ref[...], TN)
            for s in range(16):
                o[s // 4 % 2, 0, s // 8, s % 4] = acc[s * rows : (s + 1) * rows].astype(BF)

    return pl.pallas_call(
        body,
        grid_spec=pltpu.PrefetchScalarGridSpec(
            num_scalar_prefetch=1,
            grid=(2, 2),
            in_specs=[cols(False), cols(False), cols(True), cols(True), held, held],
            out_specs=[out, out],
        ),
        out_shape=[jax.ShapeDtypeStruct((2, 2, 4, 4, rows, D), BF)] * 2,
        compiler_params=params(),
        cost_estimate=cost(15),
        name="wgrad_back",
    )(core, two, one, two, one, e_two, e_one)


def layer_forward(x, low, weights, lengths, renorm):
    first, w_in, w_back, vec = weights
    qkv = qkv_call(low, first, vec)
    ctx, lse = attend_call(qkv, lengths)
    z1, h1, g, slope, z2, y = ffn_call(x, ctx, first, vec, w_in, w_back, renorm)
    return z2, y, (low, qkv, lse, ctx, z1, h1, g, slope, z2)


class Grid:
    def __init__(self, sizes):
        self.dp, self.fsdp = sizes["dp"], sizes["fsdp"]
        self.count = self.dp * self.fsdp
        self.x, self.core = self.dp // 2, 2
        self.y = self.fsdp // 4
        self.z = self.fsdp // self.y if self.y else 0
        self.staged = self.x == 2 and self.y == 2

    def place(self):
        dp, fsdp = lax.axis_index("dp"), lax.axis_index("fsdp")
        return dp // 2, dp % 2, fsdp // self.y, fsdp % self.y

    def shift(self, dim, step):
        sizes = (self.x, self.core, self.z, self.y)
        pairs = []
        for i in range(self.count):
            at = [i // (self.core * self.fsdp), i // self.fsdp % self.core, i % self.fsdp // self.y, i % self.y]
            at[dim] = (at[dim] + step) % sizes[dim]
            pairs.append((i, ((at[0] * self.core + at[1]) * self.z + at[2]) * self.y + at[3]))
        return pairs

    def send(self, value, dim, step=1):
        return lax.ppermute(value, AXES, self.shift(dim, step))

    def trade(self, value):
        groups = [[z * self.y + y for z in range(self.z)] for y in range(self.y)]
        return lax.all_to_all(value, "fsdp", 0, 0, tiled=True, axis_index_groups=groups)


X, CORE, Z, Y = range(4)


def pack_one_body(wq_ref, wo_ref, *rest):
    vectors, span_ref, one_ref, line_s = rest[:8], rest[8], rest[9], rest[10]
    rows = wq_ref.shape[0]
    groups = rows // 8
    for i in range(4):
        for g in range(groups):
            lines = slice(8 * g, 8 * g + 8)
            one_ref[i * groups + g] = wo_ref[lines, :] if i == 3 else wq_ref[lines, i * D : (i + 1) * D]
    line_s[...] = jnp.zeros_like(line_s)
    for i, ref in enumerate(vectors):
        line_s[i : i + 1, :rows] = ref[...].astype(F32)
    line_s[0:1, SHARE : SHARE + span_ref.shape[1]] = span_ref[...].astype(F32)
    one_ref[4 * groups] = line_s[...].astype(BF)


SHARE = 128


def pack_one(w_qkv, w_out, vectors, span):
    groups = 4 * w_qkv.shape[0] // 8 + 1
    operands = [w_qkv, w_out, *[v[None] for v in vectors], span[None]]
    return pl.pallas_call(
        pack_one_body,
        grid=(1,),
        in_specs=[whole_block(v) for v in operands],
        out_specs=pl.BlockSpec((groups, 8, D), lambda *_: (0, 0, 0)),
        out_shape=jax.ShapeDtypeStruct((groups, 8, D), BF),
        scratch_shapes=[pltpu.VMEM((8, D), F32)],
        compiler_params=params(),
        name="pack_one",
    )(*operands)


def pack_two_body(wi_ref, wb_ref, two_ref):
    rows = wi_ref.shape[0]
    for i in range(4):
        two_ref[i] = wi_ref[:, i * D : (i + 1) * D]
        two_ref[4 + i] = wb_ref[i * rows : (i + 1) * rows]


def pack_two(w_in, w_back):
    rows = w_in.shape[0]
    return pl.pallas_call(
        pack_two_body,
        grid=(1,),
        in_specs=[whole_block(w_in), whole_block(w_back)],
        out_specs=pl.BlockSpec((8, rows, D), lambda *_: (0, 0, 0)),
        out_shape=jax.ShapeDtypeStruct((8, rows, D), BF),
        compiler_params=params(),
        name="pack_two",
    )(w_in, w_back)


def place_body(split, at_ref, *refs):
    outs = 2 if split else 3
    parts, outs, held, sems, out_sems = refs[:8], refs[8 : 8 + outs], refs[8 + outs : -2], refs[-2], refs[-1]
    x, core, z, y = at_ref[0], at_ref[1], at_ref[2], at_ref[3]
    sides = ([], [])
    for i, part in enumerate(parts):
        side, far, other = i >> 2, (i >> 1) & 1, i & 1
        for near in range(2):
            px = (x + (far if side == 0 else near)) % 2
            py = (y + (near if side == 0 else far)) % 2
            pc = (core + other) % 2
            for dz in range(4):
                pz = dz if split else (z + 4 - dz) % 4
                source = part.at[near, dz]
                if side == 0:
                    pairs = [(source, held[0].at[:, px, pc, pz, py])]
                elif split:
                    pairs = [(source, held[1].at[px, pc, pz, py])]
                else:
                    count = held[1].shape[5]
                    pairs = [(source.at[pl.ds(u * count, count)], held[1].at[u, px, pc, pz, py]) for u in range(2)]
                    pairs.append((source.at[2 * count], held[2].at[px, pc, pz, py]))
                for pair in pairs:
                    at = len(sides[0]) + len(sides[1])
                    sides[side].append(pltpu.make_async_copy(*pair, sems.at[at]))
    for side in sides:
        for copy in side:
            copy.start()
    back = []
    for side in range(2):
        for copy in sides[side]:
            copy.wait()
        back.append(pltpu.make_async_copy(held[side], outs[side], out_sems.at[side]))
        back[-1].start()
    if not split:
        shares, vec_ref, rows = held[2], outs[2], D // 32
        span = 4 * rows
        lines = lax.broadcasted_iota(jnp.int32, (8, D), 0)
        lane = lax.broadcasted_iota(jnp.int32, (8, D), 1)
        top, low = jnp.zeros((8, D), F32), jnp.zeros((8, D), F32)
        for i in range(32):
            share = shares[i // 16, i // 8 % 2, i // 2 % 4, i % 2].astype(F32)
            top += pltpu.roll(jnp.where(lane < rows, share, 0.0), i * rows, 1)
            wide = jnp.where((lane >= SHARE) & (lane < SHARE + span), share, 0.0)
            wide = pltpu.roll(wide, (i % 8 * span - SHARE) % D, 1)
            low += jnp.where(lines == i // 8, jnp.broadcast_to(wide[:1], (8, D)), 0.0)
        vec_ref[...] = jnp.concatenate([top, low, jnp.zeros((8, D), F32)], axis=0)
    for copy in back:
        copy.wait()


def place(at, parts, split):
    rows = parts[0].shape[-2]
    if split:
        shapes = [(4, 2, 2, 4, 2, rows, D), (2, 2, 4, 2, 4, rows, D)]
    else:
        shapes = [(2, 2, 2, 4, 2, rows, D), (2, 2, 2, 4, 2, rows // 8, 8, D)]
    held = [pltpu.VMEM(shape, BF) for shape in shapes]
    out_specs = [ANY, ANY]
    out_shape = [jax.ShapeDtypeStruct(shape, BF) for shape in shapes]
    if not split:
        held.append(pltpu.VMEM((2, 2, 4, 2, 8, D), BF))
        out_specs.append(pl.BlockSpec((24, D), lambda *_: (0, 0)))
        out_shape.append(jax.ShapeDtypeStruct((24, D), F32))
    return pl.pallas_call(
        lambda *refs: place_body(split, *refs),
        grid_spec=pltpu.PrefetchScalarGridSpec(
            num_scalar_prefetch=1,
            grid=(1,),
            in_specs=[ANY] * 8,
            out_specs=out_specs,
            scratch_shapes=held + [pltpu.SemaphoreType.DMA((64 if split else 128,)), pltpu.SemaphoreType.DMA((2,))],
        ),
        out_shape=out_shape,
        compiler_params=params(),
        cost_estimate=cost(6),
        name="place",
    )(at, *parts)


def after(value, *others):
    return lax.optimization_barrier((value, *others))[0]


class Gather:
    def __init__(self, grid, packet, first, at_once):
        self.grid, self.first = grid, first
        if at_once:
            self.ring = grid.trade(jnp.broadcast_to(packet, (4,) + packet.shape))
        else:
            self.ring = jnp.stack([packet] + [grid.send(packet, Z, k) for k in range(1, 4)])

    def one(self, *others):
        ring = after(self.ring, *others)
        self.line = [ring[:, : self.first], ring[:, self.first :]]
        if ring.shape[2] == 8:
            self.line[0] = self.line[0].reshape(4, 2, -1, D)
        self.came = [self.grid.send(v, d) for v, d in zip(self.line, (Y, X))]

    def two(self, *others):
        held = lax.optimization_barrier((*self.line, *others))
        self.near = [jnp.stack(pair) for pair in zip(held, self.came)]
        self.far = [self.grid.send(v, d) for v, d in zip(self.near, (X, Y))]
        self.near_core = [self.grid.send(v, CORE) for v in self.near]

    def parts(self, *others):
        far = lax.optimization_barrier((*self.far, *others))[:2]
        out = []
        for i in range(2):
            out += [self.near[i], self.near_core[i], far[i], self.grid.send(far[i], CORE)]
        return out


def pick(value, index, dim):
    return lax.dynamic_index_in_dim(value, index, dim, keepdims=False)


def added(a, b, *picks):
    for index, dim in picks:
        a, b = pick(a, index, dim), pick(b, index, dim)
    return (a.astype(F32) + b.astype(F32)).astype(BF)


class Sum:
    def __init__(self, grid, place, order, pair, later=()):
        self.grid, self.place, self.order = grid, place, order
        self.mine, self.came = pair[0], grid.send(after(pair[1], *later), CORE)

    def cut(self, dim, others):
        here = self.place[dim]
        mine = after(self.mine, *others)
        out = added(mine, self.came, (1 - here, 0))
        self.mine = added(mine, self.came, (here, 0))
        self.came = self.grid.send(out, dim)
        return [out, self.mine]

    def one(self, *others):
        return self.cut(self.order[0], others)

    def two(self, *others):
        return self.cut(self.order[1], others)

    def three(self, *others):
        return added(after(self.mine, *others), self.came)


def along_z(grid, lines):
    line = jnp.concatenate(lines, axis=1)
    return line, jnp.sum(grid.trade(line).astype(F32), axis=0)


def staged(grid, lengths, tokens, cotangent, shards):
    w_qkv, bias_q, bias_v, w_out, bias_out, gain_one, shift_one, w_in, bias_in, w_back, bias_back, gain_two, shift_two = shards
    rows, span = bias_q.shape[0], bias_in.shape[0]
    where = grid.place()
    x, core, z, y = where
    device = lax.axis_index(AXES)
    at = jnp.stack([x, core, z, y]).astype(jnp.int32)
    core = core.astype(jnp.int32)[None]
    vectors = [bias_q, bias_v, bias_out, gain_one, shift_one, bias_back, gain_two, shift_two]
    one = Gather(grid, pack_one(w_qkv, w_out, vectors, bias_in), 2 * rows // 8, False)
    packet = after(pack_two(w_in, w_back), one.ring)
    two = Gather(grid, packet, 4, True)
    one.one()
    one.two()
    two.one(*one.far)
    w_a, w_b, vec = place(at, one.parts(), False)
    first = (w_a.reshape(2, grid.count * rows, D), w_b.reshape(2, grid.count * rows, D))
    qkv = qkv_call(tokens, first, vec)
    two.two(vec)
    ctx, lse = attend_call(after(qkv, *two.near), lengths)
    w_in, w_back = place(at, two.parts(ctx), True)
    w_in = w_in.reshape(4, grid.count * rows, D)
    w_back = w_back.reshape(grid.count * span, D)
    z1, h1, g, slope, z2, low = ffn_call(tokens, ctx, first, vec, w_in, w_back, False)
    saved = [(tokens, qkv, lse, ctx, z1, h1, g, slope, z2)]
    weights = (first, w_in, w_back, vec)
    _, low, stored = layer_forward(z2, low, weights, lengths, True)
    saved.append(stored)
    activations = low

    low2, qkv, lse, ctx2, z1, h2, g2, slope, z2 = saved[1]
    e2_2, e1_2, dz1, ea_2, dctx, sums_2 = ffn_back_call(cotangent, z2, z1, slope, w_back, w_in, first, vec)
    e_qkv_2, *lines_2 = attend_back_call(qkv, dctx, lse, lengths, 0, PARTS)
    grad = dx_call(dz1, [e_qkv_2], first, F32)

    low1, qkv, lse, ctx1, z1, h1, g1, slope, z2 = saved[0]
    e2_1, e1_1, dz1, ea_1, dctx, sums_1 = ffn_back_call(grad, z2, z1, slope, w_back, w_in, first, vec)
    count = tokens.shape[0]

    back = wgrad_back_call(core, g2, g1, e2_2, e2_1, rows)
    sum_back = Sum(grid, where, (Y, X), back)
    into = wgrad_in_call(core, after(h2, back[0]), h1, e1_2, e1_1, rows)
    sum_in = Sum(grid, where, (X, Y), into)
    steps = sum_back.one(into[0]) + sum_in.one(into[0])
    e_0, *lines_0 = attend_back_call(qkv, after(dctx, *steps), lse, lengths, 0, 1)
    e_1, *lines_1 = attend_back_call(qkv, after(dctx, e_0), lse, lengths, 1, 1)
    steps = sum_back.two(e_1) + sum_in.two(e_1)
    others = [ctx2, ctx1, ea_2, ea_1]
    group = wgrad_heads_call(core, after(low2, *steps), low1, e_qkv_2, e_0, rows, 0, others, False)
    line, total = along_z(grid, [sum_in.three(group[0]), sum_back.three(group[0])])
    sum_0 = Sum(grid, where, (Y, X), group, [line])
    steps = [line]
    sums = [sums_1, sums_2, *lines_2, *lines_0, *lines_1]
    group = wgrad_heads_call(core, after(low2, *steps), low1, e_qkv_2, e_1, rows, 1, sums, True)
    sum_1 = Sum(grid, where, (X, Y), group)
    steps = sum_0.one(group[0]) + sum_1.one()
    grad = dx_call(after(dz1, *steps), [e_0, e_1], first, BF)
    sum_0.two(grad)
    sum_1.two(grad)
    _, halves = along_z(grid, [sum_0.three(), sum_1.three()])
    total_in, total_back, half_0, half_1 = total[:4], total[4:], halves[:5], halves[5:]

    w_in_grad = total_in.swapaxes(0, 1).reshape(rows, 4 * D)
    w_back_grad = total_back.reshape(4 * rows, D)
    w_qkv_grad = jnp.stack([half_0[:3], half_1[:3]], axis=1).transpose(2, 0, 1, 3).reshape(rows, 3 * D)
    w_out_grad = half_0[3:].swapaxes(0, 1).reshape(rows, D)
    small = jnp.concatenate([half_1[3][: rows // 2], half_1[3][rows // 2 :]], axis=1)
    mine = lax.dynamic_slice(small, (0, device * rows), (8, rows))
    per = D // span
    last = lax.dynamic_slice(small, (8 + device // per, device % per * span), (1, span))[0]
    return activations, grad, w_qkv_grad, w_out_grad, w_in_grad, w_back_grad, [mine[i] for i in range(8)] + [last]


def plain(grid, lengths, tokens, cotangent, shards):
    w_qkv, bias_q, bias_v, w_out, bias_out, gain_one, shift_one, w_in, bias_in, w_back, bias_back, gain_two, shift_two = shards
    vectors = [bias_q, bias_v, bias_out, gain_one, shift_one, bias_back, gain_two, shift_two]

    def whole(v):
        return lax.all_gather(v, AXES, axis=0, tiled=True)

    lines = jnp.stack([whole(v) for v in vectors])
    vec = jnp.concatenate([lines, whole(bias_in).reshape(4, D), jnp.zeros((4, D), BF)], axis=0).astype(F32)

    def blocks(w):
        return w.reshape(D, -1, D).swapaxes(0, 1)

    first = jnp.concatenate([blocks(whole(w_qkv)), whole(w_out)[None]], axis=0)
    first = (first[:2], first[2:])
    w_in, w_back = blocks(whole(w_in)), whole(w_back)
    weights = (first, w_in, w_back, vec)
    value, low = tokens, tokens
    saved = []
    for step in range(APPS):
        value, low, stored = layer_forward(value, low, weights, lengths, step > 0)
        saved.append(stored)
    activations, grad, totals = low, cotangent, None
    for step in reversed(range(APPS)):
        low, qkv, lse, ctx, z1, h1, g, slope, z2 = saved[step]
        e2, e1, dz1, ea, dctx, sums = ffn_back_call(grad, z2, z1, slope, w_back, w_in, first, vec)
        e, *lines = attend_back_call(qkv, dctx, lse, lengths, 0, PARTS)
        grad = dx_call(dz1, [e], first, F32 if step else BF)
        e = e.swapaxes(0, 1).reshape(-1, 3 * D)
        lines = [jnp.sum(v, axis=0) for v in lines]
        grads = [mm(low, e, TN), mm(ctx, ea, TN), mm(h1, e1, TN), mm(g, e2, TN)]
        grads += [jnp.concatenate(lines + [sums[2:]], axis=0)]
        totals = grads if totals is None else [a + b for a, b in zip(totals, grads)]
    lines = list(totals.pop())
    totals += lines[:8] + [jnp.concatenate(lines[8:12])]
    owned = [lax.psum_scatter(v, AXES, scatter_dimension=0, tiled=True) for v in totals]
    return activations, grad, *owned[:4], owned[4:]


def make_local(grid):
    def local(tokens, lengths, *rest):
        run = staged if grid.staged else plain
        activations, grad, w_qkv, w_out, w_in, w_back, lines = run(grid, lengths, tokens, rest[-1], rest[:-1])
        return (
            activations, grad, w_qkv, lines[BQ], lines[BV], w_out, lines[BO], lines[G1], lines[S1],
            w_in, lines[8], w_back, lines[BB], lines[G2], lines[S2],
        )

    return local


def solution(mesh):
    wide, line = P(AXES, None), P(AXES)
    return jax.shard_map(
        make_local(Grid(mesh.shape)),
        mesh=mesh,
        in_specs=(wide, line, wide, line, line, wide, line, line, line, wide, line, wide, line, line, line, wide),
        out_specs=(wide, wide, wide, line, line, wide, line, line, line, wide, line, wide, line, line, line),
        check_vma=False,
    )
```

```python
import jax
import jax.numpy as jnp
from jax import lax
from jax.experimental import pallas as pl
from jax.experimental.pallas import tpu as pltpu
from jax.sharding import PartitionSpec as P

D = 768
HEADS = 12
HEAD_DIM = 64
APPS = 2
PAIR = 2 * HEAD_DIM
AXES = ("dp", "fsdp")
BF = jnp.bfloat16
F32 = jnp.float32
NN = (((1,), (0,)), ((), ()))
NT = (((1,), (1,)), ((), ()))
TN = (((0,), (0,)), ((), ()))
VMEM = 56 * 2**20
BQ, BV, BO, G1, S1, BB, G2, S2 = range(8)


def mm(left, right, dims):
    return lax.dot_general(left, right, dims, preferred_element_type=F32)


def params(limit=VMEM):
    return pltpu.CompilerParams(vmem_limit_bytes=limit)


def cost(micros):
    return pl.CostEstimate(flops=int(micros * 2e8), bytes_accessed=int(micros * 1e5), transcendentals=0)


def once(shape, index):
    return pl.BlockSpec(shape, index, pipeline_mode=pl.Buffered(1))


def whole_block(v):
    return pl.BlockSpec(v.shape, lambda *_: (0,) * v.ndim)


def normed(z):
    centered = z - jnp.mean(z, axis=-1, keepdims=True)
    root = lax.rsqrt(jnp.mean(centered * centered, axis=-1, keepdims=True) + 1e-12)
    return centered * root, root


def normed_back(n, root, e):
    return root * (e - jnp.mean(e, axis=-1, keepdims=True) - n * jnp.mean(e * n, axis=-1, keepdims=True))


def colsum(v):
    return jnp.sum(v, axis=0, keepdims=True)


def qkv_body(x_ref, a_ref, b_ref, vec_ref, o_ref):
    part = pl.program_id(0)

    @pl.when(part == 0)
    def _():
        o_ref[...] = (mm(x_ref[...], a_ref[0], NN) + vec_ref[BQ : BQ + 1, :]).astype(BF)

    @pl.when(part == 1)
    def _():
        o_ref[...] = mm(x_ref[...], a_ref[0], NN).astype(BF)

    @pl.when(part == 2)
    def _():
        o_ref[...] = (mm(x_ref[...], b_ref[0], NN) + vec_ref[BV : BV + 1, :]).astype(BF)


def qkv_call(x, first, vec):
    rows = x.shape[0]
    return pl.pallas_call(
        qkv_body,
        grid=(3,),
        in_specs=[
            once((rows, D), lambda i: (0, 0)),
            pl.BlockSpec((1, D, D), lambda i: (jnp.minimum(i, 1), 0, 0)),
            once((1, D, D), lambda i: (0, 0, 0)),
            once(vec.shape, lambda i: (0, 0)),
        ],
        out_specs=pl.BlockSpec((rows, D), lambda i: (0, i)),
        out_shape=jax.ShapeDtypeStruct((rows, 3 * D), BF),
        compiler_params=params(),
        cost_estimate=cost(8),
        name="qkv",
    )(x, *first, vec)


def attend_body(seq, pairs, len_ref, q_ref, k_ref, v_ref, o_ref, l_ref):
    count = len_ref[pl.program_id(0)]
    lane = lax.broadcasted_iota(jnp.int32, (seq, PAIR), 1)
    row = lax.broadcasted_iota(jnp.int32, (seq, PAIR), 0)
    mask = jnp.where(row < count, 0.0, -1e30).astype(BF)
    units = [(pr, h) for pr in range(pairs) for h in range(2)]

    def score(unit):
        pr, h = unit
        cols = slice(pr * PAIR, (pr + 1) * PAIR)
        mine = (lane >= HEAD_DIM) == (h == 1)
        spare = lane == HEAD_DIM * (1 - h)
        q = jnp.where(mine, q_ref[:, cols] * BF(0.125), jnp.where(spare, BF(1), BF(0)))
        k = jnp.where(mine, k_ref[:, cols], jnp.where(spare, mask, BF(0)))
        return mm(q, k, NT)

    ahead = score(units[0])
    held = {}
    for i, (pr, h) in enumerate(units):
        s = ahead
        if i + 1 < len(units):
            ahead = score(units[i + 1])
        cols = slice(pr * PAIR, (pr + 1) * PAIR)
        top = jnp.max(s, axis=1, keepdims=True)
        p = jnp.exp(s - top)
        total = jnp.sum(p, axis=1, keepdims=True)
        held[h] = mm(p.astype(BF), v_ref[:, cols], NN) / total
        l_ref[0, pr, h : h + 1, :] = (top + jnp.log(total)).reshape(1, seq)
        if h == 1:
            o_ref[:, cols] = jnp.where(lane < HEAD_DIM, held[0], held[1]).astype(BF)


def attend_call(qkv, lengths, pairs=3):
    rows = qkv.shape[0]
    count = lengths.shape[0]
    seq = rows // count
    groups = D // PAIR // pairs
    wide = PAIR * pairs

    def part(o):
        return pl.BlockSpec((seq, wide), lambda s, p, n: (s, o * groups + p))

    def body(*refs):
        attend_body(seq, pairs, *refs)

    return pl.pallas_call(
        body,
        grid_spec=pltpu.PrefetchScalarGridSpec(
            num_scalar_prefetch=1,
            grid=(count, groups),
            in_specs=[part(0), part(1), part(2)],
            out_specs=[part(0), pl.BlockSpec((1, pairs, 2, seq), lambda s, p, n: (s, p, 0, 0))],
        ),
        out_shape=[
            jax.ShapeDtypeStruct((rows, D), BF),
            jax.ShapeDtypeStruct((count, D // PAIR, 2, seq), F32),
        ],
        compiler_params=params(),
        cost_estimate=cost(13),
        name="attend",
    )(lengths, qkv, qkv, qkv)


def gelu_both(u):
    a = 0.7978845608028654
    c = a + (a * 0.044715) * (u * u)
    s = 0.5 + 0.5 * jnp.tanh(u * c)
    g = u * s
    return g, s + (g * (1.0 - s)) * (6.0 * c - 4.0 * a)


ANY = pl.BlockSpec(memory_space=pl.ANY)


def by_rows(block, width):
    return pl.BlockSpec((block, width), lambda i: (i, 0))


def ffn_body(
    renorm, x_ref, ctx_ref, vec_ref, wo_h, wi_h, wb_h,
    z1_ref, h1_ref, g_ref, slope_ref, z2_ref, y_ref, wo_s, wi_s, wb_s, sems,
):
    step = pl.program_id(0)
    copies = [
        pltpu.make_async_copy(wo_h.at[1], wo_s, sems.at[0]),
        pltpu.make_async_copy(wi_h, wi_s, sems.at[1]),
        pltpu.make_async_copy(wb_h, wb_s, sems.at[2]),
    ]

    @pl.when(step == 0)
    def _():
        for copy in copies:
            copy.start()
        copies[0].wait()

    x = x_ref[...].astype(F32)
    if renorm:
        n, _ = normed(x)
        x = n * vec_ref[G2 : G2 + 1, :] + vec_ref[S2 : S2 + 1, :]
    z1 = x + mm(ctx_ref[...], wo_s[...], NN) + vec_ref[BO : BO + 1, :]
    z1_ref[...] = z1
    n, _ = normed(z1)
    h1 = n * vec_ref[G1 : G1 + 1, :] + vec_ref[S1 : S1 + 1, :]
    low = h1.astype(BF)
    h1_ref[...] = low

    @pl.when(step == 0)
    def _():
        copies[1].wait()
        copies[2].wait()

    units = wi_s.shape[0]

    def up(j):
        return mm(low, wi_s[j], NN) + vec_ref[8 + j : 9 + j, :]

    acc = h1 + vec_ref[BB : BB + 1, :]
    f = up(0)
    for j in range(units):
        ahead = up(j + 1) if j + 1 < units else None
        cols = slice(j * D, (j + 1) * D)
        g, slope = gelu_both(f)
        g = g.astype(BF)
        g_ref[:, cols] = g
        slope_ref[:, cols] = slope.astype(BF)
        acc += mm(g, wb_s[cols, :], NN)
        f = ahead
    z2_ref[...] = acc
    n, _ = normed(acc)
    y_ref[...] = (n * vec_ref[G2 : G2 + 1, :] + vec_ref[S2 : S2 + 1, :]).astype(BF)


def weight_scratch(ff):
    return [
        pltpu.VMEM((D, D), BF),
        pltpu.VMEM((ff // D, D, D), BF),
        pltpu.VMEM((ff, D), BF),
        pltpu.SemaphoreType.DMA((3,)),
    ]


def ffn_call(x, ctx, first, vec, wi, wb, renorm, block=512):
    rows = x.shape[0]
    ff = wb.shape[0]
    line, wide = by_rows(block, D), by_rows(block, ff)
    return pl.pallas_call(
        lambda *refs: ffn_body(renorm, *refs),
        grid=(rows // block,),
        in_specs=[line, line, once(vec.shape, lambda i: (0, 0)), ANY, ANY, ANY],
        out_specs=[line, line, wide, wide, line, line],
        out_shape=[
            jax.ShapeDtypeStruct((rows, D), F32),
            jax.ShapeDtypeStruct((rows, D), BF),
            jax.ShapeDtypeStruct((rows, ff), BF),
            jax.ShapeDtypeStruct((rows, ff), BF),
            jax.ShapeDtypeStruct((rows, D), F32),
            jax.ShapeDtypeStruct((rows, D), BF),
        ],
        scratch_shapes=weight_scratch(ff),
        compiler_params=params(),
        cost_estimate=cost(22),
        name="ffn",
    )(x, ctx, vec, first[1], wi, wb)


def ffn_back_body(
    dy_ref, z2_ref, z1_ref, slope_ref, vec_ref, wb_h, wi_h, wo_h,
    e2_ref, e1_ref, dz1_ref, ea_ref, dctx_ref, sums_ref, wo_s, wi_s, wb_s, sems,
):
    step = pl.program_id(0)
    copies = [
        pltpu.make_async_copy(wb_h, wb_s, sems.at[0]),
        pltpu.make_async_copy(wi_h, wi_s, sems.at[1]),
        pltpu.make_async_copy(wo_h.at[1], wo_s, sems.at[2]),
    ]

    @pl.when(step == 0)
    def _():
        for copy in copies:
            copy.start()
        sums_ref[...] = jnp.zeros_like(sums_ref)

    dy = dy_ref[...].astype(F32)
    n, root = normed(z2_ref[...])
    sums_ref[G2 : G2 + 1, :] += colsum(dy * n)
    sums_ref[S2 : S2 + 1, :] += colsum(dy)
    dz2 = normed_back(n, root, dy * vec_ref[G2 : G2 + 1, :])
    e2 = dz2.astype(BF)
    e2_ref[...] = e2
    sums_ref[BB : BB + 1, :] += colsum(e2.astype(F32))

    @pl.when(step == 0)
    def _():
        for copy in copies:
            copy.wait()

    units = wi_s.shape[0]

    def up(j):
        return mm(e2, wb_s[j * D : (j + 1) * D, :], NT)

    acc = dz2
    f = up(0)
    for j in range(units):
        ahead = up(j + 1) if j + 1 < units else None
        cols = slice(j * D, (j + 1) * D)
        e1 = (f * slope_ref[:, cols].astype(F32)).astype(BF)
        e1_ref[:, cols] = e1
        sums_ref[8 + j : 9 + j, :] += colsum(e1.astype(F32))
        acc += mm(e1, wi_s[j], NT)
        f = ahead
    n, root = normed(z1_ref[...])
    sums_ref[G1 : G1 + 1, :] += colsum(acc * n)
    sums_ref[S1 : S1 + 1, :] += colsum(acc)
    dz1 = normed_back(n, root, acc * vec_ref[G1 : G1 + 1, :])
    dz1_ref[...] = dz1
    ea = dz1.astype(BF)
    ea_ref[...] = ea
    sums_ref[BO : BO + 1, :] += colsum(ea.astype(F32))
    dctx_ref[...] = mm(ea, wo_s[...], NT).astype(BF)


def ffn_back_call(dy, z2, z1, slope, wb, wi, first, vec, block=256):
    rows = dy.shape[0]
    ff = wb.shape[0]
    line, wide = by_rows(block, D), by_rows(block, ff)
    held = once(vec.shape, lambda i: (0, 0))
    return pl.pallas_call(
        ffn_back_body,
        grid=(rows // block,),
        in_specs=[line, line, line, wide, held, ANY, ANY, ANY],
        out_specs=[line, wide, line, line, line, held],
        out_shape=[
            jax.ShapeDtypeStruct((rows, D), BF),
            jax.ShapeDtypeStruct((rows, ff), BF),
            jax.ShapeDtypeStruct((rows, D), F32),
            jax.ShapeDtypeStruct((rows, D), BF),
            jax.ShapeDtypeStruct((rows, D), BF),
            jax.ShapeDtypeStruct(vec.shape, F32),
        ],
        scratch_shapes=weight_scratch(ff),
        compiler_params=params(),
        cost_estimate=cost(24),
        name="ffn_back",
    )(dy, z2, z1, slope, vec, wb, wi, first[1])


def attend_back_body(seq, pairs, len_ref, q_ref, k_ref, v_ref, d_ref, l_ref, e_ref, bq_ref, bv_ref):
    count = len_ref[pl.program_id(0)]
    lane = lax.broadcasted_iota(jnp.int32, (seq, PAIR), 1)
    ok = lax.broadcasted_iota(jnp.int32, (seq, seq), 0) < count
    units = [(pr, h) for pr in range(pairs) for h in range(2)]

    def score(unit):
        pr, h = unit
        cols = slice(pr * PAIR, (pr + 1) * PAIR)
        mine = (lane >= HEAD_DIM) == (h == 1)
        q = jnp.where(mine, q_ref[:, cols] * BF(0.125), BF(0))
        s = jnp.where(ok, mm(k_ref[:, cols], q, NT), -1e30)
        return s, mm(v_ref[:, cols], jnp.where(mine, d_ref[:, cols], BF(0)), NT)

    ahead = score(units[0])
    eq, ek, ev = {}, {}, {}
    for i, (pr, h) in enumerate(units):
        s, dp = ahead
        if i + 1 < len(units):
            ahead = score(units[i + 1])
        cols = slice(pr * PAIR, (pr + 1) * PAIR)
        if h == 0:
            kt = (k_ref[:, cols] * BF(0.125)).T
        p = jnp.exp(s - l_ref[0, pr, h : h + 1, :])
        pd = p * dp
        ds = (pd - p * colsum(pd)).astype(BF)
        ev[h] = mm(p.astype(BF), d_ref[:, cols], NN)
        ek[h] = mm(ds, q_ref[:, cols] * BF(0.125), NN)
        eq[h] = mm(kt[h * HEAD_DIM : (h + 1) * HEAD_DIM], ds, NN)
        if h == 1:
            low = jnp.concatenate([eq[0], eq[1]], axis=0).T.astype(BF)
            e_ref[0, :, cols] = low
            bq_ref[0, :, cols] = colsum(low.astype(F32))
            e_ref[1, :, cols] = jnp.where(lane < HEAD_DIM, ek[0], ek[1]).astype(BF)
            low = jnp.where(lane < HEAD_DIM, ev[0], ev[1]).astype(BF)
            e_ref[2, :, cols] = low
            bv_ref[0, :, cols] = colsum(low.astype(F32))


WIDE = 3 * PAIR
PARTS = D // WIDE


def attend_back_call(qkv, dctx, lse, lengths, start, number):
    rows = qkv.shape[0]
    count = lengths.shape[0]
    seq = rows // count
    pairs = WIDE // PAIR

    def part(o):
        return pl.BlockSpec((seq, WIDE), lambda s, p, n: (s, o * PARTS + start + p))

    def body(*refs):
        attend_back_body(seq, pairs, *refs)

    line = pl.BlockSpec((1, 1, WIDE), lambda s, p, n: (s, 0, p))
    return pl.pallas_call(
        body,
        grid_spec=pltpu.PrefetchScalarGridSpec(
            num_scalar_prefetch=1,
            grid=(count, number),
            in_specs=[
                part(0),
                part(1),
                part(2),
                part(0),
                pl.BlockSpec((1, pairs, 2, seq), lambda s, p, n: (s, start + p, 0, 0)),
            ],
            out_specs=[pl.BlockSpec((3, seq, WIDE), lambda s, p, n: (0, s, p)), line, line],
        ),
        out_shape=[jax.ShapeDtypeStruct((3, rows, number * WIDE), BF)]
        + [jax.ShapeDtypeStruct((count, 1, number * WIDE), F32)] * 2,
        compiler_params=params(),
        cost_estimate=cost(12 * number),
        name="attend_back",
    )(lengths, qkv, qkv, qkv, dctx, lse)


def dx_body(dz1_ref, *rest):
    e_refs, (a_ref, b_ref, o_ref) = rest[:-3], rest[-3:]
    acc = dz1_ref[...]
    for i in range(3):
        at = 0
        for e_ref in e_refs:
            width = e_ref.shape[2]
            w = a_ref[i, :, at : at + width] if i < 2 else b_ref[0, :, at : at + width]
            acc += mm(e_ref[i], w, NT)
            at += width
    o_ref[...] = acc.astype(o_ref.dtype)


def dx_call(dz1, parts, w, dtype, block=512):
    rows = dz1.shape[0]
    line = pl.BlockSpec((block, D), lambda i: (i, 0))
    specs = [pl.BlockSpec((3, block, e.shape[2]), lambda i: (0, i, 0)) for e in parts]
    return pl.pallas_call(
        dx_body,
        grid=(rows // block,),
        in_specs=[line, *specs, once((2, D, D), lambda i: (0, 0, 0)), once((1, D, D), lambda i: (0, 0, 0))],
        out_specs=line,
        out_shape=jax.ShapeDtypeStruct((rows, D), dtype),
        compiler_params=params(),
        cost_estimate=cost(9),
        name="dx",
    )(dz1, *parts, *w)


def deal(acc_s, rows, x_first, core_ref, keep_ref, send_ref):
    part = 8 * rows
    for out, core in ((keep_ref, core_ref[0]), (send_ref, 1 - core_ref[0])):
        for xi in range(2):
            for s in range(8):
                zi, yi = s // 2, s % 2
                start = pl.multiple_of(core * part + (2 * xi * part + s * rows), 8)
                value = acc_s[pl.ds(start, rows), :].astype(BF)
                if x_first:
                    out[xi, yi, zi, 0] = value
                else:
                    out[yi, xi, zi, 0] = value


def packet(rows, units, width):
    spec = pl.BlockSpec((2, 2, 4, 1, rows, width), lambda i, n: (0, 0, 0, i, 0, 0))
    return [spec] * 2, [jax.ShapeDtypeStruct((2, 2, 4, units, rows, width), BF)] * 2


def wgrad_in_call(core, a, c, b, d, rows):
    k, n = b.shape
    held = once((k, D), lambda i, n: (0, 0))
    spec = pl.BlockSpec((k, D), lambda i, n: (0, i))
    out_specs, out_shape = packet(rows, n // D, D)

    def body(core_ref, a_ref, c_ref, b_ref, d_ref, keep_ref, send_ref, acc_s):
        acc_s[...] = mm(a_ref[...], b_ref[...], TN) + mm(c_ref[...], d_ref[...], TN)
        deal(acc_s, rows, True, core_ref, keep_ref, send_ref)

    return pl.pallas_call(
        body,
        grid_spec=pltpu.PrefetchScalarGridSpec(
            num_scalar_prefetch=1,
            grid=(n // D,),
            in_specs=[held, held, spec, spec],
            out_specs=out_specs,
            scratch_shapes=[pltpu.VMEM((D, D), F32)],
        ),
        out_shape=out_shape,
        compiler_params=params(),
        cost_estimate=cost(15),
        name="wgrad_in",
    )(core, a, c, b, d)


def wgrad_heads_call(core, low2, low1, e2, e1, rows, group, others, x_first):
    k = low2.shape[0]
    last = len(others) == 4
    held = once((k, D), lambda i, n: (0, 0))
    spec_2 = pl.BlockSpec((1, k, WIDE), lambda i, n: (jnp.minimum(i, 2), 0, group))
    spec_1 = pl.BlockSpec((1, k, WIDE), lambda i, n: (jnp.minimum(i, 2), 0, 0))
    units = 5 if last else 4
    out_specs, out_shape = packet(rows, units, WIDE)
    if last:
        half = pl.BlockSpec((k, WIDE), lambda i, n: (0, jnp.maximum(i - 3, 0)))
        more = [held, held, half, half]
    else:
        more = [whole_block(v) for v in others]

    def body(core_ref, a_ref, c_ref, b_ref, d_ref, *rest):
        rest, (keep_ref, send_ref, acc_s) = rest[:-3], rest[-3:]
        step = pl.program_id(0)

        @pl.when(step < 3)
        def _():
            acc_s[...] = mm(a_ref[...], b_ref[0], TN) + mm(c_ref[...], d_ref[0], TN)

        if last:

            @pl.when(step >= 3)
            def _():
                acc_s[...] = mm(rest[0][...], rest[2][...], TN) + mm(rest[1][...], rest[3][...], TN)

            deal(acc_s, rows, x_first, core_ref, keep_ref, send_ref)
        else:

            @pl.when(step < 3)
            def _():
                deal(acc_s, rows, x_first, core_ref, keep_ref, send_ref)

            @pl.when(step == 3)
            def _():
                sums = rest[0][...] + rest[1][...]
                small = []
                for g in range(PARTS):
                    cols = slice(g * WIDE, (g + 1) * WIDE)
                    for j in range(2):
                        small.append(colsum(rest[2 + j][:, 0, cols] + rest[4 + 2 * g + j][:, 0, :]))
                    small.append(sums[2 : rows // 2, g * WIDE : (g + 1) * WIDE])
                small = jnp.concatenate(small, axis=0).astype(BF)
                for i in range(16):
                    keep_ref[i // 8, i // 4 % 2, i % 4, 0] = small
                    send_ref[i // 8, i // 4 % 2, i % 4, 0] = small

    return pl.pallas_call(
        body,
        grid_spec=pltpu.PrefetchScalarGridSpec(
            num_scalar_prefetch=1,
            grid=(units,),
            in_specs=[held, held, spec_2, spec_1] + more,
            out_specs=out_specs,
            scratch_shapes=[pltpu.VMEM((D, WIDE), F32)],
        ),
        out_shape=out_shape,
        compiler_params=params(),
        cost_estimate=cost(12),
        name="wgrad_heads",
    )(core, low2, low1, e2, e1, *others)


def wgrad_back_call(core, two, one, e_two, e_one, rows):
    k, ff = two.shape
    block = ff // 8

    def cols(other):
        def index(x, s, n):
            c = 1 - n[0] if other else n[0]
            return (0, (x * 2 + c) * 2 + s)

        return pl.BlockSpec((k, block), index)

    held = once((k, D), lambda x, s, n: (0, 0))
    out = pl.BlockSpec((2, 1, 2, 4, rows, D), lambda x, s, n: (0, x, s, 0, 0, 0))

    def body(core_ref, g2k, g1k, g2s, g1s, e2_ref, e1_ref, keep_ref, send_ref):
        for a, c, o in ((g2k, g1k, keep_ref), (g2s, g1s, send_ref)):
            acc = mm(a[...], e2_ref[...], TN) + mm(c[...], e1_ref[...], TN)
            for s in range(16):
                o[s // 4 % 2, 0, s // 8, s % 4] = acc[s * rows : (s + 1) * rows].astype(BF)

    return pl.pallas_call(
        body,
        grid_spec=pltpu.PrefetchScalarGridSpec(
            num_scalar_prefetch=1,
            grid=(2, 2),
            in_specs=[cols(False), cols(False), cols(True), cols(True), held, held],
            out_specs=[out, out],
        ),
        out_shape=[jax.ShapeDtypeStruct((2, 2, 4, 4, rows, D), BF)] * 2,
        compiler_params=params(),
        cost_estimate=cost(15),
        name="wgrad_back",
    )(core, two, one, two, one, e_two, e_one)


def layer_forward(x, low, weights, lengths, renorm):
    first, w_in, w_back, vec = weights
    qkv = qkv_call(low, first, vec)
    ctx, lse = attend_call(qkv, lengths)
    z1, h1, g, slope, z2, y = ffn_call(x, ctx, first, vec, w_in, w_back, renorm)
    return z2, y, (low, qkv, lse, ctx, z1, h1, g, slope, z2)


class Grid:
    def __init__(self, sizes):
        self.dp, self.fsdp = sizes["dp"], sizes["fsdp"]
        self.count = self.dp * self.fsdp
        self.x, self.core = self.dp // 2, 2
        self.y = self.fsdp // 4
        self.z = self.fsdp // self.y if self.y else 0
        self.staged = self.x == 2 and self.y == 2

    def place(self):
        dp, fsdp = lax.axis_index("dp"), lax.axis_index("fsdp")
        return dp // 2, dp % 2, fsdp // self.y, fsdp % self.y

    def shift(self, dim, step):
        sizes = (self.x, self.core, self.z, self.y)
        pairs = []
        for i in range(self.count):
            at = [i // (self.core * self.fsdp), i // self.fsdp % self.core, i % self.fsdp // self.y, i % self.y]
            at[dim] = (at[dim] + step) % sizes[dim]
            pairs.append((i, ((at[0] * self.core + at[1]) * self.z + at[2]) * self.y + at[3]))
        return pairs

    def send(self, value, dim, step=1):
        return lax.ppermute(value, AXES, self.shift(dim, step))

    def trade(self, value):
        groups = [[z * self.y + y for z in range(self.z)] for y in range(self.y)]
        return lax.all_to_all(value, "fsdp", 0, 0, tiled=True, axis_index_groups=groups)


X, CORE, Z, Y = range(4)


def pack_one_body(wq_ref, wo_ref, *rest):
    vectors, span_ref, one_ref, line_s = rest[:8], rest[8], rest[9], rest[10]
    rows = wq_ref.shape[0]
    groups = rows // 8
    for i in range(4):
        for g in range(groups):
            lines = slice(8 * g, 8 * g + 8)
            one_ref[i * groups + g] = wo_ref[lines, :] if i == 3 else wq_ref[lines, i * D : (i + 1) * D]
    line_s[...] = jnp.zeros_like(line_s)
    for i, ref in enumerate(vectors):
        line_s[i : i + 1, :rows] = ref[...].astype(F32)
    line_s[0:1, SHARE : SHARE + span_ref.shape[1]] = span_ref[...].astype(F32)
    one_ref[4 * groups] = line_s[...].astype(BF)


SHARE = 128


def pack_one(w_qkv, w_out, vectors, span):
    groups = 4 * w_qkv.shape[0] // 8 + 1
    operands = [w_qkv, w_out, *[v[None] for v in vectors], span[None]]
    return pl.pallas_call(
        pack_one_body,
        grid=(1,),
        in_specs=[whole_block(v) for v in operands],
        out_specs=pl.BlockSpec((groups, 8, D), lambda *_: (0, 0, 0)),
        out_shape=jax.ShapeDtypeStruct((groups, 8, D), BF),
        scratch_shapes=[pltpu.VMEM((8, D), F32)],
        compiler_params=params(),
        name="pack_one",
    )(*operands)


def pack_two_body(wi_ref, wb_ref, two_ref):
    rows = wi_ref.shape[0]
    for i in range(4):
        two_ref[i] = wi_ref[:, i * D : (i + 1) * D]
        two_ref[4 + i] = wb_ref[i * rows : (i + 1) * rows]


def pack_two(w_in, w_back):
    rows = w_in.shape[0]
    return pl.pallas_call(
        pack_two_body,
        grid=(1,),
        in_specs=[whole_block(w_in), whole_block(w_back)],
        out_specs=pl.BlockSpec((8, rows, D), lambda *_: (0, 0, 0)),
        out_shape=jax.ShapeDtypeStruct((8, rows, D), BF),
        compiler_params=params(),
        name="pack_two",
    )(w_in, w_back)


def place_body(split, at_ref, *refs):
    outs = 2 if split else 3
    parts, outs, held, sems, out_sems = refs[:8], refs[8 : 8 + outs], refs[8 + outs : -2], refs[-2], refs[-1]
    x, core, z, y = at_ref[0], at_ref[1], at_ref[2], at_ref[3]
    sides = ([], [])
    for i, part in enumerate(parts):
        side, far, other = i >> 2, (i >> 1) & 1, i & 1
        for near in range(2):
            px = (x + (far if side == 0 else near)) % 2
            py = (y + (near if side == 0 else far)) % 2
            pc = (core + other) % 2
            for dz in range(4):
                pz = dz if split else (z + 4 - dz) % 4
                source = part.at[near, dz]
                if side == 0:
                    pairs = [(source, held[0].at[:, px, pc, pz, py])]
                elif split:
                    pairs = [(source, held[1].at[px, pc, pz, py])]
                else:
                    count = held[1].shape[5]
                    pairs = [(source.at[pl.ds(u * count, count)], held[1].at[u, px, pc, pz, py]) for u in range(2)]
                    pairs.append((source.at[2 * count], held[2].at[px, pc, pz, py]))
                for pair in pairs:
                    at = len(sides[0]) + len(sides[1])
                    sides[side].append(pltpu.make_async_copy(*pair, sems.at[at]))
    for side in sides:
        for copy in side:
            copy.start()
    back = []
    for side in range(2):
        for copy in sides[side]:
            copy.wait()
        back.append(pltpu.make_async_copy(held[side], outs[side], out_sems.at[side]))
        back[-1].start()
    if not split:
        shares, vec_ref, rows = held[2], outs[2], D // 32
        span = 4 * rows
        lines = lax.broadcasted_iota(jnp.int32, (8, D), 0)
        lane = lax.broadcasted_iota(jnp.int32, (8, D), 1)
        top, low = jnp.zeros((8, D), F32), jnp.zeros((8, D), F32)
        for i in range(32):
            share = shares[i // 16, i // 8 % 2, i // 2 % 4, i % 2].astype(F32)
            top += pltpu.roll(jnp.where(lane < rows, share, 0.0), i * rows, 1)
            wide = jnp.where((lane >= SHARE) & (lane < SHARE + span), share, 0.0)
            wide = pltpu.roll(wide, (i % 8 * span - SHARE) % D, 1)
            low += jnp.where(lines == i // 8, jnp.broadcast_to(wide[:1], (8, D)), 0.0)
        vec_ref[...] = jnp.concatenate([top, low, jnp.zeros((8, D), F32)], axis=0)
    for copy in back:
        copy.wait()


def place(at, parts, split):
    rows = parts[0].shape[-2]
    if split:
        shapes = [(4, 2, 2, 4, 2, rows, D), (2, 2, 4, 2, 4, rows, D)]
    else:
        shapes = [(2, 2, 2, 4, 2, rows, D), (2, 2, 2, 4, 2, rows // 8, 8, D)]
    held = [pltpu.VMEM(shape, BF) for shape in shapes]
    out_specs = [ANY, ANY]
    out_shape = [jax.ShapeDtypeStruct(shape, BF) for shape in shapes]
    if not split:
        held.append(pltpu.VMEM((2, 2, 4, 2, 8, D), BF))
        out_specs.append(pl.BlockSpec((24, D), lambda *_: (0, 0)))
        out_shape.append(jax.ShapeDtypeStruct((24, D), F32))
    return pl.pallas_call(
        lambda *refs: place_body(split, *refs),
        grid_spec=pltpu.PrefetchScalarGridSpec(
            num_scalar_prefetch=1,
            grid=(1,),
            in_specs=[ANY] * 8,
            out_specs=out_specs,
            scratch_shapes=held + [pltpu.SemaphoreType.DMA((64 if split else 128,)), pltpu.SemaphoreType.DMA((2,))],
        ),
        out_shape=out_shape,
        compiler_params=params(),
        cost_estimate=cost(6),
        name="place",
    )(at, *parts)


def after(value, *others):
    return lax.optimization_barrier((value, *others))[0]


class Gather:
    def __init__(self, grid, packet, first, at_once):
        self.grid, self.first = grid, first
        if at_once:
            self.ring = grid.trade(jnp.broadcast_to(packet, (4,) + packet.shape))
        else:
            self.ring = jnp.stack([packet] + [grid.send(packet, Z, k) for k in range(1, 4)])

    def one(self, *others):
        ring = after(self.ring, *others)
        self.line = [ring[:, : self.first], ring[:, self.first :]]
        if ring.shape[2] == 8:
            self.line[0] = self.line[0].reshape(4, 2, -1, D)
        self.came = [self.grid.send(v, d) for v, d in zip(self.line, (Y, X))]

    def two(self, *others):
        held = lax.optimization_barrier((*self.line, *others))
        self.near = [jnp.stack(pair) for pair in zip(held, self.came)]
        self.far = [self.grid.send(v, d) for v, d in zip(self.near, (X, Y))]
        self.near_core = [self.grid.send(v, CORE) for v in self.near]

    def parts(self, *others):
        far = lax.optimization_barrier((*self.far, *others))[:2]
        out = []
        for i in range(2):
            out += [self.near[i], self.near_core[i], far[i], self.grid.send(far[i], CORE)]
        return out


def pick(value, index, dim):
    return lax.dynamic_index_in_dim(value, index, dim, keepdims=False)


def added(a, b, *picks):
    for index, dim in picks:
        a, b = pick(a, index, dim), pick(b, index, dim)
    return (a.astype(F32) + b.astype(F32)).astype(BF)


class Sum:
    def __init__(self, grid, place, order, pair, later=()):
        self.grid, self.place, self.order = grid, place, order
        self.mine, self.came = pair[0], grid.send(after(pair[1], *later), CORE)

    def cut(self, dim, others):
        here = self.place[dim]
        mine = after(self.mine, *others)
        out = added(mine, self.came, (1 - here, 0))
        self.mine = added(mine, self.came, (here, 0))
        self.came = self.grid.send(out, dim)
        return [out, self.mine]

    def one(self, *others):
        return self.cut(self.order[0], others)

    def two(self, *others):
        return self.cut(self.order[1], others)

    def three(self, *others):
        return added(after(self.mine, *others), self.came)


def along_z(grid, lines):
    line = jnp.concatenate(lines, axis=1)
    return line, jnp.sum(grid.trade(line).astype(F32), axis=0)


def staged(grid, lengths, tokens, cotangent, shards):
    w_qkv, bias_q, bias_v, w_out, bias_out, gain_one, shift_one, w_in, bias_in, w_back, bias_back, gain_two, shift_two = shards
    rows, span = bias_q.shape[0], bias_in.shape[0]
    where = grid.place()
    x, core, z, y = where
    device = lax.axis_index(AXES)
    at = jnp.stack([x, core, z, y]).astype(jnp.int32)
    core = core.astype(jnp.int32)[None]
    vectors = [bias_q, bias_v, bias_out, gain_one, shift_one, bias_back, gain_two, shift_two]
    one = Gather(grid, pack_one(w_qkv, w_out, vectors, bias_in), 2 * rows // 8, False)
    packet = after(pack_two(w_in, w_back), one.ring)
    two = Gather(grid, packet, 4, True)
    one.one()
    one.two()
    two.one(*one.far)
    w_a, w_b, vec = place(at, one.parts(), False)
    first = (w_a.reshape(2, grid.count * rows, D), w_b.reshape(2, grid.count * rows, D))
    qkv = qkv_call(tokens, first, vec)
    two.two(vec)
    ctx, lse = attend_call(after(qkv, *two.near), lengths)
    w_in, w_back = place(at, two.parts(ctx), True)
    w_in = w_in.reshape(4, grid.count * rows, D)
    w_back = w_back.reshape(grid.count * span, D)
    z1, h1, g, slope, z2, low = ffn_call(tokens, ctx, first, vec, w_in, w_back, False)
    saved = [(tokens, qkv, lse, ctx, z1, h1, g, slope, z2)]
    weights = (first, w_in, w_back, vec)
    _, low, stored = layer_forward(z2, low, weights, lengths, True)
    saved.append(stored)
    activations = low

    low2, qkv, lse, ctx2, z1, h2, g2, slope, z2 = saved[1]
    e2_2, e1_2, dz1, ea_2, dctx, sums_2 = ffn_back_call(cotangent, z2, z1, slope, w_back, w_in, first, vec)
    e_qkv_2, *lines_2 = attend_back_call(qkv, dctx, lse, lengths, 0, PARTS)
    grad = dx_call(dz1, [e_qkv_2], first, F32)

    low1, qkv, lse, ctx1, z1, h1, g1, slope, z2 = saved[0]
    e2_1, e1_1, dz1, ea_1, dctx, sums_1 = ffn_back_call(grad, z2, z1, slope, w_back, w_in, first, vec)
    count = tokens.shape[0]

    back = wgrad_back_call(core, g2, g1, e2_2, e2_1, rows)
    sum_back = Sum(grid, where, (Y, X), back)
    into = wgrad_in_call(core, after(h2, back[0]), h1, e1_2, e1_1, rows)
    sum_in = Sum(grid, where, (X, Y), into)
    steps = sum_back.one(into[0])
    steps += sum_in.one(*steps)
    e_0, *lines_0 = attend_back_call(qkv, after(dctx, *steps), lse, lengths, 0, 1)
    e_1, *lines_1 = attend_back_call(qkv, after(dctx, e_0), lse, lengths, 1, 1)
    steps = sum_back.two(e_1) + sum_in.two(e_1)
    others = [ctx2, ctx1, ea_2, ea_1]
    group = wgrad_heads_call(core, after(low2, *steps), low1, e_qkv_2, e_0, rows, 0, others, True)
    line, total = along_z(grid, [sum_in.three(group[0]), sum_back.three(group[0])])
    sum_0 = Sum(grid, where, (X, Y), group, [line])
    steps = [line]
    sums = [sums_1, sums_2, *lines_2, *lines_0, *lines_1]
    group = wgrad_heads_call(core, after(low2, *steps), low1, e_qkv_2, e_1, rows, 1, sums, False)
    sum_1 = Sum(grid, where, (Y, X), group)
    steps = sum_0.one(group[0]) + sum_1.one()
    grad = dx_call(after(dz1, *steps), [e_0, e_1], first, BF)
    sum_0.two(grad)
    sum_1.two(grad)
    _, halves = along_z(grid, [sum_0.three(), sum_1.three()])
    total_in, total_back, half_0, half_1 = total[:4], total[4:], halves[:5], halves[5:]

    w_in_grad = total_in.swapaxes(0, 1).reshape(rows, 4 * D)
    w_back_grad = total_back.reshape(4 * rows, D)
    w_qkv_grad = jnp.stack([half_0[:3], half_1[:3]], axis=1).transpose(2, 0, 1, 3).reshape(rows, 3 * D)
    w_out_grad = half_0[3:].swapaxes(0, 1).reshape(rows, D)
    small = jnp.concatenate([half_1[3][: rows // 2], half_1[3][rows // 2 :]], axis=1)
    mine = lax.dynamic_slice(small, (0, device * rows), (8, rows))
    per = D // span
    last = lax.dynamic_slice(small, (8 + device // per, device % per * span), (1, span))[0]
    return activations, grad, w_qkv_grad, w_out_grad, w_in_grad, w_back_grad, [mine[i] for i in range(8)] + [last]


def plain(grid, lengths, tokens, cotangent, shards):
    w_qkv, bias_q, bias_v, w_out, bias_out, gain_one, shift_one, w_in, bias_in, w_back, bias_back, gain_two, shift_two = shards
    vectors = [bias_q, bias_v, bias_out, gain_one, shift_one, bias_back, gain_two, shift_two]

    def whole(v):
        return lax.all_gather(v, AXES, axis=0, tiled=True)

    lines = jnp.stack([whole(v) for v in vectors])
    vec = jnp.concatenate([lines, whole(bias_in).reshape(4, D), jnp.zeros((4, D), BF)], axis=0).astype(F32)

    def blocks(w):
        return w.reshape(D, -1, D).swapaxes(0, 1)

    first = jnp.concatenate([blocks(whole(w_qkv)), whole(w_out)[None]], axis=0)
    first = (first[:2], first[2:])
    w_in, w_back = blocks(whole(w_in)), whole(w_back)
    weights = (first, w_in, w_back, vec)
    value, low = tokens, tokens
    saved = []
    for step in range(APPS):
        value, low, stored = layer_forward(value, low, weights, lengths, step > 0)
        saved.append(stored)
    activations, grad, totals = low, cotangent, None
    for step in reversed(range(APPS)):
        low, qkv, lse, ctx, z1, h1, g, slope, z2 = saved[step]
        e2, e1, dz1, ea, dctx, sums = ffn_back_call(grad, z2, z1, slope, w_back, w_in, first, vec)
        e, *lines = attend_back_call(qkv, dctx, lse, lengths, 0, PARTS)
        grad = dx_call(dz1, [e], first, F32 if step else BF)
        e = e.swapaxes(0, 1).reshape(-1, 3 * D)
        lines = [jnp.sum(v, axis=0) for v in lines]
        grads = [mm(low, e, TN), mm(ctx, ea, TN), mm(h1, e1, TN), mm(g, e2, TN)]
        grads += [jnp.concatenate(lines + [sums[2:]], axis=0)]
        totals = grads if totals is None else [a + b for a, b in zip(totals, grads)]
    lines = list(totals.pop())
    totals += lines[:8] + [jnp.concatenate(lines[8:12])]
    owned = [lax.psum_scatter(v, AXES, scatter_dimension=0, tiled=True) for v in totals]
    return activations, grad, *owned[:4], owned[4:]


def make_local(grid):
    def local(tokens, lengths, *rest):
        run = staged if grid.staged else plain
        activations, grad, w_qkv, w_out, w_in, w_back, lines = run(grid, lengths, tokens, rest[-1], rest[:-1])
        return (
            activations, grad, w_qkv, lines[BQ], lines[BV], w_out, lines[BO], lines[G1], lines[S1],
            w_in, lines[8], w_back, lines[BB], lines[G2], lines[S2],
        )

    return local


def solution(mesh):
    wide, line = P(AXES, None), P(AXES)
    return jax.shard_map(
        make_local(Grid(mesh.shape)),
        mesh=mesh,
        in_specs=(wide, line, wide, line, line, wide, line, line, line, wide, line, wide, line, line, line, wide),
        out_specs=(wide, wide, wide, line, line, wide, line, line, line, wide, line, wide, line, line, line),
        check_vma=False,
    )
```

```python
import jax
import jax.numpy as jnp
from jax import lax
from jax.experimental import pallas as pl
from jax.experimental.pallas import tpu as pltpu
from jax.sharding import PartitionSpec as P

D = 768
HEADS = 12
HEAD_DIM = 64
APPS = 2
PAIR = 2 * HEAD_DIM
AXES = ("dp", "fsdp")
BF = jnp.bfloat16
F32 = jnp.float32
NN = (((1,), (0,)), ((), ()))
NT = (((1,), (1,)), ((), ()))
TN = (((0,), (0,)), ((), ()))
VMEM = 56 * 2**20
BQ, BV, BO, G1, S1, BB, G2, S2 = range(8)


def mm(left, right, dims):
    return lax.dot_general(left, right, dims, preferred_element_type=F32)


def params(limit=VMEM):
    return pltpu.CompilerParams(vmem_limit_bytes=limit)


def cost(micros):
    return pl.CostEstimate(flops=int(micros * 2e8), bytes_accessed=int(micros * 1e5), transcendentals=0)


def once(shape, index):
    return pl.BlockSpec(shape, index, pipeline_mode=pl.Buffered(1))


def whole_block(v):
    return pl.BlockSpec(v.shape, lambda *_: (0,) * v.ndim)


def normed(z):
    centered = z - jnp.mean(z, axis=-1, keepdims=True)
    root = lax.rsqrt(jnp.mean(centered * centered, axis=-1, keepdims=True) + 1e-12)
    return centered * root, root


def normed_back(n, root, e):
    return root * (e - jnp.mean(e, axis=-1, keepdims=True) - n * jnp.mean(e * n, axis=-1, keepdims=True))


def colsum(v):
    return jnp.sum(v, axis=0, keepdims=True)


def qkv_body(x_ref, a_ref, b_ref, vec_ref, o_ref):
    part = pl.program_id(0)

    @pl.when(part == 0)
    def _():
        o_ref[...] = (mm(x_ref[...], a_ref[0], NN) + vec_ref[BQ : BQ + 1, :]).astype(BF)

    @pl.when(part == 1)
    def _():
        o_ref[...] = mm(x_ref[...], a_ref[0], NN).astype(BF)

    @pl.when(part == 2)
    def _():
        o_ref[...] = (mm(x_ref[...], b_ref[0], NN) + vec_ref[BV : BV + 1, :]).astype(BF)


def qkv_call(x, first, vec):
    rows = x.shape[0]
    return pl.pallas_call(
        qkv_body,
        grid=(3,),
        in_specs=[
            once((rows, D), lambda i: (0, 0)),
            pl.BlockSpec((1, D, D), lambda i: (jnp.minimum(i, 1), 0, 0)),
            once((1, D, D), lambda i: (0, 0, 0)),
            once(vec.shape, lambda i: (0, 0)),
        ],
        out_specs=pl.BlockSpec((rows, D), lambda i: (0, i)),
        out_shape=jax.ShapeDtypeStruct((rows, 3 * D), BF),
        compiler_params=params(),
        cost_estimate=cost(8),
        name="qkv",
    )(x, *first, vec)


def attend_body(seq, pairs, len_ref, q_ref, k_ref, v_ref, o_ref, l_ref):
    count = len_ref[pl.program_id(0)]
    lane = lax.broadcasted_iota(jnp.int32, (seq, PAIR), 1)
    row = lax.broadcasted_iota(jnp.int32, (seq, PAIR), 0)
    mask = jnp.where(row < count, 0.0, -1e30).astype(BF)
    units = [(pr, h) for pr in range(pairs) for h in range(2)]

    def score(unit):
        pr, h = unit
        cols = slice(pr * PAIR, (pr + 1) * PAIR)
        mine = (lane >= HEAD_DIM) == (h == 1)
        spare = lane == HEAD_DIM * (1 - h)
        q = jnp.where(mine, q_ref[:, cols] * BF(0.125), jnp.where(spare, BF(1), BF(0)))
        k = jnp.where(mine, k_ref[:, cols], jnp.where(spare, mask, BF(0)))
        return mm(q, k, NT)

    ahead = score(units[0])
    held = {}
    for i, (pr, h) in enumerate(units):
        s = ahead
        if i + 1 < len(units):
            ahead = score(units[i + 1])
        cols = slice(pr * PAIR, (pr + 1) * PAIR)
        top = jnp.max(s, axis=1, keepdims=True)
        p = jnp.exp(s - top)
        total = jnp.sum(p, axis=1, keepdims=True)
        held[h] = mm(p.astype(BF), v_ref[:, cols], NN) / total
        l_ref[0, pr, h : h + 1, :] = (top + jnp.log(total)).reshape(1, seq)
        if h == 1:
            o_ref[:, cols] = jnp.where(lane < HEAD_DIM, held[0], held[1]).astype(BF)


def attend_call(qkv, lengths, pairs=3):
    rows = qkv.shape[0]
    count = lengths.shape[0]
    seq = rows // count
    groups = D // PAIR // pairs
    wide = PAIR * pairs

    def part(o):
        return pl.BlockSpec((seq, wide), lambda s, p, n: (s, o * groups + p))

    def body(*refs):
        attend_body(seq, pairs, *refs)

    return pl.pallas_call(
        body,
        grid_spec=pltpu.PrefetchScalarGridSpec(
            num_scalar_prefetch=1,
            grid=(count, groups),
            in_specs=[part(0), part(1), part(2)],
            out_specs=[part(0), pl.BlockSpec((1, pairs, 2, seq), lambda s, p, n: (s, p, 0, 0))],
        ),
        out_shape=[
            jax.ShapeDtypeStruct((rows, D), BF),
            jax.ShapeDtypeStruct((count, D // PAIR, 2, seq), F32),
        ],
        compiler_params=params(),
        cost_estimate=cost(13),
        name="attend",
    )(lengths, qkv, qkv, qkv)


def gelu_both(u):
    a = 0.7978845608028654
    c = a + (a * 0.044715) * (u * u)
    s = 0.5 + 0.5 * jnp.tanh(u * c)
    g = u * s
    return g, s + (g * (1.0 - s)) * (6.0 * c - 4.0 * a)


ANY = pl.BlockSpec(memory_space=pl.ANY)


def by_rows(block, width):
    return pl.BlockSpec((block, width), lambda i: (i, 0))


def ffn_body(
    renorm, x_ref, ctx_ref, vec_ref, wo_h, wi_h, wb_h,
    z1_ref, h1_ref, g_ref, slope_ref, z2_ref, y_ref, wo_s, wi_s, wb_s, sems,
):
    step = pl.program_id(0)
    copies = [
        pltpu.make_async_copy(wo_h.at[1], wo_s, sems.at[0]),
        pltpu.make_async_copy(wi_h, wi_s, sems.at[1]),
        pltpu.make_async_copy(wb_h, wb_s, sems.at[2]),
    ]

    @pl.when(step == 0)
    def _():
        for copy in copies:
            copy.start()
        copies[0].wait()

    x = x_ref[...].astype(F32)
    if renorm:
        n, _ = normed(x)
        x = n * vec_ref[G2 : G2 + 1, :] + vec_ref[S2 : S2 + 1, :]
    z1 = x + mm(ctx_ref[...], wo_s[...], NN) + vec_ref[BO : BO + 1, :]
    z1_ref[...] = z1
    n, _ = normed(z1)
    h1 = n * vec_ref[G1 : G1 + 1, :] + vec_ref[S1 : S1 + 1, :]
    low = h1.astype(BF)
    h1_ref[...] = low

    @pl.when(step == 0)
    def _():
        copies[1].wait()
        copies[2].wait()

    units = wi_s.shape[0]

    def up(j):
        return mm(low, wi_s[j], NN) + vec_ref[8 + j : 9 + j, :]

    acc = h1 + vec_ref[BB : BB + 1, :]
    f = up(0)
    for j in range(units):
        ahead = up(j + 1) if j + 1 < units else None
        cols = slice(j * D, (j + 1) * D)
        g, slope = gelu_both(f)
        g = g.astype(BF)
        g_ref[:, cols] = g
        slope_ref[:, cols] = slope.astype(BF)
        acc += mm(g, wb_s[cols, :], NN)
        f = ahead
    z2_ref[...] = acc
    n, _ = normed(acc)
    y_ref[...] = (n * vec_ref[G2 : G2 + 1, :] + vec_ref[S2 : S2 + 1, :]).astype(BF)


def weight_scratch(ff):
    return [
        pltpu.VMEM((D, D), BF),
        pltpu.VMEM((ff // D, D, D), BF),
        pltpu.VMEM((ff, D), BF),
        pltpu.SemaphoreType.DMA((3,)),
    ]


def ffn_call(x, ctx, first, vec, wi, wb, renorm, block=512):
    rows = x.shape[0]
    ff = wb.shape[0]
    line, wide = by_rows(block, D), by_rows(block, ff)
    return pl.pallas_call(
        lambda *refs: ffn_body(renorm, *refs),
        grid=(rows // block,),
        in_specs=[line, line, once(vec.shape, lambda i: (0, 0)), ANY, ANY, ANY],
        out_specs=[line, line, wide, wide, line, line],
        out_shape=[
            jax.ShapeDtypeStruct((rows, D), F32),
            jax.ShapeDtypeStruct((rows, D), BF),
            jax.ShapeDtypeStruct((rows, ff), BF),
            jax.ShapeDtypeStruct((rows, ff), BF),
            jax.ShapeDtypeStruct((rows, D), F32),
            jax.ShapeDtypeStruct((rows, D), BF),
        ],
        scratch_shapes=weight_scratch(ff),
        compiler_params=params(),
        cost_estimate=cost(22),
        name="ffn",
    )(x, ctx, vec, first[1], wi, wb)


def ffn_back_body(
    dy_ref, z2_ref, z1_ref, slope_ref, vec_ref, wb_h, wi_h, wo_h,
    e2_ref, e1_ref, dz1_ref, ea_ref, dctx_ref, sums_ref, wo_s, wi_s, wb_s, sems,
):
    step = pl.program_id(0)
    copies = [
        pltpu.make_async_copy(wb_h, wb_s, sems.at[0]),
        pltpu.make_async_copy(wi_h, wi_s, sems.at[1]),
        pltpu.make_async_copy(wo_h.at[1], wo_s, sems.at[2]),
    ]

    @pl.when(step == 0)
    def _():
        for copy in copies:
            copy.start()
        sums_ref[...] = jnp.zeros_like(sums_ref)

    dy = dy_ref[...].astype(F32)
    n, root = normed(z2_ref[...])
    sums_ref[G2 : G2 + 1, :] += colsum(dy * n)
    sums_ref[S2 : S2 + 1, :] += colsum(dy)
    dz2 = normed_back(n, root, dy * vec_ref[G2 : G2 + 1, :])
    e2 = dz2.astype(BF)
    e2_ref[...] = e2
    sums_ref[BB : BB + 1, :] += colsum(e2.astype(F32))

    @pl.when(step == 0)
    def _():
        for copy in copies:
            copy.wait()

    units = wi_s.shape[0]

    def up(j):
        return mm(e2, wb_s[j * D : (j + 1) * D, :], NT)

    acc = dz2
    f = up(0)
    for j in range(units):
        ahead = up(j + 1) if j + 1 < units else None
        cols = slice(j * D, (j + 1) * D)
        e1 = (f * slope_ref[:, cols].astype(F32)).astype(BF)
        e1_ref[:, cols] = e1
        sums_ref[8 + j : 9 + j, :] += colsum(e1.astype(F32))
        acc += mm(e1, wi_s[j], NT)
        f = ahead
    n, root = normed(z1_ref[...])
    sums_ref[G1 : G1 + 1, :] += colsum(acc * n)
    sums_ref[S1 : S1 + 1, :] += colsum(acc)
    dz1 = normed_back(n, root, acc * vec_ref[G1 : G1 + 1, :])
    dz1_ref[...] = dz1
    ea = dz1.astype(BF)
    ea_ref[...] = ea
    sums_ref[BO : BO + 1, :] += colsum(ea.astype(F32))
    dctx_ref[...] = mm(ea, wo_s[...], NT).astype(BF)


def ffn_back_call(dy, z2, z1, slope, wb, wi, first, vec, block=256):
    rows = dy.shape[0]
    ff = wb.shape[0]
    line, wide = by_rows(block, D), by_rows(block, ff)
    held = once(vec.shape, lambda i: (0, 0))
    return pl.pallas_call(
        ffn_back_body,
        grid=(rows // block,),
        in_specs=[line, line, line, wide, held, ANY, ANY, ANY],
        out_specs=[line, wide, line, line, line, held],
        out_shape=[
            jax.ShapeDtypeStruct((rows, D), BF),
            jax.ShapeDtypeStruct((rows, ff), BF),
            jax.ShapeDtypeStruct((rows, D), F32),
            jax.ShapeDtypeStruct((rows, D), BF),
            jax.ShapeDtypeStruct((rows, D), BF),
            jax.ShapeDtypeStruct(vec.shape, F32),
        ],
        scratch_shapes=weight_scratch(ff),
        compiler_params=params(),
        cost_estimate=cost(24),
        name="ffn_back",
    )(dy, z2, z1, slope, vec, wb, wi, first[1])


def attend_back_body(seq, pairs, len_ref, q_ref, k_ref, v_ref, d_ref, l_ref, e_ref, bq_ref, bv_ref):
    count = len_ref[pl.program_id(0)]
    lane = lax.broadcasted_iota(jnp.int32, (seq, PAIR), 1)
    ok = lax.broadcasted_iota(jnp.int32, (seq, seq), 0) < count
    units = [(pr, h) for pr in range(pairs) for h in range(2)]

    def score(unit):
        pr, h = unit
        cols = slice(pr * PAIR, (pr + 1) * PAIR)
        mine = (lane >= HEAD_DIM) == (h == 1)
        q = jnp.where(mine, q_ref[:, cols] * BF(0.125), BF(0))
        s = jnp.where(ok, mm(k_ref[:, cols], q, NT), -1e30)
        return s, mm(v_ref[:, cols], jnp.where(mine, d_ref[:, cols], BF(0)), NT)

    ahead = score(units[0])
    eq, ek, ev = {}, {}, {}
    for i, (pr, h) in enumerate(units):
        s, dp = ahead
        if i + 1 < len(units):
            ahead = score(units[i + 1])
        cols = slice(pr * PAIR, (pr + 1) * PAIR)
        if h == 0:
            kt = (k_ref[:, cols] * BF(0.125)).T
        p = jnp.exp(s - l_ref[0, pr, h : h + 1, :])
        pd = p * dp
        ds = (pd - p * colsum(pd)).astype(BF)
        ev[h] = mm(p.astype(BF), d_ref[:, cols], NN)
        ek[h] = mm(ds, q_ref[:, cols] * BF(0.125), NN)
        eq[h] = mm(kt[h * HEAD_DIM : (h + 1) * HEAD_DIM], ds, NN)
        if h == 1:
            low = jnp.concatenate([eq[0], eq[1]], axis=0).T.astype(BF)
            e_ref[0, :, cols] = low
            bq_ref[0, :, cols] = colsum(low.astype(F32))
            e_ref[1, :, cols] = jnp.where(lane < HEAD_DIM, ek[0], ek[1]).astype(BF)
            low = jnp.where(lane < HEAD_DIM, ev[0], ev[1]).astype(BF)
            e_ref[2, :, cols] = low
            bv_ref[0, :, cols] = colsum(low.astype(F32))


WIDE = 3 * PAIR
PARTS = D // WIDE


def attend_back_call(qkv, dctx, lse, lengths, start, number):
    rows = qkv.shape[0]
    count = lengths.shape[0]
    seq = rows // count
    pairs = WIDE // PAIR

    def part(o):
        return pl.BlockSpec((seq, WIDE), lambda s, p, n: (s, o * PARTS + start + p))

    def body(*refs):
        attend_back_body(seq, pairs, *refs)

    line = pl.BlockSpec((1, 1, WIDE), lambda s, p, n: (s, 0, p))
    return pl.pallas_call(
        body,
        grid_spec=pltpu.PrefetchScalarGridSpec(
            num_scalar_prefetch=1,
            grid=(count, number),
            in_specs=[
                part(0),
                part(1),
                part(2),
                part(0),
                pl.BlockSpec((1, pairs, 2, seq), lambda s, p, n: (s, start + p, 0, 0)),
            ],
            out_specs=[pl.BlockSpec((3, seq, WIDE), lambda s, p, n: (0, s, p)), line, line],
        ),
        out_shape=[jax.ShapeDtypeStruct((3, rows, number * WIDE), BF)]
        + [jax.ShapeDtypeStruct((count, 1, number * WIDE), F32)] * 2,
        compiler_params=params(),
        cost_estimate=cost(12 * number),
        name="attend_back",
    )(lengths, qkv, qkv, qkv, dctx, lse)


def dx_body(dz1_ref, *rest):
    e_refs, (a_ref, b_ref, o_ref) = rest[:-3], rest[-3:]
    acc = dz1_ref[...]
    for i in range(3):
        at = 0
        for e_ref in e_refs:
            width = e_ref.shape[2]
            w = a_ref[i, :, at : at + width] if i < 2 else b_ref[0, :, at : at + width]
            acc += mm(e_ref[i], w, NT)
            at += width
    o_ref[...] = acc.astype(o_ref.dtype)


def dx_call(dz1, parts, w, dtype, block=512):
    rows = dz1.shape[0]
    line = pl.BlockSpec((block, D), lambda i: (i, 0))
    specs = [pl.BlockSpec((3, block, e.shape[2]), lambda i: (0, i, 0)) for e in parts]
    return pl.pallas_call(
        dx_body,
        grid=(rows // block,),
        in_specs=[line, *specs, once((2, D, D), lambda i: (0, 0, 0)), once((1, D, D), lambda i: (0, 0, 0))],
        out_specs=line,
        out_shape=jax.ShapeDtypeStruct((rows, D), dtype),
        compiler_params=params(),
        cost_estimate=cost(9),
        name="dx",
    )(dz1, *parts, *w)


def deal(acc_s, rows, x_first, core_ref, keep_ref, send_ref):
    part = 8 * rows
    for out, core in ((keep_ref, core_ref[0]), (send_ref, 1 - core_ref[0])):
        for xi in range(2):
            for s in range(8):
                zi, yi = s // 2, s % 2
                start = pl.multiple_of(core * part + (2 * xi * part + s * rows), 8)
                value = acc_s[pl.ds(start, rows), :].astype(BF)
                if x_first:
                    out[xi, yi, zi, 0] = value
                else:
                    out[yi, xi, zi, 0] = value


def packet(rows, units, width):
    spec = pl.BlockSpec((2, 2, 4, 1, rows, width), lambda i, n: (0, 0, 0, i, 0, 0))
    return [spec] * 2, [jax.ShapeDtypeStruct((2, 2, 4, units, rows, width), BF)] * 2


def wgrad_in_call(core, a, c, b, d, rows):
    k, n = b.shape
    held = once((k, D), lambda i, n: (0, 0))
    spec = pl.BlockSpec((k, D), lambda i, n: (0, i))
    out_specs, out_shape = packet(rows, n // D, D)

    def body(core_ref, a_ref, c_ref, b_ref, d_ref, keep_ref, send_ref, acc_s):
        acc_s[...] = mm(a_ref[...], b_ref[...], TN) + mm(c_ref[...], d_ref[...], TN)
        deal(acc_s, rows, True, core_ref, keep_ref, send_ref)

    return pl.pallas_call(
        body,
        grid_spec=pltpu.PrefetchScalarGridSpec(
            num_scalar_prefetch=1,
            grid=(n // D,),
            in_specs=[held, held, spec, spec],
            out_specs=out_specs,
            scratch_shapes=[pltpu.VMEM((D, D), F32)],
        ),
        out_shape=out_shape,
        compiler_params=params(),
        cost_estimate=cost(15),
        name="wgrad_in",
    )(core, a, c, b, d)


def wgrad_heads_call(core, low2, low1, e2, e1, rows, group, others, x_first):
    k = low2.shape[0]
    last = len(others) == 4
    held = once((k, D), lambda i, n: (0, 0))
    spec_2 = pl.BlockSpec((1, k, WIDE), lambda i, n: (jnp.minimum(i, 2), 0, group))
    spec_1 = pl.BlockSpec((1, k, WIDE), lambda i, n: (jnp.minimum(i, 2), 0, 0))
    units = 5 if last else 4
    out_specs, out_shape = packet(rows, units, WIDE)
    if last:
        half = pl.BlockSpec((k, WIDE), lambda i, n: (0, jnp.maximum(i - 3, 0)))
        more = [held, held, half, half]
    else:
        more = [whole_block(v) for v in others]

    def body(core_ref, a_ref, c_ref, b_ref, d_ref, *rest):
        rest, (keep_ref, send_ref, acc_s) = rest[:-3], rest[-3:]
        step = pl.program_id(0)

        @pl.when(step < 3)
        def _():
            acc_s[...] = mm(a_ref[...], b_ref[0], TN) + mm(c_ref[...], d_ref[0], TN)

        if last:

            @pl.when(step >= 3)
            def _():
                acc_s[...] = mm(rest[0][...], rest[2][...], TN) + mm(rest[1][...], rest[3][...], TN)

            deal(acc_s, rows, x_first, core_ref, keep_ref, send_ref)
        else:

            @pl.when(step < 3)
            def _():
                deal(acc_s, rows, x_first, core_ref, keep_ref, send_ref)

            @pl.when(step == 3)
            def _():
                sums = rest[0][...] + rest[1][...]
                small = []
                for g in range(PARTS):
                    cols = slice(g * WIDE, (g + 1) * WIDE)
                    for j in range(2):
                        small.append(colsum(rest[2 + j][:, 0, cols] + rest[4 + 2 * g + j][:, 0, :]))
                    small.append(sums[2 : rows // 2, g * WIDE : (g + 1) * WIDE])
                small = jnp.concatenate(small, axis=0).astype(BF)
                for i in range(16):
                    keep_ref[i // 8, i // 4 % 2, i % 4, 0] = small
                    send_ref[i // 8, i // 4 % 2, i % 4, 0] = small

    return pl.pallas_call(
        body,
        grid_spec=pltpu.PrefetchScalarGridSpec(
            num_scalar_prefetch=1,
            grid=(units,),
            in_specs=[held, held, spec_2, spec_1] + more,
            out_specs=out_specs,
            scratch_shapes=[pltpu.VMEM((D, WIDE), F32)],
        ),
        out_shape=out_shape,
        compiler_params=params(),
        cost_estimate=cost(12),
        name="wgrad_heads",
    )(core, low2, low1, e2, e1, *others)


def wgrad_back_call(core, two, one, e_two, e_one, rows):
    k, ff = two.shape
    block = ff // 8

    def cols(other):
        def index(x, s, n):
            c = 1 - n[0] if other else n[0]
            return (0, (x * 2 + c) * 2 + s)

        return pl.BlockSpec((k, block), index)

    held = once((k, D), lambda x, s, n: (0, 0))
    out = pl.BlockSpec((2, 1, 2, 4, rows, D), lambda x, s, n: (0, x, s, 0, 0, 0))

    def body(core_ref, g2k, g1k, g2s, g1s, e2_ref, e1_ref, keep_ref, send_ref):
        for a, c, o in ((g2k, g1k, keep_ref), (g2s, g1s, send_ref)):
            acc = mm(a[...], e2_ref[...], TN) + mm(c[...], e1_ref[...], TN)
            for s in range(16):
                o[s // 4 % 2, 0, s // 8, s % 4] = acc[s * rows : (s + 1) * rows].astype(BF)

    return pl.pallas_call(
        body,
        grid_spec=pltpu.PrefetchScalarGridSpec(
            num_scalar_prefetch=1,
            grid=(2, 2),
            in_specs=[cols(False), cols(False), cols(True), cols(True), held, held],
            out_specs=[out, out],
        ),
        out_shape=[jax.ShapeDtypeStruct((2, 2, 4, 4, rows, D), BF)] * 2,
        compiler_params=params(),
        cost_estimate=cost(15),
        name="wgrad_back",
    )(core, two, one, two, one, e_two, e_one)


def layer_forward(x, low, weights, lengths, renorm):
    first, w_in, w_back, vec = weights
    qkv = qkv_call(low, first, vec)
    ctx, lse = attend_call(qkv, lengths)
    z1, h1, g, slope, z2, y = ffn_call(x, ctx, first, vec, w_in, w_back, renorm)
    return z2, y, (low, qkv, lse, ctx, z1, h1, g, slope, z2)


class Grid:
    def __init__(self, sizes):
        self.dp, self.fsdp = sizes["dp"], sizes["fsdp"]
        self.count = self.dp * self.fsdp
        self.x, self.core = self.dp // 2, 2
        self.y = self.fsdp // 4
        self.z = self.fsdp // self.y if self.y else 0
        self.staged = self.x == 2 and self.y == 2

    def place(self):
        dp, fsdp = lax.axis_index("dp"), lax.axis_index("fsdp")
        return dp // 2, dp % 2, fsdp // self.y, fsdp % self.y

    def shift(self, dim, step):
        sizes = (self.x, self.core, self.z, self.y)
        pairs = []
        for i in range(self.count):
            at = [i // (self.core * self.fsdp), i // self.fsdp % self.core, i % self.fsdp // self.y, i % self.y]
            at[dim] = (at[dim] + step) % sizes[dim]
            pairs.append((i, ((at[0] * self.core + at[1]) * self.z + at[2]) * self.y + at[3]))
        return pairs

    def send(self, value, dim, step=1):
        return lax.ppermute(value, AXES, self.shift(dim, step))

    def trade(self, value):
        groups = [[z * self.y + y for z in range(self.z)] for y in range(self.y)]
        return lax.all_to_all(value, "fsdp", 0, 0, tiled=True, axis_index_groups=groups)


X, CORE, Z, Y = range(4)


def pack_one_body(wq_ref, wo_ref, *rest):
    vectors, span_ref, one_ref, line_s = rest[:8], rest[8], rest[9], rest[10]
    rows = wq_ref.shape[0]
    groups = rows // 8
    for i in range(4):
        for g in range(groups):
            lines = slice(8 * g, 8 * g + 8)
            one_ref[i * groups + g] = wo_ref[lines, :] if i == 3 else wq_ref[lines, i * D : (i + 1) * D]
    line_s[...] = jnp.zeros_like(line_s)
    for i, ref in enumerate(vectors):
        line_s[i : i + 1, :rows] = ref[...].astype(F32)
    line_s[0:1, SHARE : SHARE + span_ref.shape[1]] = span_ref[...].astype(F32)
    one_ref[4 * groups] = line_s[...].astype(BF)


SHARE = 128


def pack_one(w_qkv, w_out, vectors, span):
    groups = 4 * w_qkv.shape[0] // 8 + 1
    operands = [w_qkv, w_out, *[v[None] for v in vectors], span[None]]
    return pl.pallas_call(
        pack_one_body,
        grid=(1,),
        in_specs=[whole_block(v) for v in operands],
        out_specs=pl.BlockSpec((groups, 8, D), lambda *_: (0, 0, 0)),
        out_shape=jax.ShapeDtypeStruct((groups, 8, D), BF),
        scratch_shapes=[pltpu.VMEM((8, D), F32)],
        compiler_params=params(),
        name="pack_one",
    )(*operands)


def pack_two_body(wi_ref, wb_ref, two_ref):
    rows = wi_ref.shape[0]
    for i in range(4):
        for to in range(4):
            two_ref[to, i] = wi_ref[:, i * D : (i + 1) * D]
            two_ref[to, 4 + i] = wb_ref[i * rows : (i + 1) * rows]


def pack_two(w_in, w_back):
    rows = w_in.shape[0]
    return pl.pallas_call(
        pack_two_body,
        grid=(1,),
        in_specs=[whole_block(w_in), whole_block(w_back)],
        out_specs=pl.BlockSpec((4, 8, rows, D), lambda *_: (0, 0, 0, 0)),
        out_shape=jax.ShapeDtypeStruct((4, 8, rows, D), BF),
        compiler_params=params(),
        name="pack_two",
    )(w_in, w_back)


def place_body(split, at_ref, *refs):
    outs = 2 if split else 3
    parts, outs, held, sems, out_sems = refs[:8], refs[8 : 8 + outs], refs[8 + outs : -2], refs[-2], refs[-1]
    x, core, z, y = at_ref[0], at_ref[1], at_ref[2], at_ref[3]
    sides = ([], [])
    for i, part in enumerate(parts):
        side, far, other = i >> 2, (i >> 1) & 1, i & 1
        for near in range(2):
            px = (x + (far if side == 0 else near)) % 2
            py = (y + (near if side == 0 else far)) % 2
            pc = (core + other) % 2
            for dz in range(4):
                pz = dz if split else (z + 4 - dz) % 4
                source = part.at[near, dz]
                if side == 0:
                    pairs = [(source, held[0].at[:, px, pc, pz, py])]
                elif split:
                    pairs = [(source, held[1].at[px, pc, pz, py])]
                else:
                    count = held[1].shape[5]
                    pairs = [(source.at[pl.ds(u * count, count)], held[1].at[u, px, pc, pz, py]) for u in range(2)]
                    pairs.append((source.at[2 * count], held[2].at[px, pc, pz, py]))
                for pair in pairs:
                    at = len(sides[0]) + len(sides[1])
                    sides[side].append(pltpu.make_async_copy(*pair, sems.at[at]))
    for side in sides:
        for copy in side:
            copy.start()
    back = []
    for side in range(2):
        for copy in sides[side]:
            copy.wait()
        back.append(pltpu.make_async_copy(held[side], outs[side], out_sems.at[side]))
        back[-1].start()
    if not split:
        shares, vec_ref, rows = held[2], outs[2], D // 32
        span = 4 * rows
        lines = lax.broadcasted_iota(jnp.int32, (8, D), 0)
        lane = lax.broadcasted_iota(jnp.int32, (8, D), 1)
        top, low = jnp.zeros((8, D), F32), jnp.zeros((8, D), F32)
        for i in range(32):
            share = shares[i // 16, i // 8 % 2, i // 2 % 4, i % 2].astype(F32)
            top += pltpu.roll(jnp.where(lane < rows, share, 0.0), i * rows, 1)
            wide = jnp.where((lane >= SHARE) & (lane < SHARE + span), share, 0.0)
            wide = pltpu.roll(wide, (i % 8 * span - SHARE) % D, 1)
            low += jnp.where(lines == i // 8, jnp.broadcast_to(wide[:1], (8, D)), 0.0)
        vec_ref[...] = jnp.concatenate([top, low, jnp.zeros((8, D), F32)], axis=0)
    for copy in back:
        copy.wait()


def place(at, parts, split):
    rows = parts[0].shape[-2]
    if split:
        shapes = [(4, 2, 2, 4, 2, rows, D), (2, 2, 4, 2, 4, rows, D)]
    else:
        shapes = [(2, 2, 2, 4, 2, rows, D), (2, 2, 2, 4, 2, rows // 8, 8, D)]
    held = [pltpu.VMEM(shape, BF) for shape in shapes]
    out_specs = [ANY, ANY]
    out_shape = [jax.ShapeDtypeStruct(shape, BF) for shape in shapes]
    if not split:
        held.append(pltpu.VMEM((2, 2, 4, 2, 8, D), BF))
        out_specs.append(pl.BlockSpec((24, D), lambda *_: (0, 0)))
        out_shape.append(jax.ShapeDtypeStruct((24, D), F32))
    return pl.pallas_call(
        lambda *refs: place_body(split, *refs),
        grid_spec=pltpu.PrefetchScalarGridSpec(
            num_scalar_prefetch=1,
            grid=(1,),
            in_specs=[ANY] * 8,
            out_specs=out_specs,
            scratch_shapes=held + [pltpu.SemaphoreType.DMA((64 if split else 128,)), pltpu.SemaphoreType.DMA((2,))],
        ),
        out_shape=out_shape,
        compiler_params=params(),
        cost_estimate=cost(6),
        name="place",
    )(at, *parts)


def after(value, *others):
    return lax.optimization_barrier((value, *others))[0]


class Gather:
    def __init__(self, grid, packet, first, at_once, *others):
        self.grid, self.first = grid, first
        if at_once:
            self.ring = grid.trade(after(packet, *others))
        else:
            self.ring = jnp.stack([packet] + [grid.send(packet, Z, k) for k in range(1, 4)])

    def one(self, *others):
        ring = after(self.ring, *others)
        self.line = [ring[:, : self.first], ring[:, self.first :]]
        if ring.shape[2] == 8:
            self.line[0] = self.line[0].reshape(4, 2, -1, D)
        self.came = [self.grid.send(v, d) for v, d in zip(self.line, (Y, X))]

    def two(self, *others):
        held = lax.optimization_barrier((*self.line, *others))
        self.near = [jnp.stack(pair) for pair in zip(held, self.came)]
        self.far = [self.grid.send(v, d) for v, d in zip(self.near, (X, Y))]
        self.near_core = [self.grid.send(v, CORE) for v in self.near]

    def parts(self, *others):
        far = lax.optimization_barrier((*self.far, *others))[:2]
        out = []
        for i in range(2):
            out += [self.near[i], self.near_core[i], far[i], self.grid.send(far[i], CORE)]
        return out


def pick(value, index, dim):
    return lax.dynamic_index_in_dim(value, index, dim, keepdims=False)


def added(a, b, *picks):
    for index, dim in picks:
        a, b = pick(a, index, dim), pick(b, index, dim)
    return (a.astype(F32) + b.astype(F32)).astype(BF)


class Sum:
    def __init__(self, grid, place, order, pair, later=()):
        self.grid, self.place, self.order = grid, place, order
        self.mine, self.came = pair[0], grid.send(after(pair[1], *later), CORE)

    def cut(self, dim, others):
        here = self.place[dim]
        mine = after(self.mine, *others)
        out = added(mine, self.came, (1 - here, 0))
        self.mine = added(mine, self.came, (here, 0))
        self.came = self.grid.send(out, dim)
        return [out, self.mine]

    def one(self, *others):
        return self.cut(self.order[0], others)

    def two(self, *others):
        return self.cut(self.order[1], others)

    def three(self, *others):
        return added(after(self.mine, *others), self.came)


def along_z(grid, lines):
    line = jnp.concatenate(lines, axis=1)
    return line, jnp.sum(grid.trade(line).astype(F32), axis=0)


def staged(grid, lengths, tokens, cotangent, shards):
    w_qkv, bias_q, bias_v, w_out, bias_out, gain_one, shift_one, w_in, bias_in, w_back, bias_back, gain_two, shift_two = shards
    rows, span = bias_q.shape[0], bias_in.shape[0]
    where = grid.place()
    x, core, z, y = where
    device = lax.axis_index(AXES)
    at = jnp.stack([x, core, z, y]).astype(jnp.int32)
    core = core.astype(jnp.int32)[None]
    vectors = [bias_q, bias_v, bias_out, gain_one, shift_one, bias_back, gain_two, shift_two]
    one = Gather(grid, pack_one(w_qkv, w_out, vectors, bias_in), 2 * rows // 8, False)
    two = Gather(grid, pack_two(w_in, w_back), 4, True, one.ring)
    one.one()
    one.two()
    two.one(*one.far)
    w_a, w_b, vec = place(at, one.parts(), False)
    first = (w_a.reshape(2, grid.count * rows, D), w_b.reshape(2, grid.count * rows, D))
    qkv = qkv_call(tokens, first, vec)
    two.two(vec)
    ctx, lse = attend_call(after(qkv, *two.near), lengths)
    w_in, w_back = place(at, two.parts(ctx), True)
    w_in = w_in.reshape(4, grid.count * rows, D)
    w_back = w_back.reshape(grid.count * span, D)
    z1, h1, g, slope, z2, low = ffn_call(tokens, ctx, first, vec, w_in, w_back, False)
    saved = [(tokens, qkv, lse, ctx, z1, h1, g, slope, z2)]
    weights = (first, w_in, w_back, vec)
    _, low, stored = layer_forward(z2, low, weights, lengths, True)
    saved.append(stored)
    activations = low

    low2, qkv, lse, ctx2, z1, h2, g2, slope, z2 = saved[1]
    e2_2, e1_2, dz1, ea_2, dctx, sums_2 = ffn_back_call(cotangent, z2, z1, slope, w_back, w_in, first, vec)
    e_qkv_2, *lines_2 = attend_back_call(qkv, dctx, lse, lengths, 0, PARTS)
    grad = dx_call(dz1, [e_qkv_2], first, F32)

    low1, qkv, lse, ctx1, z1, h1, g1, slope, z2 = saved[0]
    e2_1, e1_1, dz1, ea_1, dctx, sums_1 = ffn_back_call(grad, z2, z1, slope, w_back, w_in, first, vec)
    count = tokens.shape[0]

    back = wgrad_back_call(core, g2, g1, e2_2, e2_1, rows)
    sum_back = Sum(grid, where, (Y, X), back)
    into = wgrad_in_call(core, after(h2, back[0]), h1, e1_2, e1_1, rows)
    sum_in = Sum(grid, where, (X, Y), into)
    steps = sum_back.one(into[0])
    steps += sum_in.one(*steps)
    e_0, *lines_0 = attend_back_call(qkv, after(dctx, *steps), lse, lengths, 0, 1)
    e_1, *lines_1 = attend_back_call(qkv, after(dctx, e_0), lse, lengths, 1, 1)
    steps = sum_back.two(e_1)
    steps += sum_in.two(*steps)
    others = [ctx2, ctx1, ea_2, ea_1]
    group = wgrad_heads_call(core, after(low2, *steps), low1, e_qkv_2, e_0, rows, 0, others, True)
    line, total = along_z(grid, [sum_in.three(group[0]), sum_back.three(group[0])])
    sum_0 = Sum(grid, where, (X, Y), group, [line])
    steps = [line]
    sums = [sums_1, sums_2, *lines_2, *lines_0, *lines_1]
    group = wgrad_heads_call(core, after(low2, *steps), low1, e_qkv_2, e_1, rows, 1, sums, False)
    sum_1 = Sum(grid, where, (Y, X), group)
    steps = sum_0.one(group[0]) + sum_1.one()
    grad = dx_call(after(dz1, *steps), [e_0, e_1], first, BF)
    sum_0.two(grad)
    sum_1.two(grad)
    _, halves = along_z(grid, [sum_0.three(), sum_1.three()])
    total_in, total_back, half_0, half_1 = total[:4], total[4:], halves[:5], halves[5:]

    w_in_grad = total_in.swapaxes(0, 1).reshape(rows, 4 * D)
    w_back_grad = total_back.reshape(4 * rows, D)
    w_qkv_grad = jnp.stack([half_0[:3], half_1[:3]], axis=1).transpose(2, 0, 1, 3).reshape(rows, 3 * D)
    w_out_grad = half_0[3:].swapaxes(0, 1).reshape(rows, D)
    small = jnp.concatenate([half_1[3][: rows // 2], half_1[3][rows // 2 :]], axis=1)
    mine = lax.dynamic_slice(small, (0, device * rows), (8, rows))
    per = D // span
    last = lax.dynamic_slice(small, (8 + device // per, device % per * span), (1, span))[0]
    return activations, grad, w_qkv_grad, w_out_grad, w_in_grad, w_back_grad, [mine[i] for i in range(8)] + [last]


def plain(grid, lengths, tokens, cotangent, shards):
    w_qkv, bias_q, bias_v, w_out, bias_out, gain_one, shift_one, w_in, bias_in, w_back, bias_back, gain_two, shift_two = shards
    vectors = [bias_q, bias_v, bias_out, gain_one, shift_one, bias_back, gain_two, shift_two]

    def whole(v):
        return lax.all_gather(v, AXES, axis=0, tiled=True)

    lines = jnp.stack([whole(v) for v in vectors])
    vec = jnp.concatenate([lines, whole(bias_in).reshape(4, D), jnp.zeros((4, D), BF)], axis=0).astype(F32)

    def blocks(w):
        return w.reshape(D, -1, D).swapaxes(0, 1)

    first = jnp.concatenate([blocks(whole(w_qkv)), whole(w_out)[None]], axis=0)
    first = (first[:2], first[2:])
    w_in, w_back = blocks(whole(w_in)), whole(w_back)
    weights = (first, w_in, w_back, vec)
    value, low = tokens, tokens
    saved = []
    for step in range(APPS):
        value, low, stored = layer_forward(value, low, weights, lengths, step > 0)
        saved.append(stored)
    activations, grad, totals = low, cotangent, None
    for step in reversed(range(APPS)):
        low, qkv, lse, ctx, z1, h1, g, slope, z2 = saved[step]
        e2, e1, dz1, ea, dctx, sums = ffn_back_call(grad, z2, z1, slope, w_back, w_in, first, vec)
        e, *lines = attend_back_call(qkv, dctx, lse, lengths, 0, PARTS)
        grad = dx_call(dz1, [e], first, F32 if step else BF)
        e = e.swapaxes(0, 1).reshape(-1, 3 * D)
        lines = [jnp.sum(v, axis=0) for v in lines]
        grads = [mm(low, e, TN), mm(ctx, ea, TN), mm(h1, e1, TN), mm(g, e2, TN)]
        grads += [jnp.concatenate(lines + [sums[2:]], axis=0)]
        totals = grads if totals is None else [a + b for a, b in zip(totals, grads)]
    lines = list(totals.pop())
    totals += lines[:8] + [jnp.concatenate(lines[8:12])]
    owned = [lax.psum_scatter(v, AXES, scatter_dimension=0, tiled=True) for v in totals]
    return activations, grad, *owned[:4], owned[4:]


def make_local(grid):
    def local(tokens, lengths, *rest):
        run = staged if grid.staged else plain
        activations, grad, w_qkv, w_out, w_in, w_back, lines = run(grid, lengths, tokens, rest[-1], rest[:-1])
        return (
            activations, grad, w_qkv, lines[BQ], lines[BV], w_out, lines[BO], lines[G1], lines[S1],
            w_in, lines[8], w_back, lines[BB], lines[G2], lines[S2],
        )

    return local


def solution(mesh):
    wide, line = P(AXES, None), P(AXES)
    return jax.shard_map(
        make_local(Grid(mesh.shape)),
        mesh=mesh,
        in_specs=(wide, line, wide, line, line, wide, line, line, line, wide, line, wide, line, line, line, wide),
        out_specs=(wide, wide, wide, line, line, wide, line, line, line, wide, line, wide, line, line, line),
        check_vma=False,
    )
```

```python
import jax
import jax.numpy as jnp
from jax import lax
from jax.experimental import pallas as pl
from jax.experimental.pallas import tpu as pltpu
from jax.sharding import PartitionSpec as P

D = 768
HEADS = 12
HEAD_DIM = 64
APPS = 2
PAIR = 2 * HEAD_DIM
AXES = ("dp", "fsdp")
BF = jnp.bfloat16
F32 = jnp.float32
NN = (((1,), (0,)), ((), ()))
NT = (((1,), (1,)), ((), ()))
TN = (((0,), (0,)), ((), ()))
VMEM = 56 * 2**20
BQ, BV, BO, G1, S1, BB, G2, S2 = range(8)


def mm(left, right, dims):
    return lax.dot_general(left, right, dims, preferred_element_type=F32)


def params(limit=VMEM):
    return pltpu.CompilerParams(vmem_limit_bytes=limit)


def cost(micros):
    return pl.CostEstimate(flops=int(micros * 2e8), bytes_accessed=int(micros * 1e5), transcendentals=0)


def once(shape, index):
    return pl.BlockSpec(shape, index, pipeline_mode=pl.Buffered(1))


def whole_block(v):
    return pl.BlockSpec(v.shape, lambda *_: (0,) * v.ndim)


def normed(z):
    centered = z - jnp.mean(z, axis=-1, keepdims=True)
    root = lax.rsqrt(jnp.mean(centered * centered, axis=-1, keepdims=True) + 1e-12)
    return centered * root, root


def normed_back(n, root, e):
    return root * (e - jnp.mean(e, axis=-1, keepdims=True) - n * jnp.mean(e * n, axis=-1, keepdims=True))


def colsum(v):
    return jnp.sum(v, axis=0, keepdims=True)


def qkv_body(x_ref, a_ref, b_ref, vec_ref, o_ref):
    part = pl.program_id(0)

    @pl.when(part == 0)
    def _():
        o_ref[...] = (mm(x_ref[...], a_ref[0], NN) + vec_ref[BQ : BQ + 1, :]).astype(BF)

    @pl.when(part == 1)
    def _():
        o_ref[...] = mm(x_ref[...], a_ref[0], NN).astype(BF)

    @pl.when(part == 2)
    def _():
        o_ref[...] = (mm(x_ref[...], b_ref[0], NN) + vec_ref[BV : BV + 1, :]).astype(BF)


def qkv_call(x, first, vec):
    rows = x.shape[0]
    return pl.pallas_call(
        qkv_body,
        grid=(3,),
        in_specs=[
            once((rows, D), lambda i: (0, 0)),
            pl.BlockSpec((1, D, D), lambda i: (jnp.minimum(i, 1), 0, 0)),
            once((1, D, D), lambda i: (0, 0, 0)),
            once(vec.shape, lambda i: (0, 0)),
        ],
        out_specs=pl.BlockSpec((rows, D), lambda i: (0, i)),
        out_shape=jax.ShapeDtypeStruct((rows, 3 * D), BF),
        compiler_params=params(),
        cost_estimate=cost(8),
        name="qkv",
    )(x, *first, vec)


def attend_body(seq, pairs, len_ref, q_ref, k_ref, v_ref, o_ref, l_ref):
    count = len_ref[pl.program_id(0)]
    lane = lax.broadcasted_iota(jnp.int32, (seq, PAIR), 1)
    row = lax.broadcasted_iota(jnp.int32, (seq, PAIR), 0)
    mask = jnp.where(row < count, 0.0, -1e30).astype(BF)
    units = [(pr, h) for pr in range(pairs) for h in range(2)]

    def score(unit):
        pr, h = unit
        cols = slice(pr * PAIR, (pr + 1) * PAIR)
        mine = (lane >= HEAD_DIM) == (h == 1)
        spare = lane == HEAD_DIM * (1 - h)
        q = jnp.where(mine, q_ref[:, cols] * BF(0.125), jnp.where(spare, BF(1), BF(0)))
        k = jnp.where(mine, k_ref[:, cols], jnp.where(spare, mask, BF(0)))
        return mm(q, k, NT)

    ahead = score(units[0])
    held = {}
    for i, (pr, h) in enumerate(units):
        s = ahead
        if i + 1 < len(units):
            ahead = score(units[i + 1])
        cols = slice(pr * PAIR, (pr + 1) * PAIR)
        top = jnp.max(s, axis=1, keepdims=True)
        p = jnp.exp(s - top)
        total = jnp.sum(p, axis=1, keepdims=True)
        held[h] = mm(p.astype(BF), v_ref[:, cols], NN) / total
        l_ref[0, pr, h : h + 1, :] = (top + jnp.log(total)).reshape(1, seq)
        if h == 1:
            o_ref[:, cols] = jnp.where(lane < HEAD_DIM, held[0], held[1]).astype(BF)


def attend_call(qkv, lengths, pairs=3):
    rows = qkv.shape[0]
    count = lengths.shape[0]
    seq = rows // count
    groups = D // PAIR // pairs
    wide = PAIR * pairs

    def part(o):
        return pl.BlockSpec((seq, wide), lambda s, p, n: (s, o * groups + p))

    def body(*refs):
        attend_body(seq, pairs, *refs)

    return pl.pallas_call(
        body,
        grid_spec=pltpu.PrefetchScalarGridSpec(
            num_scalar_prefetch=1,
            grid=(count, groups),
            in_specs=[part(0), part(1), part(2)],
            out_specs=[part(0), pl.BlockSpec((1, pairs, 2, seq), lambda s, p, n: (s, p, 0, 0))],
        ),
        out_shape=[
            jax.ShapeDtypeStruct((rows, D), BF),
            jax.ShapeDtypeStruct((count, D // PAIR, 2, seq), F32),
        ],
        compiler_params=params(),
        cost_estimate=cost(13),
        name="attend",
    )(lengths, qkv, qkv, qkv)


def gelu_both(u):
    a = 0.7978845608028654
    c = a + (a * 0.044715) * (u * u)
    s = 0.5 + 0.5 * jnp.tanh(u * c)
    g = u * s
    return g, s + (g * (1.0 - s)) * (6.0 * c - 4.0 * a)


ANY = pl.BlockSpec(memory_space=pl.ANY)


def by_rows(block, width):
    return pl.BlockSpec((block, width), lambda i: (i, 0))


def ffn_body(
    renorm, x_ref, ctx_ref, vec_ref, wo_h, wi_h, wb_h,
    z1_ref, h1_ref, g_ref, slope_ref, z2_ref, y_ref, wo_s, wi_s, wb_s, sems,
):
    step = pl.program_id(0)
    copies = [
        pltpu.make_async_copy(wo_h.at[1], wo_s, sems.at[0]),
        pltpu.make_async_copy(wi_h, wi_s, sems.at[1]),
        pltpu.make_async_copy(wb_h, wb_s, sems.at[2]),
    ]

    @pl.when(step == 0)
    def _():
        for copy in copies:
            copy.start()
        copies[0].wait()

    x = x_ref[...].astype(F32)
    if renorm:
        n, _ = normed(x)
        x = n * vec_ref[G2 : G2 + 1, :] + vec_ref[S2 : S2 + 1, :]
    z1 = x + mm(ctx_ref[...], wo_s[...], NN) + vec_ref[BO : BO + 1, :]
    z1_ref[...] = z1
    n, _ = normed(z1)
    h1 = n * vec_ref[G1 : G1 + 1, :] + vec_ref[S1 : S1 + 1, :]
    low = h1.astype(BF)
    h1_ref[...] = low

    @pl.when(step == 0)
    def _():
        copies[1].wait()
        copies[2].wait()

    units = wi_s.shape[0]

    def up(j):
        return mm(low, wi_s[j], NN) + vec_ref[8 + j : 9 + j, :]

    acc = h1 + vec_ref[BB : BB + 1, :]
    f = up(0)
    for j in range(units):
        ahead = up(j + 1) if j + 1 < units else None
        cols = slice(j * D, (j + 1) * D)
        g, slope = gelu_both(f)
        g = g.astype(BF)
        g_ref[:, cols] = g
        slope_ref[:, cols] = slope.astype(BF)
        acc += mm(g, wb_s[cols, :], NN)
        f = ahead
    z2_ref[...] = acc
    n, _ = normed(acc)
    y_ref[...] = (n * vec_ref[G2 : G2 + 1, :] + vec_ref[S2 : S2 + 1, :]).astype(BF)


def weight_scratch(ff):
    return [
        pltpu.VMEM((D, D), BF),
        pltpu.VMEM((ff // D, D, D), BF),
        pltpu.VMEM((ff, D), BF),
        pltpu.SemaphoreType.DMA((3,)),
    ]


def ffn_call(x, ctx, first, vec, wi, wb, renorm, block=512):
    rows = x.shape[0]
    ff = wb.shape[0]
    line, wide = by_rows(block, D), by_rows(block, ff)
    return pl.pallas_call(
        lambda *refs: ffn_body(renorm, *refs),
        grid=(rows // block,),
        in_specs=[line, line, once(vec.shape, lambda i: (0, 0)), ANY, ANY, ANY],
        out_specs=[line, line, wide, wide, line, line],
        out_shape=[
            jax.ShapeDtypeStruct((rows, D), F32),
            jax.ShapeDtypeStruct((rows, D), BF),
            jax.ShapeDtypeStruct((rows, ff), BF),
            jax.ShapeDtypeStruct((rows, ff), BF),
            jax.ShapeDtypeStruct((rows, D), F32),
            jax.ShapeDtypeStruct((rows, D), BF),
        ],
        scratch_shapes=weight_scratch(ff),
        compiler_params=params(),
        cost_estimate=cost(22),
        name="ffn",
    )(x, ctx, vec, first[1], wi, wb)


def ffn_back_body(
    dy_ref, z2_ref, z1_ref, slope_ref, vec_ref, wb_h, wi_h, wo_h,
    e2_ref, e1_ref, dz1_ref, ea_ref, dctx_ref, sums_ref, wo_s, wi_s, wb_s, sems,
):
    step = pl.program_id(0)
    copies = [
        pltpu.make_async_copy(wb_h, wb_s, sems.at[0]),
        pltpu.make_async_copy(wi_h, wi_s, sems.at[1]),
        pltpu.make_async_copy(wo_h.at[1], wo_s, sems.at[2]),
    ]

    @pl.when(step == 0)
    def _():
        for copy in copies:
            copy.start()
        sums_ref[...] = jnp.zeros_like(sums_ref)

    dy = dy_ref[...].astype(F32)
    n, root = normed(z2_ref[...])
    sums_ref[G2 : G2 + 1, :] += colsum(dy * n)
    sums_ref[S2 : S2 + 1, :] += colsum(dy)
    dz2 = normed_back(n, root, dy * vec_ref[G2 : G2 + 1, :])
    e2 = dz2.astype(BF)
    e2_ref[...] = e2
    sums_ref[BB : BB + 1, :] += colsum(e2.astype(F32))

    @pl.when(step == 0)
    def _():
        for copy in copies:
            copy.wait()

    units = wi_s.shape[0]

    def up(j):
        return mm(e2, wb_s[j * D : (j + 1) * D, :], NT)

    acc = dz2
    f = up(0)
    for j in range(units):
        ahead = up(j + 1) if j + 1 < units else None
        cols = slice(j * D, (j + 1) * D)
        e1 = (f * slope_ref[:, cols].astype(F32)).astype(BF)
        e1_ref[:, cols] = e1
        sums_ref[8 + j : 9 + j, :] += colsum(e1.astype(F32))
        acc += mm(e1, wi_s[j], NT)
        f = ahead
    n, root = normed(z1_ref[...])
    sums_ref[G1 : G1 + 1, :] += colsum(acc * n)
    sums_ref[S1 : S1 + 1, :] += colsum(acc)
    dz1 = normed_back(n, root, acc * vec_ref[G1 : G1 + 1, :])
    dz1_ref[...] = dz1
    ea = dz1.astype(BF)
    ea_ref[...] = ea
    sums_ref[BO : BO + 1, :] += colsum(ea.astype(F32))
    dctx_ref[...] = mm(ea, wo_s[...], NT).astype(BF)


def ffn_back_call(dy, z2, z1, slope, wb, wi, first, vec, block=256):
    rows = dy.shape[0]
    ff = wb.shape[0]
    line, wide = by_rows(block, D), by_rows(block, ff)
    held = once(vec.shape, lambda i: (0, 0))
    return pl.pallas_call(
        ffn_back_body,
        grid=(rows // block,),
        in_specs=[line, line, line, wide, held, ANY, ANY, ANY],
        out_specs=[line, wide, line, line, line, held],
        out_shape=[
            jax.ShapeDtypeStruct((rows, D), BF),
            jax.ShapeDtypeStruct((rows, ff), BF),
            jax.ShapeDtypeStruct((rows, D), F32),
            jax.ShapeDtypeStruct((rows, D), BF),
            jax.ShapeDtypeStruct((rows, D), BF),
            jax.ShapeDtypeStruct(vec.shape, F32),
        ],
        scratch_shapes=weight_scratch(ff),
        compiler_params=params(),
        cost_estimate=cost(24),
        name="ffn_back",
    )(dy, z2, z1, slope, vec, wb, wi, first[1])


def attend_back_body(seq, pairs, len_ref, q_ref, k_ref, v_ref, d_ref, l_ref, e_ref, bq_ref, bv_ref):
    count = len_ref[pl.program_id(0)]
    lane = lax.broadcasted_iota(jnp.int32, (seq, PAIR), 1)
    ok = lax.broadcasted_iota(jnp.int32, (seq, seq), 0) < count
    units = [(pr, h) for pr in range(pairs) for h in range(2)]

    def score(unit):
        pr, h = unit
        cols = slice(pr * PAIR, (pr + 1) * PAIR)
        mine = (lane >= HEAD_DIM) == (h == 1)
        q = jnp.where(mine, q_ref[:, cols] * BF(0.125), BF(0))
        s = jnp.where(ok, mm(k_ref[:, cols], q, NT), -1e30)
        return s, mm(v_ref[:, cols], jnp.where(mine, d_ref[:, cols], BF(0)), NT)

    ahead = score(units[0])
    eq, ek, ev = {}, {}, {}
    for i, (pr, h) in enumerate(units):
        s, dp = ahead
        if i + 1 < len(units):
            ahead = score(units[i + 1])
        cols = slice(pr * PAIR, (pr + 1) * PAIR)
        if h == 0:
            kt = (k_ref[:, cols] * BF(0.125)).T
        p = jnp.exp(s - l_ref[0, pr, h : h + 1, :])
        pd = p * dp
        ds = (pd - p * colsum(pd)).astype(BF)
        ev[h] = mm(p.astype(BF), d_ref[:, cols], NN)
        ek[h] = mm(ds, q_ref[:, cols] * BF(0.125), NN)
        eq[h] = mm(kt[h * HEAD_DIM : (h + 1) * HEAD_DIM], ds, NN)
        if h == 1:
            low = jnp.concatenate([eq[0], eq[1]], axis=0).T.astype(BF)
            e_ref[0, :, cols] = low
            bq_ref[0, :, cols] = colsum(low.astype(F32))
            e_ref[1, :, cols] = jnp.where(lane < HEAD_DIM, ek[0], ek[1]).astype(BF)
            low = jnp.where(lane < HEAD_DIM, ev[0], ev[1]).astype(BF)
            e_ref[2, :, cols] = low
            bv_ref[0, :, cols] = colsum(low.astype(F32))


WIDE = 3 * PAIR
PARTS = D // WIDE


def attend_back_call(qkv, dctx, lse, lengths, start, number):
    rows = qkv.shape[0]
    count = lengths.shape[0]
    seq = rows // count
    pairs = WIDE // PAIR

    def part(o):
        return pl.BlockSpec((seq, WIDE), lambda s, p, n: (s, o * PARTS + start + p))

    def body(*refs):
        attend_back_body(seq, pairs, *refs)

    line = pl.BlockSpec((1, 1, WIDE), lambda s, p, n: (s, 0, p))
    return pl.pallas_call(
        body,
        grid_spec=pltpu.PrefetchScalarGridSpec(
            num_scalar_prefetch=1,
            grid=(count, number),
            in_specs=[
                part(0),
                part(1),
                part(2),
                part(0),
                pl.BlockSpec((1, pairs, 2, seq), lambda s, p, n: (s, start + p, 0, 0)),
            ],
            out_specs=[pl.BlockSpec((3, seq, WIDE), lambda s, p, n: (0, s, p)), line, line],
        ),
        out_shape=[jax.ShapeDtypeStruct((3, rows, number * WIDE), BF)]
        + [jax.ShapeDtypeStruct((count, 1, number * WIDE), F32)] * 2,
        compiler_params=params(),
        cost_estimate=cost(12 * number),
        name="attend_back",
    )(lengths, qkv, qkv, qkv, dctx, lse)


def dx_body(dz1_ref, *rest):
    e_refs, (a_ref, b_ref, o_ref) = rest[:-3], rest[-3:]
    acc = dz1_ref[...]
    for i in range(3):
        at = 0
        for e_ref in e_refs:
            width = e_ref.shape[2]
            w = a_ref[i, :, at : at + width] if i < 2 else b_ref[0, :, at : at + width]
            acc += mm(e_ref[i], w, NT)
            at += width
    o_ref[...] = acc.astype(o_ref.dtype)


def dx_call(dz1, parts, w, dtype, block=512):
    rows = dz1.shape[0]
    line = pl.BlockSpec((block, D), lambda i: (i, 0))
    specs = [pl.BlockSpec((3, block, e.shape[2]), lambda i: (0, i, 0)) for e in parts]
    return pl.pallas_call(
        dx_body,
        grid=(rows // block,),
        in_specs=[line, *specs, once((2, D, D), lambda i: (0, 0, 0)), once((1, D, D), lambda i: (0, 0, 0))],
        out_specs=line,
        out_shape=jax.ShapeDtypeStruct((rows, D), dtype),
        compiler_params=params(),
        cost_estimate=cost(9),
        name="dx",
    )(dz1, *parts, *w)


def deal(acc_s, rows, x_first, core_ref, keep_ref, send_ref):
    part = 8 * rows
    for out, core in ((keep_ref, core_ref[0]), (send_ref, 1 - core_ref[0])):
        for xi in range(2):
            for s in range(8):
                zi, yi = s // 2, s % 2
                start = pl.multiple_of(core * part + (2 * xi * part + s * rows), 8)
                value = acc_s[pl.ds(start, rows), :].astype(BF)
                if x_first:
                    out[xi, yi, zi, 0] = value
                else:
                    out[yi, xi, zi, 0] = value


def packet(rows, units, width):
    spec = pl.BlockSpec((2, 2, 4, 1, rows, width), lambda i, n: (0, 0, 0, i, 0, 0))
    return [spec] * 2, [jax.ShapeDtypeStruct((2, 2, 4, units, rows, width), BF)] * 2


def wgrad_in_call(core, a, c, b, d, rows):
    k, n = b.shape
    held = once((k, D), lambda i, n: (0, 0))
    spec = pl.BlockSpec((k, D), lambda i, n: (0, i))
    out_specs, out_shape = packet(rows, n // D, D)

    def body(core_ref, a_ref, c_ref, b_ref, d_ref, keep_ref, send_ref, acc_s):
        acc_s[...] = mm(a_ref[...], b_ref[...], TN) + mm(c_ref[...], d_ref[...], TN)
        deal(acc_s, rows, True, core_ref, keep_ref, send_ref)

    return pl.pallas_call(
        body,
        grid_spec=pltpu.PrefetchScalarGridSpec(
            num_scalar_prefetch=1,
            grid=(n // D,),
            in_specs=[held, held, spec, spec],
            out_specs=out_specs,
            scratch_shapes=[pltpu.VMEM((D, D), F32)],
        ),
        out_shape=out_shape,
        compiler_params=params(),
        cost_estimate=cost(15),
        name="wgrad_in",
    )(core, a, c, b, d)


def wgrad_heads_call(core, low2, low1, e2, e1, rows, group, others, x_first):
    k = low2.shape[0]
    last = len(others) == 4
    held = once((k, D), lambda i, n: (0, 0))
    spec_2 = pl.BlockSpec((1, k, WIDE), lambda i, n: (jnp.minimum(i, 2), 0, group))
    spec_1 = pl.BlockSpec((1, k, WIDE), lambda i, n: (jnp.minimum(i, 2), 0, 0))
    units = 5 if last else 4
    out_specs, out_shape = packet(rows, units, WIDE)
    if last:
        half = pl.BlockSpec((k, WIDE), lambda i, n: (0, jnp.maximum(i - 3, 0)))
        more = [held, held, half, half]
    else:
        more = [whole_block(v) for v in others]

    def body(core_ref, a_ref, c_ref, b_ref, d_ref, *rest):
        rest, (keep_ref, send_ref, acc_s) = rest[:-3], rest[-3:]
        step = pl.program_id(0)

        @pl.when(step < 3)
        def _():
            acc_s[...] = mm(a_ref[...], b_ref[0], TN) + mm(c_ref[...], d_ref[0], TN)

        if last:

            @pl.when(step >= 3)
            def _():
                acc_s[...] = mm(rest[0][...], rest[2][...], TN) + mm(rest[1][...], rest[3][...], TN)

            deal(acc_s, rows, x_first, core_ref, keep_ref, send_ref)
        else:

            @pl.when(step < 3)
            def _():
                deal(acc_s, rows, x_first, core_ref, keep_ref, send_ref)

            @pl.when(step == 3)
            def _():
                sums = rest[0][...] + rest[1][...]
                small = []
                for g in range(PARTS):
                    cols = slice(g * WIDE, (g + 1) * WIDE)
                    for j in range(2):
                        small.append(colsum(rest[2 + j][:, 0, cols] + rest[4 + 2 * g + j][:, 0, :]))
                    small.append(sums[2 : rows // 2, g * WIDE : (g + 1) * WIDE])
                small = jnp.concatenate(small, axis=0).astype(BF)
                for i in range(16):
                    keep_ref[i // 8, i // 4 % 2, i % 4, 0] = small
                    send_ref[i // 8, i // 4 % 2, i % 4, 0] = small

    return pl.pallas_call(
        body,
        grid_spec=pltpu.PrefetchScalarGridSpec(
            num_scalar_prefetch=1,
            grid=(units,),
            in_specs=[held, held, spec_2, spec_1] + more,
            out_specs=out_specs,
            scratch_shapes=[pltpu.VMEM((D, WIDE), F32)],
        ),
        out_shape=out_shape,
        compiler_params=params(),
        cost_estimate=cost(12),
        name="wgrad_heads",
    )(core, low2, low1, e2, e1, *others)


def wgrad_back_call(core, two, one, e_two, e_one, rows):
    k, ff = two.shape
    block = ff // 8

    def cols(other):
        def index(x, s, n):
            c = 1 - n[0] if other else n[0]
            return (0, (x * 2 + c) * 2 + s)

        return pl.BlockSpec((k, block), index)

    held = once((k, D), lambda x, s, n: (0, 0))
    out = pl.BlockSpec((2, 1, 2, 4, rows, D), lambda x, s, n: (0, x, s, 0, 0, 0))

    def body(core_ref, g2k, g1k, g2s, g1s, e2_ref, e1_ref, keep_ref, send_ref):
        for a, c, o in ((g2k, g1k, keep_ref), (g2s, g1s, send_ref)):
            acc = mm(a[...], e2_ref[...], TN) + mm(c[...], e1_ref[...], TN)
            for s in range(16):
                o[s // 4 % 2, 0, s // 8, s % 4] = acc[s * rows : (s + 1) * rows].astype(BF)

    return pl.pallas_call(
        body,
        grid_spec=pltpu.PrefetchScalarGridSpec(
            num_scalar_prefetch=1,
            grid=(2, 2),
            in_specs=[cols(False), cols(False), cols(True), cols(True), held, held],
            out_specs=[out, out],
        ),
        out_shape=[jax.ShapeDtypeStruct((2, 2, 4, 4, rows, D), BF)] * 2,
        compiler_params=params(),
        cost_estimate=cost(15),
        name="wgrad_back",
    )(core, two, one, two, one, e_two, e_one)


def layer_forward(x, low, weights, lengths, renorm):
    first, w_in, w_back, vec = weights
    qkv = qkv_call(low, first, vec)
    ctx, lse = attend_call(qkv, lengths)
    z1, h1, g, slope, z2, y = ffn_call(x, ctx, first, vec, w_in, w_back, renorm)
    return z2, y, (low, qkv, lse, ctx, z1, h1, g, slope, z2)


class Grid:
    def __init__(self, sizes):
        self.dp, self.fsdp = sizes["dp"], sizes["fsdp"]
        self.count = self.dp * self.fsdp
        self.x, self.core = self.dp // 2, 2
        self.y = self.fsdp // 4
        self.z = self.fsdp // self.y if self.y else 0
        self.staged = self.x == 2 and self.y == 2

    def place(self):
        dp, fsdp = lax.axis_index("dp"), lax.axis_index("fsdp")
        return dp // 2, dp % 2, fsdp // self.y, fsdp % self.y

    def shift(self, dim, step):
        sizes = (self.x, self.core, self.z, self.y)
        pairs = []
        for i in range(self.count):
            at = [i // (self.core * self.fsdp), i // self.fsdp % self.core, i % self.fsdp // self.y, i % self.y]
            at[dim] = (at[dim] + step) % sizes[dim]
            pairs.append((i, ((at[0] * self.core + at[1]) * self.z + at[2]) * self.y + at[3]))
        return pairs

    def send(self, value, dim, step=1):
        return lax.ppermute(value, AXES, self.shift(dim, step))

    def trade(self, value):
        groups = [[z * self.y + y for z in range(self.z)] for y in range(self.y)]
        return lax.all_to_all(value, "fsdp", 0, 0, tiled=True, axis_index_groups=groups)


X, CORE, Z, Y = range(4)


def pack_one_body(wq_ref, wo_ref, *rest):
    vectors, span_ref, one_ref, line_s = rest[:8], rest[8], rest[9], rest[10]
    rows = wq_ref.shape[0]
    groups = rows // 8
    for i in range(4):
        for g in range(groups):
            lines = slice(8 * g, 8 * g + 8)
            one_ref[i * groups + g] = wo_ref[lines, :] if i == 3 else wq_ref[lines, i * D : (i + 1) * D]
    line_s[...] = jnp.zeros_like(line_s)
    for i, ref in enumerate(vectors):
        line_s[i : i + 1, :rows] = ref[...].astype(F32)
    line_s[0:1, SHARE : SHARE + span_ref.shape[1]] = span_ref[...].astype(F32)
    one_ref[4 * groups] = line_s[...].astype(BF)


SHARE = 128


def pack_one(w_qkv, w_out, vectors, span):
    groups = 4 * w_qkv.shape[0] // 8 + 1
    operands = [w_qkv, w_out, *[v[None] for v in vectors], span[None]]
    return pl.pallas_call(
        pack_one_body,
        grid=(1,),
        in_specs=[whole_block(v) for v in operands],
        out_specs=pl.BlockSpec((groups, 8, D), lambda *_: (0, 0, 0)),
        out_shape=jax.ShapeDtypeStruct((groups, 8, D), BF),
        scratch_shapes=[pltpu.VMEM((8, D), F32)],
        compiler_params=params(),
        name="pack_one",
    )(*operands)


def pack_two_body(wi_ref, wb_ref, two_ref):
    rows = wi_ref.shape[0]
    for i in range(4):
        for to in range(4):
            two_ref[to, i] = wi_ref[:, i * D : (i + 1) * D]
            two_ref[to, 4 + i] = wb_ref[i * rows : (i + 1) * rows]


def pack_two(w_in, w_back):
    rows = w_in.shape[0]
    return pl.pallas_call(
        pack_two_body,
        grid=(1,),
        in_specs=[whole_block(w_in), whole_block(w_back)],
        out_specs=pl.BlockSpec((4, 8, rows, D), lambda *_: (0, 0, 0, 0)),
        out_shape=jax.ShapeDtypeStruct((4, 8, rows, D), BF),
        compiler_params=params(),
        name="pack_two",
    )(w_in, w_back)


def place_body(split, at_ref, *refs):
    outs = 2 if split else 3
    parts, outs, held, sems, out_sems = refs[:8], refs[8 : 8 + outs], refs[8 + outs : -2], refs[-2], refs[-1]
    x, core, z, y = at_ref[0], at_ref[1], at_ref[2], at_ref[3]
    sides = ([], [])
    for i, part in enumerate(parts):
        side, far, other = i >> 2, (i >> 1) & 1, i & 1
        for near in range(2):
            px = (x + (far if side == 0 else near)) % 2
            py = (y + (near if side == 0 else far)) % 2
            pc = (core + other) % 2
            for dz in range(4):
                pz = dz if split else (z + 4 - dz) % 4
                source = part.at[near, dz]
                if side == 0:
                    pairs = [(source, held[0].at[:, px, pc, pz, py])]
                elif split:
                    pairs = [(source, held[1].at[px, pc, pz, py])]
                else:
                    count = held[1].shape[5]
                    pairs = [(source.at[pl.ds(u * count, count)], held[1].at[u, px, pc, pz, py]) for u in range(2)]
                    pairs.append((source.at[2 * count], held[2].at[px, pc, pz, py]))
                for pair in pairs:
                    at = len(sides[0]) + len(sides[1])
                    sides[side].append(pltpu.make_async_copy(*pair, sems.at[at]))
    for side in sides:
        for copy in side:
            copy.start()
    back = []
    for side in range(2):
        for copy in sides[side]:
            copy.wait()
        back.append(pltpu.make_async_copy(held[side], outs[side], out_sems.at[side]))
        back[-1].start()
    if not split:
        shares, vec_ref, rows = held[2], outs[2], D // 32
        span = 4 * rows
        lines = lax.broadcasted_iota(jnp.int32, (8, D), 0)
        lane = lax.broadcasted_iota(jnp.int32, (8, D), 1)
        top, low = jnp.zeros((8, D), F32), jnp.zeros((8, D), F32)
        for i in range(32):
            share = shares[i // 16, i // 8 % 2, i // 2 % 4, i % 2].astype(F32)
            top += pltpu.roll(jnp.where(lane < rows, share, 0.0), i * rows, 1)
            wide = jnp.where((lane >= SHARE) & (lane < SHARE + span), share, 0.0)
            wide = pltpu.roll(wide, (i % 8 * span - SHARE) % D, 1)
            low += jnp.where(lines == i // 8, jnp.broadcast_to(wide[:1], (8, D)), 0.0)
        vec_ref[...] = jnp.concatenate([top, low, jnp.zeros((8, D), F32)], axis=0)
    for copy in back:
        copy.wait()


def place(at, parts, split):
    rows = parts[0].shape[-2]
    if split:
        shapes = [(4, 2, 2, 4, 2, rows, D), (2, 2, 4, 2, 4, rows, D)]
    else:
        shapes = [(2, 2, 2, 4, 2, rows, D), (2, 2, 2, 4, 2, rows // 8, 8, D)]
    held = [pltpu.VMEM(shape, BF) for shape in shapes]
    out_specs = [ANY, ANY]
    out_shape = [jax.ShapeDtypeStruct(shape, BF) for shape in shapes]
    if not split:
        held.append(pltpu.VMEM((2, 2, 4, 2, 8, D), BF))
        out_specs.append(pl.BlockSpec((24, D), lambda *_: (0, 0)))
        out_shape.append(jax.ShapeDtypeStruct((24, D), F32))
    return pl.pallas_call(
        lambda *refs: place_body(split, *refs),
        grid_spec=pltpu.PrefetchScalarGridSpec(
            num_scalar_prefetch=1,
            grid=(1,),
            in_specs=[ANY] * 8,
            out_specs=out_specs,
            scratch_shapes=held + [pltpu.SemaphoreType.DMA((64 if split else 128,)), pltpu.SemaphoreType.DMA((2,))],
        ),
        out_shape=out_shape,
        compiler_params=params(),
        cost_estimate=cost(6),
        name="place",
    )(at, *parts)


def place_half_body(far, at_ref, *refs):
    parts, (outs, held, sems, out_sems) = refs[:4], (refs[-6:-4], refs[-4:-2], refs[-2], refs[-1])
    x, core, y = at_ref[0], at_ref[1], at_ref[3]
    copies = []
    for i, part in enumerate(parts):
        side, other = i >> 1, i & 1
        pc = (core + other) % 2
        for near in range(2):
            if side == 0:
                target = held[0].at[:, pc, :, (y + near) % 2]
            else:
                target = held[1].at[(x + near) % 2, pc]
            for dz in range(4):
                to = target.at[:, dz] if side == 0 else target.at[dz]
                copies.append(pltpu.make_async_copy(part.at[near, dz], to, sems.at[len(copies)]))
    for copy in copies:
        copy.start()
    for copy in copies:
        copy.wait()
    back = [
        pltpu.make_async_copy(held[0], outs[0].at[:, (x + far) % 2], out_sems.at[0]),
        pltpu.make_async_copy(held[1], outs[1].at[:, :, :, (y + far) % 2], out_sems.at[1]),
    ]
    for copy in back:
        copy.start()
    for copy in back:
        copy.wait()


def place_half(at, parts, far, begun=()):
    rows = parts[0].shape[-2]
    shapes = [(4, 2, 2, 4, 2, rows, D), (2, 2, 4, 2, 4, rows, D)]
    held = [(4, 2, 4, 2, rows, D), (2, 2, 4, 4, rows, D)]
    return pl.pallas_call(
        lambda *refs: place_half_body(far, *refs),
        grid_spec=pltpu.PrefetchScalarGridSpec(
            num_scalar_prefetch=1,
            grid=(1,),
            in_specs=[ANY] * (4 + len(begun)),
            out_specs=[ANY, ANY],
            scratch_shapes=[pltpu.VMEM(shape, BF) for shape in held]
            + [pltpu.SemaphoreType.DMA((32,)), pltpu.SemaphoreType.DMA((2,))],
        ),
        out_shape=[jax.ShapeDtypeStruct(shape, BF) for shape in shapes],
        input_output_aliases={5: 0, 6: 1} if begun else {},
        compiler_params=params(),
        cost_estimate=cost(4),
        name="place_half",
    )(at, *parts, *begun)


def after(value, *others):
    return lax.optimization_barrier((value, *others))[0]


class Gather:
    def __init__(self, grid, packet, first, at_once, *others):
        self.grid, self.first = grid, first
        if at_once:
            self.ring = grid.trade(after(packet, *others))
        else:
            self.ring = jnp.stack([packet] + [grid.send(packet, Z, k) for k in range(1, 4)])

    def one(self, *others):
        ring = after(self.ring, *others)
        self.line = [ring[:, : self.first], ring[:, self.first :]]
        if ring.shape[2] == 8:
            self.line[0] = self.line[0].reshape(4, 2, -1, D)
        self.came = [self.grid.send(v, d) for v, d in zip(self.line, (Y, X))]

    def two(self, *others):
        held = lax.optimization_barrier((*self.line, *others))
        self.near = [jnp.stack(pair) for pair in zip(held, self.came)]
        self.far = [self.grid.send(v, d) for v, d in zip(self.near, (X, Y))]
        self.near_core = [self.grid.send(v, CORE) for v in self.near]

    def parts(self, *others):
        far = lax.optimization_barrier((*self.far, *others))[:2]
        out = []
        for i in range(2):
            out += [self.near[i], self.near_core[i], far[i], self.grid.send(far[i], CORE)]
        return out


def pick(value, index, dim):
    return lax.dynamic_index_in_dim(value, index, dim, keepdims=False)


def added(a, b, *picks):
    for index, dim in picks:
        a, b = pick(a, index, dim), pick(b, index, dim)
    return (a.astype(F32) + b.astype(F32)).astype(BF)


class Sum:
    def __init__(self, grid, place, order, pair, later=()):
        self.grid, self.place, self.order = grid, place, order
        self.mine, self.came = pair[0], grid.send(after(pair[1], *later), CORE)

    def cut(self, dim, others):
        here = self.place[dim]
        mine = after(self.mine, *others)
        out = added(mine, self.came, (1 - here, 0))
        self.mine = added(mine, self.came, (here, 0))
        self.came = self.grid.send(out, dim)
        return [out, self.mine]

    def one(self, *others):
        return self.cut(self.order[0], others)

    def two(self, *others):
        return self.cut(self.order[1], others)

    def three(self, *others):
        return added(after(self.mine, *others), self.came)


def along_z(grid, lines):
    line = jnp.concatenate(lines, axis=1)
    return line, jnp.sum(grid.trade(line).astype(F32), axis=0)


def staged(grid, lengths, tokens, cotangent, shards):
    w_qkv, bias_q, bias_v, w_out, bias_out, gain_one, shift_one, w_in, bias_in, w_back, bias_back, gain_two, shift_two = shards
    rows, span = bias_q.shape[0], bias_in.shape[0]
    where = grid.place()
    x, core, z, y = where
    device = lax.axis_index(AXES)
    at = jnp.stack([x, core, z, y]).astype(jnp.int32)
    core = core.astype(jnp.int32)[None]
    vectors = [bias_q, bias_v, bias_out, gain_one, shift_one, bias_back, gain_two, shift_two]
    one = Gather(grid, pack_one(w_qkv, w_out, vectors, bias_in), 2 * rows // 8, False)
    two = Gather(grid, pack_two(w_in, w_back), 4, True, one.ring)
    one.one()
    one.two()
    two.one(*one.far)
    w_a, w_b, vec = place(at, one.parts(), False)
    first = (w_a.reshape(2, grid.count * rows, D), w_b.reshape(2, grid.count * rows, D))
    qkv = qkv_call(tokens, first, vec)
    two.two(vec)
    ctx, lse = attend_call(after(qkv, *two.near), lengths)
    parts = two.parts(ctx)
    begun = place_half(at, [parts[i] for i in (0, 1, 4, 5)], 0)
    w_in, w_back = place_half(at, [parts[i] for i in (2, 3, 6, 7)], 1, begun)
    w_in = w_in.reshape(4, grid.count * rows, D)
    w_back = w_back.reshape(grid.count * span, D)
    z1, h1, g, slope, z2, low = ffn_call(tokens, ctx, first, vec, w_in, w_back, False)
    saved = [(tokens, qkv, lse, ctx, z1, h1, g, slope, z2)]
    weights = (first, w_in, w_back, vec)
    _, low, stored = layer_forward(z2, low, weights, lengths, True)
    saved.append(stored)
    activations = low

    low2, qkv, lse, ctx2, z1, h2, g2, slope, z2 = saved[1]
    e2_2, e1_2, dz1, ea_2, dctx, sums_2 = ffn_back_call(cotangent, z2, z1, slope, w_back, w_in, first, vec)
    e_qkv_2, *lines_2 = attend_back_call(qkv, dctx, lse, lengths, 0, PARTS)
    grad = dx_call(dz1, [e_qkv_2], first, F32)

    low1, qkv, lse, ctx1, z1, h1, g1, slope, z2 = saved[0]
    e2_1, e1_1, dz1, ea_1, dctx, sums_1 = ffn_back_call(grad, z2, z1, slope, w_back, w_in, first, vec)
    count = tokens.shape[0]

    back = wgrad_back_call(core, g2, g1, e2_2, e2_1, rows)
    sum_back = Sum(grid, where, (Y, X), back)
    into = wgrad_in_call(core, after(h2, back[0]), h1, e1_2, e1_1, rows)
    sum_in = Sum(grid, where, (X, Y), into)
    steps = sum_back.one(into[0])
    steps += sum_in.one(*steps)
    e_0, *lines_0 = attend_back_call(qkv, after(dctx, *steps), lse, lengths, 0, 1)
    e_1, *lines_1 = attend_back_call(qkv, after(dctx, e_0), lse, lengths, 1, 1)
    steps = sum_back.two(e_1)
    steps += sum_in.two(*steps)
    others = [ctx2, ctx1, ea_2, ea_1]
    group = wgrad_heads_call(core, after(low2, *steps), low1, e_qkv_2, e_0, rows, 0, others, True)
    line, total = along_z(grid, [sum_in.three(group[0]), sum_back.three(group[0])])
    sum_0 = Sum(grid, where, (X, Y), group, [line])
    steps = [line]
    sums = [sums_1, sums_2, *lines_2, *lines_0, *lines_1]
    group = wgrad_heads_call(core, after(low2, *steps), low1, e_qkv_2, e_1, rows, 1, sums, False)
    sum_1 = Sum(grid, where, (Y, X), group)
    steps = sum_0.one(group[0]) + sum_1.one()
    grad = dx_call(after(dz1, *steps), [e_0, e_1], first, BF)
    sum_0.two(grad)
    sum_1.two(grad)
    _, halves = along_z(grid, [sum_0.three(), sum_1.three()])
    total_in, total_back, half_0, half_1 = total[:4], total[4:], halves[:5], halves[5:]

    w_in_grad = total_in.swapaxes(0, 1).reshape(rows, 4 * D)
    w_back_grad = total_back.reshape(4 * rows, D)
    w_qkv_grad = jnp.stack([half_0[:3], half_1[:3]], axis=1).transpose(2, 0, 1, 3).reshape(rows, 3 * D)
    w_out_grad = half_0[3:].swapaxes(0, 1).reshape(rows, D)
    small = jnp.concatenate([half_1[3][: rows // 2], half_1[3][rows // 2 :]], axis=1)
    mine = lax.dynamic_slice(small, (0, device * rows), (8, rows))
    per = D // span
    last = lax.dynamic_slice(small, (8 + device // per, device % per * span), (1, span))[0]
    return activations, grad, w_qkv_grad, w_out_grad, w_in_grad, w_back_grad, [mine[i] for i in range(8)] + [last]


def plain(grid, lengths, tokens, cotangent, shards):
    w_qkv, bias_q, bias_v, w_out, bias_out, gain_one, shift_one, w_in, bias_in, w_back, bias_back, gain_two, shift_two = shards
    vectors = [bias_q, bias_v, bias_out, gain_one, shift_one, bias_back, gain_two, shift_two]

    def whole(v):
        return lax.all_gather(v, AXES, axis=0, tiled=True)

    lines = jnp.stack([whole(v) for v in vectors])
    vec = jnp.concatenate([lines, whole(bias_in).reshape(4, D), jnp.zeros((4, D), BF)], axis=0).astype(F32)

    def blocks(w):
        return w.reshape(D, -1, D).swapaxes(0, 1)

    first = jnp.concatenate([blocks(whole(w_qkv)), whole(w_out)[None]], axis=0)
    first = (first[:2], first[2:])
    w_in, w_back = blocks(whole(w_in)), whole(w_back)
    weights = (first, w_in, w_back, vec)
    value, low = tokens, tokens
    saved = []
    for step in range(APPS):
        value, low, stored = layer_forward(value, low, weights, lengths, step > 0)
        saved.append(stored)
    activations, grad, totals = low, cotangent, None
    for step in reversed(range(APPS)):
        low, qkv, lse, ctx, z1, h1, g, slope, z2 = saved[step]
        e2, e1, dz1, ea, dctx, sums = ffn_back_call(grad, z2, z1, slope, w_back, w_in, first, vec)
        e, *lines = attend_back_call(qkv, dctx, lse, lengths, 0, PARTS)
        grad = dx_call(dz1, [e], first, F32 if step else BF)
        e = e.swapaxes(0, 1).reshape(-1, 3 * D)
        lines = [jnp.sum(v, axis=0) for v in lines]
        grads = [mm(low, e, TN), mm(ctx, ea, TN), mm(h1, e1, TN), mm(g, e2, TN)]
        grads += [jnp.concatenate(lines + [sums[2:]], axis=0)]
        totals = grads if totals is None else [a + b for a, b in zip(totals, grads)]
    lines = list(totals.pop())
    totals += lines[:8] + [jnp.concatenate(lines[8:12])]
    owned = [lax.psum_scatter(v, AXES, scatter_dimension=0, tiled=True) for v in totals]
    return activations, grad, *owned[:4], owned[4:]


def make_local(grid):
    def local(tokens, lengths, *rest):
        run = staged if grid.staged else plain
        activations, grad, w_qkv, w_out, w_in, w_back, lines = run(grid, lengths, tokens, rest[-1], rest[:-1])
        return (
            activations, grad, w_qkv, lines[BQ], lines[BV], w_out, lines[BO], lines[G1], lines[S1],
            w_in, lines[8], w_back, lines[BB], lines[G2], lines[S2],
        )

    return local


def solution(mesh):
    wide, line = P(AXES, None), P(AXES)
    return jax.shard_map(
        make_local(Grid(mesh.shape)),
        mesh=mesh,
        in_specs=(wide, line, wide, line, line, wide, line, line, line, wide, line, wide, line, line, line, wide),
        out_specs=(wide, wide, wide, line, line, wide, line, line, line, wide, line, wide, line, line, line),
        check_vma=False,
    )
```
